32 devices in a mesh: dom: 2 (over x), orb: 16 (over z, y, core).
Axes of the slice: x: 2, y: 2, z: 4, core: 2. Of those that a mesh axis runs over, the one named last changes fastest.
Arguments:
- orbitals: float32 [2, 80, 12, 16, 128], P('dom', 'orb'), may hold values from -6 to 6
- potential: float32 [2, 12, 16, 128], P('dom'), may hold values from -3 to 0
- projectors: float32 [4, 8, 512], replicated, may hold values from -0.25 to 0.25
- projector_energy: float32 [8], replicated, may hold values from 20 to 160
- atom_first: int32 [4], replicated, may hold values from 0 to 23
- atom_second: int32 [4], replicated, may hold values from 0 to 15
- atom_third: int32 [4], replicated, may hold values from 0 to 127
- rotation: bfloat16 [80, 80], P('orb'), may hold values from -0.625 to 0.625
Outputs:
- rotated: bfloat16 [2, 80, 12, 16, 128], P('dom', 'orb')
The draws below stay inside these ranges and needn't reach their ends.
All inputs are finite; a program needn't handle non-finite values.
Results may differ from the reference program's by a relative error of at most 0.0049.
Values may be sent and summed in bfloat16 or wider, within the bound.
No kernel may reach another device: no remote copies, remote signals or barrier semaphores. Data moves between devices by JAX's collectives and lax.ppermute only.
A program may use at most 64 MiB of HBM per device.

```python
import math
import jax
import jax.numpy as jnp
from jax import lax

CX = 12
CY = 16
CZ = 128
NORB = 80
ATOMS = 4
NPROJ = 8
SIDE = 8
SUP = 512
NX = 24
NY = 16
NZ = 128
N_DOM = 2


def place_ends(array, own_key, smallest, top_value):
    extent = array.shape
    index_at = [jax.random.randint(jax.random.fold_in(own_key, axis), (), 0, extent[axis]) for axis in range(len(extent))]
    array = array.at[tuple(index_at)].set(smallest)
    longest = extent.index(max(extent))
    index_at[longest] = (index_at[longest] + 1) % extent[longest]
    return array.at[tuple(index_at)].set(top_value)


def levels(stream_key, extent, cuts, smallest, largest):
    level = 1.0
    for dim, shards_of in cuts:
        steps = jax.random.uniform(jax.random.fold_in(jax.random.fold_in(stream_key, 6), dim), (shards_of,), jnp.float32, smallest / len(cuts), largest / len(cuts))
        level = level * jnp.repeat(jnp.exp(steps), extent[dim] // shards_of).reshape((-1,) + (1,) * (len(extent) - 1 - dim))
    return level


def noise(own_key, shape, scale, limit, shards=(), kind=jnp.bfloat16):
    values = scale * jax.random.normal(own_key, shape, jnp.float32)
    if shards:
        values = values * levels(own_key, shape, shards, -0.22, 0.18)
    return jnp.clip(values, -limit, limit).astype(kind)


def setup_inputs(seed: int = 0) -> dict:
    splits = jax.random.split(jax.random.key(seed), 9)
    orbitals = noise(splits[0], (N_DOM, NORB, CX, CY, CZ), 1.0, 6.0, ((0, 2), (1, 16)), jnp.float32)
    potential = jnp.clip(-3.0 + 3.0 * jax.random.uniform(splits[1], (N_DOM, CX, CY, CZ), jnp.float32) ** levels(splits[1], (N_DOM, CX, CY, CZ), ((0, 2),), -0.2, 0.2), -3.0, 0.0)
    projectors = noise(splits[2], (ATOMS, NPROJ, SUP), SUP ** -0.5, 0.25, (), jnp.float32)
    projector_energy = jnp.clip(jnp.exp(jax.random.uniform(splits[3], (NPROJ,), jnp.float32, math.log(20.0), math.log(160.0))), 20.0, 160.0)
    atom_first = place_ends(jax.random.randint(splits[4], (ATOMS,), 0, NX), jax.random.fold_in(splits[4], 1), 0, NX - 1).astype(jnp.int32)
    atom_second = place_ends(jax.random.randint(splits[5], (ATOMS,), 0, NY), jax.random.fold_in(splits[5], 1), 0, NY - 1).astype(jnp.int32)
    atom_third = place_ends(jax.random.randint(splits[6], (ATOMS,), 0, NZ), jax.random.fold_in(splits[6], 1), 0, NZ - 1).astype(jnp.int32)
    rotation = noise(splits[7], (NORB, NORB), NORB ** -0.5, 0.625, ((0, 16),))
    return {"orbitals": orbitals, "potential": potential, "projectors": projectors, "projector_energy": projector_energy, "atom_first": atom_first, "atom_second": atom_second, "atom_third": atom_third, "rotation": rotation}


stencil_weights = (-5369.0 / 1800.0, 12.0 / 7.0, -15.0 / 56.0, 10.0 / 189.0, -1.0 / 112.0, 2.0 / 1925.0, -1.0 / 16632.0)
inverse_spacing = 4.0
filter_center = 120.0
filter_width = 110.0


def to_grid(blocks):
    orbital_count = blocks.shape[1]
    stacked = blocks.reshape(NZ // CZ, NY // CY, NX // CX, orbital_count, CX, CY, CZ)
    stacked = stacked.transpose(3, 2, 4, 1, 5, 0, 6)
    return stacked.reshape(orbital_count, NX, NY, NZ)


def to_blocks(grid_values):
    orbital_count = grid_values.shape[0]
    stacked = grid_values.reshape(orbital_count, NX // CX, CX, NY // CY, CY, NZ // CZ, CZ)
    stacked = stacked.transpose(5, 3, 1, 0, 2, 4, 6)
    return stacked.reshape(N_DOM, orbital_count, CX, CY, CZ)


def support_points(atom_first, atom_second, atom_third):
    offsets = jnp.arange(SIDE, dtype=jnp.int32) - SIDE // 2
    coord_first = (atom_first[:, None] + offsets[None, :]) % NX
    coord_second = (atom_second[:, None] + offsets[None, :]) % NY
    coord_third = (atom_third[:, None] + offsets[None, :]) % NZ
    flattened = (coord_first[:, :, None, None] * NY + coord_second[:, None, :, None]) * NZ + coord_third[:, None, None, :]
    return flattened.reshape(ATOMS * SUP).astype(jnp.int32)


def apply_operator(values, local_field, support, projectors, projector_energy):
    summed = 3.0 * stencil_weights[0] * values
    for direction in (1, 2, 3):
        for offset in range(1, 7):
            summed = summed + stencil_weights[offset] * (jnp.roll(values, -offset, direction) + jnp.roll(values, offset, direction))
    orbital_count = values.shape[0]
    flattened = values.reshape(orbital_count, NX * NY * NZ)
    picked = jnp.take(flattened, support, axis=1).reshape(orbital_count, ATOMS, SUP)
    coeffs = jnp.einsum("aps,kas->kap", projectors, picked, precision=lax.Precision.HIGHEST)
    scaled = coeffs * projector_energy[None, None, :]
    spread = jnp.einsum("aps,kap->kas", projectors, scaled, precision=lax.Precision.HIGHEST)
    projected_part = jnp.zeros_like(flattened).at[:, support].add(spread.reshape(orbital_count, ATOMS * SUP))
    kinetic = -0.5 * inverse_spacing * inverse_spacing
    return kinetic * summed + local_field[None] * values + projected_part.reshape(values.shape)


def reference(orbitals, potential, projectors, projector_energy, atom_first, atom_second, atom_third, rotation):
    support = support_points(atom_first, atom_second, atom_third)
    start_values = to_grid(orbitals)
    local_field = to_grid(potential[:, None])[0]
    first_term = (apply_operator(start_values, local_field, support, projectors, projector_energy) - filter_center * start_values) / filter_width
    second_term = 2.0 * (apply_operator(first_term, local_field, support, projectors, projector_energy) - filter_center * first_term) / filter_width - start_values
    filtered = second_term.astype(jnp.bfloat16).reshape(NORB, NX * NY * NZ)
    rotated = jnp.dot(rotation.T, filtered, preferred_element_type=jnp.float32).astype(jnp.bfloat16)
    return to_blocks(rotated.reshape(NORB, NX, NY, NZ))
```

```python
import functools

import jax
import jax.numpy as jnp
import numpy as np
from jax import lax
from jax.experimental import pallas as pl
from jax.experimental.pallas import tpu as pltpu
from jax.sharding import PartitionSpec as P

SIDE = 8
SUP = 512


stencil_weights = (
    -5369.0 / 1800.0,
    12.0 / 7.0,
    -15.0 / 56.0,
    10.0 / 189.0,
    -1.0 / 112.0,
    2.0 / 1925.0,
    -1.0 / 16632.0,
)
inverse_spacing = 4.0
filter_center = 120.0
filter_width = 110.0
stencil_reach = 6


def partner_2(block, axis, bit):
    count = lax.axis_size(axis)
    route = []
    for low in range(count):
        high = low | 1 << bit
        if high != low and high < count:
            route += [(low, high), (high, low)]
    return lax.ppermute(block, axis, route)


def outgoing(values, direction, width):
    extent = values.shape[direction]
    if 2 * width < extent:
        return jnp.concatenate(
            (
                lax.slice_in_dim(values, 0, width, axis=direction),
                lax.slice_in_dim(values, extent - width, extent, axis=direction),
            ),
            axis=direction,
        )
    return values


def assemble(values, partner, direction, width):
    extent = values.shape[direction]
    if 2 * width < extent:
        lower_rim = lax.slice_in_dim(partner, width, 2 * width, axis=direction)
        upper_rim = lax.slice_in_dim(partner, 0, width, axis=direction)
        return jnp.concatenate((lower_rim, values, upper_rim), axis=direction)
    cyclic = jnp.concatenate((values, partner), axis=direction)
    chosen = np.arange(-width, extent + width) % (2 * extent)
    return jnp.take(cyclic, jnp.asarray(chosen, dtype=jnp.int32), axis=direction)


def face_padded(values, direction, bit_number):
    sent = outgoing(values, direction, stencil_reach)
    partner = partner_2(sent.astype(jnp.bfloat16), "dom", bit_number).astype(sent.dtype)
    return assemble(values, partner, direction, stencil_reach)


def stencil_sum(center, along):
    lead = center.ndim - 3
    summed = 3.0 * stencil_weights[0] * center
    for index in range(3):
        direction = lead + index
        extent = center.shape[direction]
        padded = along[index]
        for offset in range(1, 7):
            if padded is None:
                upward = jnp.roll(center, -offset, direction)
                downward = jnp.roll(center, offset, direction)
            else:
                upward = lax.slice_in_dim(
                    padded, stencil_reach + offset, stencil_reach + offset + extent, axis=direction
                )
                downward = lax.slice_in_dim(
                    padded, stencil_reach - offset, stencil_reach - offset + extent, axis=direction
                )
            summed = summed + stencil_weights[offset] * (upward + downward)
    return summed


def support_map(atom_coords, starts, extents, periods):
    offsets = jnp.arange(SIDE, dtype=jnp.int32) - SIDE // 2
    clipped_list = []
    inside_list = []
    for index in range(3):
        local = (atom_coords[index][:, None] + offsets[None, :] - starts[index]) % periods[index]
        inside_list.append(local < extents[index])
        clipped_list.append(jnp.minimum(local, extents[index] - 1))
    inside = (
        inside_list[0][:, :, None, None]
        & inside_list[1][:, None, :, None]
        & inside_list[2][:, None, None, :]
    )
    flattened = (
        clipped_list[0][:, :, None, None] * extents[1] + clipped_list[1][:, None, :, None]
    ) * extents[2] + clipped_list[2][:, None, None, :]
    atom_count = atom_coords[0].shape[0]
    return (
        flattened.reshape(atom_count * SUP),
        inside.reshape(atom_count, SUP).astype(jnp.float32),
    )


def coefficients(values, support, inside, projectors):
    orbital_count = values.shape[0]
    atom_count = projectors.shape[0]
    flattened = values.reshape(orbital_count, -1)
    picked = (
        jnp.take(flattened, support, axis=1).reshape(orbital_count, atom_count, SUP) * inside[None]
    )
    partial_coeffs = jnp.einsum("aps,kas->kap", projectors, picked, precision=lax.Precision.HIGHEST)
    return lax.psum(partial_coeffs, "dom")


def spread_into(coeffs, shape, support, inside, projectors, projector_energy):
    orbital_count = shape[0]
    atom_count = projectors.shape[0]
    scaled = coeffs * projector_energy[None, None, :]
    spread = (
        jnp.einsum("aps,kap->kas", projectors, scaled, precision=lax.Precision.HIGHEST)
        * inside[None]
    )
    total_cells = shape[1] * shape[2] * shape[3]
    projected_part = (
        jnp.zeros((orbital_count, total_cells), jnp.float32)
        .at[:, support]
        .add(spread.reshape(orbital_count, atom_count * SUP))
    )
    return projected_part.reshape(shape)


def own_hamiltonian(center, along, local_field, support, inside, projectors, projector_energy):
    kinetic = -0.5 * inverse_spacing * inverse_spacing
    coeffs = coefficients(center, support, inside, projectors)
    projected_part = spread_into(
        coeffs, center.shape, support, inside, projectors, projector_energy
    )
    return kinetic * stencil_sum(center, along) + local_field[None] * center + projected_part


def body(
    orbitals, potential, projectors, projector_energy, atom_first, atom_second, atom_third, rotation
):
    domain_count = lax.axis_size("dom")
    domain_bits = domain_count.bit_length() - 1
    split = [index < domain_bits for index in range(3)]
    start_values = orbitals[0]
    local_field = potential[0]
    extents = start_values.shape[1:]
    periods = (
        extents[0] * min(domain_count, 2),
        extents[1] * min(max(domain_count // 2, 1), 2),
        extents[2] * max(domain_count // 4, 1),
    )
    domain_index = lax.axis_index("dom")
    anchors = (
        domain_index % 2 * extents[0],
        domain_index // 2 % 2 * extents[1],
        domain_index // 4 * extents[2],
    )
    atom_coords = (atom_first, atom_second, atom_third)
    support, inside = support_map(atom_coords, anchors, extents, periods)
    along = [
        face_padded(start_values, index + 1, index) if split[index] else None for index in range(3)
    ]
    first_apply = own_hamiltonian(
        start_values, along, local_field, support, inside, projectors, projector_energy
    )
    first_term = (first_apply - filter_center * start_values) / filter_width
    along = [
        face_padded(first_term, index + 1, index) if split[index] else None for index in range(3)
    ]
    second_apply = own_hamiltonian(
        first_term, along, local_field, support, inside, projectors, projector_energy
    )
    second_term = 2.0 * (second_apply - filter_center * first_term) / filter_width - start_values
    per_device = start_values.shape[0]
    filtered = second_term.astype(jnp.bfloat16).reshape(per_device, -1)
    by_cells = lax.all_to_all(filtered, "orb", split_axis=1, concat_axis=0, tiled=True)
    whole_rotation = lax.all_gather(rotation, "orb", axis=0, tiled=True)
    rotated = lax.dot_general(
        whole_rotation, by_cells, (((0,), (0,)), ((), ())), preferred_element_type=jnp.float32
    ).astype(jnp.bfloat16)
    result = lax.all_to_all(rotated, "orb", split_axis=0, concat_axis=1, tiled=True)
    return result.reshape((1,) + start_values.shape)


SCALE = 15.0
MIB = 1 << 20


def scaled_weights():
    ratios = np.array(stencil_weights[1:], np.float64) / stencil_weights[1]
    return SCALE * ratios


def cyclic_stencil(size):
    matrix = np.zeros((size, size), np.float64)
    rows = np.arange(size)
    for offset, weight in enumerate(scaled_weights(), 1):
        np.add.at(matrix, (rows, (rows + offset) % size), weight)
        np.add.at(matrix, (rows, (rows - offset) % size), weight)
    return matrix


def plane_stencil(x_size, y_size):
    matrix = np.kron(cyclic_stencil(x_size), np.eye(y_size))
    matrix += np.kron(np.eye(x_size), cyclic_stencil(y_size))
    return np.concatenate((matrix, matrix), axis=1).astype(jnp.bfloat16)


def third_stencil(z_size):
    matrix = cyclic_stencil(z_size)
    return np.concatenate((matrix, matrix), axis=0).astype(jnp.bfloat16)


def third_first():
    picked = np.zeros((SUP, SUP), np.float32)
    source = np.arange(SUP)
    picked[source, source % SIDE * SIDE * SIDE + source // SIDE] = 1.0
    return picked.astype(jnp.bfloat16)


def halves(values):
    high = values.astype(jnp.bfloat16)
    return high, (values - high.astype(jnp.float32)).astype(jnp.bfloat16)


def matmul(left, right):
    return jnp.dot(left, right, preferred_element_type=jnp.float32)


def face_kernel(orbital_ref, potential_ref, out_ref):
    count = orbital_ref.shape[1]
    out_ref[0:count] = orbital_ref[0].astype(jnp.bfloat16)
    out_ref[count] = potential_ref[0].astype(jnp.bfloat16)


def projector_kernel(
    first_ref,
    second_ref,
    third_ref,
    energy_ref,
    projector_ref,
    order_ref,
    q_ref,
    q_low_ref,
    qt_ref,
    mask_ref,
    energy_out_ref,
    *,
    cells,
):
    block_x, x_size, y_size, z_size = cells
    atoms, nproj = projector_ref.shape[:2]
    pairs = atoms * nproj
    per_plane = SIDE * SIDE
    spots = atoms * per_plane
    own_start = lax.axis_index("dom") * block_x
    high, low = halves(projector_ref[...].reshape(pairs, SUP))
    ordered = matmul(jnp.concatenate((high, low), axis=0), order_ref[...])

    lane = lax.broadcasted_iota(jnp.int32, (pairs, 2 * per_plane), 1)
    row_atom = lax.broadcasted_iota(jnp.int32, (pairs, spots), 0) // nproj
    lane_atom = lax.broadcasted_iota(jnp.int32, (pairs, spots), 1) // per_plane
    same_atom = row_atom == lane_atom
    expanded = []
    for part in range(2):
        rows = []
        for third in range(SIDE):
            start = third // 2 * 2 * per_plane
            both = ordered[part * pairs : (part + 1) * pairs, start : start + 2 * per_plane]
            swapped = pltpu.roll(both, per_plane, 1)
            if third % 2:
                both, swapped = swapped, both
            doubled = jnp.where(lane < per_plane, both, swapped)
            doubled = jnp.concatenate([doubled] * (atoms // 2), axis=1)
            rows.append(jnp.where(same_atom, doubled, 0.0))
        expanded.append(jnp.concatenate(rows, axis=0).astype(jnp.bfloat16))

    place = []
    spot = lax.broadcasted_iota(jnp.int32, (per_plane, x_size * y_size), 0)
    place_lane = lax.broadcasted_iota(jnp.int32, (per_plane, x_size * y_size), 1)
    for atom in range(atoms):
        x_start = lax.rem(first_ref[atom] - SIDE // 2 - own_start + 2 * x_size, x_size)
        y_start = lax.rem(second_ref[atom] - SIDE // 2 + y_size, y_size)
        x_index = x_start + spot // SIDE
        x_index = jnp.where(x_index >= x_size, x_index - x_size, x_index)
        y_index = y_start + spot % SIDE
        y_index = jnp.where(y_index >= y_size, y_index - y_size, y_index)
        target = x_index * y_size + y_index
        place.append(jnp.where(place_lane == target, 1.0, 0.0).astype(jnp.bfloat16))
    place = jnp.concatenate(place, axis=0)
    cell_count = x_size * y_size
    q_high = matmul(expanded[0], place)
    q_low = matmul(expanded[1], place)
    q_ref[:, 0:cell_count] = q_high.astype(jnp.bfloat16)
    q_ref[:, cell_count : 2 * cell_count] = q_high.astype(jnp.bfloat16)
    q_low_ref[...] = q_low.astype(jnp.bfloat16)
    rows = q_high.shape[0]
    q_high = q_high.T.astype(jnp.bfloat16)
    qt_ref[:, 0:rows] = q_high
    qt_ref[:, rows : 2 * rows] = q_high
    qt_ref[:, 2 * rows : 3 * rows] = q_low.T.astype(jnp.bfloat16)

    z_lane = lax.broadcasted_iota(jnp.int32, (nproj, z_size), 1)
    for third in range(SIDE):
        for atom in range(atoms):
            z_index = lax.rem(third_ref[atom] + third - SIDE // 2 + z_size, z_size)
            start = third * pairs + atom * nproj
            mask_ref[start : start + nproj] = jnp.where(z_lane == z_index, 1.0, 0.0)
    sublane = lax.broadcasted_iota(jnp.int32, (nproj, z_size), 0)
    energy = jnp.zeros((nproj, z_size), jnp.float32)
    for index in range(nproj):
        energy = jnp.where(sublane == index, energy_ref[index], energy)
    for atom in range(atoms):
        energy_out_ref[atom * nproj : (atom + 1) * nproj] = energy


def filter_kernel(
    orbital_ref,
    partner_ref,
    potential_ref,
    q_ref,
    q_low_ref,
    qt_ref,
    mask_ref,
    energy_ref,
    rotation_ref,
    plane_ref,
    third_ref,
    out_ref,
    start_ref,
    first_ref,
    diagonal_ref,
    right_ref,
    coeff_ref,
    rows_ref,
    chunk_ref,
):
    count, block_x, y_size, z_size = orbital_ref.shape[1:]
    own = block_x * y_size
    cell_count = 2 * own
    pairs = energy_ref.shape[0]
    spots = mask_ref.shape[0]
    kinetic = -0.5 * inverse_spacing * inverse_spacing
    unit = kinetic * stencil_weights[1] / SCALE / filter_width

    shift = 3.0 * kinetic * stencil_weights[0] - filter_center
    diagonal_ref[0:own] = (potential_ref[0].reshape(own, z_size) + shift) / filter_width
    partner_potential = partner_ref[count].astype(jnp.float32).reshape(own, z_size)
    diagonal_ref[own:] = (partner_potential + shift) / filter_width
    for orbital in range(count):
        lanes = slice(orbital * z_size, (orbital + 1) * z_size)
        start_ref[0:own, lanes] = orbital_ref[0, orbital].reshape(own, z_size)
        start_ref[own:, lanes] = (
            partner_ref[orbital].astype(jnp.float32).reshape(own, z_size)
        )

    def operate(source_ref, rows, finish):
        high, low = halves(source_ref[...])
        right_ref[0:cell_count] = high
        right_ref[cell_count:] = low
        products = matmul(q_ref[...], right_ref[...])
        products = products + matmul(q_low_ref[...], right_ref[0:cell_count])
        mask = mask_ref[...]
        for orbital in range(count):
            lanes = slice(orbital * z_size, (orbital + 1) * z_size)
            picked = (products[:, lanes] * mask).reshape(SIDE, pairs, z_size)
            coeffs = jnp.sum(jnp.sum(picked, axis=0), axis=1, keepdims=True)
            scaled = coeffs * energy_ref[...] * (1.0 / (unit * filter_width))
            spread = jnp.concatenate([scaled] * SIDE, axis=0) * mask
            high, low = halves(spread)
            coeff_ref[0:spots, lanes] = high
            coeff_ref[spots : 2 * spots, lanes] = low
            coeff_ref[2 * spots :, lanes] = high
        summed = matmul(plane_ref[0:rows], right_ref[...])
        summed = summed + matmul(qt_ref[0:rows], coeff_ref[...])
        for orbital in range(count):
            lanes = slice(orbital * z_size, (orbital + 1) * z_size)
            left = jnp.concatenate(
                (
                    right_ref[0:rows, lanes],
                    right_ref[cell_count : cell_count + rows, lanes],
                ),
                axis=1,
            )
            along = summed[:, lanes] + matmul(left, third_ref[...])
            values = diagonal_ref[0:rows] * source_ref[0:rows, lanes] + unit * along
            finish(orbital, lanes, values)

    def keep(orbital, lanes, values):
        first_ref[:, lanes] = values

    def emit(orbital, lanes, values):
        rows_ref[orbital * own : (orbital + 1) * own] = 2.0 * values - start_ref[0:own, lanes]

    operate(start_ref, cell_count, keep)
    operate(first_ref, own, emit)

    wide = rotation_ref.shape[1]
    spare = z_size - wide
    block = jnp.zeros((8, z_size), jnp.float32)
    block = jnp.concatenate(
        (rotation_ref[...].astype(jnp.float32), jnp.zeros((count, spare), jnp.float32)), axis=1
    )
    block = jnp.concatenate((block, jnp.zeros((8 - count, z_size), jnp.float32)), axis=0)
    sublane = lax.broadcasted_iota(jnp.int32, (8, z_size), 0)
    lane = lax.broadcasted_iota(jnp.int32, (8, z_size), 1)
    packed = block
    for piece in range(-(-wide // spare)):
        moved = pltpu.roll(block, (piece - (count - 1)) % 8, 0)
        moved = pltpu.roll(moved, (wide - piece * spare) % z_size, 1)
        packed = jnp.where((sublane == piece) & (lane >= wide), moved, packed)

    used = count * block_x
    for part in range(y_size):
        chunk_ref[part, 0:used] = rows_ref[pl.ds(part, used, stride=y_size), :]
        chunk_ref[part, used : used + count - 1] = packed[0 : count - 1]
    out_ref[...] = chunk_ref[...].astype(jnp.bfloat16)


def rotate_kernel(received_ref, out_ref, wide_ref, rows_ref, *, count, block_x):
    sources, chunk, z_size = received_ref.shape
    total = sources * count
    used = count * block_x
    spare = z_size - total
    wide_ref[...] = received_ref[...].astype(jnp.float32).reshape(sources * chunk, z_size)
    packed = [wide_ref[pl.ds(used + row, sources, stride=chunk), :] for row in range(count - 1)]
    lane = lax.broadcasted_iota(jnp.int32, (sources, z_size), 1)
    last = jnp.zeros((sources, z_size), jnp.float32)
    for piece in range(-(-total // spare)):
        moved = pltpu.roll(packed[piece], (piece * spare - total) % z_size, 1)
        last = jnp.where(lane >= piece * spare, moved, last)
    rotation = jnp.concatenate(packed + [last], axis=0)[:, 0:total].astype(jnp.bfloat16)
    columns = []
    for plane in range(block_x):
        rows = [
            wide_ref[pl.ds(orbital * block_x + plane, sources, stride=chunk), :]
            for orbital in range(count)
        ]
        columns.append(jnp.concatenate(rows, axis=0).astype(jnp.bfloat16))
    values = jnp.concatenate(columns, axis=1)
    rotated = lax.dot_general(
        rotation, values, (((0,), (0,)), ((), ())), preferred_element_type=jnp.float32
    )
    rows_ref[total * block_x :] = jnp.zeros((chunk - used, z_size), jnp.float32)
    for plane in range(block_x):
        lanes = slice(plane * z_size, (plane + 1) * z_size)
        rows_ref[pl.ds(plane, total, stride=block_x), :] = rotated[:, lanes]
    for part in range(sources):
        out_ref[part] = rows_ref[part * used : part * used + chunk].astype(jnp.bfloat16)


def unpack_kernel(received_ref, out_ref, rows_ref):
    sources, chunk, z_size = received_ref.shape
    used = rows_ref.shape[0] // sources
    for part in range(sources):
        values = received_ref[part].astype(jnp.float32)
        rows_ref[pl.ds(part, used, stride=sources), :] = values[0:used]
    out_ref[...] = rows_ref[...].astype(jnp.bfloat16).reshape(out_ref.shape)


def in_vmem(count):
    return [pl.BlockSpec(memory_space=pltpu.VMEM)] * count


def in_smem(count):
    return [pl.BlockSpec(memory_space=pltpu.SMEM)] * count


def params(mib):
    return pltpu.CompilerParams(vmem_limit_bytes=mib * MIB)


def shape_of(shape, kind):
    return jax.ShapeDtypeStruct(shape, kind)


def pair_body(
    orbitals, potential, projectors, projector_energy, atom_first, atom_second, atom_third, rotation
):
    bf16, f32 = jnp.bfloat16, jnp.float32
    count, block_x, y_size, z_size = orbitals.shape[1:]
    x_size = 2 * block_x
    own = block_x * y_size
    cell_count = x_size * y_size
    atoms, nproj = projectors.shape[:2]
    spots = SIDE * atoms * nproj
    sources = lax.axis_size("orb")
    used = count * block_x
    chunk = -(-(used + count - 1) // 16) * 16

    sent = pl.pallas_call(
        face_kernel,
        out_shape=shape_of((count + 1, block_x, y_size, z_size), bf16),
        in_specs=in_vmem(2),
        out_specs=in_vmem(1)[0],
        compiler_params=params(16),
        name="faces",
    )(orbitals, potential)
    partner = lax.ppermute(sent, "dom", [(0, 1), (1, 0)])

    q, q_low, qt, mask, energy = pl.pallas_call(
        functools.partial(projector_kernel, cells=(block_x, x_size, y_size, z_size)),
        out_shape=(
            shape_of((spots, 2 * cell_count), bf16),
            shape_of((spots, cell_count), bf16),
            shape_of((cell_count, 3 * spots), bf16),
            shape_of((spots, z_size), f32),
            shape_of((atoms * nproj, z_size), f32),
        ),
        in_specs=in_smem(4) + in_vmem(2),
        out_specs=tuple(in_vmem(5)),
        compiler_params=params(24),
        cost_estimate=pl.CostEstimate(flops=1 << 30, bytes_accessed=3 << 20, transcendentals=0),
        name="projector_tables",
    )(atom_first, atom_second, atom_third, projector_energy, projectors, third_first())

    filtered = pl.pallas_call(
        filter_kernel,
        out_shape=shape_of((sources, chunk, z_size), bf16),
        in_specs=in_vmem(11),
        out_specs=in_vmem(1)[0],
        scratch_shapes=[
            pltpu.VMEM((cell_count, count * z_size), f32),
            pltpu.VMEM((cell_count, count * z_size), f32),
            pltpu.VMEM((cell_count, z_size), f32),
            pltpu.VMEM((2 * cell_count, count * z_size), bf16),
            pltpu.VMEM((3 * spots, count * z_size), bf16),
            pltpu.VMEM((count * own, z_size), f32),
            pltpu.VMEM((sources, chunk, z_size), f32),
        ],
        compiler_params=params(40),
        name="filter",
    )(
        orbitals,
        partner,
        potential,
        q,
        q_low,
        qt,
        mask,
        energy,
        rotation,
        plane_stencil(x_size, y_size),
        third_stencil(z_size),
    )
    by_plane = lax.all_to_all(filtered, "orb", split_axis=0, concat_axis=0, tiled=True)

    rotated = pl.pallas_call(
        functools.partial(rotate_kernel, count=count, block_x=block_x),
        out_shape=shape_of((sources, chunk, z_size), bf16),
        in_specs=in_vmem(1),
        out_specs=in_vmem(1)[0],
        scratch_shapes=[
            pltpu.VMEM((sources * chunk, z_size), f32),
            pltpu.VMEM((sources * used + chunk - used, z_size), f32),
        ],
        compiler_params=params(24),
        name="rotate",
    )(by_plane)
    by_orbital = lax.all_to_all(rotated, "orb", split_axis=0, concat_axis=0, tiled=True)

    return pl.pallas_call(
        unpack_kernel,
        out_shape=shape_of(orbitals.shape, bf16),
        in_specs=in_vmem(1),
        out_specs=in_vmem(1)[0],
        scratch_shapes=[pltpu.VMEM((sources * used, z_size), f32)],
        compiler_params=params(16),
        name="unpack",
    )(by_orbital)


def fits_pair(mesh, orbitals, projectors, rotation):
    count = orbitals.shape[1] // mesh.shape["orb"]
    return (
        mesh.shape["dom"] == 2
        and orbitals.shape[3] == mesh.shape["orb"]
        and orbitals.shape[2] == 2 * stencil_reach
        and projectors.shape[0] % 2 == 0
        and projectors.shape[1] == 8
        and count <= 8
        and rotation.shape[1] < orbitals.shape[4]
        and -(-rotation.shape[1] // (orbitals.shape[4] - rotation.shape[1])) < count
    )


def solution(mesh):
    def whole(*arrays):
        chosen = pair_body if fits_pair(mesh, arrays[0], arrays[2], arrays[7]) else body
        return jax.shard_map(
            chosen,
            mesh=mesh,
            in_specs=(
                P("dom", "orb", None, None, None),
                P("dom", None, None, None),
                P(),
                P(),
                P(),
                P(),
                P(),
                P("orb", None),
            ),
            out_specs=P("dom", "orb", None, None, None),
            check_vma=False,
        )(*arrays)

    return whole
```

```python
import functools

import jax
import jax.numpy as jnp
import numpy as np
from jax import lax
from jax.experimental import pallas as pl
from jax.experimental.pallas import tpu as pltpu
from jax.sharding import PartitionSpec as P

SIDE = 8
SUP = 512


stencil_weights = (
    -5369.0 / 1800.0,
    12.0 / 7.0,
    -15.0 / 56.0,
    10.0 / 189.0,
    -1.0 / 112.0,
    2.0 / 1925.0,
    -1.0 / 16632.0,
)
inverse_spacing = 4.0
filter_center = 120.0
filter_width = 110.0
stencil_reach = 6


def partner_2(block, axis, bit):
    count = lax.axis_size(axis)
    route = []
    for low in range(count):
        high = low | 1 << bit
        if high != low and high < count:
            route += [(low, high), (high, low)]
    return lax.ppermute(block, axis, route)


def outgoing(values, direction, width):
    extent = values.shape[direction]
    if 2 * width < extent:
        return jnp.concatenate(
            (
                lax.slice_in_dim(values, 0, width, axis=direction),
                lax.slice_in_dim(values, extent - width, extent, axis=direction),
            ),
            axis=direction,
        )
    return values


def assemble(values, partner, direction, width):
    extent = values.shape[direction]
    if 2 * width < extent:
        lower_rim = lax.slice_in_dim(partner, width, 2 * width, axis=direction)
        upper_rim = lax.slice_in_dim(partner, 0, width, axis=direction)
        return jnp.concatenate((lower_rim, values, upper_rim), axis=direction)
    cyclic = jnp.concatenate((values, partner), axis=direction)
    chosen = np.arange(-width, extent + width) % (2 * extent)
    return jnp.take(cyclic, jnp.asarray(chosen, dtype=jnp.int32), axis=direction)


def face_padded(values, direction, bit_number):
    sent = outgoing(values, direction, stencil_reach)
    partner = partner_2(sent.astype(jnp.bfloat16), "dom", bit_number).astype(sent.dtype)
    return assemble(values, partner, direction, stencil_reach)


def stencil_sum(center, along):
    lead = center.ndim - 3
    summed = 3.0 * stencil_weights[0] * center
    for index in range(3):
        direction = lead + index
        extent = center.shape[direction]
        padded = along[index]
        for offset in range(1, 7):
            if padded is None:
                upward = jnp.roll(center, -offset, direction)
                downward = jnp.roll(center, offset, direction)
            else:
                upward = lax.slice_in_dim(
                    padded, stencil_reach + offset, stencil_reach + offset + extent, axis=direction
                )
                downward = lax.slice_in_dim(
                    padded, stencil_reach - offset, stencil_reach - offset + extent, axis=direction
                )
            summed = summed + stencil_weights[offset] * (upward + downward)
    return summed


def support_map(atom_coords, starts, extents, periods):
    offsets = jnp.arange(SIDE, dtype=jnp.int32) - SIDE // 2
    clipped_list = []
    inside_list = []
    for index in range(3):
        local = (atom_coords[index][:, None] + offsets[None, :] - starts[index]) % periods[index]
        inside_list.append(local < extents[index])
        clipped_list.append(jnp.minimum(local, extents[index] - 1))
    inside = (
        inside_list[0][:, :, None, None]
        & inside_list[1][:, None, :, None]
        & inside_list[2][:, None, None, :]
    )
    flattened = (
        clipped_list[0][:, :, None, None] * extents[1] + clipped_list[1][:, None, :, None]
    ) * extents[2] + clipped_list[2][:, None, None, :]
    atom_count = atom_coords[0].shape[0]
    return (
        flattened.reshape(atom_count * SUP),
        inside.reshape(atom_count, SUP).astype(jnp.float32),
    )


def coefficients(values, support, inside, projectors):
    orbital_count = values.shape[0]
    atom_count = projectors.shape[0]
    flattened = values.reshape(orbital_count, -1)
    picked = (
        jnp.take(flattened, support, axis=1).reshape(orbital_count, atom_count, SUP) * inside[None]
    )
    partial_coeffs = jnp.einsum("aps,kas->kap", projectors, picked, precision=lax.Precision.HIGHEST)
    return lax.psum(partial_coeffs, "dom")


def spread_into(coeffs, shape, support, inside, projectors, projector_energy):
    orbital_count = shape[0]
    atom_count = projectors.shape[0]
    scaled = coeffs * projector_energy[None, None, :]
    spread = (
        jnp.einsum("aps,kap->kas", projectors, scaled, precision=lax.Precision.HIGHEST)
        * inside[None]
    )
    total_cells = shape[1] * shape[2] * shape[3]
    projected_part = (
        jnp.zeros((orbital_count, total_cells), jnp.float32)
        .at[:, support]
        .add(spread.reshape(orbital_count, atom_count * SUP))
    )
    return projected_part.reshape(shape)


def own_hamiltonian(center, along, local_field, support, inside, projectors, projector_energy):
    kinetic = -0.5 * inverse_spacing * inverse_spacing
    coeffs = coefficients(center, support, inside, projectors)
    projected_part = spread_into(
        coeffs, center.shape, support, inside, projectors, projector_energy
    )
    return kinetic * stencil_sum(center, along) + local_field[None] * center + projected_part


def body(
    orbitals, potential, projectors, projector_energy, atom_first, atom_second, atom_third, rotation
):
    domain_count = lax.axis_size("dom")
    domain_bits = domain_count.bit_length() - 1
    split = [index < domain_bits for index in range(3)]
    start_values = orbitals[0]
    local_field = potential[0]
    extents = start_values.shape[1:]
    periods = (
        extents[0] * min(domain_count, 2),
        extents[1] * min(max(domain_count // 2, 1), 2),
        extents[2] * max(domain_count // 4, 1),
    )
    domain_index = lax.axis_index("dom")
    anchors = (
        domain_index % 2 * extents[0],
        domain_index // 2 % 2 * extents[1],
        domain_index // 4 * extents[2],
    )
    atom_coords = (atom_first, atom_second, atom_third)
    support, inside = support_map(atom_coords, anchors, extents, periods)
    along = [
        face_padded(start_values, index + 1, index) if split[index] else None for index in range(3)
    ]
    first_apply = own_hamiltonian(
        start_values, along, local_field, support, inside, projectors, projector_energy
    )
    first_term = (first_apply - filter_center * start_values) / filter_width
    along = [
        face_padded(first_term, index + 1, index) if split[index] else None for index in range(3)
    ]
    second_apply = own_hamiltonian(
        first_term, along, local_field, support, inside, projectors, projector_energy
    )
    second_term = 2.0 * (second_apply - filter_center * first_term) / filter_width - start_values
    per_device = start_values.shape[0]
    filtered = second_term.astype(jnp.bfloat16).reshape(per_device, -1)
    by_cells = lax.all_to_all(filtered, "orb", split_axis=1, concat_axis=0, tiled=True)
    whole_rotation = lax.all_gather(rotation, "orb", axis=0, tiled=True)
    rotated = lax.dot_general(
        whole_rotation, by_cells, (((0,), (0,)), ((), ())), preferred_element_type=jnp.float32
    ).astype(jnp.bfloat16)
    result = lax.all_to_all(rotated, "orb", split_axis=0, concat_axis=1, tiled=True)
    return result.reshape((1,) + start_values.shape)


SCALE = 15.0
MIB = 1 << 20


def scaled_weights():
    ratios = np.array(stencil_weights[1:], np.float64) / stencil_weights[1]
    return SCALE * ratios


def cyclic_stencil(size):
    matrix = np.zeros((size, size), np.float64)
    rows = np.arange(size)
    for offset, weight in enumerate(scaled_weights(), 1):
        np.add.at(matrix, (rows, (rows + offset) % size), weight)
        np.add.at(matrix, (rows, (rows - offset) % size), weight)
    return matrix


def plane_stencil(x_size, y_size):
    matrix = np.kron(cyclic_stencil(x_size), np.eye(y_size))
    matrix += np.kron(np.eye(x_size), cyclic_stencil(y_size))
    return np.concatenate((matrix, matrix), axis=1).astype(jnp.bfloat16)


def third_stencil(z_size):
    matrix = cyclic_stencil(z_size)
    return np.concatenate((matrix, matrix), axis=0).astype(jnp.bfloat16)


def third_first():
    picked = np.zeros((SUP, SUP), np.float32)
    source = np.arange(SUP)
    picked[source, source % SIDE * SIDE * SIDE + source // SIDE] = 1.0
    return picked.astype(jnp.bfloat16)


def halves(values):
    high = values.astype(jnp.bfloat16)
    return high, (values - high.astype(jnp.float32)).astype(jnp.bfloat16)


def matmul(left, right):
    return jnp.dot(left, right, preferred_element_type=jnp.float32)


def face_kernel(orbital_ref, potential_ref, out_ref):
    count = orbital_ref.shape[1]
    out_ref[0:count] = orbital_ref[0].astype(jnp.bfloat16)
    out_ref[count] = potential_ref[0].astype(jnp.bfloat16)


def projector_kernel(
    first_ref,
    second_ref,
    third_ref,
    energy_ref,
    projector_ref,
    order_ref,
    q_ref,
    q_low_ref,
    qt_ref,
    mask_ref,
    energy_out_ref,
    *,
    cells,
):
    block_x, x_size, y_size, z_size = cells
    atoms, nproj = projector_ref.shape[:2]
    pairs = atoms * nproj
    per_plane = SIDE * SIDE
    spots = atoms * per_plane
    own_start = lax.axis_index("dom") * block_x
    high, low = halves(projector_ref[...].reshape(pairs, SUP))
    ordered = matmul(jnp.concatenate((high, low), axis=0), order_ref[...])

    lane = lax.broadcasted_iota(jnp.int32, (pairs, 2 * per_plane), 1)
    row_atom = lax.broadcasted_iota(jnp.int32, (pairs, spots), 0) // nproj
    lane_atom = lax.broadcasted_iota(jnp.int32, (pairs, spots), 1) // per_plane
    same_atom = row_atom == lane_atom
    expanded = []
    for part in range(2):
        rows = []
        for third in range(SIDE):
            start = third // 2 * 2 * per_plane
            both = ordered[part * pairs : (part + 1) * pairs, start : start + 2 * per_plane]
            swapped = pltpu.roll(both, per_plane, 1)
            if third % 2:
                both, swapped = swapped, both
            doubled = jnp.where(lane < per_plane, both, swapped)
            doubled = jnp.concatenate([doubled] * (atoms // 2), axis=1)
            rows.append(jnp.where(same_atom, doubled, 0.0))
        expanded.append(jnp.concatenate(rows, axis=0).astype(jnp.bfloat16))

    place = []
    spot = lax.broadcasted_iota(jnp.int32, (per_plane, x_size * y_size), 0)
    place_lane = lax.broadcasted_iota(jnp.int32, (per_plane, x_size * y_size), 1)
    for atom in range(atoms):
        x_start = lax.rem(first_ref[atom] - SIDE // 2 - own_start + 2 * x_size, x_size)
        y_start = lax.rem(second_ref[atom] - SIDE // 2 + y_size, y_size)
        x_index = x_start + spot // SIDE
        x_index = jnp.where(x_index >= x_size, x_index - x_size, x_index)
        y_index = y_start + spot % SIDE
        y_index = jnp.where(y_index >= y_size, y_index - y_size, y_index)
        target = x_index * y_size + y_index
        place.append(jnp.where(place_lane == target, 1.0, 0.0).astype(jnp.bfloat16))
    place = jnp.concatenate(place, axis=0)
    cell_count = x_size * y_size
    q_high = matmul(expanded[0], place)
    q_low = matmul(expanded[1], place)
    q_ref[:, 0:cell_count] = q_high.astype(jnp.bfloat16)
    q_ref[:, cell_count : 2 * cell_count] = q_high.astype(jnp.bfloat16)
    q_low_ref[...] = q_low.astype(jnp.bfloat16)
    rows = q_high.shape[0]
    q_high = q_high.T.astype(jnp.bfloat16)
    qt_ref[:, 0:rows] = q_high
    qt_ref[:, rows : 2 * rows] = q_high
    qt_ref[:, 2 * rows : 3 * rows] = q_low.T.astype(jnp.bfloat16)

    z_lane = lax.broadcasted_iota(jnp.int32, (nproj, z_size), 1)
    for third in range(SIDE):
        for atom in range(atoms):
            z_index = lax.rem(third_ref[atom] + third - SIDE // 2 + z_size, z_size)
            start = third * pairs + atom * nproj
            mask_ref[start : start + nproj] = jnp.where(z_lane == z_index, 1.0, 0.0)
    sublane = lax.broadcasted_iota(jnp.int32, (nproj, z_size), 0)
    energy = jnp.zeros((nproj, z_size), jnp.float32)
    for index in range(nproj):
        energy = jnp.where(sublane == index, energy_ref[index], energy)
    for atom in range(atoms):
        energy_out_ref[atom * nproj : (atom + 1) * nproj] = energy


def filter_kernel(
    orbital_ref,
    partner_ref,
    potential_ref,
    q_ref,
    q_low_ref,
    qt_ref,
    mask_ref,
    energy_ref,
    rotation_ref,
    plane_ref,
    third_ref,
    *refs,
):
    out_refs = refs[:-7]
    start_ref, first_ref, diagonal_ref, right_ref, coeff_ref, rows_ref, chunk_ref = refs[-7:]
    count, block_x, y_size, z_size = orbital_ref.shape[1:]
    own = block_x * y_size
    cell_count = 2 * own
    pairs = energy_ref.shape[0]
    spots = mask_ref.shape[0]
    kinetic = -0.5 * inverse_spacing * inverse_spacing
    unit = kinetic * stencil_weights[1] / SCALE / filter_width

    shift = 3.0 * kinetic * stencil_weights[0] - filter_center
    diagonal_ref[0:own] = (potential_ref[0].reshape(own, z_size) + shift) / filter_width
    partner_potential = partner_ref[count].astype(jnp.float32).reshape(own, z_size)
    diagonal_ref[own:] = (partner_potential + shift) / filter_width
    for orbital in range(count):
        lanes = slice(orbital * z_size, (orbital + 1) * z_size)
        start_ref[0:own, lanes] = orbital_ref[0, orbital].reshape(own, z_size)
        start_ref[own:, lanes] = (
            partner_ref[orbital].astype(jnp.float32).reshape(own, z_size)
        )

    def operate(source_ref, rows, finish):
        high, low = halves(source_ref[...])
        right_ref[0:cell_count] = high
        right_ref[cell_count:] = low
        products = matmul(q_ref[...], right_ref[...])
        products = products + matmul(q_low_ref[...], right_ref[0:cell_count])
        mask = mask_ref[...]
        for orbital in range(count):
            lanes = slice(orbital * z_size, (orbital + 1) * z_size)
            picked = (products[:, lanes] * mask).reshape(SIDE, pairs, z_size)
            coeffs = jnp.sum(jnp.sum(picked, axis=0), axis=1, keepdims=True)
            scaled = coeffs * energy_ref[...] * (1.0 / (unit * filter_width))
            spread = jnp.concatenate([scaled] * SIDE, axis=0) * mask
            high, low = halves(spread)
            coeff_ref[0:spots, lanes] = high
            coeff_ref[spots : 2 * spots, lanes] = low
            coeff_ref[2 * spots :, lanes] = high
        summed = matmul(plane_ref[0:rows], right_ref[...])
        summed = summed + matmul(qt_ref[0:rows], coeff_ref[...])
        for orbital in range(count):
            lanes = slice(orbital * z_size, (orbital + 1) * z_size)
            left = jnp.concatenate(
                (
                    right_ref[0:rows, lanes],
                    right_ref[cell_count : cell_count + rows, lanes],
                ),
                axis=1,
            )
            along = summed[:, lanes] + matmul(left, third_ref[...])
            values = diagonal_ref[0:rows] * source_ref[0:rows, lanes] + unit * along
            finish(orbital, lanes, values)

    def keep(orbital, lanes, values):
        first_ref[:, lanes] = values

    def emit(orbital, lanes, values):
        rows_ref[orbital * own : (orbital + 1) * own] = 2.0 * values - start_ref[0:own, lanes]

    operate(start_ref, cell_count, keep)
    operate(first_ref, own, emit)

    packed = packed_rotation(rotation_ref, z_size, y_size)
    used = count * block_x
    me = lax.axis_index("orb")
    for step in range(y_size):
        chunk_ref[step, 0:used] = rows_ref[pl.ds(me ^ step, used, stride=y_size), :]
        chunk_ref[step, used : used + count - 1] = packed[0 : count - 1]
        out_refs[step][...] = chunk_ref[step].astype(jnp.bfloat16)


def packed_rotation(rotation_ref, z_size, sources):
    count, wide = rotation_ref.shape
    spare = z_size - wide
    block = jnp.concatenate(
        (rotation_ref[...].astype(jnp.float32), jnp.zeros((count, spare), jnp.float32)), axis=1
    )
    block = jnp.concatenate((block, jnp.zeros((8 - count, z_size), jnp.float32)), axis=0)
    row = lax.broadcasted_iota(jnp.int32, (z_size, z_size), 0)
    column = lax.broadcasted_iota(jnp.int32, (z_size, z_size), 1)
    origin = column % sources * count + column // sources
    order = jnp.where((origin == row) & (column < wide), 1.0, 0.0)
    block = matmul(block.astype(jnp.bfloat16), order.astype(jnp.bfloat16))
    sublane = lax.broadcasted_iota(jnp.int32, (8, z_size), 0)
    lane = lax.broadcasted_iota(jnp.int32, (8, z_size), 1)
    packed = block
    for piece in range(-(-wide // spare)):
        moved = pltpu.roll(block, (piece - (count - 1)) % 8, 0)
        moved = pltpu.roll(moved, (wide - piece * spare) % z_size, 1)
        packed = jnp.where((sublane == piece) & (lane >= wide), moved, packed)
    return packed


def rotate_kernel(*refs, count, block_x, sources):
    received_refs, out_refs = refs[:sources], refs[sources : 2 * sources]
    wide_ref, rows_ref = refs[2 * sources :]
    chunk, z_size = received_refs[0].shape
    total = sources * count
    used = count * block_x
    spare = z_size - total
    for step in range(sources):
        wide_ref[step * chunk : (step + 1) * chunk] = received_refs[step][...].astype(jnp.float32)
    packed = [wide_ref[pl.ds(used + row, sources, stride=chunk), :] for row in range(count - 1)]
    lane = lax.broadcasted_iota(jnp.int32, (sources, z_size), 1)
    last = jnp.zeros((sources, z_size), jnp.float32)
    for piece in range(-(-total // spare)):
        moved = pltpu.roll(packed[piece], (piece * spare - total) % z_size, 1)
        last = jnp.where(lane >= piece * spare, moved, last)
    rotation = jnp.concatenate(packed + [last], axis=0)[:, 0:total].astype(jnp.bfloat16)
    columns = []
    for plane in range(block_x):
        rows = [
            wide_ref[pl.ds(orbital * block_x + plane, sources, stride=chunk), :]
            for orbital in range(count)
        ]
        columns.append(jnp.concatenate(rows, axis=0).astype(jnp.bfloat16))
    values = jnp.concatenate(columns, axis=1)
    rotated = lax.dot_general(
        rotation, values, (((0,), (0,)), ((), ())), preferred_element_type=jnp.float32
    )
    for orbital in range(count):
        rows = slice(orbital * sources, (orbital + 1) * sources)
        for plane in range(block_x):
            lanes = slice(plane * z_size, (plane + 1) * z_size)
            start = orbital * block_x + plane
            rows_ref[pl.ds(start, sources, stride=chunk), :] = rotated[rows, lanes]
    blank = jnp.zeros((sources, z_size), jnp.float32)
    for row in range(used, chunk):
        rows_ref[pl.ds(row, sources, stride=chunk), :] = blank
    me = lax.axis_index("orb")
    for step in range(sources):
        start = pl.multiple_of((me ^ step) * chunk, chunk)
        out_refs[step][...] = rows_ref[pl.ds(start, chunk), :].astype(jnp.bfloat16)


def unpack_kernel(*refs):
    received_refs, out_ref, rows_ref = refs[:-2], refs[-2], refs[-1]
    sources = len(received_refs)
    used = rows_ref.shape[0] // sources
    me = lax.axis_index("orb")
    for step in range(sources):
        values = received_refs[step][...].astype(jnp.float32)
        rows_ref[pl.ds(me ^ step, used, stride=sources), :] = values[0:used]
    out_ref[...] = rows_ref[...].astype(jnp.bfloat16).reshape(out_ref.shape)


def swap_chunks(chunks):
    sources = len(chunks)
    received = [chunks[0]]
    for step in range(1, sources):
        route = [(index, index ^ step) for index in range(sources)]
        received.append(lax.ppermute(chunks[step], "orb", route))
    return received


def in_vmem(count):
    return [pl.BlockSpec(memory_space=pltpu.VMEM)] * count


def in_smem(count):
    return [pl.BlockSpec(memory_space=pltpu.SMEM)] * count


def params(mib):
    return pltpu.CompilerParams(vmem_limit_bytes=mib * MIB)


def shape_of(shape, kind):
    return jax.ShapeDtypeStruct(shape, kind)


def pair_body(
    orbitals, potential, projectors, projector_energy, atom_first, atom_second, atom_third, rotation
):
    bf16, f32 = jnp.bfloat16, jnp.float32
    count, block_x, y_size, z_size = orbitals.shape[1:]
    x_size = 2 * block_x
    own = block_x * y_size
    cell_count = x_size * y_size
    atoms, nproj = projectors.shape[:2]
    spots = SIDE * atoms * nproj
    sources = lax.axis_size("orb")
    used = count * block_x
    chunk = -(-(used + count - 1) // 16) * 16

    sent = pl.pallas_call(
        face_kernel,
        out_shape=shape_of((count + 1, block_x, y_size, z_size), bf16),
        in_specs=in_vmem(2),
        out_specs=in_vmem(1)[0],
        compiler_params=params(16),
        name="faces",
    )(orbitals, potential)
    partner = lax.ppermute(sent, "dom", [(0, 1), (1, 0)])

    q, q_low, qt, mask, energy = pl.pallas_call(
        functools.partial(projector_kernel, cells=(block_x, x_size, y_size, z_size)),
        out_shape=(
            shape_of((spots, 2 * cell_count), bf16),
            shape_of((spots, cell_count), bf16),
            shape_of((cell_count, 3 * spots), bf16),
            shape_of((spots, z_size), f32),
            shape_of((atoms * nproj, z_size), f32),
        ),
        in_specs=in_smem(4) + in_vmem(2),
        out_specs=tuple(in_vmem(5)),
        compiler_params=params(24),
        cost_estimate=pl.CostEstimate(flops=1 << 30, bytes_accessed=3 << 20, transcendentals=0),
        name="projector_tables",
    )(atom_first, atom_second, atom_third, projector_energy, projectors, third_first())

    filtered = pl.pallas_call(
        filter_kernel,
        out_shape=(shape_of((chunk, z_size), bf16),) * sources,
        in_specs=in_vmem(11),
        out_specs=tuple(in_vmem(sources)),
        scratch_shapes=[
            pltpu.VMEM((cell_count, count * z_size), f32),
            pltpu.VMEM((cell_count, count * z_size), f32),
            pltpu.VMEM((cell_count, z_size), f32),
            pltpu.VMEM((2 * cell_count, count * z_size), bf16),
            pltpu.VMEM((3 * spots, count * z_size), bf16),
            pltpu.VMEM((count * own, z_size), f32),
            pltpu.VMEM((sources, chunk, z_size), f32),
        ],
        compiler_params=params(40),
        name="filter",
    )(
        orbitals,
        partner,
        potential,
        q,
        q_low,
        qt,
        mask,
        energy,
        rotation,
        plane_stencil(x_size, y_size),
        third_stencil(z_size),
    )
    by_plane = swap_chunks(filtered)

    rotated = pl.pallas_call(
        functools.partial(rotate_kernel, count=count, block_x=block_x, sources=sources),
        out_shape=(shape_of((chunk, z_size), bf16),) * sources,
        in_specs=in_vmem(sources),
        out_specs=tuple(in_vmem(sources)),
        scratch_shapes=[
            pltpu.VMEM((sources * chunk, z_size), f32),
            pltpu.VMEM((sources * chunk, z_size), f32),
        ],
        compiler_params=params(24),
        name="rotate",
    )(*by_plane)
    by_orbital = swap_chunks(rotated)

    return pl.pallas_call(
        unpack_kernel,
        out_shape=shape_of(orbitals.shape, bf16),
        in_specs=in_vmem(sources),
        out_specs=in_vmem(1)[0],
        scratch_shapes=[pltpu.VMEM((sources * used, z_size), f32)],
        compiler_params=params(16),
        name="unpack",
    )(*by_orbital)


def fits_pair(mesh, orbitals, projectors, rotation):
    count = orbitals.shape[1] // mesh.shape["orb"]
    return (
        mesh.shape["dom"] == 2
        and mesh.shape["orb"] & (mesh.shape["orb"] - 1) == 0
        and orbitals.shape[3] == mesh.shape["orb"]
        and orbitals.shape[2] == 2 * stencil_reach
        and projectors.shape[0] % 2 == 0
        and projectors.shape[1] == 8
        and count <= 8
        and rotation.shape[1] < orbitals.shape[4]
        and -(-rotation.shape[1] // (orbitals.shape[4] - rotation.shape[1])) < count
    )


def solution(mesh):
    def whole(*arrays):
        chosen = pair_body if fits_pair(mesh, arrays[0], arrays[2], arrays[7]) else body
        return jax.shard_map(
            chosen,
            mesh=mesh,
            in_specs=(
                P("dom", "orb", None, None, None),
                P("dom", None, None, None),
                P(),
                P(),
                P(),
                P(),
                P(),
                P("orb", None),
            ),
            out_specs=P("dom", "orb", None, None, None),
            check_vma=False,
        )(*arrays)

    return whole
```

```python
import functools

import jax
import jax.numpy as jnp
import numpy as np
from jax import lax
from jax.experimental import pallas as pl
from jax.experimental.pallas import tpu as pltpu
from jax.sharding import PartitionSpec as P

SIDE = 8
SUP = 512


stencil_weights = (
    -5369.0 / 1800.0,
    12.0 / 7.0,
    -15.0 / 56.0,
    10.0 / 189.0,
    -1.0 / 112.0,
    2.0 / 1925.0,
    -1.0 / 16632.0,
)
inverse_spacing = 4.0
filter_center = 120.0
filter_width = 110.0
stencil_reach = 6


def partner_2(block, axis, bit):
    count = lax.axis_size(axis)
    route = []
    for low in range(count):
        high = low | 1 << bit
        if high != low and high < count:
            route += [(low, high), (high, low)]
    return lax.ppermute(block, axis, route)


def outgoing(values, direction, width):
    extent = values.shape[direction]
    if 2 * width < extent:
        return jnp.concatenate(
            (
                lax.slice_in_dim(values, 0, width, axis=direction),
                lax.slice_in_dim(values, extent - width, extent, axis=direction),
            ),
            axis=direction,
        )
    return values


def assemble(values, partner, direction, width):
    extent = values.shape[direction]
    if 2 * width < extent:
        lower_rim = lax.slice_in_dim(partner, width, 2 * width, axis=direction)
        upper_rim = lax.slice_in_dim(partner, 0, width, axis=direction)
        return jnp.concatenate((lower_rim, values, upper_rim), axis=direction)
    cyclic = jnp.concatenate((values, partner), axis=direction)
    chosen = np.arange(-width, extent + width) % (2 * extent)
    return jnp.take(cyclic, jnp.asarray(chosen, dtype=jnp.int32), axis=direction)


def face_padded(values, direction, bit_number):
    sent = outgoing(values, direction, stencil_reach)
    partner = partner_2(sent.astype(jnp.bfloat16), "dom", bit_number).astype(sent.dtype)
    return assemble(values, partner, direction, stencil_reach)


def stencil_sum(center, along):
    lead = center.ndim - 3
    summed = 3.0 * stencil_weights[0] * center
    for index in range(3):
        direction = lead + index
        extent = center.shape[direction]
        padded = along[index]
        for offset in range(1, 7):
            if padded is None:
                upward = jnp.roll(center, -offset, direction)
                downward = jnp.roll(center, offset, direction)
            else:
                upward = lax.slice_in_dim(
                    padded, stencil_reach + offset, stencil_reach + offset + extent, axis=direction
                )
                downward = lax.slice_in_dim(
                    padded, stencil_reach - offset, stencil_reach - offset + extent, axis=direction
                )
            summed = summed + stencil_weights[offset] * (upward + downward)
    return summed


def support_map(atom_coords, starts, extents, periods):
    offsets = jnp.arange(SIDE, dtype=jnp.int32) - SIDE // 2
    clipped_list = []
    inside_list = []
    for index in range(3):
        local = (atom_coords[index][:, None] + offsets[None, :] - starts[index]) % periods[index]
        inside_list.append(local < extents[index])
        clipped_list.append(jnp.minimum(local, extents[index] - 1))
    inside = (
        inside_list[0][:, :, None, None]
        & inside_list[1][:, None, :, None]
        & inside_list[2][:, None, None, :]
    )
    flattened = (
        clipped_list[0][:, :, None, None] * extents[1] + clipped_list[1][:, None, :, None]
    ) * extents[2] + clipped_list[2][:, None, None, :]
    atom_count = atom_coords[0].shape[0]
    return (
        flattened.reshape(atom_count * SUP),
        inside.reshape(atom_count, SUP).astype(jnp.float32),
    )


def coefficients(values, support, inside, projectors):
    orbital_count = values.shape[0]
    atom_count = projectors.shape[0]
    flattened = values.reshape(orbital_count, -1)
    picked = (
        jnp.take(flattened, support, axis=1).reshape(orbital_count, atom_count, SUP) * inside[None]
    )
    partial_coeffs = jnp.einsum("aps,kas->kap", projectors, picked, precision=lax.Precision.HIGHEST)
    return lax.psum(partial_coeffs, "dom")


def spread_into(coeffs, shape, support, inside, projectors, projector_energy):
    orbital_count = shape[0]
    atom_count = projectors.shape[0]
    scaled = coeffs * projector_energy[None, None, :]
    spread = (
        jnp.einsum("aps,kap->kas", projectors, scaled, precision=lax.Precision.HIGHEST)
        * inside[None]
    )
    total_cells = shape[1] * shape[2] * shape[3]
    projected_part = (
        jnp.zeros((orbital_count, total_cells), jnp.float32)
        .at[:, support]
        .add(spread.reshape(orbital_count, atom_count * SUP))
    )
    return projected_part.reshape(shape)


def own_hamiltonian(center, along, local_field, support, inside, projectors, projector_energy):
    kinetic = -0.5 * inverse_spacing * inverse_spacing
    coeffs = coefficients(center, support, inside, projectors)
    projected_part = spread_into(
        coeffs, center.shape, support, inside, projectors, projector_energy
    )
    return kinetic * stencil_sum(center, along) + local_field[None] * center + projected_part


def body(
    orbitals, potential, projectors, projector_energy, atom_first, atom_second, atom_third, rotation
):
    domain_count = lax.axis_size("dom")
    domain_bits = domain_count.bit_length() - 1
    split = [index < domain_bits for index in range(3)]
    start_values = orbitals[0]
    local_field = potential[0]
    extents = start_values.shape[1:]
    periods = (
        extents[0] * min(domain_count, 2),
        extents[1] * min(max(domain_count // 2, 1), 2),
        extents[2] * max(domain_count // 4, 1),
    )
    domain_index = lax.axis_index("dom")
    anchors = (
        domain_index % 2 * extents[0],
        domain_index // 2 % 2 * extents[1],
        domain_index // 4 * extents[2],
    )
    atom_coords = (atom_first, atom_second, atom_third)
    support, inside = support_map(atom_coords, anchors, extents, periods)
    along = [
        face_padded(start_values, index + 1, index) if split[index] else None for index in range(3)
    ]
    first_apply = own_hamiltonian(
        start_values, along, local_field, support, inside, projectors, projector_energy
    )
    first_term = (first_apply - filter_center * start_values) / filter_width
    along = [
        face_padded(first_term, index + 1, index) if split[index] else None for index in range(3)
    ]
    second_apply = own_hamiltonian(
        first_term, along, local_field, support, inside, projectors, projector_energy
    )
    second_term = 2.0 * (second_apply - filter_center * first_term) / filter_width - start_values
    per_device = start_values.shape[0]
    filtered = second_term.astype(jnp.bfloat16).reshape(per_device, -1)
    by_cells = lax.all_to_all(filtered, "orb", split_axis=1, concat_axis=0, tiled=True)
    whole_rotation = lax.all_gather(rotation, "orb", axis=0, tiled=True)
    rotated = lax.dot_general(
        whole_rotation, by_cells, (((0,), (0,)), ((), ())), preferred_element_type=jnp.float32
    ).astype(jnp.bfloat16)
    result = lax.all_to_all(rotated, "orb", split_axis=0, concat_axis=1, tiled=True)
    return result.reshape((1,) + start_values.shape)


SCALE = 15.0
MIB = 1 << 20


def scaled_weights():
    ratios = np.array(stencil_weights[1:], np.float64) / stencil_weights[1]
    return SCALE * ratios


def cyclic_stencil(size):
    matrix = np.zeros((size, size), np.float64)
    rows = np.arange(size)
    for offset, weight in enumerate(scaled_weights(), 1):
        np.add.at(matrix, (rows, (rows + offset) % size), weight)
        np.add.at(matrix, (rows, (rows - offset) % size), weight)
    return matrix


def plane_stencil(x_size, y_size):
    matrix = np.kron(cyclic_stencil(x_size), np.eye(y_size))
    matrix += np.kron(np.eye(x_size), cyclic_stencil(y_size))
    return np.concatenate((matrix, matrix), axis=1).astype(jnp.bfloat16)


def third_stencil(z_size):
    matrix = cyclic_stencil(z_size)
    return np.concatenate((matrix, matrix), axis=0).astype(jnp.bfloat16)


def third_first():
    picked = np.zeros((SUP, SUP), np.float32)
    source = np.arange(SUP)
    picked[source, source % SIDE * SIDE * SIDE + source // SIDE] = 1.0
    return picked.astype(jnp.bfloat16)


def halves(values):
    high = values.astype(jnp.bfloat16)
    return high, (values - high.astype(jnp.float32)).astype(jnp.bfloat16)


def matmul(left, right):
    return jnp.dot(left, right, preferred_element_type=jnp.float32)


def face_kernel(orbital_ref, potential_ref, out_ref):
    count = orbital_ref.shape[1]
    out_ref[0:count] = orbital_ref[0].astype(jnp.bfloat16)
    out_ref[count] = potential_ref[0].astype(jnp.bfloat16)


def projector_kernel(
    first_ref,
    second_ref,
    third_ref,
    energy_ref,
    projector_ref,
    order_ref,
    q_ref,
    q_low_ref,
    qt_ref,
    mask_ref,
    energy_out_ref,
    *,
    cells,
):
    block_x, x_size, y_size, z_size = cells
    atoms, nproj = projector_ref.shape[:2]
    pairs = atoms * nproj
    per_plane = SIDE * SIDE
    spots = atoms * per_plane
    own_start = lax.axis_index("dom") * block_x
    high, low = halves(projector_ref[...].reshape(pairs, SUP))
    ordered = matmul(jnp.concatenate((high, low), axis=0), order_ref[...])

    lane = lax.broadcasted_iota(jnp.int32, (pairs, 2 * per_plane), 1)
    row_atom = lax.broadcasted_iota(jnp.int32, (pairs, spots), 0) // nproj
    lane_atom = lax.broadcasted_iota(jnp.int32, (pairs, spots), 1) // per_plane
    same_atom = row_atom == lane_atom
    expanded = []
    for part in range(2):
        rows = []
        for third in range(SIDE):
            start = third // 2 * 2 * per_plane
            both = ordered[part * pairs : (part + 1) * pairs, start : start + 2 * per_plane]
            swapped = pltpu.roll(both, per_plane, 1)
            if third % 2:
                both, swapped = swapped, both
            doubled = jnp.where(lane < per_plane, both, swapped)
            doubled = jnp.concatenate([doubled] * (atoms // 2), axis=1)
            rows.append(jnp.where(same_atom, doubled, 0.0))
        expanded.append(jnp.concatenate(rows, axis=0).astype(jnp.bfloat16))

    place = []
    spot = lax.broadcasted_iota(jnp.int32, (per_plane, x_size * y_size), 0)
    place_lane = lax.broadcasted_iota(jnp.int32, (per_plane, x_size * y_size), 1)
    for atom in range(atoms):
        x_start = lax.rem(first_ref[atom] - SIDE // 2 - own_start + 2 * x_size, x_size)
        y_start = lax.rem(second_ref[atom] - SIDE // 2 + y_size, y_size)
        x_index = x_start + spot // SIDE
        x_index = jnp.where(x_index >= x_size, x_index - x_size, x_index)
        y_index = y_start + spot % SIDE
        y_index = jnp.where(y_index >= y_size, y_index - y_size, y_index)
        target = x_index * y_size + y_index
        place.append(jnp.where(place_lane == target, 1.0, 0.0).astype(jnp.bfloat16))
    place = jnp.concatenate(place, axis=0)
    cell_count = x_size * y_size
    q_high = matmul(expanded[0], place)
    q_low = matmul(expanded[1], place)
    q_ref[:, 0:cell_count] = q_high.astype(jnp.bfloat16)
    q_ref[:, cell_count : 2 * cell_count] = q_high.astype(jnp.bfloat16)
    q_low_ref[...] = q_low.astype(jnp.bfloat16)
    rows = q_high.shape[0]
    q_high = q_high.T.astype(jnp.bfloat16)
    qt_ref[:, 0:rows] = q_high
    qt_ref[:, rows : 2 * rows] = q_high
    qt_ref[:, 2 * rows : 3 * rows] = q_low.T.astype(jnp.bfloat16)

    z_lane = lax.broadcasted_iota(jnp.int32, (nproj, z_size), 1)
    for third in range(SIDE):
        for atom in range(atoms):
            z_index = lax.rem(third_ref[atom] + third - SIDE // 2 + z_size, z_size)
            start = third * pairs + atom * nproj
            mask_ref[start : start + nproj] = jnp.where(z_lane == z_index, 1.0, 0.0)
    sublane = lax.broadcasted_iota(jnp.int32, (nproj, z_size), 0)
    energy = jnp.zeros((nproj, z_size), jnp.float32)
    for index in range(nproj):
        energy = jnp.where(sublane == index, energy_ref[index], energy)
    for atom in range(atoms):
        energy_out_ref[atom * nproj : (atom + 1) * nproj] = energy


def filter_kernel(
    orbital_ref,
    partner_ref,
    potential_ref,
    q_ref,
    q_low_ref,
    qt_ref,
    mask_ref,
    energy_ref,
    rotation_ref,
    plane_ref,
    third_ref,
    out_ref,
    start_ref,
    first_ref,
    diagonal_ref,
    right_ref,
    coeff_ref,
):
    count, block_x, y_size, z_size = orbital_ref.shape[1:]
    own = block_x * y_size
    cell_count = 2 * own
    pairs = energy_ref.shape[0]
    spots = mask_ref.shape[0]
    kinetic = -0.5 * inverse_spacing * inverse_spacing
    unit = kinetic * stencil_weights[1] / SCALE / filter_width

    shift = 3.0 * kinetic * stencil_weights[0] - filter_center
    diagonal_ref[0:own] = (potential_ref[0].reshape(own, z_size) + shift) / filter_width
    partner_potential = partner_ref[count].astype(jnp.float32).reshape(own, z_size)
    diagonal_ref[own:] = (partner_potential + shift) / filter_width
    for orbital in range(count):
        lanes = slice(orbital * z_size, (orbital + 1) * z_size)
        start_ref[0:own, lanes] = orbital_ref[0, orbital].reshape(own, z_size)
        start_ref[own:, lanes] = (
            partner_ref[orbital].astype(jnp.float32).reshape(own, z_size)
        )

    def operate(source_ref, rows, finish):
        high, low = halves(source_ref[...])
        right_ref[0:cell_count] = high
        right_ref[cell_count:] = low
        products = matmul(q_ref[...], right_ref[...])
        products = products + matmul(q_low_ref[...], right_ref[0:cell_count])
        mask = mask_ref[...]
        for orbital in range(count):
            lanes = slice(orbital * z_size, (orbital + 1) * z_size)
            picked = (products[:, lanes] * mask).reshape(SIDE, pairs, z_size)
            coeffs = jnp.sum(jnp.sum(picked, axis=0), axis=1, keepdims=True)
            scaled = coeffs * energy_ref[...] * (1.0 / (unit * filter_width))
            spread = jnp.concatenate([scaled] * SIDE, axis=0) * mask
            high, low = halves(spread)
            coeff_ref[0:spots, lanes] = high
            coeff_ref[spots : 2 * spots, lanes] = low
            coeff_ref[2 * spots :, lanes] = high
        summed = matmul(plane_ref[0:rows], right_ref[...])
        summed = summed + matmul(qt_ref[0:rows], coeff_ref[...])
        for orbital in range(count):
            lanes = slice(orbital * z_size, (orbital + 1) * z_size)
            left = jnp.concatenate(
                (
                    right_ref[0:rows, lanes],
                    right_ref[cell_count : cell_count + rows, lanes],
                ),
                axis=1,
            )
            along = summed[:, lanes] + matmul(left, third_ref[...])
            values = diagonal_ref[0:rows] * source_ref[0:rows, lanes] + unit * along
            finish(orbital, lanes, values)

    def keep(orbital, lanes, values):
        first_ref[:, lanes] = values

    def emit(orbital, lanes, values):
        values = (2.0 * values - start_ref[0:own, lanes]).astype(jnp.bfloat16)
        for plane in range(block_x):
            start = (plane * count + orbital) * y_size
            out_ref[start : start + y_size] = values[plane * y_size : (plane + 1) * y_size]

    operate(start_ref, cell_count, keep)
    operate(first_ref, own, emit)

    tail = block_x * count * y_size
    wide = rotation_ref.shape[1]
    block = jnp.concatenate(
        (rotation_ref[...].astype(jnp.float32), jnp.zeros((count, z_size - wide), jnp.float32)),
        axis=1,
    )
    pad = out_ref.shape[0] - tail - count
    block = jnp.concatenate((block, jnp.zeros((pad, z_size), jnp.float32)), axis=0)
    out_ref[tail:] = block.astype(jnp.bfloat16)


def rotate_kernel(rows_ref, received_ref, out_ref, kron_ref, *, count, y_size):
    sources, z_size = received_ref.shape[0], received_ref.shape[2]
    total = sources * count
    made = count * y_size

    @pl.when(pl.program_id(0) == 0)
    def build():
        rotation = jnp.concatenate([rows_ref[part, 0:count] for part in range(sources)], axis=0)
        first = lax.axis_index("orb") * count
        row = lax.broadcasted_iota(jnp.int32, (made, z_size), 0)
        lane = lax.broadcasted_iota(jnp.int32, (made, z_size), 1)
        pick = jnp.where(lane == first + row // y_size, 1.0, 0.0).astype(jnp.bfloat16)
        own = lax.dot_general(
            pick, rotation, (((1,), (1,)), ((), ())), preferred_element_type=jnp.float32
        ).astype(jnp.bfloat16)
        row = lax.broadcasted_iota(jnp.int32, (total, total * y_size), 0)
        lane = lax.broadcasted_iota(jnp.int32, (total, total * y_size), 1)
        spread = matmul(own, jnp.where(lane // y_size == row, 1.0, 0.0).astype(jnp.bfloat16))
        row = lax.broadcasted_iota(jnp.int32, (made, total * y_size), 0)
        lane = lax.broadcasted_iota(jnp.int32, (made, total * y_size), 1)
        same = row % y_size == lane % y_size
        kron_ref[...] = jnp.where(same, spread, 0.0).astype(jnp.bfloat16)

    planes = received_ref.shape[1] // made
    columns = [
        received_ref[:, plane * made : (plane + 1) * made].reshape(total * y_size, z_size)
        for plane in range(planes)
    ]
    rotated = matmul(kron_ref[...], jnp.concatenate(columns, axis=1)).astype(jnp.bfloat16)
    for plane in range(planes):
        lanes = slice(plane * z_size, (plane + 1) * z_size)
        out_ref[0, :, plane] = rotated[:, lanes].reshape(count, y_size, z_size)


def in_vmem(count):
    return [pl.BlockSpec(memory_space=pltpu.VMEM)] * count


def in_smem(count):
    return [pl.BlockSpec(memory_space=pltpu.SMEM)] * count


def params(mib):
    return pltpu.CompilerParams(vmem_limit_bytes=mib * MIB)


def shape_of(shape, kind):
    return jax.ShapeDtypeStruct(shape, kind)


def pair_body(
    orbitals, potential, projectors, projector_energy, atom_first, atom_second, atom_third, rotation
):
    bf16, f32 = jnp.bfloat16, jnp.float32
    count, block_x, y_size, z_size = orbitals.shape[1:]
    x_size = 2 * block_x
    own = block_x * y_size
    cell_count = x_size * y_size
    atoms, nproj = projectors.shape[:2]
    spots = SIDE * atoms * nproj
    sources = lax.axis_size("orb")
    made = count * y_size
    height = block_x * made + -(-count // 16) * 16

    sent = pl.pallas_call(
        face_kernel,
        out_shape=shape_of((count + 1, block_x, y_size, z_size), bf16),
        in_specs=in_vmem(2),
        out_specs=in_vmem(1)[0],
        compiler_params=params(16),
        name="faces",
    )(orbitals, potential)
    partner = lax.ppermute(sent, "dom", [(0, 1), (1, 0)])

    q, q_low, qt, mask, energy = pl.pallas_call(
        functools.partial(projector_kernel, cells=(block_x, x_size, y_size, z_size)),
        out_shape=(
            shape_of((spots, 2 * cell_count), bf16),
            shape_of((spots, cell_count), bf16),
            shape_of((cell_count, 3 * spots), bf16),
            shape_of((spots, z_size), f32),
            shape_of((atoms * nproj, z_size), f32),
        ),
        in_specs=in_smem(4) + in_vmem(2),
        out_specs=tuple(in_vmem(5)),
        compiler_params=params(24),
        cost_estimate=pl.CostEstimate(flops=1 << 30, bytes_accessed=3 << 20, transcendentals=0),
        name="projector_tables",
    )(atom_first, atom_second, atom_third, projector_energy, projectors, third_first())

    filtered = pl.pallas_call(
        filter_kernel,
        out_shape=shape_of((height, z_size), bf16),
        in_specs=in_vmem(11),
        out_specs=in_vmem(1)[0],
        scratch_shapes=[
            pltpu.VMEM((cell_count, count * z_size), f32),
            pltpu.VMEM((cell_count, count * z_size), f32),
            pltpu.VMEM((cell_count, z_size), f32),
            pltpu.VMEM((2 * cell_count, count * z_size), bf16),
            pltpu.VMEM((3 * spots, count * z_size), bf16),
        ],
        compiler_params=params(40),
        name="filter",
    )(
        orbitals,
        partner,
        potential,
        q,
        q_low,
        qt,
        mask,
        energy,
        rotation,
        plane_stencil(x_size, y_size),
        third_stencil(z_size),
    )
    everything = lax.all_gather(filtered, "orb", axis=0, tiled=False)
    planes = 2
    return pl.pallas_call(
        functools.partial(rotate_kernel, count=count, y_size=y_size),
        out_shape=shape_of(orbitals.shape, bf16),
        grid=(block_x // planes,),
        in_specs=[
            pl.BlockSpec((sources, 16, z_size), lambda step: (0, block_x * made // 16, 0)),
            pl.BlockSpec((sources, planes * made, z_size), lambda step: (0, step, 0)),
        ],
        out_specs=pl.BlockSpec(
            (1, count, planes, y_size, z_size), lambda step: (0, 0, step, 0, 0)
        ),
        scratch_shapes=[pltpu.VMEM((made, sources * made), bf16)],
        compiler_params=params(32),
        name="rotate",
    )(everything, everything)


def fits_pair(mesh, orbitals, projectors, rotation):
    count = orbitals.shape[1] // mesh.shape["orb"]
    return (
        mesh.shape["dom"] == 2
        and orbitals.shape[3] == mesh.shape["orb"]
        and orbitals.shape[2] == 2 * stencil_reach
        and projectors.shape[0] % 2 == 0
        and projectors.shape[1] == 8
        and orbitals.shape[3] % 16 == 0
        and rotation.shape[1] < orbitals.shape[4]
    )


def solution(mesh):
    def whole(*arrays):
        chosen = pair_body if fits_pair(mesh, arrays[0], arrays[2], arrays[7]) else body
        return jax.shard_map(
            chosen,
            mesh=mesh,
            in_specs=(
                P("dom", "orb", None, None, None),
                P("dom", None, None, None),
                P(),
                P(),
                P(),
                P(),
                P(),
                P("orb", None),
            ),
            out_specs=P("dom", "orb", None, None, None),
            check_vma=False,
        )(*arrays)

    return whole
```

```python
import functools

import jax
import jax.numpy as jnp
import numpy as np
from jax import lax
from jax.experimental import pallas as pl
from jax.experimental.pallas import tpu as pltpu
from jax.sharding import PartitionSpec as P

SIDE = 8
SUP = 512


stencil_weights = (
    -5369.0 / 1800.0,
    12.0 / 7.0,
    -15.0 / 56.0,
    10.0 / 189.0,
    -1.0 / 112.0,
    2.0 / 1925.0,
    -1.0 / 16632.0,
)
inverse_spacing = 4.0
filter_center = 120.0
filter_width = 110.0
stencil_reach = 6


def partner_2(block, axis, bit):
    count = lax.axis_size(axis)
    route = []
    for low in range(count):
        high = low | 1 << bit
        if high != low and high < count:
            route += [(low, high), (high, low)]
    return lax.ppermute(block, axis, route)


def outgoing(values, direction, width):
    extent = values.shape[direction]
    if 2 * width < extent:
        return jnp.concatenate(
            (
                lax.slice_in_dim(values, 0, width, axis=direction),
                lax.slice_in_dim(values, extent - width, extent, axis=direction),
            ),
            axis=direction,
        )
    return values


def assemble(values, partner, direction, width):
    extent = values.shape[direction]
    if 2 * width < extent:
        lower_rim = lax.slice_in_dim(partner, width, 2 * width, axis=direction)
        upper_rim = lax.slice_in_dim(partner, 0, width, axis=direction)
        return jnp.concatenate((lower_rim, values, upper_rim), axis=direction)
    cyclic = jnp.concatenate((values, partner), axis=direction)
    chosen = np.arange(-width, extent + width) % (2 * extent)
    return jnp.take(cyclic, jnp.asarray(chosen, dtype=jnp.int32), axis=direction)


def face_padded(values, direction, bit_number):
    sent = outgoing(values, direction, stencil_reach)
    partner = partner_2(sent.astype(jnp.bfloat16), "dom", bit_number).astype(sent.dtype)
    return assemble(values, partner, direction, stencil_reach)


def stencil_sum(center, along):
    lead = center.ndim - 3
    summed = 3.0 * stencil_weights[0] * center
    for index in range(3):
        direction = lead + index
        extent = center.shape[direction]
        padded = along[index]
        for offset in range(1, 7):
            if padded is None:
                upward = jnp.roll(center, -offset, direction)
                downward = jnp.roll(center, offset, direction)
            else:
                upward = lax.slice_in_dim(
                    padded, stencil_reach + offset, stencil_reach + offset + extent, axis=direction
                )
                downward = lax.slice_in_dim(
                    padded, stencil_reach - offset, stencil_reach - offset + extent, axis=direction
                )
            summed = summed + stencil_weights[offset] * (upward + downward)
    return summed


def support_map(atom_coords, starts, extents, periods):
    offsets = jnp.arange(SIDE, dtype=jnp.int32) - SIDE // 2
    clipped_list = []
    inside_list = []
    for index in range(3):
        local = (atom_coords[index][:, None] + offsets[None, :] - starts[index]) % periods[index]
        inside_list.append(local < extents[index])
        clipped_list.append(jnp.minimum(local, extents[index] - 1))
    inside = (
        inside_list[0][:, :, None, None]
        & inside_list[1][:, None, :, None]
        & inside_list[2][:, None, None, :]
    )
    flattened = (
        clipped_list[0][:, :, None, None] * extents[1] + clipped_list[1][:, None, :, None]
    ) * extents[2] + clipped_list[2][:, None, None, :]
    atom_count = atom_coords[0].shape[0]
    return (
        flattened.reshape(atom_count * SUP),
        inside.reshape(atom_count, SUP).astype(jnp.float32),
    )


def coefficients(values, support, inside, projectors):
    orbital_count = values.shape[0]
    atom_count = projectors.shape[0]
    flattened = values.reshape(orbital_count, -1)
    picked = (
        jnp.take(flattened, support, axis=1).reshape(orbital_count, atom_count, SUP) * inside[None]
    )
    partial_coeffs = jnp.einsum("aps,kas->kap", projectors, picked, precision=lax.Precision.HIGHEST)
    return lax.psum(partial_coeffs, "dom")


def spread_into(coeffs, shape, support, inside, projectors, projector_energy):
    orbital_count = shape[0]
    atom_count = projectors.shape[0]
    scaled = coeffs * projector_energy[None, None, :]
    spread = (
        jnp.einsum("aps,kap->kas", projectors, scaled, precision=lax.Precision.HIGHEST)
        * inside[None]
    )
    total_cells = shape[1] * shape[2] * shape[3]
    projected_part = (
        jnp.zeros((orbital_count, total_cells), jnp.float32)
        .at[:, support]
        .add(spread.reshape(orbital_count, atom_count * SUP))
    )
    return projected_part.reshape(shape)


def own_hamiltonian(center, along, local_field, support, inside, projectors, projector_energy):
    kinetic = -0.5 * inverse_spacing * inverse_spacing
    coeffs = coefficients(center, support, inside, projectors)
    projected_part = spread_into(
        coeffs, center.shape, support, inside, projectors, projector_energy
    )
    return kinetic * stencil_sum(center, along) + local_field[None] * center + projected_part


def body(
    orbitals, potential, projectors, projector_energy, atom_first, atom_second, atom_third, rotation
):
    domain_count = lax.axis_size("dom")
    domain_bits = domain_count.bit_length() - 1
    split = [index < domain_bits for index in range(3)]
    start_values = orbitals[0]
    local_field = potential[0]
    extents = start_values.shape[1:]
    periods = (
        extents[0] * min(domain_count, 2),
        extents[1] * min(max(domain_count // 2, 1), 2),
        extents[2] * max(domain_count // 4, 1),
    )
    domain_index = lax.axis_index("dom")
    anchors = (
        domain_index % 2 * extents[0],
        domain_index // 2 % 2 * extents[1],
        domain_index // 4 * extents[2],
    )
    atom_coords = (atom_first, atom_second, atom_third)
    support, inside = support_map(atom_coords, anchors, extents, periods)
    along = [
        face_padded(start_values, index + 1, index) if split[index] else None for index in range(3)
    ]
    first_apply = own_hamiltonian(
        start_values, along, local_field, support, inside, projectors, projector_energy
    )
    first_term = (first_apply - filter_center * start_values) / filter_width
    along = [
        face_padded(first_term, index + 1, index) if split[index] else None for index in range(3)
    ]
    second_apply = own_hamiltonian(
        first_term, along, local_field, support, inside, projectors, projector_energy
    )
    second_term = 2.0 * (second_apply - filter_center * first_term) / filter_width - start_values
    per_device = start_values.shape[0]
    filtered = second_term.astype(jnp.bfloat16).reshape(per_device, -1)
    by_cells = lax.all_to_all(filtered, "orb", split_axis=1, concat_axis=0, tiled=True)
    whole_rotation = lax.all_gather(rotation, "orb", axis=0, tiled=True)
    rotated = lax.dot_general(
        whole_rotation, by_cells, (((0,), (0,)), ((), ())), preferred_element_type=jnp.float32
    ).astype(jnp.bfloat16)
    result = lax.all_to_all(rotated, "orb", split_axis=0, concat_axis=1, tiled=True)
    return result.reshape((1,) + start_values.shape)


SCALE = 15.0
MIB = 1 << 20


def scaled_weights():
    ratios = np.array(stencil_weights[1:], np.float64) / stencil_weights[1]
    return SCALE * ratios


def cyclic_stencil(size):
    matrix = np.zeros((size, size), np.float64)
    rows = np.arange(size)
    for offset, weight in enumerate(scaled_weights(), 1):
        np.add.at(matrix, (rows, (rows + offset) % size), weight)
        np.add.at(matrix, (rows, (rows - offset) % size), weight)
    return matrix


def plane_stencil(x_size, y_size):
    matrix = np.kron(cyclic_stencil(x_size), np.eye(y_size))
    matrix += np.kron(np.eye(x_size), cyclic_stencil(y_size))
    own = x_size * y_size // 2
    pieces = (
        np.concatenate((matrix[:, :own], matrix[:, :own]), axis=1),
        matrix[:, own:],
        np.concatenate((matrix[:own], matrix[:own]), axis=1),
    )
    return [piece.astype(jnp.bfloat16) for piece in pieces]


def third_stencil(z_size):
    matrix = cyclic_stencil(z_size)
    return np.concatenate((matrix, matrix), axis=0).astype(jnp.bfloat16)


def third_first():
    picked = np.zeros((SUP, SUP), np.float32)
    source = np.arange(SUP)
    picked[source, source % SIDE * SIDE * SIDE + source // SIDE] = 1.0
    return picked.astype(jnp.bfloat16)


def halves(values):
    high = values.astype(jnp.bfloat16)
    return high, (values - high.astype(jnp.float32)).astype(jnp.bfloat16)


def matmul(left, right):
    return jnp.dot(left, right, preferred_element_type=jnp.float32)


def shared_operator():
    kinetic = -0.5 * inverse_spacing * inverse_spacing
    unit = kinetic * stencil_weights[1] / SCALE / filter_width
    shift = 3.0 * kinetic * stencil_weights[0] - filter_center
    return unit, shift


def face_kernel(orbital_ref, potential_ref, sent_ref, start_ref, field_ref, sem_ref):
    count = orbital_ref.shape[1]
    load = pltpu.make_async_copy(orbital_ref.at[0], start_ref, sem_ref.at[0])
    load_field = pltpu.make_async_copy(potential_ref.at[0], field_ref, sem_ref.at[1])
    load.start()
    load_field.start()
    load.wait()
    sent_ref[0:count] = start_ref[...].astype(jnp.bfloat16)
    load_field.wait()
    sent_ref[count] = field_ref[...].astype(jnp.bfloat16)


def placement(rows, targets, first_cell, cells, copies):
    shape = (rows, cells * copies)
    lane = lax.broadcasted_iota(jnp.int32, shape, 1)
    cell = lane
    for copy in range(1, copies):
        cell = jnp.where(lane >= copy * cells, lane - copy * cells, cell)
    cell = cell + first_cell
    return [jnp.where(cell == target, 1.0, 0.0).astype(jnp.bfloat16) for target in targets], lane


def prepare_kernel(
    first_at_ref,
    second_at_ref,
    third_at_ref,
    energy_at_ref,
    projector_ref,
    order_ref,
    start_ref,
    field_ref,
    plane_ref,
    third_ref,
    q_partner_ref,
    q_ref,
    q_low_ref,
    qt_ref,
    mask_ref,
    energy_ref,
    diagonal_ref,
    part_ref,
    product_ref,
    right_ref,
):
    count, block_x, y_size, z_size = start_ref.shape
    x_size = 2 * block_x
    own = block_x * y_size
    cell_count = x_size * y_size
    atoms, nproj = projector_ref.shape[:2]
    pairs = atoms * nproj
    per_plane = SIDE * SIDE
    spots = atoms * per_plane
    unit, shift = shared_operator()
    own_start = lax.axis_index("dom") * block_x
    high, low = halves(projector_ref[...].reshape(pairs, SUP))
    ordered = matmul(jnp.concatenate((high, low), axis=0), order_ref[...])

    lane = lax.broadcasted_iota(jnp.int32, (pairs, 2 * per_plane), 1)
    row_atom = lax.broadcasted_iota(jnp.int32, (pairs, spots), 0) // nproj
    lane_atom = lax.broadcasted_iota(jnp.int32, (pairs, spots), 1) // per_plane
    same_atom = row_atom == lane_atom
    expanded = []
    for part in range(2):
        rows = []
        for third in range(SIDE):
            start = third // 2 * 2 * per_plane
            both = ordered[part * pairs : (part + 1) * pairs, start : start + 2 * per_plane]
            swapped = pltpu.roll(both, per_plane, 1)
            if third % 2:
                both, swapped = swapped, both
            doubled = jnp.where(lane < per_plane, both, swapped)
            doubled = jnp.concatenate([doubled] * (atoms // 2), axis=1)
            rows.append(jnp.where(same_atom, doubled, 0.0))
        expanded.append(jnp.concatenate(rows, axis=0).astype(jnp.bfloat16))
    high, low = expanded

    targets = []
    spot = lax.broadcasted_iota(jnp.int32, (per_plane, 1), 0)
    for atom in range(atoms):
        x_start = lax.rem(first_at_ref[atom] - SIDE // 2 - own_start + 2 * x_size, x_size)
        y_start = lax.rem(second_at_ref[atom] - SIDE // 2 + y_size, y_size)
        x_index = x_start + spot // SIDE
        x_index = jnp.where(x_index >= x_size, x_index - x_size, x_index)
        y_index = y_start + spot % SIDE
        y_index = jnp.where(y_index >= y_size, y_index - y_size, y_index)
        targets.append(x_index * y_size + y_index)

    place, _ = placement(per_plane, targets, 0, cell_count, 1)
    place = jnp.concatenate(place, axis=0)
    q_high = matmul(high, place)
    q_low = matmul(low, place)
    q_ref[:, 0:cell_count] = q_high.astype(jnp.bfloat16)
    q_ref[:, cell_count : 2 * cell_count] = q_high.astype(jnp.bfloat16)
    q_low_ref[...] = q_low.astype(jnp.bfloat16)
    q_high = q_high.T.astype(jnp.bfloat16)
    qt_ref[:, 0:spots] = q_high
    qt_ref[:, spots : 2 * spots] = q_high
    qt_ref[:, 2 * spots : 3 * spots] = q_low.T.astype(jnp.bfloat16)

    place, place_lane = placement(per_plane, targets, own, own, 2)
    place = jnp.concatenate(place, axis=0)
    place_lane = lax.broadcasted_iota(jnp.int32, (spots, 2 * own), 1)
    both = jnp.where(place_lane < own, matmul(high, place), matmul(low, place))
    q_partner_ref[...] = both.astype(jnp.bfloat16)

    place, place_lane = placement(per_plane, targets, 0, own, 3)
    place = jnp.concatenate(place, axis=0)
    place_lane = lax.broadcasted_iota(jnp.int32, (spots, 3 * own), 1)
    q_own = jnp.where(place_lane < 2 * own, matmul(high, place), matmul(low, place))
    q_own = q_own.astype(jnp.bfloat16)

    z_lane = lax.broadcasted_iota(jnp.int32, (nproj, z_size), 1)
    for third in range(SIDE):
        for atom in range(atoms):
            z_index = lax.rem(third_at_ref[atom] + third - SIDE // 2 + z_size, z_size)
            start = third * pairs + atom * nproj
            mask_ref[start : start + nproj] = jnp.where(z_lane == z_index, 1.0, 0.0)
    sublane = lax.broadcasted_iota(jnp.int32, (nproj, z_size), 0)
    energy = jnp.zeros((nproj, z_size), jnp.float32)
    for index in range(nproj):
        energy = jnp.where(sublane == index, energy_at_ref[index], energy)
    energy = energy * (1.0 / (unit * filter_width))
    for atom in range(atoms):
        energy_ref[atom * nproj : (atom + 1) * nproj] = energy

    diagonal_ref[...] = (field_ref[...].reshape(own, z_size) + shift) / filter_width
    for orbital in range(count):
        lanes = slice(orbital * z_size, (orbital + 1) * z_size)
        high, low = halves(start_ref[orbital].reshape(own, z_size))
        right_ref[0:own, lanes] = high
        right_ref[own : 2 * own, lanes] = low
        right_ref[2 * own :, lanes] = high
    product_ref[...] = matmul(q_own, right_ref[...])
    summed = matmul(plane_ref[...], right_ref[0 : 2 * own])
    for orbital in range(count):
        lanes = slice(orbital * z_size, (orbital + 1) * z_size)
        left = jnp.concatenate((right_ref[0:own, lanes], right_ref[own : 2 * own, lanes]), axis=1)
        along = summed[0:own, lanes] + matmul(left, third_ref[...])
        values = diagonal_ref[...] * start_ref[orbital].reshape(own, z_size)
        part_ref[0:own, lanes] = values + unit * along
        part_ref[own:, lanes] = unit * summed[own:, lanes]


def filter_kernel(
    partner_ref,
    start_ref,
    q_partner_ref,
    q_ref,
    q_low_ref,
    qt_ref,
    mask_ref,
    energy_ref,
    diagonal_ref,
    part_ref,
    product_ref,
    rotation_ref,
    plane_partner_ref,
    plane_own_ref,
    third_ref,
    out_ref,
    right_ref,
    coeff_ref,
    rows_ref,
    chunk_ref,
    first_ref,
):
    count, block_x, y_size, z_size = start_ref.shape
    own = block_x * y_size
    cell_count = 2 * own
    pairs = energy_ref.shape[0]
    spots = mask_ref.shape[0]
    unit, shift = shared_operator()
    columns = [slice(orbital * z_size, (orbital + 1) * z_size) for orbital in range(count)]

    def spread(products):
        mask = mask_ref[...]
        for lanes in columns:
            picked = (products[:, lanes] * mask).reshape(SIDE, pairs, z_size)
            coeffs = jnp.sum(jnp.sum(picked, axis=0), axis=1, keepdims=True)
            high, low = halves(jnp.concatenate([coeffs * energy_ref[...]] * SIDE, axis=0) * mask)
            coeff_ref[0:spots, lanes] = high
            coeff_ref[spots : 2 * spots, lanes] = low
            coeff_ref[2 * spots :, lanes] = high

    for orbital, lanes in enumerate(columns):
        values = partner_ref[orbital].reshape(own, z_size)
        right_ref[0:own, lanes] = values
        right_ref[own : 2 * own, lanes] = values
    spread(product_ref[...] + matmul(q_partner_ref[...], right_ref[0:cell_count]))
    summed = matmul(plane_partner_ref[...], right_ref[0:own])
    summed = summed + matmul(qt_ref[...], coeff_ref[...])
    field = partner_ref[count].astype(jnp.float32).reshape(own, z_size)
    field = (field + shift) / filter_width
    for lanes in columns:
        values = right_ref[0:own, lanes]
        along = summed[own:, lanes] + matmul(values, third_ref[0:z_size])
        values = part_ref[own:, lanes] + field * values.astype(jnp.float32)
        first_ref[0:own, lanes] = part_ref[0:own, lanes] + unit * summed[0:own, lanes]
        first_ref[own:, lanes] = values + unit * along

    high, low = halves(first_ref[...])
    right_ref[0:cell_count] = high
    right_ref[cell_count:] = low
    spread(matmul(q_ref[...], right_ref[...]) + matmul(q_low_ref[...], right_ref[0:cell_count]))
    summed = matmul(plane_own_ref[...], right_ref[...])
    summed = summed + matmul(qt_ref[0:own], coeff_ref[...])
    for orbital, lanes in enumerate(columns):
        left = jnp.concatenate(
            (right_ref[0:own, lanes], right_ref[cell_count : cell_count + own, lanes]), axis=1
        )
        along = summed[:, lanes] + matmul(left, third_ref[...])
        values = diagonal_ref[...] * first_ref[0:own, lanes] + unit * along
        values = 2.0 * values - start_ref[orbital].reshape(own, z_size)
        rows_ref[orbital * own : (orbital + 1) * own] = values

    wide = rotation_ref.shape[1]
    spare = z_size - wide
    block = jnp.zeros((8, z_size), jnp.float32)
    block = jnp.concatenate(
        (rotation_ref[...].astype(jnp.float32), jnp.zeros((count, spare), jnp.float32)), axis=1
    )
    block = jnp.concatenate((block, jnp.zeros((8 - count, z_size), jnp.float32)), axis=0)
    sublane = lax.broadcasted_iota(jnp.int32, (8, z_size), 0)
    lane = lax.broadcasted_iota(jnp.int32, (8, z_size), 1)
    packed = block
    for piece in range(-(-wide // spare)):
        moved = pltpu.roll(block, (piece - (count - 1)) % 8, 0)
        moved = pltpu.roll(moved, (wide - piece * spare) % z_size, 1)
        packed = jnp.where((sublane == piece) & (lane >= wide), moved, packed)

    used = count * block_x
    for part in range(y_size):
        chunk_ref[part, 0:used] = rows_ref[pl.ds(part, used, stride=y_size), :]
        chunk_ref[part, used : used + count - 1] = packed[0 : count - 1]
    out_ref[...] = chunk_ref[...].astype(jnp.bfloat16)


def rotate_kernel(received_ref, out_ref, wide_ref, rows_ref, *, count, block_x):
    sources, chunk, z_size = received_ref.shape
    total = sources * count
    used = count * block_x
    spare = z_size - total
    wide_ref[...] = received_ref[...].astype(jnp.float32).reshape(sources * chunk, z_size)
    packed = [wide_ref[pl.ds(used + row, sources, stride=chunk), :] for row in range(count - 1)]
    lane = lax.broadcasted_iota(jnp.int32, (sources, z_size), 1)
    last = jnp.zeros((sources, z_size), jnp.float32)
    for piece in range(-(-total // spare)):
        moved = pltpu.roll(packed[piece], (piece * spare - total) % z_size, 1)
        last = jnp.where(lane >= piece * spare, moved, last)
    rotation = jnp.concatenate(packed + [last], axis=0)[:, 0:total].astype(jnp.bfloat16)
    columns = []
    for plane in range(block_x):
        rows = [
            wide_ref[pl.ds(orbital * block_x + plane, sources, stride=chunk), :]
            for orbital in range(count)
        ]
        columns.append(jnp.concatenate(rows, axis=0).astype(jnp.bfloat16))
    values = jnp.concatenate(columns, axis=1)
    rotated = lax.dot_general(
        rotation, values, (((0,), (0,)), ((), ())), preferred_element_type=jnp.float32
    )
    rows_ref[total * block_x :] = jnp.zeros((chunk - used, z_size), jnp.float32)
    for plane in range(block_x):
        lanes = slice(plane * z_size, (plane + 1) * z_size)
        rows_ref[pl.ds(plane, total, stride=block_x), :] = rotated[:, lanes]
    for part in range(sources):
        out_ref[part] = rows_ref[part * used : part * used + chunk].astype(jnp.bfloat16)


def unpack_kernel(received_ref, out_ref, rows_ref):
    sources, chunk, z_size = received_ref.shape
    used = rows_ref.shape[0] // sources
    for part in range(sources):
        values = received_ref[part].astype(jnp.float32)
        rows_ref[pl.ds(part, used, stride=sources), :] = values[0:used]
    out_ref[...] = rows_ref[...].astype(jnp.bfloat16).reshape(out_ref.shape)


def in_vmem(count):
    return [pl.BlockSpec(memory_space=pltpu.VMEM)] * count


def in_smem(count):
    return [pl.BlockSpec(memory_space=pltpu.SMEM)] * count


def params(mib):
    return pltpu.CompilerParams(vmem_limit_bytes=mib * MIB)


def shape_of(shape, kind):
    return jax.ShapeDtypeStruct(shape, kind)


def pair_body(
    orbitals, potential, projectors, projector_energy, atom_first, atom_second, atom_third, rotation
):
    bf16, f32 = jnp.bfloat16, jnp.float32
    count, block_x, y_size, z_size = orbitals.shape[1:]
    x_size = 2 * block_x
    own = block_x * y_size
    cell_count = x_size * y_size
    atoms, nproj = projectors.shape[:2]
    spots = SIDE * atoms * nproj
    sources = lax.axis_size("orb")
    used = count * block_x
    chunk = -(-(used + count - 1) // 16) * 16

    block = orbitals.shape[1:]
    sent, start, field = pl.pallas_call(
        face_kernel,
        out_shape=(
            shape_of((count + 1,) + block[1:], bf16),
            shape_of(block, f32),
            shape_of(block[1:], f32),
        ),
        in_specs=[pl.BlockSpec(memory_space=pltpu.HBM)] * 2,
        out_specs=tuple(in_vmem(3)),
        scratch_shapes=[pltpu.SemaphoreType.DMA((2,))],
        compiler_params=params(16),
        name="faces",
    )(orbitals, potential)
    partner = lax.ppermute(sent, "dom", [(0, 1), (1, 0)])

    plane_first, plane_partner, plane_own = plane_stencil(x_size, y_size)
    third = third_stencil(z_size)
    tables = pl.pallas_call(
        prepare_kernel,
        out_shape=(
            shape_of((spots, cell_count), bf16),
            shape_of((spots, 2 * cell_count), bf16),
            shape_of((spots, cell_count), bf16),
            shape_of((cell_count, 3 * spots), bf16),
            shape_of((spots, z_size), f32),
            shape_of((atoms * nproj, z_size), f32),
            shape_of((own, z_size), f32),
            shape_of((cell_count, count * z_size), f32),
            shape_of((spots, count * z_size), f32),
        ),
        in_specs=in_smem(4) + in_vmem(6),
        out_specs=tuple(in_vmem(9)),
        scratch_shapes=[pltpu.VMEM((3 * own, count * z_size), bf16)],
        compiler_params=params(24),
        cost_estimate=pl.CostEstimate(flops=1 << 31, bytes_accessed=6 << 20, transcendentals=0),
        name="prepare",
    )(
        atom_first,
        atom_second,
        atom_third,
        projector_energy,
        projectors,
        third_first(),
        start,
        field,
        plane_first,
        third,
    )

    filtered = pl.pallas_call(
        filter_kernel,
        out_shape=shape_of((sources, chunk, z_size), bf16),
        in_specs=in_vmem(15),
        out_specs=in_vmem(1)[0],
        scratch_shapes=[
            pltpu.VMEM((2 * cell_count, count * z_size), bf16),
            pltpu.VMEM((3 * spots, count * z_size), bf16),
            pltpu.VMEM((count * own, z_size), f32),
            pltpu.VMEM((sources, chunk, z_size), f32),
            pltpu.VMEM((cell_count, count * z_size), f32),
        ],
        compiler_params=params(40),
        name="filter",
    )(partner, start, *tables, rotation, plane_partner, plane_own, third)
    by_plane = lax.all_to_all(filtered, "orb", split_axis=0, concat_axis=0, tiled=True)

    rotated = pl.pallas_call(
        functools.partial(rotate_kernel, count=count, block_x=block_x),
        out_shape=shape_of((sources, chunk, z_size), bf16),
        in_specs=in_vmem(1),
        out_specs=in_vmem(1)[0],
        scratch_shapes=[
            pltpu.VMEM((sources * chunk, z_size), f32),
            pltpu.VMEM((sources * used + chunk - used, z_size), f32),
        ],
        compiler_params=params(24),
        name="rotate",
    )(by_plane)
    by_orbital = lax.all_to_all(rotated, "orb", split_axis=0, concat_axis=0, tiled=True)

    return pl.pallas_call(
        unpack_kernel,
        out_shape=shape_of(orbitals.shape, bf16),
        in_specs=in_vmem(1),
        out_specs=in_vmem(1)[0],
        scratch_shapes=[pltpu.VMEM((sources * used, z_size), f32)],
        compiler_params=params(16),
        name="unpack",
    )(by_orbital)


def fits_pair(mesh, orbitals, projectors, rotation):
    count = orbitals.shape[1] // mesh.shape["orb"]
    return (
        mesh.shape["dom"] == 2
        and orbitals.shape[3] == mesh.shape["orb"]
        and orbitals.shape[2] == 2 * stencil_reach
        and projectors.shape[0] % 2 == 0
        and projectors.shape[1] == 8
        and count <= 8
        and rotation.shape[1] < orbitals.shape[4]
        and -(-rotation.shape[1] // (orbitals.shape[4] - rotation.shape[1])) < count
    )


def solution(mesh):
    def whole(*arrays):
        chosen = pair_body if fits_pair(mesh, arrays[0], arrays[2], arrays[7]) else body
        return jax.shard_map(
            chosen,
            mesh=mesh,
            in_specs=(
                P("dom", "orb", None, None, None),
                P("dom", None, None, None),
                P(),
                P(),
                P(),
                P(),
                P(),
                P("orb", None),
            ),
            out_specs=P("dom", "orb", None, None, None),
            check_vma=False,
        )(*arrays)

    return whole
```

```python
import functools

import jax
import jax.numpy as jnp
import numpy as np
from jax import lax
from jax.experimental import pallas as pl
from jax.experimental.pallas import tpu as pltpu
from jax.sharding import PartitionSpec as P

SIDE = 8
SUP = 512


stencil_weights = (
    -5369.0 / 1800.0,
    12.0 / 7.0,
    -15.0 / 56.0,
    10.0 / 189.0,
    -1.0 / 112.0,
    2.0 / 1925.0,
    -1.0 / 16632.0,
)
inverse_spacing = 4.0
filter_center = 120.0
filter_width = 110.0
stencil_reach = 6


def partner_2(block, axis, bit):
    count = lax.axis_size(axis)
    route = []
    for low in range(count):
        high = low | 1 << bit
        if high != low and high < count:
            route += [(low, high), (high, low)]
    return lax.ppermute(block, axis, route)


def outgoing(values, direction, width):
    extent = values.shape[direction]
    if 2 * width < extent:
        return jnp.concatenate(
            (
                lax.slice_in_dim(values, 0, width, axis=direction),
                lax.slice_in_dim(values, extent - width, extent, axis=direction),
            ),
            axis=direction,
        )
    return values


def assemble(values, partner, direction, width):
    extent = values.shape[direction]
    if 2 * width < extent:
        lower_rim = lax.slice_in_dim(partner, width, 2 * width, axis=direction)
        upper_rim = lax.slice_in_dim(partner, 0, width, axis=direction)
        return jnp.concatenate((lower_rim, values, upper_rim), axis=direction)
    cyclic = jnp.concatenate((values, partner), axis=direction)
    chosen = np.arange(-width, extent + width) % (2 * extent)
    return jnp.take(cyclic, jnp.asarray(chosen, dtype=jnp.int32), axis=direction)


def face_padded(values, direction, bit_number):
    sent = outgoing(values, direction, stencil_reach)
    partner = partner_2(sent.astype(jnp.bfloat16), "dom", bit_number).astype(sent.dtype)
    return assemble(values, partner, direction, stencil_reach)


def stencil_sum(center, along):
    lead = center.ndim - 3
    summed = 3.0 * stencil_weights[0] * center
    for index in range(3):
        direction = lead + index
        extent = center.shape[direction]
        padded = along[index]
        for offset in range(1, 7):
            if padded is None:
                upward = jnp.roll(center, -offset, direction)
                downward = jnp.roll(center, offset, direction)
            else:
                upward = lax.slice_in_dim(
                    padded, stencil_reach + offset, stencil_reach + offset + extent, axis=direction
                )
                downward = lax.slice_in_dim(
                    padded, stencil_reach - offset, stencil_reach - offset + extent, axis=direction
                )
            summed = summed + stencil_weights[offset] * (upward + downward)
    return summed


def support_map(atom_coords, starts, extents, periods):
    offsets = jnp.arange(SIDE, dtype=jnp.int32) - SIDE // 2
    clipped_list = []
    inside_list = []
    for index in range(3):
        local = (atom_coords[index][:, None] + offsets[None, :] - starts[index]) % periods[index]
        inside_list.append(local < extents[index])
        clipped_list.append(jnp.minimum(local, extents[index] - 1))
    inside = (
        inside_list[0][:, :, None, None]
        & inside_list[1][:, None, :, None]
        & inside_list[2][:, None, None, :]
    )
    flattened = (
        clipped_list[0][:, :, None, None] * extents[1] + clipped_list[1][:, None, :, None]
    ) * extents[2] + clipped_list[2][:, None, None, :]
    atom_count = atom_coords[0].shape[0]
    return (
        flattened.reshape(atom_count * SUP),
        inside.reshape(atom_count, SUP).astype(jnp.float32),
    )


def coefficients(values, support, inside, projectors):
    orbital_count = values.shape[0]
    atom_count = projectors.shape[0]
    flattened = values.reshape(orbital_count, -1)
    picked = (
        jnp.take(flattened, support, axis=1).reshape(orbital_count, atom_count, SUP) * inside[None]
    )
    partial_coeffs = jnp.einsum("aps,kas->kap", projectors, picked, precision=lax.Precision.HIGHEST)
    return lax.psum(partial_coeffs, "dom")


def spread_into(coeffs, shape, support, inside, projectors, projector_energy):
    orbital_count = shape[0]
    atom_count = projectors.shape[0]
    scaled = coeffs * projector_energy[None, None, :]
    spread = (
        jnp.einsum("aps,kap->kas", projectors, scaled, precision=lax.Precision.HIGHEST)
        * inside[None]
    )
    total_cells = shape[1] * shape[2] * shape[3]
    projected_part = (
        jnp.zeros((orbital_count, total_cells), jnp.float32)
        .at[:, support]
        .add(spread.reshape(orbital_count, atom_count * SUP))
    )
    return projected_part.reshape(shape)


def own_hamiltonian(center, along, local_field, support, inside, projectors, projector_energy):
    kinetic = -0.5 * inverse_spacing * inverse_spacing
    coeffs = coefficients(center, support, inside, projectors)
    projected_part = spread_into(
        coeffs, center.shape, support, inside, projectors, projector_energy
    )
    return kinetic * stencil_sum(center, along) + local_field[None] * center + projected_part


def body(
    orbitals, potential, projectors, projector_energy, atom_first, atom_second, atom_third, rotation
):
    domain_count = lax.axis_size("dom")
    domain_bits = domain_count.bit_length() - 1
    split = [index < domain_bits for index in range(3)]
    start_values = orbitals[0]
    local_field = potential[0]
    extents = start_values.shape[1:]
    periods = (
        extents[0] * min(domain_count, 2),
        extents[1] * min(max(domain_count // 2, 1), 2),
        extents[2] * max(domain_count // 4, 1),
    )
    domain_index = lax.axis_index("dom")
    anchors = (
        domain_index % 2 * extents[0],
        domain_index // 2 % 2 * extents[1],
        domain_index // 4 * extents[2],
    )
    atom_coords = (atom_first, atom_second, atom_third)
    support, inside = support_map(atom_coords, anchors, extents, periods)
    along = [
        face_padded(start_values, index + 1, index) if split[index] else None for index in range(3)
    ]
    first_apply = own_hamiltonian(
        start_values, along, local_field, support, inside, projectors, projector_energy
    )
    first_term = (first_apply - filter_center * start_values) / filter_width
    along = [
        face_padded(first_term, index + 1, index) if split[index] else None for index in range(3)
    ]
    second_apply = own_hamiltonian(
        first_term, along, local_field, support, inside, projectors, projector_energy
    )
    second_term = 2.0 * (second_apply - filter_center * first_term) / filter_width - start_values
    per_device = start_values.shape[0]
    filtered = second_term.astype(jnp.bfloat16).reshape(per_device, -1)
    by_cells = lax.all_to_all(filtered, "orb", split_axis=1, concat_axis=0, tiled=True)
    whole_rotation = lax.all_gather(rotation, "orb", axis=0, tiled=True)
    rotated = lax.dot_general(
        whole_rotation, by_cells, (((0,), (0,)), ((), ())), preferred_element_type=jnp.float32
    ).astype(jnp.bfloat16)
    result = lax.all_to_all(rotated, "orb", split_axis=0, concat_axis=1, tiled=True)
    return result.reshape((1,) + start_values.shape)


SCALE = 15.0
MIB = 1 << 20


def scaled_weights():
    ratios = np.array(stencil_weights[1:], np.float64) / stencil_weights[1]
    return SCALE * ratios


def cyclic_stencil(size):
    matrix = np.zeros((size, size), np.float64)
    rows = np.arange(size)
    for offset, weight in enumerate(scaled_weights(), 1):
        np.add.at(matrix, (rows, (rows + offset) % size), weight)
        np.add.at(matrix, (rows, (rows - offset) % size), weight)
    return matrix


def plane_stencil(x_size, y_size):
    matrix = np.kron(cyclic_stencil(x_size), np.eye(y_size))
    matrix += np.kron(np.eye(x_size), cyclic_stencil(y_size))
    own = x_size * y_size // 2
    pieces = (
        np.concatenate((matrix[:, :own], matrix[:, :own]), axis=1),
        matrix[:, own:],
        np.concatenate((matrix[:own], matrix[:own]), axis=1),
    )
    return [piece.astype(jnp.bfloat16) for piece in pieces]


def third_stencil(z_size):
    matrix = cyclic_stencil(z_size)
    return np.concatenate((matrix, matrix), axis=0).astype(jnp.bfloat16)


def third_first():
    picked = np.zeros((SUP, SUP), np.float32)
    source = np.arange(SUP)
    picked[source, source % SIDE * SIDE * SIDE + source // SIDE] = 1.0
    return picked.astype(jnp.bfloat16)


def halves(values):
    high = values.astype(jnp.bfloat16)
    return high, (values - high.astype(jnp.float32)).astype(jnp.bfloat16)


def matmul(left, right):
    return jnp.dot(left, right, preferred_element_type=jnp.float32)


def shared_operator():
    kinetic = -0.5 * inverse_spacing * inverse_spacing
    unit = kinetic * stencil_weights[1] / SCALE / filter_width
    shift = 3.0 * kinetic * stencil_weights[0] - filter_center
    return unit, shift


def face_kernel(orbital_ref, potential_ref, sent_ref, start_ref, field_ref, sem_ref):
    count = orbital_ref.shape[1]
    loads = [
        pltpu.make_async_copy(orbital_ref.at[0, index], start_ref.at[index], sem_ref.at[index])
        for index in range(count)
    ]
    loads.append(pltpu.make_async_copy(potential_ref.at[0], field_ref, sem_ref.at[count]))
    for load in loads:
        load.start()
    for index, load in enumerate(loads):
        load.wait()
        values = start_ref[index] if index < count else field_ref[...]
        sent_ref[index] = values.astype(jnp.bfloat16)


def prepare_kernel(
    first_at_ref,
    second_at_ref,
    third_at_ref,
    energy_at_ref,
    projector_ref,
    order_ref,
    start_ref,
    field_ref,
    rotation_ref,
    plane_ref,
    third_ref,
    q_ref,
    q_partner_ref,
    qt_ref,
    mask_ref,
    energy_ref,
    diagonal_ref,
    part_ref,
    product_ref,
    packed_ref,
    right_ref,
):
    count, block_x, y_size, z_size = start_ref.shape
    x_size = 2 * block_x
    own = block_x * y_size
    cell_count = x_size * y_size
    atoms, nproj = projector_ref.shape[:2]
    pairs = atoms * nproj
    per_plane = SIDE * SIDE
    spots = atoms * per_plane
    unit, shift = shared_operator()
    own_start = lax.axis_index("dom") * block_x
    high, low = halves(projector_ref[...].reshape(pairs, SUP))
    ordered = matmul(jnp.concatenate((high, low), axis=0), order_ref[...])

    lane = lax.broadcasted_iota(jnp.int32, (pairs, 2 * per_plane), 1)
    row_atom = lax.broadcasted_iota(jnp.int32, (pairs, spots), 0) // nproj
    lane_atom = lax.broadcasted_iota(jnp.int32, (pairs, spots), 1) // per_plane
    same_atom = row_atom == lane_atom
    expanded = []
    for part in range(2):
        rows = []
        for third in range(SIDE):
            start = third // 2 * 2 * per_plane
            both = ordered[part * pairs : (part + 1) * pairs, start : start + 2 * per_plane]
            swapped = pltpu.roll(both, per_plane, 1)
            if third % 2:
                both, swapped = swapped, both
            doubled = jnp.where(lane < per_plane, both, swapped)
            doubled = jnp.concatenate([doubled] * (atoms // 2), axis=1)
            rows.append(jnp.where(same_atom, doubled, 0.0))
        expanded.append(jnp.concatenate(rows, axis=0).astype(jnp.bfloat16))
    high, low = expanded

    place = []
    spot = lax.broadcasted_iota(jnp.int32, (per_plane, cell_count), 0)
    place_lane = lax.broadcasted_iota(jnp.int32, (per_plane, cell_count), 1)
    for atom in range(atoms):
        x_start = lax.rem(first_at_ref[atom] - SIDE // 2 - own_start + 2 * x_size, x_size)
        y_start = lax.rem(second_at_ref[atom] - SIDE // 2 + y_size, y_size)
        x_index = x_start + spot // SIDE
        x_index = jnp.where(x_index >= x_size, x_index - x_size, x_index)
        y_index = y_start + spot % SIDE
        y_index = jnp.where(y_index >= y_size, y_index - y_size, y_index)
        target = x_index * y_size + y_index
        place.append(jnp.where(place_lane == target, 1.0, 0.0).astype(jnp.bfloat16))
    place = jnp.concatenate(place, axis=0)
    q_high = matmul(high, place)
    q_ref[...] = q_high.astype(jnp.bfloat16)
    q_partner_ref[...] = q_high[:, own:].astype(jnp.bfloat16)
    q_high = q_high.T.astype(jnp.bfloat16)
    qt_ref[:, 0:spots] = q_high
    qt_ref[:, spots : 2 * spots] = q_high
    qt_ref[:, 2 * spots : 3 * spots] = matmul(low, place).T.astype(jnp.bfloat16)

    z_lane = lax.broadcasted_iota(jnp.int32, (nproj, z_size), 1)
    for third in range(SIDE):
        for atom in range(atoms):
            z_index = lax.rem(third_at_ref[atom] + third - SIDE // 2 + z_size, z_size)
            start = third * pairs + atom * nproj
            mask_ref[start : start + nproj] = jnp.where(z_lane == z_index, 1.0, 0.0)
    sublane = lax.broadcasted_iota(jnp.int32, (nproj, z_size), 0)
    energy = jnp.zeros((nproj, z_size), jnp.float32)
    for index in range(nproj):
        energy = jnp.where(sublane == index, energy_at_ref[index], energy)
    energy = energy * (1.0 / (unit * filter_width))
    for atom in range(atoms):
        energy_ref[atom * nproj : (atom + 1) * nproj] = energy

    diagonal_ref[...] = (field_ref[...].reshape(own, z_size) + shift) / filter_width
    for orbital in range(count):
        lanes = slice(orbital * z_size, (orbital + 1) * z_size)
        high, low = halves(start_ref[orbital].reshape(own, z_size))
        right_ref[0:own, lanes] = high
        right_ref[own:, lanes] = low
    product_ref[...] = matmul(q_ref[:, 0:own], right_ref[0:own])
    summed = matmul(plane_ref[...], right_ref[...])
    for orbital in range(count):
        lanes = slice(orbital * z_size, (orbital + 1) * z_size)
        left = jnp.concatenate((right_ref[0:own, lanes], right_ref[own:, lanes]), axis=1)
        along = summed[0:own, lanes] + matmul(left, third_ref[...])
        values = diagonal_ref[...] * start_ref[orbital].reshape(own, z_size)
        part_ref[0:own, lanes] = values + unit * along
        part_ref[own:, lanes] = unit * summed[own:, lanes]
    packed_ref[...] = packed_rotation(rotation_ref, z_size)


def packed_rotation(rotation_ref, z_size):
    count, wide = rotation_ref.shape
    spare = z_size - wide
    block = jnp.concatenate(
        (rotation_ref[...].astype(jnp.float32), jnp.zeros((count, spare), jnp.float32)), axis=1
    )
    block = jnp.concatenate((block, jnp.zeros((8 - count, z_size), jnp.float32)), axis=0)
    sublane = lax.broadcasted_iota(jnp.int32, (8, z_size), 0)
    lane = lax.broadcasted_iota(jnp.int32, (8, z_size), 1)
    packed = block
    for piece in range(-(-wide // spare)):
        moved = pltpu.roll(block, (piece - (count - 1)) % 8, 0)
        moved = pltpu.roll(moved, (wide - piece * spare) % z_size, 1)
        packed = jnp.where((sublane == piece) & (lane >= wide), moved, packed)
    return packed


def filter_kernel(
    partner_ref,
    start_ref,
    q_ref,
    q_partner_ref,
    qt_ref,
    mask_ref,
    energy_ref,
    diagonal_ref,
    part_ref,
    product_ref,
    packed_ref,
    plane_partner_ref,
    plane_own_ref,
    third_ref,
    out_ref,
    right_ref,
    coeff_ref,
    rows_ref,
    chunk_ref,
    first_ref,
):
    count, block_x, y_size, z_size = start_ref.shape
    own = block_x * y_size
    cell_count = 2 * own
    pairs = energy_ref.shape[0]
    spots = mask_ref.shape[0]
    unit, shift = shared_operator()
    columns = [slice(orbital * z_size, (orbital + 1) * z_size) for orbital in range(count)]

    def spread(products):
        mask = mask_ref[...]
        for lanes in columns:
            picked = (products[:, lanes] * mask).reshape(SIDE, pairs, z_size)
            coeffs = jnp.sum(jnp.sum(picked, axis=0), axis=1, keepdims=True)
            high, low = halves(jnp.concatenate([coeffs * energy_ref[...]] * SIDE, axis=0) * mask)
            coeff_ref[0:spots, lanes] = high
            coeff_ref[spots : 2 * spots, lanes] = low
            coeff_ref[2 * spots :, lanes] = high

    for orbital, lanes in enumerate(columns):
        right_ref[0:own, lanes] = partner_ref[orbital].reshape(own, z_size)
    spread(product_ref[...] + matmul(q_partner_ref[...], right_ref[0:own]))
    summed = matmul(plane_partner_ref[...], right_ref[0:own])
    summed = summed + matmul(qt_ref[...], coeff_ref[...])
    field = partner_ref[count].astype(jnp.float32).reshape(own, z_size)
    field = (field + shift) / filter_width
    for lanes in columns:
        values = right_ref[0:own, lanes]
        along = summed[own:, lanes] + matmul(values, third_ref[0:z_size])
        values = part_ref[own:, lanes] + field * values.astype(jnp.float32)
        first_ref[0:own, lanes] = part_ref[0:own, lanes] + unit * summed[0:own, lanes]
        first_ref[own:, lanes] = values + unit * along

    high, low = halves(first_ref[...])
    right_ref[0:cell_count] = high
    right_ref[cell_count:] = low
    spread(matmul(q_ref[...], right_ref[0:cell_count]))
    summed = matmul(plane_own_ref[...], right_ref[...])
    summed = summed + matmul(qt_ref[0:own], coeff_ref[...])
    for orbital, lanes in enumerate(columns):
        left = jnp.concatenate(
            (right_ref[0:own, lanes], right_ref[cell_count : cell_count + own, lanes]), axis=1
        )
        along = summed[:, lanes] + matmul(left, third_ref[...])
        values = diagonal_ref[...] * first_ref[0:own, lanes] + unit * along
        values = 2.0 * values - start_ref[orbital].reshape(own, z_size)
        rows_ref[orbital * own : (orbital + 1) * own] = values

    used = count * block_x
    for part in range(y_size):
        chunk_ref[part, 0:used] = rows_ref[pl.ds(part, used, stride=y_size), :]
        chunk_ref[part, used : used + count - 1] = packed_ref[0 : count - 1]
    out_ref[...] = chunk_ref[...].astype(jnp.bfloat16)


def rotate_kernel(received_ref, out_ref, wide_ref, rows_ref, *, count, block_x):
    sources, chunk, z_size = received_ref.shape
    total = sources * count
    used = count * block_x
    spare = z_size - total
    wide_ref[...] = received_ref[...].astype(jnp.float32).reshape(sources * chunk, z_size)
    packed = [wide_ref[pl.ds(used + row, sources, stride=chunk), :] for row in range(count - 1)]
    lane = lax.broadcasted_iota(jnp.int32, (sources, z_size), 1)
    last = jnp.zeros((sources, z_size), jnp.float32)
    for piece in range(-(-total // spare)):
        moved = pltpu.roll(packed[piece], (piece * spare - total) % z_size, 1)
        last = jnp.where(lane >= piece * spare, moved, last)
    rotation = jnp.concatenate(packed + [last], axis=0)[:, 0:total].astype(jnp.bfloat16)
    columns = []
    for plane in range(block_x):
        rows = [
            wide_ref[pl.ds(orbital * block_x + plane, sources, stride=chunk), :]
            for orbital in range(count)
        ]
        columns.append(jnp.concatenate(rows, axis=0).astype(jnp.bfloat16))
    values = jnp.concatenate(columns, axis=1)
    rotated = lax.dot_general(
        rotation, values, (((0,), (0,)), ((), ())), preferred_element_type=jnp.float32
    )
    rows_ref[total * block_x :] = jnp.zeros((chunk - used, z_size), jnp.float32)
    for plane in range(block_x):
        lanes = slice(plane * z_size, (plane + 1) * z_size)
        rows_ref[pl.ds(plane, total, stride=block_x), :] = rotated[:, lanes]
    for part in range(sources):
        out_ref[part] = rows_ref[part * used : part * used + chunk].astype(jnp.bfloat16)


def unpack_kernel(received_ref, out_ref, rows_ref):
    sources, chunk, z_size = received_ref.shape
    used = rows_ref.shape[0] // sources
    for part in range(sources):
        values = received_ref[part].astype(jnp.float32)
        rows_ref[pl.ds(part, used, stride=sources), :] = values[0:used]
    out_ref[...] = rows_ref[...].astype(jnp.bfloat16).reshape(out_ref.shape)


def in_vmem(count):
    return [pl.BlockSpec(memory_space=pltpu.VMEM)] * count


def in_smem(count):
    return [pl.BlockSpec(memory_space=pltpu.SMEM)] * count


def params(mib):
    return pltpu.CompilerParams(vmem_limit_bytes=mib * MIB)


def shape_of(shape, kind):
    return jax.ShapeDtypeStruct(shape, kind)


def pair_body(
    orbitals, potential, projectors, projector_energy, atom_first, atom_second, atom_third, rotation
):
    bf16, f32 = jnp.bfloat16, jnp.float32
    count, block_x, y_size, z_size = orbitals.shape[1:]
    x_size = 2 * block_x
    own = block_x * y_size
    cell_count = x_size * y_size
    atoms, nproj = projectors.shape[:2]
    spots = SIDE * atoms * nproj
    sources = lax.axis_size("orb")
    used = count * block_x
    chunk = -(-(used + count - 1) // 16) * 16

    block = orbitals.shape[1:]
    sent = pl.pallas_call(
        face_kernel,
        out_shape=shape_of((count + 1,) + block[1:], bf16),
        in_specs=[pl.BlockSpec(memory_space=pltpu.HBM)] * 2,
        out_specs=in_vmem(1)[0],
        scratch_shapes=[
            pltpu.VMEM(block, f32),
            pltpu.VMEM(block[1:], f32),
            pltpu.SemaphoreType.DMA((count + 1,)),
        ],
        compiler_params=params(60),
        name="faces",
    )(orbitals, potential)
    partner = lax.ppermute(sent, "dom", [(0, 1), (1, 0)])

    plane_first, plane_partner, plane_own = plane_stencil(x_size, y_size)
    third = third_stencil(z_size)
    tables = pl.pallas_call(
        prepare_kernel,
        out_shape=(
            shape_of((spots, cell_count), bf16),
            shape_of((spots, own), bf16),
            shape_of((cell_count, 3 * spots), bf16),
            shape_of((spots, z_size), f32),
            shape_of((atoms * nproj, z_size), f32),
            shape_of((own, z_size), f32),
            shape_of((cell_count, count * z_size), f32),
            shape_of((spots, count * z_size), f32),
            shape_of((8, z_size), f32),
        ),
        in_specs=in_smem(4) + in_vmem(7),
        out_specs=tuple(in_vmem(9)),
        scratch_shapes=[pltpu.VMEM((2 * own, count * z_size), bf16)],
        compiler_params=params(24),
        cost_estimate=pl.CostEstimate(flops=1 << 31, bytes_accessed=6 << 20, transcendentals=0),
        name="prepare",
    )(
        atom_first,
        atom_second,
        atom_third,
        projector_energy,
        projectors,
        third_first(),
        orbitals[0],
        potential[0],
        rotation,
        plane_first,
        third,
    )

    filtered = pl.pallas_call(
        filter_kernel,
        out_shape=shape_of((sources, chunk, z_size), bf16),
        in_specs=in_vmem(14),
        out_specs=in_vmem(1)[0],
        scratch_shapes=[
            pltpu.VMEM((2 * cell_count, count * z_size), bf16),
            pltpu.VMEM((3 * spots, count * z_size), bf16),
            pltpu.VMEM((count * own, z_size), f32),
            pltpu.VMEM((sources, chunk, z_size), f32),
            pltpu.VMEM((cell_count, count * z_size), f32),
        ],
        compiler_params=params(40),
        name="filter",
    )(partner, orbitals[0], *tables, plane_partner, plane_own, third)
    by_plane = lax.all_to_all(filtered, "orb", split_axis=0, concat_axis=0, tiled=True)

    rotated = pl.pallas_call(
        functools.partial(rotate_kernel, count=count, block_x=block_x),
        out_shape=shape_of((sources, chunk, z_size), bf16),
        in_specs=in_vmem(1),
        out_specs=in_vmem(1)[0],
        scratch_shapes=[
            pltpu.VMEM((sources * chunk, z_size), f32),
            pltpu.VMEM((sources * used + chunk - used, z_size), f32),
        ],
        compiler_params=params(24),
        name="rotate",
    )(by_plane)
    by_orbital = lax.all_to_all(rotated, "orb", split_axis=0, concat_axis=0, tiled=True)

    return pl.pallas_call(
        unpack_kernel,
        out_shape=shape_of(orbitals.shape, bf16),
        in_specs=in_vmem(1),
        out_specs=in_vmem(1)[0],
        scratch_shapes=[pltpu.VMEM((sources * used, z_size), f32)],
        compiler_params=params(16),
        name="unpack",
    )(by_orbital)


def fits_pair(mesh, orbitals, projectors, rotation):
    count = orbitals.shape[1] // mesh.shape["orb"]
    return (
        mesh.shape["dom"] == 2
        and orbitals.shape[3] == mesh.shape["orb"]
        and orbitals.shape[2] == 2 * stencil_reach
        and projectors.shape[0] % 2 == 0
        and projectors.shape[1] == 8
        and count <= 8
        and rotation.shape[1] < orbitals.shape[4]
        and -(-rotation.shape[1] // (orbitals.shape[4] - rotation.shape[1])) < count
    )


def solution(mesh):
    def whole(*arrays):
        chosen = pair_body if fits_pair(mesh, arrays[0], arrays[2], arrays[7]) else body
        return jax.shard_map(
            chosen,
            mesh=mesh,
            in_specs=(
                P("dom", "orb", None, None, None),
                P("dom", None, None, None),
                P(),
                P(),
                P(),
                P(),
                P(),
                P("orb", None),
            ),
            out_specs=P("dom", "orb", None, None, None),
            check_vma=False,
        )(*arrays)

    return whole
```

```python
import functools

import jax
import jax.numpy as jnp
import numpy as np
from jax import lax
from jax.experimental import pallas as pl
from jax.experimental.pallas import tpu as pltpu
from jax.sharding import PartitionSpec as P

SIDE = 8
SUP = 512


stencil_weights = (
    -5369.0 / 1800.0,
    12.0 / 7.0,
    -15.0 / 56.0,
    10.0 / 189.0,
    -1.0 / 112.0,
    2.0 / 1925.0,
    -1.0 / 16632.0,
)
inverse_spacing = 4.0
filter_center = 120.0
filter_width = 110.0
stencil_reach = 6


def partner_2(block, axis, bit):
    count = lax.axis_size(axis)
    route = []
    for low in range(count):
        high = low | 1 << bit
        if high != low and high < count:
            route += [(low, high), (high, low)]
    return lax.ppermute(block, axis, route)


def outgoing(values, direction, width):
    extent = values.shape[direction]
    if 2 * width < extent:
        return jnp.concatenate(
            (
                lax.slice_in_dim(values, 0, width, axis=direction),
                lax.slice_in_dim(values, extent - width, extent, axis=direction),
            ),
            axis=direction,
        )
    return values


def assemble(values, partner, direction, width):
    extent = values.shape[direction]
    if 2 * width < extent:
        lower_rim = lax.slice_in_dim(partner, width, 2 * width, axis=direction)
        upper_rim = lax.slice_in_dim(partner, 0, width, axis=direction)
        return jnp.concatenate((lower_rim, values, upper_rim), axis=direction)
    cyclic = jnp.concatenate((values, partner), axis=direction)
    chosen = np.arange(-width, extent + width) % (2 * extent)
    return jnp.take(cyclic, jnp.asarray(chosen, dtype=jnp.int32), axis=direction)


def face_padded(values, direction, bit_number):
    sent = outgoing(values, direction, stencil_reach)
    partner = partner_2(sent.astype(jnp.bfloat16), "dom", bit_number).astype(sent.dtype)
    return assemble(values, partner, direction, stencil_reach)


def stencil_sum(center, along):
    lead = center.ndim - 3
    summed = 3.0 * stencil_weights[0] * center
    for index in range(3):
        direction = lead + index
        extent = center.shape[direction]
        padded = along[index]
        for offset in range(1, 7):
            if padded is None:
                upward = jnp.roll(center, -offset, direction)
                downward = jnp.roll(center, offset, direction)
            else:
                upward = lax.slice_in_dim(
                    padded, stencil_reach + offset, stencil_reach + offset + extent, axis=direction
                )
                downward = lax.slice_in_dim(
                    padded, stencil_reach - offset, stencil_reach - offset + extent, axis=direction
                )
            summed = summed + stencil_weights[offset] * (upward + downward)
    return summed


def support_map(atom_coords, starts, extents, periods):
    offsets = jnp.arange(SIDE, dtype=jnp.int32) - SIDE // 2
    clipped_list = []
    inside_list = []
    for index in range(3):
        local = (atom_coords[index][:, None] + offsets[None, :] - starts[index]) % periods[index]
        inside_list.append(local < extents[index])
        clipped_list.append(jnp.minimum(local, extents[index] - 1))
    inside = (
        inside_list[0][:, :, None, None]
        & inside_list[1][:, None, :, None]
        & inside_list[2][:, None, None, :]
    )
    flattened = (
        clipped_list[0][:, :, None, None] * extents[1] + clipped_list[1][:, None, :, None]
    ) * extents[2] + clipped_list[2][:, None, None, :]
    atom_count = atom_coords[0].shape[0]
    return (
        flattened.reshape(atom_count * SUP),
        inside.reshape(atom_count, SUP).astype(jnp.float32),
    )


def coefficients(values, support, inside, projectors):
    orbital_count = values.shape[0]
    atom_count = projectors.shape[0]
    flattened = values.reshape(orbital_count, -1)
    picked = (
        jnp.take(flattened, support, axis=1).reshape(orbital_count, atom_count, SUP) * inside[None]
    )
    partial_coeffs = jnp.einsum("aps,kas->kap", projectors, picked, precision=lax.Precision.HIGHEST)
    return lax.psum(partial_coeffs, "dom")


def spread_into(coeffs, shape, support, inside, projectors, projector_energy):
    orbital_count = shape[0]
    atom_count = projectors.shape[0]
    scaled = coeffs * projector_energy[None, None, :]
    spread = (
        jnp.einsum("aps,kap->kas", projectors, scaled, precision=lax.Precision.HIGHEST)
        * inside[None]
    )
    total_cells = shape[1] * shape[2] * shape[3]
    projected_part = (
        jnp.zeros((orbital_count, total_cells), jnp.float32)
        .at[:, support]
        .add(spread.reshape(orbital_count, atom_count * SUP))
    )
    return projected_part.reshape(shape)


def own_hamiltonian(center, along, local_field, support, inside, projectors, projector_energy):
    kinetic = -0.5 * inverse_spacing * inverse_spacing
    coeffs = coefficients(center, support, inside, projectors)
    projected_part = spread_into(
        coeffs, center.shape, support, inside, projectors, projector_energy
    )
    return kinetic * stencil_sum(center, along) + local_field[None] * center + projected_part


def body(
    orbitals, potential, projectors, projector_energy, atom_first, atom_second, atom_third, rotation
):
    domain_count = lax.axis_size("dom")
    domain_bits = domain_count.bit_length() - 1
    split = [index < domain_bits for index in range(3)]
    start_values = orbitals[0]
    local_field = potential[0]
    extents = start_values.shape[1:]
    periods = (
        extents[0] * min(domain_count, 2),
        extents[1] * min(max(domain_count // 2, 1), 2),
        extents[2] * max(domain_count // 4, 1),
    )
    domain_index = lax.axis_index("dom")
    anchors = (
        domain_index % 2 * extents[0],
        domain_index // 2 % 2 * extents[1],
        domain_index // 4 * extents[2],
    )
    atom_coords = (atom_first, atom_second, atom_third)
    support, inside = support_map(atom_coords, anchors, extents, periods)
    along = [
        face_padded(start_values, index + 1, index) if split[index] else None for index in range(3)
    ]
    first_apply = own_hamiltonian(
        start_values, along, local_field, support, inside, projectors, projector_energy
    )
    first_term = (first_apply - filter_center * start_values) / filter_width
    along = [
        face_padded(first_term, index + 1, index) if split[index] else None for index in range(3)
    ]
    second_apply = own_hamiltonian(
        first_term, along, local_field, support, inside, projectors, projector_energy
    )
    second_term = 2.0 * (second_apply - filter_center * first_term) / filter_width - start_values
    per_device = start_values.shape[0]
    filtered = second_term.astype(jnp.bfloat16).reshape(per_device, -1)
    by_cells = lax.all_to_all(filtered, "orb", split_axis=1, concat_axis=0, tiled=True)
    whole_rotation = lax.all_gather(rotation, "orb", axis=0, tiled=True)
    rotated = lax.dot_general(
        whole_rotation, by_cells, (((0,), (0,)), ((), ())), preferred_element_type=jnp.float32
    ).astype(jnp.bfloat16)
    result = lax.all_to_all(rotated, "orb", split_axis=0, concat_axis=1, tiled=True)
    return result.reshape((1,) + start_values.shape)


SCALE = 15.0
MIB = 1 << 20


def scaled_weights():
    ratios = np.array(stencil_weights[1:], np.float64) / stencil_weights[1]
    return SCALE * ratios


def cyclic_stencil(size):
    matrix = np.zeros((size, size), np.float64)
    rows = np.arange(size)
    for offset, weight in enumerate(scaled_weights(), 1):
        np.add.at(matrix, (rows, (rows + offset) % size), weight)
        np.add.at(matrix, (rows, (rows - offset) % size), weight)
    return matrix


def plane_stencil(x_size, y_size):
    matrix = np.kron(cyclic_stencil(x_size), np.eye(y_size))
    matrix += np.kron(np.eye(x_size), cyclic_stencil(y_size))
    own = x_size * y_size // 2
    pieces = (
        np.concatenate((matrix[:, :own], matrix[:, :own]), axis=1),
        np.concatenate((matrix, matrix), axis=1),
    )
    return [piece.astype(jnp.bfloat16) for piece in pieces]


def third_stencil(z_size):
    matrix = cyclic_stencil(z_size)
    return np.concatenate((matrix, matrix), axis=0).astype(jnp.bfloat16)


def third_first():
    picked = np.zeros((SUP, SUP), np.float32)
    source = np.arange(SUP)
    picked[source, source % SIDE * SIDE * SIDE + source // SIDE] = 1.0
    return picked.astype(jnp.bfloat16)


def halves(values):
    high = values.astype(jnp.bfloat16)
    return high, (values - high.astype(jnp.float32)).astype(jnp.bfloat16)


def matmul(left, right):
    return jnp.dot(left, right, preferred_element_type=jnp.float32)


def shared_operator():
    kinetic = -0.5 * inverse_spacing * inverse_spacing
    unit = kinetic * stencil_weights[1] / SCALE / filter_width
    shift = 3.0 * kinetic * stencil_weights[0] - filter_center
    return unit, shift


def spread(products, mask_ref, energy_ref, coeff_ref):
    spots, z_size = mask_ref.shape
    pairs = energy_ref.shape[0]
    mask = mask_ref[...]
    for start in range(0, products.shape[1], z_size):
        lanes = slice(start, start + z_size)
        picked = (products[:, lanes] * mask).reshape(SIDE, pairs, z_size)
        coeffs = jnp.sum(jnp.sum(picked, axis=0), axis=1, keepdims=True)
        high, low = halves(jnp.concatenate([coeffs * energy_ref[...]] * SIDE, axis=0) * mask)
        coeff_ref[0:spots, lanes] = high
        coeff_ref[spots : 2 * spots, lanes] = low
        coeff_ref[2 * spots :, lanes] = high


def prepare_kernel(
    first_at_ref,
    second_at_ref,
    third_at_ref,
    energy_at_ref,
    projector_ref,
    order_ref,
    start_ref,
    field_ref,
    rotation_ref,
    plane_ref,
    third_ref,
    q_ref,
    qt_ref,
    mask_ref,
    energy_ref,
    diagonal_ref,
    first_ref,
    packed_ref,
    right_ref,
    coeff_ref,
):
    count, block_x, y_size, z_size = start_ref.shape
    x_size = 2 * block_x
    own = block_x * y_size
    cell_count = x_size * y_size
    atoms, nproj = projector_ref.shape[:2]
    pairs = atoms * nproj
    per_plane = SIDE * SIDE
    spots = atoms * per_plane
    unit, shift = shared_operator()
    own_start = lax.axis_index("dom") * block_x
    high, low = halves(projector_ref[...].reshape(pairs, SUP))
    ordered = matmul(jnp.concatenate((high, low), axis=0), order_ref[...])

    lane = lax.broadcasted_iota(jnp.int32, (pairs, 2 * per_plane), 1)
    row_atom = lax.broadcasted_iota(jnp.int32, (pairs, spots), 0) // nproj
    lane_atom = lax.broadcasted_iota(jnp.int32, (pairs, spots), 1) // per_plane
    same_atom = row_atom == lane_atom
    expanded = []
    for part in range(2):
        rows = []
        for third in range(SIDE):
            start = third // 2 * 2 * per_plane
            both = ordered[part * pairs : (part + 1) * pairs, start : start + 2 * per_plane]
            swapped = pltpu.roll(both, per_plane, 1)
            if third % 2:
                both, swapped = swapped, both
            doubled = jnp.where(lane < per_plane, both, swapped)
            doubled = jnp.concatenate([doubled] * (atoms // 2), axis=1)
            rows.append(jnp.where(same_atom, doubled, 0.0))
        expanded.append(jnp.concatenate(rows, axis=0).astype(jnp.bfloat16))
    high, low = expanded

    place = []
    spot = lax.broadcasted_iota(jnp.int32, (per_plane, cell_count), 0)
    place_lane = lax.broadcasted_iota(jnp.int32, (per_plane, cell_count), 1)
    for atom in range(atoms):
        x_start = lax.rem(first_at_ref[atom] - SIDE // 2 - own_start + 2 * x_size, x_size)
        y_start = lax.rem(second_at_ref[atom] - SIDE // 2 + y_size, y_size)
        x_index = x_start + spot // SIDE
        x_index = jnp.where(x_index >= x_size, x_index - x_size, x_index)
        y_index = y_start + spot % SIDE
        y_index = jnp.where(y_index >= y_size, y_index - y_size, y_index)
        target = x_index * y_size + y_index
        place.append(jnp.where(place_lane == target, 1.0, 0.0).astype(jnp.bfloat16))
    place = jnp.concatenate(place, axis=0)
    q_high = matmul(high, place)
    q_ref[...] = q_high.astype(jnp.bfloat16)
    q_high = q_high.T.astype(jnp.bfloat16)
    qt_ref[:, 0:spots] = q_high
    qt_ref[:, spots : 2 * spots] = q_high
    qt_ref[:, 2 * spots : 3 * spots] = matmul(low, place).T.astype(jnp.bfloat16)

    z_lane = lax.broadcasted_iota(jnp.int32, (nproj, z_size), 1)
    for third in range(SIDE):
        for atom in range(atoms):
            z_index = lax.rem(third_at_ref[atom] + third - SIDE // 2 + z_size, z_size)
            start = third * pairs + atom * nproj
            mask_ref[start : start + nproj] = jnp.where(z_lane == z_index, 1.0, 0.0)
    sublane = lax.broadcasted_iota(jnp.int32, (nproj, z_size), 0)
    energy = jnp.zeros((nproj, z_size), jnp.float32)
    for index in range(nproj):
        energy = jnp.where(sublane == index, energy_at_ref[index], energy)
    energy = energy * (1.0 / (unit * filter_width))
    for atom in range(atoms):
        energy_ref[atom * nproj : (atom + 1) * nproj] = energy

    diagonal_ref[...] = (field_ref[...].reshape(own, z_size) + shift) / filter_width
    for orbital in range(count):
        lanes = slice(orbital * z_size, (orbital + 1) * z_size)
        high, low = halves(start_ref[orbital].reshape(own, z_size))
        right_ref[0:own, lanes] = high
        right_ref[own:, lanes] = low
    spread(matmul(q_ref[:, 0:own], right_ref[0:own]), mask_ref, energy_ref, coeff_ref)
    summed = matmul(plane_ref[...], right_ref[...]) + matmul(qt_ref[...], coeff_ref[...])
    for orbital in range(count):
        lanes = slice(orbital * z_size, (orbital + 1) * z_size)
        left = jnp.concatenate((right_ref[0:own, lanes], right_ref[own:, lanes]), axis=1)
        along = summed[0:own, lanes] + matmul(left, third_ref[...])
        values = diagonal_ref[...] * start_ref[orbital].reshape(own, z_size)
        first_ref[0:own, lanes] = values + unit * along
        first_ref[own:, lanes] = unit * summed[own:, lanes]
    packed_ref[...] = packed_rotation(rotation_ref, z_size)


def packed_rotation(rotation_ref, z_size):
    count, wide = rotation_ref.shape
    spare = z_size - wide
    block = jnp.concatenate(
        (rotation_ref[...].astype(jnp.float32), jnp.zeros((count, spare), jnp.float32)), axis=1
    )
    block = jnp.concatenate((block, jnp.zeros((8 - count, z_size), jnp.float32)), axis=0)
    sublane = lax.broadcasted_iota(jnp.int32, (8, z_size), 0)
    lane = lax.broadcasted_iota(jnp.int32, (8, z_size), 1)
    packed = block
    for piece in range(-(-wide // spare)):
        moved = pltpu.roll(block, (piece - (count - 1)) % 8, 0)
        moved = pltpu.roll(moved, (wide - piece * spare) % z_size, 1)
        packed = jnp.where((sublane == piece) & (lane >= wide), moved, packed)
    return packed


def filter_kernel(
    first_ref,
    start_ref,
    partner_field_ref,
    q_ref,
    qt_ref,
    mask_ref,
    energy_ref,
    diagonal_ref,
    packed_ref,
    plane_ref,
    third_ref,
    out_ref,
    right_ref,
    coeff_ref,
    rows_ref,
    chunk_ref,
):
    count, block_x, y_size, z_size = start_ref.shape
    own = block_x * y_size
    cell_count = 2 * own
    unit, shift = shared_operator()
    high, low = halves(first_ref[...])
    right_ref[0:cell_count] = high
    right_ref[cell_count:] = low
    spread(matmul(q_ref[...], right_ref[0:cell_count]), mask_ref, energy_ref, coeff_ref)
    summed = matmul(plane_ref[...], right_ref[...]) + matmul(qt_ref[...], coeff_ref[...])
    partner_diagonal = (partner_field_ref[...].reshape(own, z_size) + shift) / filter_width
    for orbital in range(count):
        lanes = slice(orbital * z_size, (orbital + 1) * z_size)
        rows = slice(orbital * own, (orbital + 1) * own)
        left = jnp.concatenate(
            (right_ref[0:cell_count, lanes], right_ref[cell_count:, lanes]), axis=1
        )
        along = unit * (summed[:, lanes] + matmul(left, third_ref[...]))
        values = diagonal_ref[...] * first_ref[0:own, lanes] + along[0:own]
        rows_ref[0, rows] = 2.0 * values - start_ref[orbital].reshape(own, z_size)
        values = partner_diagonal * first_ref[own:, lanes] + along[own:]
        rows_ref[1, rows] = 2.0 * values

    used = count * block_x
    me = lax.axis_index("dom")
    for half in range(2):
        tail = packed_ref[0 : count - 1] if half == 0 else jnp.zeros((count - 1, z_size))
        for part in range(y_size):
            target = (me ^ half) * y_size + part
            chunk_ref[target, 0:used] = rows_ref[half, pl.ds(part, used, stride=y_size), :]
            chunk_ref[target, used : used + count - 1] = tail
    out_ref[...] = chunk_ref[...].astype(jnp.bfloat16)


def rotate_kernel(received_ref, out_ref, wide_ref, rows_ref, *, count, block_x):
    sources, chunk, z_size = out_ref.shape
    total = sources * count
    used = count * block_x
    spare = z_size - total
    summed = received_ref[0:sources].astype(jnp.float32)
    summed = summed + received_ref[sources:].astype(jnp.float32)
    wide_ref[...] = summed.reshape(sources * chunk, z_size)
    packed = [wide_ref[pl.ds(used + row, sources, stride=chunk), :] for row in range(count - 1)]
    lane = lax.broadcasted_iota(jnp.int32, (sources, z_size), 1)
    last = jnp.zeros((sources, z_size), jnp.float32)
    for piece in range(-(-total // spare)):
        moved = pltpu.roll(packed[piece], (piece * spare - total) % z_size, 1)
        last = jnp.where(lane >= piece * spare, moved, last)
    rotation = jnp.concatenate(packed + [last], axis=0)[:, 0:total].astype(jnp.bfloat16)
    columns = []
    for plane in range(block_x):
        rows = [
            wide_ref[pl.ds(orbital * block_x + plane, sources, stride=chunk), :]
            for orbital in range(count)
        ]
        columns.append(jnp.concatenate(rows, axis=0).astype(jnp.bfloat16))
    values = jnp.concatenate(columns, axis=1)
    rotated = lax.dot_general(
        rotation, values, (((0,), (0,)), ((), ())), preferred_element_type=jnp.float32
    )
    rows_ref[total * block_x :] = jnp.zeros((chunk - used, z_size), jnp.float32)
    for plane in range(block_x):
        lanes = slice(plane * z_size, (plane + 1) * z_size)
        rows_ref[pl.ds(plane, total, stride=block_x), :] = rotated[:, lanes]
    for part in range(sources):
        out_ref[part] = rows_ref[part * used : part * used + chunk].astype(jnp.bfloat16)


def unpack_kernel(received_ref, out_ref, rows_ref):
    sources, chunk, z_size = received_ref.shape
    used = rows_ref.shape[0] // sources
    for part in range(sources):
        values = received_ref[part].astype(jnp.float32)
        rows_ref[pl.ds(part, used, stride=sources), :] = values[0:used]
    out_ref[...] = rows_ref[...].astype(jnp.bfloat16).reshape(out_ref.shape)


def in_vmem(count):
    return [pl.BlockSpec(memory_space=pltpu.VMEM)] * count


def in_smem(count):
    return [pl.BlockSpec(memory_space=pltpu.SMEM)] * count


def params(mib):
    return pltpu.CompilerParams(vmem_limit_bytes=mib * MIB)


def shape_of(shape, kind):
    return jax.ShapeDtypeStruct(shape, kind)


def pair_body(
    orbitals, potential, projectors, projector_energy, atom_first, atom_second, atom_third, rotation
):
    bf16, f32 = jnp.bfloat16, jnp.float32
    count, block_x, y_size, z_size = orbitals.shape[1:]
    x_size = 2 * block_x
    own = block_x * y_size
    cell_count = x_size * y_size
    atoms, nproj = projectors.shape[:2]
    spots = SIDE * atoms * nproj
    sources = lax.axis_size("orb")
    used = count * block_x
    chunk = -(-(used + count - 1) // 16) * 16

    partner_field = lax.ppermute(potential[0], "dom", [(0, 1), (1, 0)])

    plane_first, plane_second = plane_stencil(x_size, y_size)
    third = third_stencil(z_size)
    q, qt, mask, energy, diagonal, first, packed = pl.pallas_call(
        prepare_kernel,
        out_shape=(
            shape_of((spots, cell_count), bf16),
            shape_of((cell_count, 3 * spots), bf16),
            shape_of((spots, z_size), f32),
            shape_of((atoms * nproj, z_size), f32),
            shape_of((own, z_size), f32),
            shape_of((cell_count, count * z_size), f32),
            shape_of((8, z_size), f32),
        ),
        in_specs=in_smem(4) + in_vmem(7),
        out_specs=tuple(in_vmem(7)),
        scratch_shapes=[
            pltpu.VMEM((2 * own, count * z_size), bf16),
            pltpu.VMEM((3 * spots, count * z_size), bf16),
        ],
        compiler_params=params(24),
        cost_estimate=pl.CostEstimate(flops=1 << 31, bytes_accessed=6 << 20, transcendentals=0),
        name="prepare",
    )(
        atom_first,
        atom_second,
        atom_third,
        projector_energy,
        projectors,
        third_first(),
        orbitals[0],
        potential[0],
        rotation,
        plane_first,
        third,
    )

    filtered = pl.pallas_call(
        filter_kernel,
        out_shape=shape_of((2 * sources, chunk, z_size), bf16),
        in_specs=in_vmem(11),
        out_specs=in_vmem(1)[0],
        scratch_shapes=[
            pltpu.VMEM((2 * cell_count, count * z_size), bf16),
            pltpu.VMEM((3 * spots, count * z_size), bf16),
            pltpu.VMEM((2, count * own, z_size), f32),
            pltpu.VMEM((2 * sources, chunk, z_size), f32),
        ],
        compiler_params=params(40),
        name="filter",
    )(
        first,
        orbitals[0],
        partner_field,
        q,
        qt,
        mask,
        energy,
        diagonal,
        packed,
        plane_second,
        third,
    )
    by_plane = lax.all_to_all(filtered, ("dom", "orb"), split_axis=0, concat_axis=0, tiled=True)

    rotated = pl.pallas_call(
        functools.partial(rotate_kernel, count=count, block_x=block_x),
        out_shape=shape_of((sources, chunk, z_size), bf16),
        in_specs=in_vmem(1),
        out_specs=in_vmem(1)[0],
        scratch_shapes=[
            pltpu.VMEM((sources * chunk, z_size), f32),
            pltpu.VMEM((sources * used + chunk - used, z_size), f32),
        ],
        compiler_params=params(24),
        name="rotate",
    )(by_plane)
    by_orbital = lax.all_to_all(rotated, "orb", split_axis=0, concat_axis=0, tiled=True)

    return pl.pallas_call(
        unpack_kernel,
        out_shape=shape_of(orbitals.shape, bf16),
        in_specs=in_vmem(1),
        out_specs=in_vmem(1)[0],
        scratch_shapes=[pltpu.VMEM((sources * used, z_size), f32)],
        compiler_params=params(16),
        name="unpack",
    )(by_orbital)


def fits_pair(mesh, orbitals, projectors, rotation):
    count = orbitals.shape[1] // mesh.shape["orb"]
    return (
        mesh.shape["dom"] == 2
        and orbitals.shape[3] == mesh.shape["orb"]
        and orbitals.shape[2] == 2 * stencil_reach
        and projectors.shape[0] % 2 == 0
        and projectors.shape[1] == 8
        and count <= 8
        and rotation.shape[1] < orbitals.shape[4]
        and -(-rotation.shape[1] // (orbitals.shape[4] - rotation.shape[1])) < count
    )


def solution(mesh):
    def whole(*arrays):
        chosen = pair_body if fits_pair(mesh, arrays[0], arrays[2], arrays[7]) else body
        return jax.shard_map(
            chosen,
            mesh=mesh,
            in_specs=(
                P("dom", "orb", None, None, None),
                P("dom", None, None, None),
                P(),
                P(),
                P(),
                P(),
                P(),
                P("orb", None),
            ),
            out_specs=P("dom", "orb", None, None, None),
            check_vma=False,
        )(*arrays)

    return whole
```

```python
import functools

import jax
import jax.numpy as jnp
import numpy as np
from jax import lax
from jax.experimental import pallas as pl
from jax.experimental.pallas import tpu as pltpu
from jax.sharding import PartitionSpec as P

SIDE = 8
SUP = 512


stencil_weights = (
    -5369.0 / 1800.0,
    12.0 / 7.0,
    -15.0 / 56.0,
    10.0 / 189.0,
    -1.0 / 112.0,
    2.0 / 1925.0,
    -1.0 / 16632.0,
)
inverse_spacing = 4.0
filter_center = 120.0
filter_width = 110.0
stencil_reach = 6


def partner_2(block, axis, bit):
    count = lax.axis_size(axis)
    route = []
    for low in range(count):
        high = low | 1 << bit
        if high != low and high < count:
            route += [(low, high), (high, low)]
    return lax.ppermute(block, axis, route)


def outgoing(values, direction, width):
    extent = values.shape[direction]
    if 2 * width < extent:
        return jnp.concatenate(
            (
                lax.slice_in_dim(values, 0, width, axis=direction),
                lax.slice_in_dim(values, extent - width, extent, axis=direction),
            ),
            axis=direction,
        )
    return values


def assemble(values, partner, direction, width):
    extent = values.shape[direction]
    if 2 * width < extent:
        lower_rim = lax.slice_in_dim(partner, width, 2 * width, axis=direction)
        upper_rim = lax.slice_in_dim(partner, 0, width, axis=direction)
        return jnp.concatenate((lower_rim, values, upper_rim), axis=direction)
    cyclic = jnp.concatenate((values, partner), axis=direction)
    chosen = np.arange(-width, extent + width) % (2 * extent)
    return jnp.take(cyclic, jnp.asarray(chosen, dtype=jnp.int32), axis=direction)


def face_padded(values, direction, bit_number):
    sent = outgoing(values, direction, stencil_reach)
    partner = partner_2(sent.astype(jnp.bfloat16), "dom", bit_number).astype(sent.dtype)
    return assemble(values, partner, direction, stencil_reach)


def stencil_sum(center, along):
    lead = center.ndim - 3
    summed = 3.0 * stencil_weights[0] * center
    for index in range(3):
        direction = lead + index
        extent = center.shape[direction]
        padded = along[index]
        for offset in range(1, 7):
            if padded is None:
                upward = jnp.roll(center, -offset, direction)
                downward = jnp.roll(center, offset, direction)
            else:
                upward = lax.slice_in_dim(
                    padded, stencil_reach + offset, stencil_reach + offset + extent, axis=direction
                )
                downward = lax.slice_in_dim(
                    padded, stencil_reach - offset, stencil_reach - offset + extent, axis=direction
                )
            summed = summed + stencil_weights[offset] * (upward + downward)
    return summed


def support_map(atom_coords, starts, extents, periods):
    offsets = jnp.arange(SIDE, dtype=jnp.int32) - SIDE // 2
    clipped_list = []
    inside_list = []
    for index in range(3):
        local = (atom_coords[index][:, None] + offsets[None, :] - starts[index]) % periods[index]
        inside_list.append(local < extents[index])
        clipped_list.append(jnp.minimum(local, extents[index] - 1))
    inside = (
        inside_list[0][:, :, None, None]
        & inside_list[1][:, None, :, None]
        & inside_list[2][:, None, None, :]
    )
    flattened = (
        clipped_list[0][:, :, None, None] * extents[1] + clipped_list[1][:, None, :, None]
    ) * extents[2] + clipped_list[2][:, None, None, :]
    atom_count = atom_coords[0].shape[0]
    return (
        flattened.reshape(atom_count * SUP),
        inside.reshape(atom_count, SUP).astype(jnp.float32),
    )


def coefficients(values, support, inside, projectors):
    orbital_count = values.shape[0]
    atom_count = projectors.shape[0]
    flattened = values.reshape(orbital_count, -1)
    picked = (
        jnp.take(flattened, support, axis=1).reshape(orbital_count, atom_count, SUP) * inside[None]
    )
    partial_coeffs = jnp.einsum("aps,kas->kap", projectors, picked, precision=lax.Precision.HIGHEST)
    return lax.psum(partial_coeffs, "dom")


def spread_into(coeffs, shape, support, inside, projectors, projector_energy):
    orbital_count = shape[0]
    atom_count = projectors.shape[0]
    scaled = coeffs * projector_energy[None, None, :]
    spread = (
        jnp.einsum("aps,kap->kas", projectors, scaled, precision=lax.Precision.HIGHEST)
        * inside[None]
    )
    total_cells = shape[1] * shape[2] * shape[3]
    projected_part = (
        jnp.zeros((orbital_count, total_cells), jnp.float32)
        .at[:, support]
        .add(spread.reshape(orbital_count, atom_count * SUP))
    )
    return projected_part.reshape(shape)


def own_hamiltonian(center, along, local_field, support, inside, projectors, projector_energy):
    kinetic = -0.5 * inverse_spacing * inverse_spacing
    coeffs = coefficients(center, support, inside, projectors)
    projected_part = spread_into(
        coeffs, center.shape, support, inside, projectors, projector_energy
    )
    return kinetic * stencil_sum(center, along) + local_field[None] * center + projected_part


def body(
    orbitals, potential, projectors, projector_energy, atom_first, atom_second, atom_third, rotation
):
    domain_count = lax.axis_size("dom")
    domain_bits = domain_count.bit_length() - 1
    split = [index < domain_bits for index in range(3)]
    start_values = orbitals[0]
    local_field = potential[0]
    extents = start_values.shape[1:]
    periods = (
        extents[0] * min(domain_count, 2),
        extents[1] * min(max(domain_count // 2, 1), 2),
        extents[2] * max(domain_count // 4, 1),
    )
    domain_index = lax.axis_index("dom")
    anchors = (
        domain_index % 2 * extents[0],
        domain_index // 2 % 2 * extents[1],
        domain_index // 4 * extents[2],
    )
    atom_coords = (atom_first, atom_second, atom_third)
    support, inside = support_map(atom_coords, anchors, extents, periods)
    along = [
        face_padded(start_values, index + 1, index) if split[index] else None for index in range(3)
    ]
    first_apply = own_hamiltonian(
        start_values, along, local_field, support, inside, projectors, projector_energy
    )
    first_term = (first_apply - filter_center * start_values) / filter_width
    along = [
        face_padded(first_term, index + 1, index) if split[index] else None for index in range(3)
    ]
    second_apply = own_hamiltonian(
        first_term, along, local_field, support, inside, projectors, projector_energy
    )
    second_term = 2.0 * (second_apply - filter_center * first_term) / filter_width - start_values
    per_device = start_values.shape[0]
    filtered = second_term.astype(jnp.bfloat16).reshape(per_device, -1)
    by_cells = lax.all_to_all(filtered, "orb", split_axis=1, concat_axis=0, tiled=True)
    whole_rotation = lax.all_gather(rotation, "orb", axis=0, tiled=True)
    rotated = lax.dot_general(
        whole_rotation, by_cells, (((0,), (0,)), ((), ())), preferred_element_type=jnp.float32
    ).astype(jnp.bfloat16)
    result = lax.all_to_all(rotated, "orb", split_axis=0, concat_axis=1, tiled=True)
    return result.reshape((1,) + start_values.shape)


SCALE = 15.0
MIB = 1 << 20


def scaled_weights():
    ratios = np.array(stencil_weights[1:], np.float64) / stencil_weights[1]
    return SCALE * ratios


def cyclic_stencil(size):
    matrix = np.zeros((size, size), np.float64)
    rows = np.arange(size)
    for offset, weight in enumerate(scaled_weights(), 1):
        np.add.at(matrix, (rows, (rows + offset) % size), weight)
        np.add.at(matrix, (rows, (rows - offset) % size), weight)
    return matrix


def plane_stencil(x_size, y_size):
    matrix = np.kron(cyclic_stencil(x_size), np.eye(y_size))
    matrix += np.kron(np.eye(x_size), cyclic_stencil(y_size))
    return np.concatenate((matrix, matrix), axis=1).astype(jnp.bfloat16)


def third_stencil(z_size):
    matrix = cyclic_stencil(z_size)
    return np.concatenate((matrix, matrix), axis=0).astype(jnp.bfloat16)


def third_first():
    picked = np.zeros((SUP, SUP), np.float32)
    source = np.arange(SUP)
    picked[source, source % SIDE * SIDE * SIDE + source // SIDE] = 1.0
    return picked.astype(jnp.bfloat16)


def halves(values):
    high = values.astype(jnp.bfloat16)
    return high, (values - high.astype(jnp.float32)).astype(jnp.bfloat16)


def matmul(left, right):
    return jnp.dot(left, right, preferred_element_type=jnp.float32)


def shared_operator():
    kinetic = -0.5 * inverse_spacing * inverse_spacing
    unit = kinetic * stencil_weights[1] / SCALE / filter_width
    shift = 3.0 * kinetic * stencil_weights[0] - filter_center
    return unit, shift


def pack_kernel(
    orbital_ref, rotation_ref, out_ref, after_ref, start_ref, rotation_copy_ref, chunk_ref, sem_ref
):
    count, block_x, y_size, z_size = orbital_ref.shape[1:]
    used = count * block_x
    loads = [
        pltpu.make_async_copy(orbital_ref.at[0], start_ref, sem_ref.at[0]),
        pltpu.make_async_copy(rotation_ref, rotation_copy_ref, sem_ref.at[1]),
    ]
    for load in loads:
        load.start()
    for load in loads:
        load.wait()
    packed = packed_rotation(rotation_copy_ref, z_size)
    after_ref[...] = jnp.zeros(after_ref.shape, jnp.float32)
    rows_ref = start_ref.reshape(used * y_size, z_size)
    for part in range(y_size):
        chunk_ref[0:used] = rows_ref[pl.ds(part, used, stride=y_size), :]
        chunk_ref[used : used + count - 1] = packed[0 : count - 1]
        out_ref[part] = chunk_ref[...].astype(jnp.bfloat16)


def spread(products, mask_ref, energy_ref, coeff_ref):
    spots, z_size = mask_ref.shape
    pairs = energy_ref.shape[0]
    mask = mask_ref[...]
    for start in range(0, products.shape[1], z_size):
        lanes = slice(start, start + z_size)
        picked = (products[:, lanes] * mask).reshape(SIDE, pairs, z_size)
        coeffs = jnp.sum(jnp.sum(picked, axis=0), axis=1, keepdims=True)
        high, low = halves(jnp.concatenate([coeffs * energy_ref[...]] * SIDE, axis=0) * mask)
        coeff_ref[0:spots, lanes] = high
        coeff_ref[spots : 2 * spots, lanes] = low
        coeff_ref[2 * spots :, lanes] = high


def table_kernel(
    first_at_ref,
    second_at_ref,
    third_at_ref,
    energy_at_ref,
    after_ref,
    projector_ref,
    order_ref,
    field_ref,
    q_ref,
    qt_ref,
    mask_ref,
    energy_ref,
    diagonal_ref,
):
    block_x, y_size, z_size = field_ref.shape[1:]
    x_size = 2 * block_x
    own = block_x * y_size
    cell_count = x_size * y_size
    atoms, nproj = projector_ref.shape[:2]
    pairs = atoms * nproj
    per_plane = SIDE * SIDE
    spots = atoms * per_plane
    unit, shift = shared_operator()
    own_start = lax.axis_index("dom") * block_x
    high, low = halves(projector_ref[...].reshape(pairs, SUP))
    ordered = matmul(jnp.concatenate((high, low), axis=0), order_ref[...])

    lane = lax.broadcasted_iota(jnp.int32, (pairs, 2 * per_plane), 1)
    row_atom = lax.broadcasted_iota(jnp.int32, (pairs, spots), 0) // nproj
    lane_atom = lax.broadcasted_iota(jnp.int32, (pairs, spots), 1) // per_plane
    same_atom = row_atom == lane_atom
    expanded = []
    for part in range(2):
        rows = []
        for third in range(SIDE):
            start = third // 2 * 2 * per_plane
            both = ordered[part * pairs : (part + 1) * pairs, start : start + 2 * per_plane]
            swapped = pltpu.roll(both, per_plane, 1)
            if third % 2:
                both, swapped = swapped, both
            doubled = jnp.where(lane < per_plane, both, swapped)
            doubled = jnp.concatenate([doubled] * (atoms // 2), axis=1)
            rows.append(jnp.where(same_atom, doubled, 0.0))
        expanded.append(jnp.concatenate(rows, axis=0).astype(jnp.bfloat16))
    high, low = expanded

    place = []
    spot = lax.broadcasted_iota(jnp.int32, (per_plane, cell_count), 0)
    place_lane = lax.broadcasted_iota(jnp.int32, (per_plane, cell_count), 1)
    for atom in range(atoms):
        x_start = lax.rem(first_at_ref[atom] - SIDE // 2 - own_start + 2 * x_size, x_size)
        y_start = lax.rem(second_at_ref[atom] - SIDE // 2 + y_size, y_size)
        x_index = x_start + spot // SIDE
        x_index = jnp.where(x_index >= x_size, x_index - x_size, x_index)
        y_index = y_start + spot % SIDE
        y_index = jnp.where(y_index >= y_size, y_index - y_size, y_index)
        target = x_index * y_size + y_index
        place.append(jnp.where(place_lane == target, 1.0, 0.0).astype(jnp.bfloat16))
    place = jnp.concatenate(place, axis=0)
    q_high = matmul(high, place)
    q_ref[...] = q_high.astype(jnp.bfloat16)
    q_high = q_high.T.astype(jnp.bfloat16)
    qt_ref[:, 0:spots] = q_high
    qt_ref[:, spots : 2 * spots] = q_high
    qt_ref[:, 2 * spots : 3 * spots] = matmul(low, place).T.astype(jnp.bfloat16)

    z_lane = lax.broadcasted_iota(jnp.int32, (nproj, z_size), 1)
    for third in range(SIDE):
        for atom in range(atoms):
            z_index = lax.rem(third_at_ref[atom] + third - SIDE // 2 + z_size, z_size)
            start = third * pairs + atom * nproj
            mask_ref[start : start + nproj] = jnp.where(z_lane == z_index, 1.0, 0.0)
    sublane = lax.broadcasted_iota(jnp.int32, (nproj, z_size), 0)
    energy = jnp.zeros((nproj, z_size), jnp.float32)
    for index in range(nproj):
        energy = jnp.where(sublane == index, energy_at_ref[index], energy)
    energy = energy * (1.0 / (unit * filter_width))
    for atom in range(atoms):
        energy_ref[atom * nproj : (atom + 1) * nproj] = energy

    diagonal_ref[...] = (field_ref[0].reshape(own, z_size) + shift) / filter_width


def packed_rotation(rotation_ref, z_size):
    count, wide = rotation_ref.shape
    spare = z_size - wide
    block = jnp.concatenate(
        (rotation_ref[...].astype(jnp.float32), jnp.zeros((count, spare), jnp.float32)), axis=1
    )
    block = jnp.concatenate((block, jnp.zeros((8 - count, z_size), jnp.float32)), axis=0)
    sublane = lax.broadcasted_iota(jnp.int32, (8, z_size), 0)
    lane = lax.broadcasted_iota(jnp.int32, (8, z_size), 1)
    packed = block
    for piece in range(-(-wide // spare)):
        moved = pltpu.roll(block, (piece - (count - 1)) % 8, 0)
        moved = pltpu.roll(moved, (wide - piece * spare) % z_size, 1)
        packed = jnp.where((sublane == piece) & (lane >= wide), moved, packed)
    return packed


def filter_kernel(
    received_ref,
    q_ref,
    qt_ref,
    mask_ref,
    energy_ref,
    diagonal_ref,
    partner_diagonal_ref,
    plane_ref,
    third_ref,
    out_ref,
    rows_ref,
    right_ref,
    coeff_ref,
    first_ref,
):
    count, block_x, y_size, z_size = out_ref.shape[1:]
    own = block_x * y_size
    cell_count = 2 * own
    used = count * block_x
    unit, _ = shared_operator()
    me = lax.axis_index("dom")
    for half in range(2):
        for part in range(y_size):
            values = received_ref[(me ^ half) * y_size + part].astype(jnp.float32)
            rows_ref[half, pl.ds(part, used, stride=y_size), :] = values[0:used]
    columns = [slice(orbital * z_size, (orbital + 1) * z_size) for orbital in range(count)]
    for orbital, lanes in enumerate(columns):
        rows = slice(orbital * own, (orbital + 1) * own)
        right_ref[0:own, lanes] = rows_ref[0, rows].astype(jnp.bfloat16)
        right_ref[own:cell_count, lanes] = rows_ref[1, rows].astype(jnp.bfloat16)
    spread(matmul(q_ref[...], right_ref[0:cell_count]), mask_ref, energy_ref, coeff_ref)
    summed = matmul(plane_ref[:, 0:cell_count], right_ref[0:cell_count])
    summed = summed + matmul(qt_ref[...], coeff_ref[...])
    for orbital, lanes in enumerate(columns):
        rows = slice(orbital * own, (orbital + 1) * own)
        along = matmul(right_ref[0:cell_count, lanes], third_ref[0:z_size])
        along = unit * (summed[:, lanes] + along)
        first_ref[0:own, lanes] = diagonal_ref[...] * rows_ref[0, rows] + along[0:own]
        first_ref[own:, lanes] = partner_diagonal_ref[...] * rows_ref[1, rows] + along[own:]

    high, low = halves(first_ref[...])
    right_ref[0:cell_count] = high
    right_ref[cell_count:] = low
    spread(matmul(q_ref[...], right_ref[0:cell_count]), mask_ref, energy_ref, coeff_ref)
    summed = matmul(plane_ref[0:own], right_ref[...])
    summed = summed + matmul(qt_ref[0:own], coeff_ref[...])
    for orbital, lanes in enumerate(columns):
        rows = slice(orbital * own, (orbital + 1) * own)
        left = jnp.concatenate(
            (right_ref[0:own, lanes], right_ref[cell_count : cell_count + own, lanes]), axis=1
        )
        along = unit * (summed[:, lanes] + matmul(left, third_ref[...]))
        values = 2.0 * (diagonal_ref[...] * first_ref[0:own, lanes] + along) - rows_ref[0, rows]
        out_ref[0, orbital] = values.astype(jnp.bfloat16).reshape(block_x, y_size, z_size)


def rotate_kernel(received_ref, out_ref, wide_ref, rows_ref, *, count, block_x):
    sources, chunk, z_size = received_ref.shape
    total = sources * count
    used = count * block_x
    spare = z_size - total
    wide_ref[...] = received_ref[...].astype(jnp.float32).reshape(sources * chunk, z_size)
    packed = [wide_ref[pl.ds(used + row, sources, stride=chunk), :] for row in range(count - 1)]
    lane = lax.broadcasted_iota(jnp.int32, (sources, z_size), 1)
    last = jnp.zeros((sources, z_size), jnp.float32)
    for piece in range(-(-total // spare)):
        moved = pltpu.roll(packed[piece], (piece * spare - total) % z_size, 1)
        last = jnp.where(lane >= piece * spare, moved, last)
    rotation = jnp.concatenate(packed + [last], axis=0)[:, 0:total].astype(jnp.bfloat16)
    columns = []
    for plane in range(block_x):
        rows = [
            wide_ref[pl.ds(orbital * block_x + plane, sources, stride=chunk), :]
            for orbital in range(count)
        ]
        columns.append(jnp.concatenate(rows, axis=0).astype(jnp.bfloat16))
    values = jnp.concatenate(columns, axis=1)
    rotated = lax.dot_general(
        rotation, values, (((0,), (0,)), ((), ())), preferred_element_type=jnp.float32
    )
    rows_ref[total * block_x :] = jnp.zeros((chunk - used, z_size), jnp.float32)
    for plane in range(block_x):
        lanes = slice(plane * z_size, (plane + 1) * z_size)
        rows_ref[pl.ds(plane, total, stride=block_x), :] = rotated[:, lanes]
    for part in range(sources):
        values = rows_ref[part * used : part * used + chunk].astype(jnp.bfloat16)
        out_ref[part] = values
        out_ref[sources + part] = values


def in_vmem(count):
    return [pl.BlockSpec(memory_space=pltpu.VMEM)] * count


def in_smem(count):
    return [pl.BlockSpec(memory_space=pltpu.SMEM)] * count


def params(mib):
    return pltpu.CompilerParams(vmem_limit_bytes=mib * MIB)


def shape_of(shape, kind):
    return jax.ShapeDtypeStruct(shape, kind)


def pair_body(
    orbitals, potential, projectors, projector_energy, atom_first, atom_second, atom_third, rotation
):
    bf16, f32 = jnp.bfloat16, jnp.float32
    count, block_x, y_size, z_size = orbitals.shape[1:]
    x_size = 2 * block_x
    own = block_x * y_size
    cell_count = x_size * y_size
    atoms, nproj = projectors.shape[:2]
    spots = SIDE * atoms * nproj
    sources = lax.axis_size("orb")
    used = count * block_x
    chunk = -(-(used + count - 1) // 16) * 16

    packed, after = pl.pallas_call(
        pack_kernel,
        out_shape=(shape_of((sources, chunk, z_size), bf16), shape_of((8, z_size), f32)),
        in_specs=[pl.BlockSpec(memory_space=pltpu.HBM)] * 2,
        out_specs=tuple(in_vmem(2)),
        scratch_shapes=[
            pltpu.VMEM(orbitals.shape[1:], f32),
            pltpu.VMEM(rotation.shape, bf16),
            pltpu.VMEM((chunk, z_size), f32),
            pltpu.SemaphoreType.DMA((2,)),
        ],
        compiler_params=params(60),
        name="pack",
    )(orbitals, rotation)
    by_plane = lax.all_to_all(packed, "orb", split_axis=0, concat_axis=0, tiled=True)

    q, qt, mask, energy, diagonal = pl.pallas_call(
        table_kernel,
        out_shape=(
            shape_of((spots, cell_count), bf16),
            shape_of((cell_count, 3 * spots), bf16),
            shape_of((spots, z_size), f32),
            shape_of((atoms * nproj, z_size), f32),
            shape_of((own, z_size), f32),
        ),
        in_specs=in_smem(4) + [pl.BlockSpec(memory_space=pl.ANY)] + in_vmem(3),
        out_specs=tuple(in_vmem(5)),
        compiler_params=params(24),
        cost_estimate=pl.CostEstimate(flops=1 << 31, bytes_accessed=6 << 20, transcendentals=0),
        name="tables",
    )(
        atom_first,
        atom_second,
        atom_third,
        projector_energy,
        after,
        projectors,
        third_first(),
        potential,
    )
    partner_diagonal = lax.ppermute(diagonal, "dom", [(0, 1), (1, 0)])

    rotated = pl.pallas_call(
        functools.partial(rotate_kernel, count=count, block_x=block_x),
        out_shape=shape_of((2 * sources, chunk, z_size), bf16),
        in_specs=in_vmem(1),
        out_specs=in_vmem(1)[0],
        scratch_shapes=[
            pltpu.VMEM((sources * chunk, z_size), f32),
            pltpu.VMEM((sources * used + chunk - used, z_size), f32),
        ],
        compiler_params=params(24),
        name="rotate",
    )(by_plane)
    by_orbital = lax.all_to_all(rotated, ("dom", "orb"), split_axis=0, concat_axis=0, tiled=True)

    return pl.pallas_call(
        filter_kernel,
        out_shape=shape_of(orbitals.shape, bf16),
        in_specs=in_vmem(9),
        out_specs=in_vmem(1)[0],
        scratch_shapes=[
            pltpu.VMEM((2, count * own, z_size), f32),
            pltpu.VMEM((2 * cell_count, count * z_size), bf16),
            pltpu.VMEM((3 * spots, count * z_size), bf16),
            pltpu.VMEM((cell_count, count * z_size), f32),
        ],
        compiler_params=params(40),
        name="filter",
    )(
        by_orbital,
        q,
        qt,
        mask,
        energy,
        diagonal,
        partner_diagonal,
        plane_stencil(x_size, y_size),
        third_stencil(z_size),
    )


def fits_pair(mesh, orbitals, projectors, rotation):
    count = orbitals.shape[1] // mesh.shape["orb"]
    return (
        mesh.shape["dom"] == 2
        and orbitals.shape[3] == mesh.shape["orb"]
        and orbitals.shape[2] == 2 * stencil_reach
        and projectors.shape[0] % 2 == 0
        and projectors.shape[1] == 8
        and count <= 8
        and rotation.shape[1] < orbitals.shape[4]
        and -(-rotation.shape[1] // (orbitals.shape[4] - rotation.shape[1])) < count
    )


def solution(mesh):
    def whole(*arrays):
        chosen = pair_body if fits_pair(mesh, arrays[0], arrays[2], arrays[7]) else body
        return jax.shard_map(
            chosen,
            mesh=mesh,
            in_specs=(
                P("dom", "orb", None, None, None),
                P("dom", None, None, None),
                P(),
                P(),
                P(),
                P(),
                P(),
                P("orb", None),
            ),
            out_specs=P("dom", "orb", None, None, None),
            check_vma=False,
        )(*arrays)

    return whole
```

```python
import functools

import jax
import jax.numpy as jnp
import numpy as np
from jax import lax
from jax.experimental import pallas as pl
from jax.experimental.pallas import tpu as pltpu
from jax.sharding import PartitionSpec as P

SIDE = 8
SUP = 512


stencil_weights = (
    -5369.0 / 1800.0,
    12.0 / 7.0,
    -15.0 / 56.0,
    10.0 / 189.0,
    -1.0 / 112.0,
    2.0 / 1925.0,
    -1.0 / 16632.0,
)
inverse_spacing = 4.0
filter_center = 120.0
filter_width = 110.0
stencil_reach = 6


def partner_2(block, axis, bit):
    count = lax.axis_size(axis)
    route = []
    for low in range(count):
        high = low | 1 << bit
        if high != low and high < count:
            route += [(low, high), (high, low)]
    return lax.ppermute(block, axis, route)


def outgoing(values, direction, width):
    extent = values.shape[direction]
    if 2 * width < extent:
        return jnp.concatenate(
            (
                lax.slice_in_dim(values, 0, width, axis=direction),
                lax.slice_in_dim(values, extent - width, extent, axis=direction),
            ),
            axis=direction,
        )
    return values


def assemble(values, partner, direction, width):
    extent = values.shape[direction]
    if 2 * width < extent:
        lower_rim = lax.slice_in_dim(partner, width, 2 * width, axis=direction)
        upper_rim = lax.slice_in_dim(partner, 0, width, axis=direction)
        return jnp.concatenate((lower_rim, values, upper_rim), axis=direction)
    cyclic = jnp.concatenate((values, partner), axis=direction)
    chosen = np.arange(-width, extent + width) % (2 * extent)
    return jnp.take(cyclic, jnp.asarray(chosen, dtype=jnp.int32), axis=direction)


def face_padded(values, direction, bit_number):
    sent = outgoing(values, direction, stencil_reach)
    partner = partner_2(sent.astype(jnp.bfloat16), "dom", bit_number).astype(sent.dtype)
    return assemble(values, partner, direction, stencil_reach)


def stencil_sum(center, along):
    lead = center.ndim - 3
    summed = 3.0 * stencil_weights[0] * center
    for index in range(3):
        direction = lead + index
        extent = center.shape[direction]
        padded = along[index]
        for offset in range(1, 7):
            if padded is None:
                upward = jnp.roll(center, -offset, direction)
                downward = jnp.roll(center, offset, direction)
            else:
                upward = lax.slice_in_dim(
                    padded, stencil_reach + offset, stencil_reach + offset + extent, axis=direction
                )
                downward = lax.slice_in_dim(
                    padded, stencil_reach - offset, stencil_reach - offset + extent, axis=direction
                )
            summed = summed + stencil_weights[offset] * (upward + downward)
    return summed


def support_map(atom_coords, starts, extents, periods):
    offsets = jnp.arange(SIDE, dtype=jnp.int32) - SIDE // 2
    clipped_list = []
    inside_list = []
    for index in range(3):
        local = (atom_coords[index][:, None] + offsets[None, :] - starts[index]) % periods[index]
        inside_list.append(local < extents[index])
        clipped_list.append(jnp.minimum(local, extents[index] - 1))
    inside = (
        inside_list[0][:, :, None, None]
        & inside_list[1][:, None, :, None]
        & inside_list[2][:, None, None, :]
    )
    flattened = (
        clipped_list[0][:, :, None, None] * extents[1] + clipped_list[1][:, None, :, None]
    ) * extents[2] + clipped_list[2][:, None, None, :]
    atom_count = atom_coords[0].shape[0]
    return (
        flattened.reshape(atom_count * SUP),
        inside.reshape(atom_count, SUP).astype(jnp.float32),
    )


def coefficients(values, support, inside, projectors):
    orbital_count = values.shape[0]
    atom_count = projectors.shape[0]
    flattened = values.reshape(orbital_count, -1)
    picked = (
        jnp.take(flattened, support, axis=1).reshape(orbital_count, atom_count, SUP) * inside[None]
    )
    partial_coeffs = jnp.einsum("aps,kas->kap", projectors, picked, precision=lax.Precision.HIGHEST)
    return lax.psum(partial_coeffs, "dom")


def spread_into(coeffs, shape, support, inside, projectors, projector_energy):
    orbital_count = shape[0]
    atom_count = projectors.shape[0]
    scaled = coeffs * projector_energy[None, None, :]
    spread = (
        jnp.einsum("aps,kap->kas", projectors, scaled, precision=lax.Precision.HIGHEST)
        * inside[None]
    )
    total_cells = shape[1] * shape[2] * shape[3]
    projected_part = (
        jnp.zeros((orbital_count, total_cells), jnp.float32)
        .at[:, support]
        .add(spread.reshape(orbital_count, atom_count * SUP))
    )
    return projected_part.reshape(shape)


def own_hamiltonian(center, along, local_field, support, inside, projectors, projector_energy):
    kinetic = -0.5 * inverse_spacing * inverse_spacing
    coeffs = coefficients(center, support, inside, projectors)
    projected_part = spread_into(
        coeffs, center.shape, support, inside, projectors, projector_energy
    )
    return kinetic * stencil_sum(center, along) + local_field[None] * center + projected_part


def body(
    orbitals, potential, projectors, projector_energy, atom_first, atom_second, atom_third, rotation
):
    domain_count = lax.axis_size("dom")
    domain_bits = domain_count.bit_length() - 1
    split = [index < domain_bits for index in range(3)]
    start_values = orbitals[0]
    local_field = potential[0]
    extents = start_values.shape[1:]
    periods = (
        extents[0] * min(domain_count, 2),
        extents[1] * min(max(domain_count // 2, 1), 2),
        extents[2] * max(domain_count // 4, 1),
    )
    domain_index = lax.axis_index("dom")
    anchors = (
        domain_index % 2 * extents[0],
        domain_index // 2 % 2 * extents[1],
        domain_index // 4 * extents[2],
    )
    atom_coords = (atom_first, atom_second, atom_third)
    support, inside = support_map(atom_coords, anchors, extents, periods)
    along = [
        face_padded(start_values, index + 1, index) if split[index] else None for index in range(3)
    ]
    first_apply = own_hamiltonian(
        start_values, along, local_field, support, inside, projectors, projector_energy
    )
    first_term = (first_apply - filter_center * start_values) / filter_width
    along = [
        face_padded(first_term, index + 1, index) if split[index] else None for index in range(3)
    ]
    second_apply = own_hamiltonian(
        first_term, along, local_field, support, inside, projectors, projector_energy
    )
    second_term = 2.0 * (second_apply - filter_center * first_term) / filter_width - start_values
    per_device = start_values.shape[0]
    filtered = second_term.astype(jnp.bfloat16).reshape(per_device, -1)
    by_cells = lax.all_to_all(filtered, "orb", split_axis=1, concat_axis=0, tiled=True)
    whole_rotation = lax.all_gather(rotation, "orb", axis=0, tiled=True)
    rotated = lax.dot_general(
        whole_rotation, by_cells, (((0,), (0,)), ((), ())), preferred_element_type=jnp.float32
    ).astype(jnp.bfloat16)
    result = lax.all_to_all(rotated, "orb", split_axis=0, concat_axis=1, tiled=True)
    return result.reshape((1,) + start_values.shape)


SCALE = 15.0
MIB = 1 << 20


def scaled_weights():
    ratios = np.array(stencil_weights[1:], np.float64) / stencil_weights[1]
    return SCALE * ratios


def cyclic_stencil(size):
    matrix = np.zeros((size, size), np.float64)
    rows = np.arange(size)
    for offset, weight in enumerate(scaled_weights(), 1):
        np.add.at(matrix, (rows, (rows + offset) % size), weight)
        np.add.at(matrix, (rows, (rows - offset) % size), weight)
    return matrix


def plane_stencil(x_size, y_size):
    matrix = np.kron(cyclic_stencil(x_size), np.eye(y_size))
    matrix += np.kron(np.eye(x_size), cyclic_stencil(y_size))
    return np.concatenate((matrix, matrix), axis=1).astype(jnp.bfloat16)


def third_stencil(z_size):
    matrix = cyclic_stencil(z_size)
    stacked = np.concatenate((matrix, matrix), axis=0)
    paired = np.kron(np.eye(2), matrix)
    return stacked.astype(jnp.bfloat16), paired.astype(jnp.bfloat16)


def third_first():
    picked = np.zeros((SUP, SUP), np.float32)
    source = np.arange(SUP)
    picked[source, source % SIDE * SIDE * SIDE + source // SIDE] = 1.0
    return picked.astype(jnp.bfloat16)


def halves(values):
    high = values.astype(jnp.bfloat16)
    return high, (values - high.astype(jnp.float32)).astype(jnp.bfloat16)


def matmul(left, right):
    return jnp.dot(left, right, preferred_element_type=jnp.float32)


def shared_operator():
    kinetic = -0.5 * inverse_spacing * inverse_spacing
    unit = kinetic * stencil_weights[1] / SCALE / filter_width
    shift = 3.0 * kinetic * stencil_weights[0] - filter_center
    return unit, shift


def pack_kernel(
    orbital_ref, rotation_ref, out_ref, after_ref, start_ref, rotation_copy_ref, chunk_ref, sem_ref
):
    count, block_x, y_size, z_size = orbital_ref.shape[1:]
    used = count * block_x
    loads = [
        pltpu.make_async_copy(orbital_ref.at[0], start_ref, sem_ref.at[0]),
        pltpu.make_async_copy(rotation_ref, rotation_copy_ref, sem_ref.at[1]),
    ]
    for load in loads:
        load.start()
    for load in loads:
        load.wait()
    packed = packed_rotation(rotation_copy_ref, z_size)
    after_ref[...] = jnp.zeros(after_ref.shape, jnp.float32)
    rows_ref = start_ref.reshape(used * y_size, z_size)
    for part in range(y_size):
        chunk_ref[0:used] = rows_ref[pl.ds(part, used, stride=y_size), :]
        chunk_ref[used : used + count - 1] = packed[0 : count - 1]
        out_ref[part] = chunk_ref[...].astype(jnp.bfloat16)


def spread(products, mask_ref, energy_ref, coeff_ref):
    spots, z_size = mask_ref.shape
    pairs = energy_ref.shape[0]
    mask = mask_ref[...]
    for start in range(0, products.shape[1], z_size):
        lanes = slice(start, start + z_size)
        picked = (products[:, lanes] * mask).reshape(SIDE, pairs, z_size)
        coeffs = jnp.sum(jnp.sum(picked, axis=0), axis=1, keepdims=True)
        high, low = halves(jnp.concatenate([coeffs * energy_ref[...]] * SIDE, axis=0) * mask)
        coeff_ref[0:spots, lanes] = high
        coeff_ref[spots : 2 * spots, lanes] = low
        coeff_ref[2 * spots :, lanes] = high


def table_kernel(
    first_at_ref,
    second_at_ref,
    third_at_ref,
    energy_at_ref,
    after_ref,
    projector_ref,
    order_ref,
    field_ref,
    q_ref,
    qt_ref,
    mask_ref,
    energy_ref,
    diagonal_ref,
):
    block_x, y_size, z_size = field_ref.shape[1:]
    x_size = 2 * block_x
    own = block_x * y_size
    cell_count = x_size * y_size
    atoms, nproj = projector_ref.shape[:2]
    pairs = atoms * nproj
    per_plane = SIDE * SIDE
    spots = atoms * per_plane
    unit, shift = shared_operator()
    own_start = lax.axis_index("dom") * block_x
    high, low = halves(projector_ref[...].reshape(pairs, SUP))
    ordered = matmul(jnp.concatenate((high, low), axis=0), order_ref[...])

    lane = lax.broadcasted_iota(jnp.int32, (pairs, 2 * per_plane), 1)
    row_atom = lax.broadcasted_iota(jnp.int32, (pairs, spots), 0) // nproj
    lane_atom = lax.broadcasted_iota(jnp.int32, (pairs, spots), 1) // per_plane
    same_atom = row_atom == lane_atom
    expanded = []
    for part in range(2):
        rows = []
        for third in range(SIDE):
            start = third // 2 * 2 * per_plane
            both = ordered[part * pairs : (part + 1) * pairs, start : start + 2 * per_plane]
            swapped = pltpu.roll(both, per_plane, 1)
            if third % 2:
                both, swapped = swapped, both
            doubled = jnp.where(lane < per_plane, both, swapped)
            doubled = jnp.concatenate([doubled] * (atoms // 2), axis=1)
            rows.append(jnp.where(same_atom, doubled, 0.0))
        expanded.append(jnp.concatenate(rows, axis=0).astype(jnp.bfloat16))
    high, low = expanded

    place = []
    spot = lax.broadcasted_iota(jnp.int32, (per_plane, cell_count), 0)
    place_lane = lax.broadcasted_iota(jnp.int32, (per_plane, cell_count), 1)
    for atom in range(atoms):
        x_start = lax.rem(first_at_ref[atom] - SIDE // 2 - own_start + 2 * x_size, x_size)
        y_start = lax.rem(second_at_ref[atom] - SIDE // 2 + y_size, y_size)
        x_index = x_start + spot // SIDE
        x_index = jnp.where(x_index >= x_size, x_index - x_size, x_index)
        y_index = y_start + spot % SIDE
        y_index = jnp.where(y_index >= y_size, y_index - y_size, y_index)
        target = x_index * y_size + y_index
        place.append(jnp.where(place_lane == target, 1.0, 0.0).astype(jnp.bfloat16))
    place = jnp.concatenate(place, axis=0)
    q_high = matmul(high, place)
    q_ref[...] = q_high.astype(jnp.bfloat16)
    q_high = q_high.T.astype(jnp.bfloat16)
    qt_ref[:, 0:spots] = q_high
    qt_ref[:, spots : 2 * spots] = q_high
    qt_ref[:, 2 * spots : 3 * spots] = matmul(low, place).T.astype(jnp.bfloat16)

    z_lane = lax.broadcasted_iota(jnp.int32, (nproj, z_size), 1)
    for third in range(SIDE):
        for atom in range(atoms):
            z_index = lax.rem(third_at_ref[atom] + third - SIDE // 2 + z_size, z_size)
            start = third * pairs + atom * nproj
            mask_ref[start : start + nproj] = jnp.where(z_lane == z_index, 1.0, 0.0)
    sublane = lax.broadcasted_iota(jnp.int32, (nproj, z_size), 0)
    energy = jnp.zeros((nproj, z_size), jnp.float32)
    for index in range(nproj):
        energy = jnp.where(sublane == index, energy_at_ref[index], energy)
    energy = energy * (1.0 / (unit * filter_width))
    for atom in range(atoms):
        energy_ref[atom * nproj : (atom + 1) * nproj] = energy

    diagonal_ref[...] = (field_ref[0].reshape(own, z_size) + shift) / filter_width


def packed_rotation(rotation_ref, z_size):
    count, wide = rotation_ref.shape
    spare = z_size - wide
    block = jnp.concatenate(
        (rotation_ref[...].astype(jnp.float32), jnp.zeros((count, spare), jnp.float32)), axis=1
    )
    block = jnp.concatenate((block, jnp.zeros((8 - count, z_size), jnp.float32)), axis=0)
    sublane = lax.broadcasted_iota(jnp.int32, (8, z_size), 0)
    lane = lax.broadcasted_iota(jnp.int32, (8, z_size), 1)
    packed = block
    for piece in range(-(-wide // spare)):
        moved = pltpu.roll(block, (piece - (count - 1)) % 8, 0)
        moved = pltpu.roll(moved, (wide - piece * spare) % z_size, 1)
        packed = jnp.where((sublane == piece) & (lane >= wide), moved, packed)
    return packed


def filter_kernel(
    received_ref,
    q_ref,
    qt_ref,
    mask_ref,
    energy_ref,
    diagonal_ref,
    partner_diagonal_ref,
    plane_ref,
    third_ref,
    paired_ref,
    out_ref,
    rows_ref,
    right_ref,
    coeff_ref,
    first_ref,
    result_ref,
    sem_ref,
):
    count, block_x, y_size, z_size = out_ref.shape[1:]
    own = block_x * y_size
    cell_count = 2 * own
    used = count * block_x
    unit, _ = shared_operator()
    me = lax.axis_index("dom")
    for half in range(2):
        for part in range(y_size):
            values = received_ref[(me ^ half) * y_size + part].astype(jnp.float32)
            rows_ref[half, pl.ds(part, used, stride=y_size), :] = values[0:used]
    columns = [slice(orbital * z_size, (orbital + 1) * z_size) for orbital in range(count)]
    for orbital, lanes in enumerate(columns):
        rows = slice(orbital * own, (orbital + 1) * own)
        right_ref[0:own, lanes] = rows_ref[0, rows].astype(jnp.bfloat16)
        right_ref[own:cell_count, lanes] = rows_ref[1, rows].astype(jnp.bfloat16)
    spread(matmul(q_ref[...], right_ref[0:cell_count]), mask_ref, energy_ref, coeff_ref)
    summed = matmul(plane_ref[:, 0:cell_count], right_ref[0:cell_count])
    spots = mask_ref.shape[0]
    summed = summed + matmul(qt_ref[:, 0 : 2 * spots], coeff_ref[0 : 2 * spots])
    pairs = count // 2 * 2
    along_all = [
        matmul(
            right_ref[0:cell_count, first * z_size : (first + 2) * z_size],
            paired_ref[...],
        )
        for first in range(0, pairs, 2)
    ]
    if pairs < count:
        along_all.append(matmul(right_ref[0:cell_count, columns[-1]], third_ref[0:z_size]))
    for orbital, lanes in enumerate(columns):
        rows = slice(orbital * own, (orbital + 1) * own)
        along = along_all[orbital // 2][:, columns[orbital % 2]]
        along = unit * (summed[:, lanes] + along)
        first_ref[0:own, lanes] = diagonal_ref[...] * rows_ref[0, rows] + along[0:own]
        first_ref[own:, lanes] = partner_diagonal_ref[...] * rows_ref[1, rows] + along[own:]

    high, low = halves(first_ref[...])
    right_ref[0:cell_count] = high
    right_ref[cell_count:] = low
    spread(matmul(q_ref[...], right_ref[0:cell_count]), mask_ref, energy_ref, coeff_ref)
    stores = []
    summed = matmul(plane_ref[0:own], right_ref[...])
    summed = summed + matmul(qt_ref[0:own], coeff_ref[...])
    for orbital, lanes in enumerate(columns):
        rows = slice(orbital * own, (orbital + 1) * own)
        left = jnp.concatenate(
            (right_ref[0:own, lanes], right_ref[cell_count : cell_count + own, lanes]), axis=1
        )
        along = unit * (summed[:, lanes] + matmul(left, third_ref[...]))
        values = 2.0 * (diagonal_ref[...] * first_ref[0:own, lanes] + along) - rows_ref[0, rows]
        values = values.astype(jnp.bfloat16).reshape(block_x, y_size, z_size)
        result_ref[orbital] = values
        stores.append(
            pltpu.make_async_copy(
                result_ref.at[orbital], out_ref.at[0, orbital], sem_ref.at[orbital]
            )
        )
        stores[-1].start()
    for store in stores:
        store.wait()


def rotate_kernel(received_ref, after_ref, out_ref, wide_ref, rows_ref, *, count, block_x):
    sources, chunk, z_size = received_ref.shape
    total = sources * count
    used = count * block_x
    spare = z_size - total
    wide_ref[...] = received_ref[...].astype(jnp.float32).reshape(sources * chunk, z_size)
    packed = [wide_ref[pl.ds(used + row, sources, stride=chunk), :] for row in range(count - 1)]
    lane = lax.broadcasted_iota(jnp.int32, (sources, z_size), 1)
    last = jnp.zeros((sources, z_size), jnp.float32)
    for piece in range(-(-total // spare)):
        moved = pltpu.roll(packed[piece], (piece * spare - total) % z_size, 1)
        last = jnp.where(lane >= piece * spare, moved, last)
    rotation = jnp.concatenate(packed + [last], axis=0)[:, 0:total].astype(jnp.bfloat16)
    columns = []
    for plane in range(block_x):
        rows = [
            wide_ref[pl.ds(orbital * block_x + plane, sources, stride=chunk), :]
            for orbital in range(count)
        ]
        columns.append(jnp.concatenate(rows, axis=0).astype(jnp.bfloat16))
    values = jnp.concatenate(columns, axis=1)
    rotated = lax.dot_general(
        rotation, values, (((0,), (0,)), ((), ())), preferred_element_type=jnp.float32
    )
    rows_ref[total * block_x :] = jnp.zeros((chunk - used, z_size), jnp.float32)
    for plane in range(block_x):
        lanes = slice(plane * z_size, (plane + 1) * z_size)
        rows_ref[pl.ds(plane, total, stride=block_x), :] = rotated[:, lanes]
    for part in range(sources):
        values = rows_ref[part * used : part * used + chunk].astype(jnp.bfloat16)
        out_ref[part] = values
        out_ref[sources + part] = values


def in_vmem(count):
    return [pl.BlockSpec(memory_space=pltpu.VMEM)] * count


def in_smem(count):
    return [pl.BlockSpec(memory_space=pltpu.SMEM)] * count


def params(mib):
    return pltpu.CompilerParams(vmem_limit_bytes=mib * MIB)


def shape_of(shape, kind):
    return jax.ShapeDtypeStruct(shape, kind)


def pair_body(
    orbitals, potential, projectors, projector_energy, atom_first, atom_second, atom_third, rotation
):
    bf16, f32 = jnp.bfloat16, jnp.float32
    count, block_x, y_size, z_size = orbitals.shape[1:]
    x_size = 2 * block_x
    own = block_x * y_size
    cell_count = x_size * y_size
    atoms, nproj = projectors.shape[:2]
    spots = SIDE * atoms * nproj
    sources = lax.axis_size("orb")
    used = count * block_x
    chunk = -(-(used + count - 1) // 16) * 16

    packed, after = pl.pallas_call(
        pack_kernel,
        out_shape=(shape_of((sources, chunk, z_size), bf16), shape_of((8, z_size), f32)),
        in_specs=[pl.BlockSpec(memory_space=pltpu.HBM)] * 2,
        out_specs=tuple(in_vmem(2)),
        scratch_shapes=[
            pltpu.VMEM(orbitals.shape[1:], f32),
            pltpu.VMEM(rotation.shape, bf16),
            pltpu.VMEM((chunk, z_size), f32),
            pltpu.SemaphoreType.DMA((2,)),
        ],
        compiler_params=params(60),
        name="pack",
    )(orbitals, rotation)
    by_plane = lax.all_to_all(packed, "orb", split_axis=0, concat_axis=0, tiled=True)

    q, qt, mask, energy, diagonal = pl.pallas_call(
        table_kernel,
        out_shape=(
            shape_of((spots, cell_count), bf16),
            shape_of((cell_count, 3 * spots), bf16),
            shape_of((spots, z_size), f32),
            shape_of((atoms * nproj, z_size), f32),
            shape_of((own, z_size), f32),
        ),
        in_specs=in_smem(4) + [pl.BlockSpec(memory_space=pl.ANY)] + in_vmem(3),
        out_specs=tuple(in_vmem(5)),
        compiler_params=params(24),
        cost_estimate=pl.CostEstimate(flops=1 << 31, bytes_accessed=6 << 20, transcendentals=0),
        name="tables",
    )(
        atom_first,
        atom_second,
        atom_third,
        projector_energy,
        after,
        projectors,
        third_first(),
        potential,
    )
    partner_diagonal = lax.ppermute(diagonal, "dom", [(0, 1), (1, 0)])

    rotated = pl.pallas_call(
        functools.partial(rotate_kernel, count=count, block_x=block_x),
        out_shape=shape_of((2 * sources, chunk, z_size), bf16),
        in_specs=in_vmem(2),
        out_specs=in_vmem(1)[0],
        scratch_shapes=[
            pltpu.VMEM((sources * chunk, z_size), f32),
            pltpu.VMEM((sources * used + chunk - used, z_size), f32),
        ],
        compiler_params=params(24),
        name="rotate",
    )(by_plane, partner_diagonal)
    by_orbital = lax.all_to_all(rotated, ("dom", "orb"), split_axis=0, concat_axis=0, tiled=True)

    return pl.pallas_call(
        filter_kernel,
        out_shape=shape_of(orbitals.shape, bf16),
        in_specs=in_vmem(10),
        out_specs=pl.BlockSpec(memory_space=pltpu.HBM),
        scratch_shapes=[
            pltpu.VMEM((2, count * own, z_size), f32),
            pltpu.VMEM((2 * cell_count, count * z_size), bf16),
            pltpu.VMEM((3 * spots, count * z_size), bf16),
            pltpu.VMEM((cell_count, count * z_size), f32),
            pltpu.VMEM(orbitals.shape[1:], bf16),
            pltpu.SemaphoreType.DMA((count,)),
        ],
        compiler_params=params(40),
        name="filter",
    )(
        by_orbital,
        q,
        qt,
        mask,
        energy,
        diagonal,
        partner_diagonal,
        plane_stencil(x_size, y_size),
        *third_stencil(z_size),
    )


def fits_pair(mesh, orbitals, projectors, rotation):
    count = orbitals.shape[1] // mesh.shape["orb"]
    return (
        mesh.shape["dom"] == 2
        and orbitals.shape[3] == mesh.shape["orb"]
        and orbitals.shape[2] == 2 * stencil_reach
        and projectors.shape[0] % 2 == 0
        and projectors.shape[1] == 8
        and count <= 8
        and rotation.shape[1] < orbitals.shape[4]
        and -(-rotation.shape[1] // (orbitals.shape[4] - rotation.shape[1])) < count
    )


def solution(mesh):
    def whole(*arrays):
        chosen = pair_body if fits_pair(mesh, arrays[0], arrays[2], arrays[7]) else body
        return jax.shard_map(
            chosen,
            mesh=mesh,
            in_specs=(
                P("dom", "orb", None, None, None),
                P("dom", None, None, None),
                P(),
                P(),
                P(),
                P(),
                P(),
                P("orb", None),
            ),
            out_specs=P("dom", "orb", None, None, None),
            check_vma=False,
        )(*arrays)

    return whole
```

```python
import functools

import jax
import jax.numpy as jnp
import numpy as np
from jax import lax
from jax.experimental import pallas as pl
from jax.experimental.pallas import tpu as pltpu
from jax.sharding import PartitionSpec as P

SIDE = 8
SUP = 512


stencil_weights = (
    -5369.0 / 1800.0,
    12.0 / 7.0,
    -15.0 / 56.0,
    10.0 / 189.0,
    -1.0 / 112.0,
    2.0 / 1925.0,
    -1.0 / 16632.0,
)
inverse_spacing = 4.0
filter_center = 120.0
filter_width = 110.0
stencil_reach = 6


def partner_2(block, axis, bit):
    count = lax.axis_size(axis)
    route = []
    for low in range(count):
        high = low | 1 << bit
        if high != low and high < count:
            route += [(low, high), (high, low)]
    return lax.ppermute(block, axis, route)


def outgoing(values, direction, width):
    extent = values.shape[direction]
    if 2 * width < extent:
        return jnp.concatenate(
            (
                lax.slice_in_dim(values, 0, width, axis=direction),
                lax.slice_in_dim(values, extent - width, extent, axis=direction),
            ),
            axis=direction,
        )
    return values


def assemble(values, partner, direction, width):
    extent = values.shape[direction]
    if 2 * width < extent:
        lower_rim = lax.slice_in_dim(partner, width, 2 * width, axis=direction)
        upper_rim = lax.slice_in_dim(partner, 0, width, axis=direction)
        return jnp.concatenate((lower_rim, values, upper_rim), axis=direction)
    cyclic = jnp.concatenate((values, partner), axis=direction)
    chosen = np.arange(-width, extent + width) % (2 * extent)
    return jnp.take(cyclic, jnp.asarray(chosen, dtype=jnp.int32), axis=direction)


def face_padded(values, direction, bit_number):
    sent = outgoing(values, direction, stencil_reach)
    partner = partner_2(sent.astype(jnp.bfloat16), "dom", bit_number).astype(sent.dtype)
    return assemble(values, partner, direction, stencil_reach)


def stencil_sum(center, along):
    lead = center.ndim - 3
    summed = 3.0 * stencil_weights[0] * center
    for index in range(3):
        direction = lead + index
        extent = center.shape[direction]
        padded = along[index]
        for offset in range(1, 7):
            if padded is None:
                upward = jnp.roll(center, -offset, direction)
                downward = jnp.roll(center, offset, direction)
            else:
                upward = lax.slice_in_dim(
                    padded, stencil_reach + offset, stencil_reach + offset + extent, axis=direction
                )
                downward = lax.slice_in_dim(
                    padded, stencil_reach - offset, stencil_reach - offset + extent, axis=direction
                )
            summed = summed + stencil_weights[offset] * (upward + downward)
    return summed


def support_map(atom_coords, starts, extents, periods):
    offsets = jnp.arange(SIDE, dtype=jnp.int32) - SIDE // 2
    clipped_list = []
    inside_list = []
    for index in range(3):
        local = (atom_coords[index][:, None] + offsets[None, :] - starts[index]) % periods[index]
        inside_list.append(local < extents[index])
        clipped_list.append(jnp.minimum(local, extents[index] - 1))
    inside = (
        inside_list[0][:, :, None, None]
        & inside_list[1][:, None, :, None]
        & inside_list[2][:, None, None, :]
    )
    flattened = (
        clipped_list[0][:, :, None, None] * extents[1] + clipped_list[1][:, None, :, None]
    ) * extents[2] + clipped_list[2][:, None, None, :]
    atom_count = atom_coords[0].shape[0]
    return (
        flattened.reshape(atom_count * SUP),
        inside.reshape(atom_count, SUP).astype(jnp.float32),
    )


def coefficients(values, support, inside, projectors):
    orbital_count = values.shape[0]
    atom_count = projectors.shape[0]
    flattened = values.reshape(orbital_count, -1)
    picked = (
        jnp.take(flattened, support, axis=1).reshape(orbital_count, atom_count, SUP) * inside[None]
    )
    partial_coeffs = jnp.einsum("aps,kas->kap", projectors, picked, precision=lax.Precision.HIGHEST)
    return lax.psum(partial_coeffs, "dom")


def spread_into(coeffs, shape, support, inside, projectors, projector_energy):
    orbital_count = shape[0]
    atom_count = projectors.shape[0]
    scaled = coeffs * projector_energy[None, None, :]
    spread = (
        jnp.einsum("aps,kap->kas", projectors, scaled, precision=lax.Precision.HIGHEST)
        * inside[None]
    )
    total_cells = shape[1] * shape[2] * shape[3]
    projected_part = (
        jnp.zeros((orbital_count, total_cells), jnp.float32)
        .at[:, support]
        .add(spread.reshape(orbital_count, atom_count * SUP))
    )
    return projected_part.reshape(shape)


def own_hamiltonian(center, along, local_field, support, inside, projectors, projector_energy):
    kinetic = -0.5 * inverse_spacing * inverse_spacing
    coeffs = coefficients(center, support, inside, projectors)
    projected_part = spread_into(
        coeffs, center.shape, support, inside, projectors, projector_energy
    )
    return kinetic * stencil_sum(center, along) + local_field[None] * center + projected_part


def body(
    orbitals, potential, projectors, projector_energy, atom_first, atom_second, atom_third, rotation
):
    domain_count = lax.axis_size("dom")
    domain_bits = domain_count.bit_length() - 1
    split = [index < domain_bits for index in range(3)]
    start_values = orbitals[0]
    local_field = potential[0]
    extents = start_values.shape[1:]
    periods = (
        extents[0] * min(domain_count, 2),
        extents[1] * min(max(domain_count // 2, 1), 2),
        extents[2] * max(domain_count // 4, 1),
    )
    domain_index = lax.axis_index("dom")
    anchors = (
        domain_index % 2 * extents[0],
        domain_index // 2 % 2 * extents[1],
        domain_index // 4 * extents[2],
    )
    atom_coords = (atom_first, atom_second, atom_third)
    support, inside = support_map(atom_coords, anchors, extents, periods)
    along = [
        face_padded(start_values, index + 1, index) if split[index] else None for index in range(3)
    ]
    first_apply = own_hamiltonian(
        start_values, along, local_field, support, inside, projectors, projector_energy
    )
    first_term = (first_apply - filter_center * start_values) / filter_width
    along = [
        face_padded(first_term, index + 1, index) if split[index] else None for index in range(3)
    ]
    second_apply = own_hamiltonian(
        first_term, along, local_field, support, inside, projectors, projector_energy
    )
    second_term = 2.0 * (second_apply - filter_center * first_term) / filter_width - start_values
    per_device = start_values.shape[0]
    filtered = second_term.astype(jnp.bfloat16).reshape(per_device, -1)
    by_cells = lax.all_to_all(filtered, "orb", split_axis=1, concat_axis=0, tiled=True)
    whole_rotation = lax.all_gather(rotation, "orb", axis=0, tiled=True)
    rotated = lax.dot_general(
        whole_rotation, by_cells, (((0,), (0,)), ((), ())), preferred_element_type=jnp.float32
    ).astype(jnp.bfloat16)
    result = lax.all_to_all(rotated, "orb", split_axis=0, concat_axis=1, tiled=True)
    return result.reshape((1,) + start_values.shape)


SCALE = 15.0
MIB = 1 << 20


def scaled_weights():
    ratios = np.array(stencil_weights[1:], np.float64) / stencil_weights[1]
    return SCALE * ratios


def cyclic_stencil(size):
    matrix = np.zeros((size, size), np.float64)
    rows = np.arange(size)
    for offset, weight in enumerate(scaled_weights(), 1):
        np.add.at(matrix, (rows, (rows + offset) % size), weight)
        np.add.at(matrix, (rows, (rows - offset) % size), weight)
    return matrix


def plane_stencil(x_size, y_size):
    matrix = np.kron(cyclic_stencil(x_size), np.eye(y_size))
    matrix += np.kron(np.eye(x_size), cyclic_stencil(y_size))
    return matrix.astype(jnp.bfloat16)


def third_stencil(z_size):
    matrix = cyclic_stencil(z_size)
    return np.kron(np.eye(2), matrix).astype(jnp.bfloat16)


def third_first():
    picked = np.zeros((SUP, SUP), np.float32)
    source = np.arange(SUP)
    picked[source, source % SIDE * SIDE * SIDE + source // SIDE] = 1.0
    return picked.astype(jnp.bfloat16)


def halves(values):
    high = values.astype(jnp.bfloat16)
    return high, (values - high.astype(jnp.float32)).astype(jnp.bfloat16)


def matmul(left, right):
    return jnp.dot(left, right, preferred_element_type=jnp.float32)


def shared_operator():
    kinetic = -0.5 * inverse_spacing * inverse_spacing
    unit = kinetic * stencil_weights[1] / SCALE / filter_width
    shift = 3.0 * kinetic * stencil_weights[0] - filter_center
    return unit, shift


def pack_kernel(
    orbital_ref,
    rotation_ref,
    out_ref,
    after_ref,
    start_ref,
    rotation_copy_ref,
    chunk_ref,
    made_ref,
    sem_ref,
    store_sem_ref,
):
    count, block_x, y_size, z_size = orbital_ref.shape[1:]
    used = count * block_x
    loads = [
        pltpu.make_async_copy(orbital_ref.at[0], start_ref, sem_ref.at[0]),
        pltpu.make_async_copy(rotation_ref, rotation_copy_ref, sem_ref.at[1]),
    ]
    for load in loads:
        load.start()
    for load in loads:
        load.wait()
    packed = packed_rotation(rotation_copy_ref, z_size)
    after_ref[...] = jnp.zeros(after_ref.shape, jnp.float32)
    rows_ref = start_ref.reshape(used * y_size, z_size)
    stores = []
    for part in range(y_size):
        chunk_ref[part, 0:used] = rows_ref[pl.ds(part, used, stride=y_size), :]
        chunk_ref[part, used : used + count - 1] = packed[0 : count - 1]
        made_ref[part] = chunk_ref[part].astype(jnp.bfloat16)
        if part % 4 == 3:
            parts = pl.ds(part - 3, 4)
            stores.append(
                pltpu.make_async_copy(
                    made_ref.at[parts], out_ref.at[parts], store_sem_ref.at[part // 4]
                )
            )
            stores[-1].start()
    for store in stores:
        store.wait()


def spread(products, mask_ref, energy_ref, coeff_ref):
    spots, z_size = mask_ref.shape
    pairs = energy_ref.shape[0]
    mask = mask_ref[...]
    for start in range(0, products.shape[1], z_size):
        lanes = slice(start, start + z_size)
        picked = (products[:, lanes] * mask).reshape(SIDE, pairs, z_size)
        coeffs = jnp.sum(jnp.sum(picked, axis=0), axis=1, keepdims=True)
        high, low = halves(jnp.concatenate([coeffs * energy_ref[...]] * SIDE, axis=0) * mask)
        coeff_ref[0:spots, lanes] = high
        coeff_ref[spots : 2 * spots, lanes] = low
        if coeff_ref.shape[0] > 2 * spots:
            coeff_ref[2 * spots :, lanes] = high


def table_kernel(
    first_at_ref,
    second_at_ref,
    third_at_ref,
    energy_at_ref,
    after_ref,
    projector_ref,
    order_ref,
    plane_ref,
    field_ref,
    q_ref,
    left_ref,
    mask_ref,
    energy_ref,
    diagonal_ref,
):
    block_x, y_size, z_size = field_ref.shape[1:]
    x_size = 2 * block_x
    own = block_x * y_size
    cell_count = x_size * y_size
    atoms, nproj = projector_ref.shape[:2]
    pairs = atoms * nproj
    per_plane = SIDE * SIDE
    spots = atoms * per_plane
    unit, shift = shared_operator()
    own_start = lax.axis_index("dom") * block_x
    high, low = halves(projector_ref[...].reshape(pairs, SUP))
    ordered = matmul(jnp.concatenate((high, low), axis=0), order_ref[...])

    lane = lax.broadcasted_iota(jnp.int32, (pairs, 2 * per_plane), 1)
    row_atom = lax.broadcasted_iota(jnp.int32, (pairs, spots), 0) // nproj
    lane_atom = lax.broadcasted_iota(jnp.int32, (pairs, spots), 1) // per_plane
    same_atom = row_atom == lane_atom
    expanded = []
    for part in range(2):
        rows = []
        for third in range(SIDE):
            start = third // 2 * 2 * per_plane
            both = ordered[part * pairs : (part + 1) * pairs, start : start + 2 * per_plane]
            swapped = pltpu.roll(both, per_plane, 1)
            if third % 2:
                both, swapped = swapped, both
            doubled = jnp.where(lane < per_plane, both, swapped)
            doubled = jnp.concatenate([doubled] * (atoms // 2), axis=1)
            rows.append(jnp.where(same_atom, doubled, 0.0))
        expanded.append(jnp.concatenate(rows, axis=0).astype(jnp.bfloat16))
    high, low = expanded

    place = []
    spot = lax.broadcasted_iota(jnp.int32, (per_plane, cell_count), 0)
    place_lane = lax.broadcasted_iota(jnp.int32, (per_plane, cell_count), 1)
    for atom in range(atoms):
        x_start = lax.rem(first_at_ref[atom] - SIDE // 2 - own_start + 2 * x_size, x_size)
        y_start = lax.rem(second_at_ref[atom] - SIDE // 2 + y_size, y_size)
        x_index = x_start + spot // SIDE
        x_index = jnp.where(x_index >= x_size, x_index - x_size, x_index)
        y_index = y_start + spot % SIDE
        y_index = jnp.where(y_index >= y_size, y_index - y_size, y_index)
        target = x_index * y_size + y_index
        place.append(jnp.where(place_lane == target, 1.0, 0.0).astype(jnp.bfloat16))
    place = jnp.concatenate(place, axis=0)
    q_high = matmul(high, place)
    q_ref[...] = q_high.astype(jnp.bfloat16)
    q_high = q_high.T.astype(jnp.bfloat16)
    left_ref[:, 0:cell_count] = plane_ref[...]
    left_ref[:, cell_count : cell_count + spots] = q_high
    left_ref[:, cell_count + spots : cell_count + 2 * spots] = q_high
    left_ref[:, cell_count + 2 * spots :] = matmul(low, place).T.astype(jnp.bfloat16)

    z_lane = lax.broadcasted_iota(jnp.int32, (nproj, z_size), 1)
    for third in range(SIDE):
        for atom in range(atoms):
            z_index = lax.rem(third_at_ref[atom] + third - SIDE // 2 + z_size, z_size)
            start = third * pairs + atom * nproj
            mask_ref[start : start + nproj] = jnp.where(z_lane == z_index, 1.0, 0.0)
    sublane = lax.broadcasted_iota(jnp.int32, (nproj, z_size), 0)
    energy = jnp.zeros((nproj, z_size), jnp.float32)
    for index in range(nproj):
        energy = jnp.where(sublane == index, energy_at_ref[index], energy)
    energy = energy * (1.0 / (unit * filter_width))
    for atom in range(atoms):
        energy_ref[atom * nproj : (atom + 1) * nproj] = energy

    diagonal_ref[...] = (field_ref[0].reshape(own, z_size) + shift) / filter_width


def packed_rotation(rotation_ref, z_size):
    count, wide = rotation_ref.shape
    spare = z_size - wide
    block = jnp.concatenate(
        (rotation_ref[...].astype(jnp.float32), jnp.zeros((count, spare), jnp.float32)), axis=1
    )
    block = jnp.concatenate((block, jnp.zeros((8 - count, z_size), jnp.float32)), axis=0)
    sublane = lax.broadcasted_iota(jnp.int32, (8, z_size), 0)
    lane = lax.broadcasted_iota(jnp.int32, (8, z_size), 1)
    packed = block
    for piece in range(-(-wide // spare)):
        moved = pltpu.roll(block, (piece - (count - 1)) % 8, 0)
        moved = pltpu.roll(moved, (wide - piece * spare) % z_size, 1)
        packed = jnp.where((sublane == piece) & (lane >= wide), moved, packed)
    return packed


def filter_kernel(
    received_ref,
    q_ref,
    left_ref,
    mask_ref,
    energy_ref,
    diagonal_ref,
    partner_diagonal_ref,
    third_ref,
    out_ref,
    rows_ref,
    right_ref,
    first_ref,
    result_ref,
    sem_ref,
):
    count, block_x, y_size, z_size = out_ref.shape[1:]
    own = block_x * y_size
    cells = 2 * own
    used = count * block_x
    spots = mask_ref.shape[0]
    unit, _ = shared_operator()
    columns = [slice(orbital * z_size, (orbital + 1) * z_size) for orbital in range(count)]

    def along_third(rows):
        pieces = []
        for first in range(0, count, 2):
            last = min(first + 2, count)
            lanes = slice(first * z_size, last * z_size)
            wide = (last - first) * z_size
            pieces.append(matmul(right_ref[0:rows, lanes], third_ref[0:wide, 0:wide]))
        return [pieces[orbital // 2][:, columns[orbital % 2]] for orbital in range(count)]

    me = lax.axis_index("dom")
    for half in range(2):
        for part in range(y_size):
            values = received_ref[(me ^ half) * y_size + part].astype(jnp.float32)
            rows_ref[half, pl.ds(part, used, stride=y_size), :] = values[0:used]
    for orbital, lanes in enumerate(columns):
        rows = slice(orbital * own, (orbital + 1) * own)
        right_ref[0:own, lanes] = rows_ref[0, rows].astype(jnp.bfloat16)
        right_ref[own:cells, lanes] = rows_ref[1, rows].astype(jnp.bfloat16)
    depth = cells + 2 * spots
    products = matmul(q_ref[...], right_ref[0:cells])
    spread(products, mask_ref, energy_ref, right_ref.at[cells:depth])
    summed = matmul(left_ref[:, 0:depth], right_ref[0:depth])
    along = along_third(cells)
    for orbital, lanes in enumerate(columns):
        rows = slice(orbital * own, (orbital + 1) * own)
        values = unit * (summed[:, lanes] + along[orbital])
        mine = diagonal_ref[...] * rows_ref[0, rows] + values[0:own]
        first_ref[:, lanes] = mine
        right_ref[0:own, lanes] = mine.astype(jnp.bfloat16)
        other = partner_diagonal_ref[...] * rows_ref[1, rows] + values[own:]
        right_ref[own:cells, lanes] = other.astype(jnp.bfloat16)

    products = matmul(q_ref[...], right_ref[0:cells])
    spread(products, mask_ref, energy_ref, right_ref.at[cells:])
    summed = matmul(left_ref[0:own], right_ref[...])
    along = along_third(own)
    stores = []
    for orbital, lanes in enumerate(columns):
        rows = slice(orbital * own, (orbital + 1) * own)
        values = diagonal_ref[...] * first_ref[:, lanes] + unit * (summed[:, lanes] + along[orbital])
        values = (2.0 * values - rows_ref[0, rows]).astype(jnp.bfloat16)
        result_ref[orbital] = values.reshape(block_x, y_size, z_size)
        stores.append(
            pltpu.make_async_copy(
                result_ref.at[orbital], out_ref.at[0, orbital], sem_ref.at[orbital]
            )
        )
        stores[-1].start()
    for store in stores:
        store.wait()


def rotate_kernel(received_ref, after_ref, out_ref, wide_ref, rows_ref, *, count, block_x):
    sources, chunk, z_size = received_ref.shape
    total = sources * count
    used = count * block_x
    spare = z_size - total
    wide_ref[...] = received_ref[...].astype(jnp.float32).reshape(sources * chunk, z_size)
    packed = [wide_ref[pl.ds(used + row, sources, stride=chunk), :] for row in range(count - 1)]
    lane = lax.broadcasted_iota(jnp.int32, (sources, z_size), 1)
    last = jnp.zeros((sources, z_size), jnp.float32)
    for piece in range(-(-total // spare)):
        moved = pltpu.roll(packed[piece], (piece * spare - total) % z_size, 1)
        last = jnp.where(lane >= piece * spare, moved, last)
    rotation = jnp.concatenate(packed + [last], axis=0)[:, 0:total].astype(jnp.bfloat16)
    columns = []
    for plane in range(block_x):
        rows = [
            wide_ref[pl.ds(orbital * block_x + plane, sources, stride=chunk), :]
            for orbital in range(count)
        ]
        columns.append(jnp.concatenate(rows, axis=0).astype(jnp.bfloat16))
    values = jnp.concatenate(columns, axis=1)
    rotated = lax.dot_general(
        rotation, values, (((0,), (0,)), ((), ())), preferred_element_type=jnp.float32
    )
    rows_ref[total * block_x :] = jnp.zeros((chunk - used, z_size), jnp.float32)
    for plane in range(block_x):
        lanes = slice(plane * z_size, (plane + 1) * z_size)
        rows_ref[pl.ds(plane, total, stride=block_x), :] = rotated[:, lanes]
    for part in range(sources):
        values = rows_ref[part * used : part * used + chunk].astype(jnp.bfloat16)
        out_ref[part] = values
        out_ref[sources + part] = values


def in_vmem(count):
    return [pl.BlockSpec(memory_space=pltpu.VMEM)] * count


def in_smem(count):
    return [pl.BlockSpec(memory_space=pltpu.SMEM)] * count


def params(mib):
    return pltpu.CompilerParams(vmem_limit_bytes=mib * MIB)


def shape_of(shape, kind):
    return jax.ShapeDtypeStruct(shape, kind)


def pair_body(
    orbitals, potential, projectors, projector_energy, atom_first, atom_second, atom_third, rotation
):
    bf16, f32 = jnp.bfloat16, jnp.float32
    count, block_x, y_size, z_size = orbitals.shape[1:]
    x_size = 2 * block_x
    own = block_x * y_size
    cell_count = x_size * y_size
    atoms, nproj = projectors.shape[:2]
    spots = SIDE * atoms * nproj
    sources = lax.axis_size("orb")
    used = count * block_x
    chunk = -(-(used + count - 1) // 16) * 16

    packed, after = pl.pallas_call(
        pack_kernel,
        out_shape=(shape_of((sources, chunk, z_size), bf16), shape_of((8, z_size), f32)),
        in_specs=[pl.BlockSpec(memory_space=pltpu.HBM)] * 2,
        out_specs=(pl.BlockSpec(memory_space=pltpu.HBM), in_vmem(1)[0]),
        scratch_shapes=[
            pltpu.VMEM(orbitals.shape[1:], f32),
            pltpu.VMEM(rotation.shape, bf16),
            pltpu.VMEM((sources, chunk, z_size), f32),
            pltpu.VMEM((sources, chunk, z_size), bf16),
            pltpu.SemaphoreType.DMA((2,)),
            pltpu.SemaphoreType.DMA((sources // 4,)),
        ],
        compiler_params=params(60),
        name="pack",
    )(orbitals, rotation)
    by_plane = lax.all_to_all(packed, "orb", split_axis=0, concat_axis=0, tiled=True)

    q, left, mask, energy, diagonal = pl.pallas_call(
        table_kernel,
        out_shape=(
            shape_of((spots, cell_count), bf16),
            shape_of((cell_count, cell_count + 3 * spots), bf16),
            shape_of((spots, z_size), f32),
            shape_of((atoms * nproj, z_size), f32),
            shape_of((own, z_size), f32),
        ),
        in_specs=in_smem(4) + [pl.BlockSpec(memory_space=pl.ANY)] + in_vmem(4),
        out_specs=tuple(in_vmem(5)),
        compiler_params=params(24),
        cost_estimate=pl.CostEstimate(flops=1 << 31, bytes_accessed=6 << 20, transcendentals=0),
        name="tables",
    )(
        atom_first,
        atom_second,
        atom_third,
        projector_energy,
        after,
        projectors,
        third_first(),
        plane_stencil(x_size, y_size),
        potential,
    )
    partner_diagonal = lax.ppermute(diagonal, "dom", [(0, 1), (1, 0)])

    rotated = pl.pallas_call(
        functools.partial(rotate_kernel, count=count, block_x=block_x),
        out_shape=shape_of((2 * sources, chunk, z_size), bf16),
        in_specs=in_vmem(2),
        out_specs=in_vmem(1)[0],
        scratch_shapes=[
            pltpu.VMEM((sources * chunk, z_size), f32),
            pltpu.VMEM((sources * used + chunk - used, z_size), f32),
        ],
        compiler_params=params(24),
        name="rotate",
    )(by_plane, partner_diagonal)
    by_orbital = lax.all_to_all(rotated, ("dom", "orb"), split_axis=0, concat_axis=0, tiled=True)

    return pl.pallas_call(
        filter_kernel,
        out_shape=shape_of(orbitals.shape, bf16),
        in_specs=in_vmem(8),
        out_specs=pl.BlockSpec(memory_space=pltpu.HBM),
        scratch_shapes=[
            pltpu.VMEM((2, count * own, z_size), f32),
            pltpu.VMEM((cell_count + 3 * spots, count * z_size), bf16),
            pltpu.VMEM((own, count * z_size), f32),
            pltpu.VMEM(orbitals.shape[1:], bf16),
            pltpu.SemaphoreType.DMA((count,)),
        ],
        compiler_params=params(40),
        name="filter",
    )(
        by_orbital,
        q,
        left,
        mask,
        energy,
        diagonal,
        partner_diagonal,
        third_stencil(z_size),
    )


def fits_pair(mesh, orbitals, projectors, rotation):
    count = orbitals.shape[1] // mesh.shape["orb"]
    return (
        mesh.shape["dom"] == 2
        and orbitals.shape[3] == mesh.shape["orb"]
        and orbitals.shape[2] == 2 * stencil_reach
        and projectors.shape[0] % 2 == 0
        and projectors.shape[1] == 8
        and count <= 8
        and rotation.shape[1] < orbitals.shape[4]
        and -(-rotation.shape[1] // (orbitals.shape[4] - rotation.shape[1])) < count
    )


def solution(mesh):
    def whole(*arrays):
        chosen = pair_body if fits_pair(mesh, arrays[0], arrays[2], arrays[7]) else body
        return jax.shard_map(
            chosen,
            mesh=mesh,
            in_specs=(
                P("dom", "orb", None, None, None),
                P("dom", None, None, None),
                P(),
                P(),
                P(),
                P(),
                P(),
                P("orb", None),
            ),
            out_specs=P("dom", "orb", None, None, None),
            check_vma=False,
        )(*arrays)

    return whole
```

```python
import functools

import jax
import jax.numpy as jnp
import numpy as np
from jax import lax
from jax.experimental import pallas as pl
from jax.experimental.pallas import tpu as pltpu
from jax.sharding import PartitionSpec as P

SIDE = 8
SUP = 512


stencil_weights = (
    -5369.0 / 1800.0,
    12.0 / 7.0,
    -15.0 / 56.0,
    10.0 / 189.0,
    -1.0 / 112.0,
    2.0 / 1925.0,
    -1.0 / 16632.0,
)
inverse_spacing = 4.0
filter_center = 120.0
filter_width = 110.0
stencil_reach = 6


def partner_2(block, axis, bit):
    count = lax.axis_size(axis)
    route = []
    for low in range(count):
        high = low | 1 << bit
        if high != low and high < count:
            route += [(low, high), (high, low)]
    return lax.ppermute(block, axis, route)


def outgoing(values, direction, width):
    extent = values.shape[direction]
    if 2 * width < extent:
        return jnp.concatenate(
            (
                lax.slice_in_dim(values, 0, width, axis=direction),
                lax.slice_in_dim(values, extent - width, extent, axis=direction),
            ),
            axis=direction,
        )
    return values


def assemble(values, partner, direction, width):
    extent = values.shape[direction]
    if 2 * width < extent:
        lower_rim = lax.slice_in_dim(partner, width, 2 * width, axis=direction)
        upper_rim = lax.slice_in_dim(partner, 0, width, axis=direction)
        return jnp.concatenate((lower_rim, values, upper_rim), axis=direction)
    cyclic = jnp.concatenate((values, partner), axis=direction)
    chosen = np.arange(-width, extent + width) % (2 * extent)
    return jnp.take(cyclic, jnp.asarray(chosen, dtype=jnp.int32), axis=direction)


def face_padded(values, direction, bit_number):
    sent = outgoing(values, direction, stencil_reach)
    partner = partner_2(sent.astype(jnp.bfloat16), "dom", bit_number).astype(sent.dtype)
    return assemble(values, partner, direction, stencil_reach)


def stencil_sum(center, along):
    lead = center.ndim - 3
    summed = 3.0 * stencil_weights[0] * center
    for index in range(3):
        direction = lead + index
        extent = center.shape[direction]
        padded = along[index]
        for offset in range(1, 7):
            if padded is None:
                upward = jnp.roll(center, -offset, direction)
                downward = jnp.roll(center, offset, direction)
            else:
                upward = lax.slice_in_dim(
                    padded, stencil_reach + offset, stencil_reach + offset + extent, axis=direction
                )
                downward = lax.slice_in_dim(
                    padded, stencil_reach - offset, stencil_reach - offset + extent, axis=direction
                )
            summed = summed + stencil_weights[offset] * (upward + downward)
    return summed


def support_map(atom_coords, starts, extents, periods):
    offsets = jnp.arange(SIDE, dtype=jnp.int32) - SIDE // 2
    clipped_list = []
    inside_list = []
    for index in range(3):
        local = (atom_coords[index][:, None] + offsets[None, :] - starts[index]) % periods[index]
        inside_list.append(local < extents[index])
        clipped_list.append(jnp.minimum(local, extents[index] - 1))
    inside = (
        inside_list[0][:, :, None, None]
        & inside_list[1][:, None, :, None]
        & inside_list[2][:, None, None, :]
    )
    flattened = (
        clipped_list[0][:, :, None, None] * extents[1] + clipped_list[1][:, None, :, None]
    ) * extents[2] + clipped_list[2][:, None, None, :]
    atom_count = atom_coords[0].shape[0]
    return (
        flattened.reshape(atom_count * SUP),
        inside.reshape(atom_count, SUP).astype(jnp.float32),
    )


def coefficients(values, support, inside, projectors):
    orbital_count = values.shape[0]
    atom_count = projectors.shape[0]
    flattened = values.reshape(orbital_count, -1)
    picked = (
        jnp.take(flattened, support, axis=1).reshape(orbital_count, atom_count, SUP) * inside[None]
    )
    partial_coeffs = jnp.einsum("aps,kas->kap", projectors, picked, precision=lax.Precision.HIGHEST)
    return lax.psum(partial_coeffs, "dom")


def spread_into(coeffs, shape, support, inside, projectors, projector_energy):
    orbital_count = shape[0]
    atom_count = projectors.shape[0]
    scaled = coeffs * projector_energy[None, None, :]
    spread = (
        jnp.einsum("aps,kap->kas", projectors, scaled, precision=lax.Precision.HIGHEST)
        * inside[None]
    )
    total_cells = shape[1] * shape[2] * shape[3]
    projected_part = (
        jnp.zeros((orbital_count, total_cells), jnp.float32)
        .at[:, support]
        .add(spread.reshape(orbital_count, atom_count * SUP))
    )
    return projected_part.reshape(shape)


def own_hamiltonian(center, along, local_field, support, inside, projectors, projector_energy):
    kinetic = -0.5 * inverse_spacing * inverse_spacing
    coeffs = coefficients(center, support, inside, projectors)
    projected_part = spread_into(
        coeffs, center.shape, support, inside, projectors, projector_energy
    )
    return kinetic * stencil_sum(center, along) + local_field[None] * center + projected_part


def body(
    orbitals, potential, projectors, projector_energy, atom_first, atom_second, atom_third, rotation
):
    domain_count = lax.axis_size("dom")
    domain_bits = domain_count.bit_length() - 1
    split = [index < domain_bits for index in range(3)]
    start_values = orbitals[0]
    local_field = potential[0]
    extents = start_values.shape[1:]
    periods = (
        extents[0] * min(domain_count, 2),
        extents[1] * min(max(domain_count // 2, 1), 2),
        extents[2] * max(domain_count // 4, 1),
    )
    domain_index = lax.axis_index("dom")
    anchors = (
        domain_index % 2 * extents[0],
        domain_index // 2 % 2 * extents[1],
        domain_index // 4 * extents[2],
    )
    atom_coords = (atom_first, atom_second, atom_third)
    support, inside = support_map(atom_coords, anchors, extents, periods)
    along = [
        face_padded(start_values, index + 1, index) if split[index] else None for index in range(3)
    ]
    first_apply = own_hamiltonian(
        start_values, along, local_field, support, inside, projectors, projector_energy
    )
    first_term = (first_apply - filter_center * start_values) / filter_width
    along = [
        face_padded(first_term, index + 1, index) if split[index] else None for index in range(3)
    ]
    second_apply = own_hamiltonian(
        first_term, along, local_field, support, inside, projectors, projector_energy
    )
    second_term = 2.0 * (second_apply - filter_center * first_term) / filter_width - start_values
    per_device = start_values.shape[0]
    filtered = second_term.astype(jnp.bfloat16).reshape(per_device, -1)
    by_cells = lax.all_to_all(filtered, "orb", split_axis=1, concat_axis=0, tiled=True)
    whole_rotation = lax.all_gather(rotation, "orb", axis=0, tiled=True)
    rotated = lax.dot_general(
        whole_rotation, by_cells, (((0,), (0,)), ((), ())), preferred_element_type=jnp.float32
    ).astype(jnp.bfloat16)
    result = lax.all_to_all(rotated, "orb", split_axis=0, concat_axis=1, tiled=True)
    return result.reshape((1,) + start_values.shape)


SCALE = 15.0
MIB = 1 << 20


def scaled_weights():
    ratios = np.array(stencil_weights[1:], np.float64) / stencil_weights[1]
    return SCALE * ratios


def cyclic_stencil(size):
    matrix = np.zeros((size, size), np.float64)
    rows = np.arange(size)
    for offset, weight in enumerate(scaled_weights(), 1):
        np.add.at(matrix, (rows, (rows + offset) % size), weight)
        np.add.at(matrix, (rows, (rows - offset) % size), weight)
    return matrix


def plane_stencil(x_size, y_size):
    matrix = np.kron(cyclic_stencil(x_size), np.eye(y_size))
    matrix += np.kron(np.eye(x_size), cyclic_stencil(y_size))
    return matrix.astype(jnp.bfloat16)


def third_stencil(z_size):
    matrix = cyclic_stencil(z_size)
    return np.kron(np.eye(2), matrix).astype(jnp.bfloat16)


def third_first():
    picked = np.zeros((SUP, SUP), np.float32)
    source = np.arange(SUP)
    picked[source, source % SIDE * SIDE * SIDE + source // SIDE] = 1.0
    return picked.astype(jnp.bfloat16)


def halves(values):
    high = values.astype(jnp.bfloat16)
    return high, (values - high.astype(jnp.float32)).astype(jnp.bfloat16)


def matmul(left, right):
    return jnp.dot(left, right, preferred_element_type=jnp.float32)


def shared_operator():
    kinetic = -0.5 * inverse_spacing * inverse_spacing
    unit = kinetic * stencil_weights[1] / SCALE / filter_width
    shift = 3.0 * kinetic * stencil_weights[0] - filter_center
    return unit, shift


def pack_kernel(
    orbital_ref, rotation_ref, out_ref, after_ref, start_ref, rotation_copy_ref, chunk_ref, sem_ref
):
    count, block_x, y_size, z_size = orbital_ref.shape[1:]
    used = count * block_x
    loads = [
        pltpu.make_async_copy(orbital_ref.at[0], start_ref, sem_ref.at[0]),
        pltpu.make_async_copy(rotation_ref, rotation_copy_ref, sem_ref.at[1]),
    ]
    for load in loads:
        load.start()
    for load in loads:
        load.wait()
    packed = packed_rotation(rotation_copy_ref, z_size)
    after_ref[...] = jnp.zeros(after_ref.shape, jnp.float32)
    rows_ref = start_ref.reshape(used * y_size, z_size)
    for part in range(y_size):
        chunk_ref[0:used] = rows_ref[pl.ds(part, used, stride=y_size), :]
        chunk_ref[used : used + count - 1] = packed[0 : count - 1]
        out_ref[part] = chunk_ref[...].astype(jnp.bfloat16)


def spread(products, lanes, mask_ref, energy_ref, coeff_ref):
    spots, z_size = mask_ref.shape
    pairs = energy_ref.shape[0]
    mask = mask_ref[...]
    for start in range(0, products.shape[1], z_size):
        picked = products[:, start : start + z_size] * mask
        coeffs = jnp.sum(picked.reshape(SIDE, pairs, z_size), axis=0)
        coeffs = jnp.sum(coeffs, axis=1, keepdims=True)
        high, low = halves(jnp.concatenate([coeffs * energy_ref[...]] * SIDE, axis=0) * mask)
        columns = slice(lanes.start + start, lanes.start + start + z_size)
        coeff_ref[0:spots, columns] = high
        coeff_ref[spots : 2 * spots, columns] = low
        if coeff_ref.shape[0] > 2 * spots:
            coeff_ref[2 * spots :, columns] = high


def table_kernel(
    first_at_ref,
    second_at_ref,
    third_at_ref,
    energy_at_ref,
    after_ref,
    projector_ref,
    order_ref,
    plane_ref,
    field_ref,
    q_ref,
    left_ref,
    mask_ref,
    energy_ref,
    diagonal_ref,
):
    block_x, y_size, z_size = field_ref.shape[1:]
    x_size = 2 * block_x
    own = block_x * y_size
    cell_count = x_size * y_size
    atoms, nproj = projector_ref.shape[:2]
    pairs = atoms * nproj
    per_plane = SIDE * SIDE
    spots = atoms * per_plane
    unit, shift = shared_operator()
    own_start = lax.axis_index("dom") * block_x
    high, low = halves(projector_ref[...].reshape(pairs, SUP))
    ordered = matmul(jnp.concatenate((high, low), axis=0), order_ref[...])

    lane = lax.broadcasted_iota(jnp.int32, (pairs, 2 * per_plane), 1)
    row_atom = lax.broadcasted_iota(jnp.int32, (pairs, spots), 0) // nproj
    lane_atom = lax.broadcasted_iota(jnp.int32, (pairs, spots), 1) // per_plane
    same_atom = row_atom == lane_atom
    expanded = []
    for part in range(2):
        rows = []
        for third in range(SIDE):
            start = third // 2 * 2 * per_plane
            both = ordered[part * pairs : (part + 1) * pairs, start : start + 2 * per_plane]
            swapped = pltpu.roll(both, per_plane, 1)
            if third % 2:
                both, swapped = swapped, both
            doubled = jnp.where(lane < per_plane, both, swapped)
            doubled = jnp.concatenate([doubled] * (atoms // 2), axis=1)
            rows.append(jnp.where(same_atom, doubled, 0.0))
        expanded.append(jnp.concatenate(rows, axis=0).astype(jnp.bfloat16))
    high, low = expanded

    place = []
    spot = lax.broadcasted_iota(jnp.int32, (per_plane, cell_count), 0)
    place_lane = lax.broadcasted_iota(jnp.int32, (per_plane, cell_count), 1)
    for atom in range(atoms):
        x_start = lax.rem(first_at_ref[atom] - SIDE // 2 - own_start + 2 * x_size, x_size)
        y_start = lax.rem(second_at_ref[atom] - SIDE // 2 + y_size, y_size)
        x_index = x_start + spot // SIDE
        x_index = jnp.where(x_index >= x_size, x_index - x_size, x_index)
        y_index = y_start + spot % SIDE
        y_index = jnp.where(y_index >= y_size, y_index - y_size, y_index)
        target = x_index * y_size + y_index
        place.append(jnp.where(place_lane == target, 1.0, 0.0).astype(jnp.bfloat16))
    place = jnp.concatenate(place, axis=0)
    q_high = matmul(high, place)
    q_ref[...] = q_high.astype(jnp.bfloat16)
    q_high = q_high.T.astype(jnp.bfloat16)
    left_ref[:, 0:cell_count] = plane_ref[...]
    left_ref[:, cell_count : cell_count + spots] = q_high
    left_ref[:, cell_count + spots : cell_count + 2 * spots] = q_high
    left_ref[:, cell_count + 2 * spots :] = matmul(low, place).T.astype(jnp.bfloat16)

    z_lane = lax.broadcasted_iota(jnp.int32, (nproj, z_size), 1)
    for third in range(SIDE):
        for atom in range(atoms):
            z_index = lax.rem(third_at_ref[atom] + third - SIDE // 2 + z_size, z_size)
            start = third * pairs + atom * nproj
            mask_ref[start : start + nproj] = jnp.where(z_lane == z_index, 1.0, 0.0)
    sublane = lax.broadcasted_iota(jnp.int32, (nproj, z_size), 0)
    energy = jnp.zeros((nproj, z_size), jnp.float32)
    for index in range(nproj):
        energy = jnp.where(sublane == index, energy_at_ref[index], energy)
    energy = energy * (1.0 / (unit * filter_width))
    for atom in range(atoms):
        energy_ref[atom * nproj : (atom + 1) * nproj] = energy

    diagonal_ref[...] = (field_ref[0].reshape(own, z_size) + shift) / filter_width


def packed_rotation(rotation_ref, z_size):
    count, wide = rotation_ref.shape
    spare = z_size - wide
    block = jnp.concatenate(
        (rotation_ref[...].astype(jnp.float32), jnp.zeros((count, spare), jnp.float32)), axis=1
    )
    block = jnp.concatenate((block, jnp.zeros((8 - count, z_size), jnp.float32)), axis=0)
    sublane = lax.broadcasted_iota(jnp.int32, (8, z_size), 0)
    lane = lax.broadcasted_iota(jnp.int32, (8, z_size), 1)
    packed = block
    for piece in range(-(-wide // spare)):
        moved = pltpu.roll(block, (piece - (count - 1)) % 8, 0)
        moved = pltpu.roll(moved, (wide - piece * spare) % z_size, 1)
        packed = jnp.where((sublane == piece) & (lane >= wide), moved, packed)
    return packed


def filter_kernel(
    received_ref,
    q_ref,
    left_ref,
    mask_ref,
    energy_ref,
    diagonal_ref,
    partner_diagonal_ref,
    third_ref,
    out_ref,
    rows_ref,
    right_ref,
    first_ref,
    result_ref,
    sem_ref,
):
    count, block_x, y_size, z_size = out_ref.shape[1:]
    own = block_x * y_size
    cells = 2 * own
    used = count * block_x
    spots = mask_ref.shape[0]
    depth = cells + 2 * spots
    unit, _ = shared_operator()
    me = lax.axis_index("dom")
    for half in range(2):
        for part in range(y_size):
            values = received_ref[(me ^ half) * y_size + part].astype(jnp.float32)
            rows_ref[half, pl.ds(part, used, stride=y_size), :] = values[0:used]

    groups = [range(first, min(first + 2, count)) for first in range(0, count, 2)]
    lanes_of = [slice(group[0] * z_size, (group[-1] + 1) * z_size) for group in groups]
    made = [{} for _ in groups]
    stores = []

    def column(position):
        return slice(position * z_size, (position + 1) * z_size)

    def load(index):
        for orbital in groups[index]:
            rows = slice(orbital * own, (orbital + 1) * own)
            right_ref[0:own, column(orbital)] = rows_ref[0, rows].astype(jnp.bfloat16)
            right_ref[own:cells, column(orbital)] = rows_ref[1, rows].astype(jnp.bfloat16)

    def project(index):
        made[index]["products"] = matmul(q_ref[...], right_ref[0:cells, lanes_of[index]])

    def spread_first(index):
        coeff_ref = right_ref.at[cells:depth]
        spread(made[index]["products"], lanes_of[index], mask_ref, energy_ref, coeff_ref)

    def spread_second(index):
        coeff_ref = right_ref.at[cells:]
        spread(made[index]["products"], lanes_of[index], mask_ref, energy_ref, coeff_ref)

    def along(index, rows):
        wide = len(groups[index]) * z_size
        values = right_ref[0:rows, lanes_of[index]]
        made[index]["along"] = matmul(values, third_ref[0:wide, 0:wide])

    def along_first(index):
        along(index, cells)

    def along_second(index):
        along(index, own)

    def plane_first(index):
        summed = matmul(left_ref[:, 0:depth], right_ref[0:depth, lanes_of[index]])
        made[index]["summed"] = summed + made[index]["along"]

    def plane_second(index):
        summed = matmul(left_ref[0:own], right_ref[:, lanes_of[index]])
        made[index]["summed"] = summed + made[index]["along"]

    def finish_first(index):
        for position, orbital in enumerate(groups[index]):
            rows = slice(orbital * own, (orbital + 1) * own)
            values = unit * made[index]["summed"][:, column(position)]
            mine = diagonal_ref[...] * rows_ref[0, rows] + values[0:own]
            other = partner_diagonal_ref[...] * rows_ref[1, rows] + values[own:]
            first_ref[:, column(orbital)] = mine
            right_ref[0:own, column(orbital)] = mine.astype(jnp.bfloat16)
            right_ref[own:cells, column(orbital)] = other.astype(jnp.bfloat16)

    def finish_second(index):
        for position, orbital in enumerate(groups[index]):
            rows = slice(orbital * own, (orbital + 1) * own)
            values = unit * made[index]["summed"][:, column(position)]
            values = diagonal_ref[...] * first_ref[:, column(orbital)] + values
            values = (2.0 * values - rows_ref[0, rows]).astype(jnp.bfloat16)
            result_ref[orbital] = values.reshape(block_x, y_size, z_size)
            stores.append(
                pltpu.make_async_copy(
                    result_ref.at[orbital], out_ref.at[0, orbital], sem_ref.at[orbital]
                )
            )
            stores[-1].start()

    steps = (
        load,
        project,
        along_first,
        spread_first,
        plane_first,
        finish_first,
        project,
        along_second,
        spread_second,
        plane_second,
        finish_second,
    )
    for time in range(len(steps) + 2 * len(groups) - 2):
        for index in range(len(groups)):
            if 0 <= time - 2 * index < len(steps):
                steps[time - 2 * index](index)
    for store in stores:
        store.wait()


def rotate_kernel(received_ref, after_ref, out_ref, wide_ref, rows_ref, *, count, block_x):
    sources, chunk, z_size = received_ref.shape
    total = sources * count
    used = count * block_x
    spare = z_size - total
    wide_ref[...] = received_ref[...].astype(jnp.float32).reshape(sources * chunk, z_size)
    packed = [wide_ref[pl.ds(used + row, sources, stride=chunk), :] for row in range(count - 1)]
    lane = lax.broadcasted_iota(jnp.int32, (sources, z_size), 1)
    last = jnp.zeros((sources, z_size), jnp.float32)
    for piece in range(-(-total // spare)):
        moved = pltpu.roll(packed[piece], (piece * spare - total) % z_size, 1)
        last = jnp.where(lane >= piece * spare, moved, last)
    rotation = jnp.concatenate(packed + [last], axis=0)[:, 0:total].astype(jnp.bfloat16)
    columns = []
    for plane in range(block_x):
        rows = [
            wide_ref[pl.ds(orbital * block_x + plane, sources, stride=chunk), :]
            for orbital in range(count)
        ]
        columns.append(jnp.concatenate(rows, axis=0).astype(jnp.bfloat16))
    values = jnp.concatenate(columns, axis=1)
    rotated = lax.dot_general(
        rotation, values, (((0,), (0,)), ((), ())), preferred_element_type=jnp.float32
    )
    rows_ref[total * block_x :] = jnp.zeros((chunk - used, z_size), jnp.float32)
    for plane in range(block_x):
        lanes = slice(plane * z_size, (plane + 1) * z_size)
        rows_ref[pl.ds(plane, total, stride=block_x), :] = rotated[:, lanes]
    for part in range(sources):
        values = rows_ref[part * used : part * used + chunk].astype(jnp.bfloat16)
        out_ref[part] = values
        out_ref[sources + part] = values


def in_vmem(count):
    return [pl.BlockSpec(memory_space=pltpu.VMEM)] * count


def in_smem(count):
    return [pl.BlockSpec(memory_space=pltpu.SMEM)] * count


def params(mib):
    return pltpu.CompilerParams(vmem_limit_bytes=mib * MIB)


def shape_of(shape, kind):
    return jax.ShapeDtypeStruct(shape, kind)


def pair_body(
    orbitals, potential, projectors, projector_energy, atom_first, atom_second, atom_third, rotation
):
    bf16, f32 = jnp.bfloat16, jnp.float32
    count, block_x, y_size, z_size = orbitals.shape[1:]
    x_size = 2 * block_x
    own = block_x * y_size
    cell_count = x_size * y_size
    atoms, nproj = projectors.shape[:2]
    spots = SIDE * atoms * nproj
    sources = lax.axis_size("orb")
    used = count * block_x
    chunk = -(-(used + count - 1) // 16) * 16

    packed, after = pl.pallas_call(
        pack_kernel,
        out_shape=(shape_of((sources, chunk, z_size), bf16), shape_of((8, z_size), f32)),
        in_specs=[pl.BlockSpec(memory_space=pltpu.HBM)] * 2,
        out_specs=tuple(in_vmem(2)),
        scratch_shapes=[
            pltpu.VMEM(orbitals.shape[1:], f32),
            pltpu.VMEM(rotation.shape, bf16),
            pltpu.VMEM((chunk, z_size), f32),
            pltpu.SemaphoreType.DMA((2,)),
        ],
        compiler_params=params(60),
        name="pack",
    )(orbitals, rotation)
    by_plane = lax.all_to_all(packed, "orb", split_axis=0, concat_axis=0, tiled=True)

    q, left, mask, energy, diagonal = pl.pallas_call(
        table_kernel,
        out_shape=(
            shape_of((spots, cell_count), bf16),
            shape_of((cell_count, cell_count + 3 * spots), bf16),
            shape_of((spots, z_size), f32),
            shape_of((atoms * nproj, z_size), f32),
            shape_of((own, z_size), f32),
        ),
        in_specs=in_smem(4) + [pl.BlockSpec(memory_space=pl.ANY)] + in_vmem(4),
        out_specs=tuple(in_vmem(5)),
        compiler_params=params(24),
        cost_estimate=pl.CostEstimate(flops=1 << 31, bytes_accessed=6 << 20, transcendentals=0),
        name="tables",
    )(
        atom_first,
        atom_second,
        atom_third,
        projector_energy,
        after,
        projectors,
        third_first(),
        plane_stencil(x_size, y_size),
        potential,
    )
    partner_diagonal = lax.ppermute(diagonal, "dom", [(0, 1), (1, 0)])

    rotated = pl.pallas_call(
        functools.partial(rotate_kernel, count=count, block_x=block_x),
        out_shape=shape_of((2 * sources, chunk, z_size), bf16),
        in_specs=in_vmem(2),
        out_specs=in_vmem(1)[0],
        scratch_shapes=[
            pltpu.VMEM((sources * chunk, z_size), f32),
            pltpu.VMEM((sources * used + chunk - used, z_size), f32),
        ],
        compiler_params=params(24),
        name="rotate",
    )(by_plane, partner_diagonal)
    by_orbital = lax.all_to_all(rotated, ("dom", "orb"), split_axis=0, concat_axis=0, tiled=True)

    return pl.pallas_call(
        filter_kernel,
        out_shape=shape_of(orbitals.shape, bf16),
        in_specs=in_vmem(8),
        out_specs=pl.BlockSpec(memory_space=pltpu.HBM),
        scratch_shapes=[
            pltpu.VMEM((2, count * own, z_size), f32),
            pltpu.VMEM((cell_count + 3 * spots, count * z_size), bf16),
            pltpu.VMEM((own, count * z_size), f32),
            pltpu.VMEM(orbitals.shape[1:], bf16),
            pltpu.SemaphoreType.DMA((count,)),
        ],
        compiler_params=params(40),
        name="filter",
    )(
        by_orbital,
        q,
        left,
        mask,
        energy,
        diagonal,
        partner_diagonal,
        third_stencil(z_size),
    )


def fits_pair(mesh, orbitals, projectors, rotation):
    count = orbitals.shape[1] // mesh.shape["orb"]
    return (
        mesh.shape["dom"] == 2
        and orbitals.shape[3] == mesh.shape["orb"]
        and orbitals.shape[2] == 2 * stencil_reach
        and projectors.shape[0] % 2 == 0
        and projectors.shape[1] == 8
        and count <= 8
        and rotation.shape[1] < orbitals.shape[4]
        and -(-rotation.shape[1] // (orbitals.shape[4] - rotation.shape[1])) < count
    )


def solution(mesh):
    def whole(*arrays):
        chosen = pair_body if fits_pair(mesh, arrays[0], arrays[2], arrays[7]) else body
        return jax.shard_map(
            chosen,
            mesh=mesh,
            in_specs=(
                P("dom", "orb", None, None, None),
                P("dom", None, None, None),
                P(),
                P(),
                P(),
                P(),
                P(),
                P("orb", None),
            ),
            out_specs=P("dom", "orb", None, None, None),
            check_vma=False,
        )(*arrays)

    return whole
```

```python
import functools

import jax
import jax.numpy as jnp
import numpy as np
from jax import lax
from jax.experimental import pallas as pl
from jax.experimental.pallas import tpu as pltpu
from jax.sharding import PartitionSpec as P

SIDE = 8
SUP = 512


stencil_weights = (
    -5369.0 / 1800.0,
    12.0 / 7.0,
    -15.0 / 56.0,
    10.0 / 189.0,
    -1.0 / 112.0,
    2.0 / 1925.0,
    -1.0 / 16632.0,
)
inverse_spacing = 4.0
filter_center = 120.0
filter_width = 110.0
stencil_reach = 6


def partner_2(block, axis, bit):
    count = lax.axis_size(axis)
    route = []
    for low in range(count):
        high = low | 1 << bit
        if high != low and high < count:
            route += [(low, high), (high, low)]
    return lax.ppermute(block, axis, route)


def outgoing(values, direction, width):
    extent = values.shape[direction]
    if 2 * width < extent:
        return jnp.concatenate(
            (
                lax.slice_in_dim(values, 0, width, axis=direction),
                lax.slice_in_dim(values, extent - width, extent, axis=direction),
            ),
            axis=direction,
        )
    return values


def assemble(values, partner, direction, width):
    extent = values.shape[direction]
    if 2 * width < extent:
        lower_rim = lax.slice_in_dim(partner, width, 2 * width, axis=direction)
        upper_rim = lax.slice_in_dim(partner, 0, width, axis=direction)
        return jnp.concatenate((lower_rim, values, upper_rim), axis=direction)
    cyclic = jnp.concatenate((values, partner), axis=direction)
    chosen = np.arange(-width, extent + width) % (2 * extent)
    return jnp.take(cyclic, jnp.asarray(chosen, dtype=jnp.int32), axis=direction)


def face_padded(values, direction, bit_number):
    sent = outgoing(values, direction, stencil_reach)
    partner = partner_2(sent.astype(jnp.bfloat16), "dom", bit_number).astype(sent.dtype)
    return assemble(values, partner, direction, stencil_reach)


def stencil_sum(center, along):
    lead = center.ndim - 3
    summed = 3.0 * stencil_weights[0] * center
    for index in range(3):
        direction = lead + index
        extent = center.shape[direction]
        padded = along[index]
        for offset in range(1, 7):
            if padded is None:
                upward = jnp.roll(center, -offset, direction)
                downward = jnp.roll(center, offset, direction)
            else:
                upward = lax.slice_in_dim(
                    padded, stencil_reach + offset, stencil_reach + offset + extent, axis=direction
                )
                downward = lax.slice_in_dim(
                    padded, stencil_reach - offset, stencil_reach - offset + extent, axis=direction
                )
            summed = summed + stencil_weights[offset] * (upward + downward)
    return summed


def support_map(atom_coords, starts, extents, periods):
    offsets = jnp.arange(SIDE, dtype=jnp.int32) - SIDE // 2
    clipped_list = []
    inside_list = []
    for index in range(3):
        local = (atom_coords[index][:, None] + offsets[None, :] - starts[index]) % periods[index]
        inside_list.append(local < extents[index])
        clipped_list.append(jnp.minimum(local, extents[index] - 1))
    inside = (
        inside_list[0][:, :, None, None]
        & inside_list[1][:, None, :, None]
        & inside_list[2][:, None, None, :]
    )
    flattened = (
        clipped_list[0][:, :, None, None] * extents[1] + clipped_list[1][:, None, :, None]
    ) * extents[2] + clipped_list[2][:, None, None, :]
    atom_count = atom_coords[0].shape[0]
    return (
        flattened.reshape(atom_count * SUP),
        inside.reshape(atom_count, SUP).astype(jnp.float32),
    )


def coefficients(values, support, inside, projectors):
    orbital_count = values.shape[0]
    atom_count = projectors.shape[0]
    flattened = values.reshape(orbital_count, -1)
    picked = (
        jnp.take(flattened, support, axis=1).reshape(orbital_count, atom_count, SUP) * inside[None]
    )
    partial_coeffs = jnp.einsum("aps,kas->kap", projectors, picked, precision=lax.Precision.HIGHEST)
    return lax.psum(partial_coeffs, "dom")


def spread_into(coeffs, shape, support, inside, projectors, projector_energy):
    orbital_count = shape[0]
    atom_count = projectors.shape[0]
    scaled = coeffs * projector_energy[None, None, :]
    spread = (
        jnp.einsum("aps,kap->kas", projectors, scaled, precision=lax.Precision.HIGHEST)
        * inside[None]
    )
    total_cells = shape[1] * shape[2] * shape[3]
    projected_part = (
        jnp.zeros((orbital_count, total_cells), jnp.float32)
        .at[:, support]
        .add(spread.reshape(orbital_count, atom_count * SUP))
    )
    return projected_part.reshape(shape)


def own_hamiltonian(center, along, local_field, support, inside, projectors, projector_energy):
    kinetic = -0.5 * inverse_spacing * inverse_spacing
    coeffs = coefficients(center, support, inside, projectors)
    projected_part = spread_into(
        coeffs, center.shape, support, inside, projectors, projector_energy
    )
    return kinetic * stencil_sum(center, along) + local_field[None] * center + projected_part


def body(
    orbitals, potential, projectors, projector_energy, atom_first, atom_second, atom_third, rotation
):
    domain_count = lax.axis_size("dom")
    domain_bits = domain_count.bit_length() - 1
    split = [index < domain_bits for index in range(3)]
    start_values = orbitals[0]
    local_field = potential[0]
    extents = start_values.shape[1:]
    periods = (
        extents[0] * min(domain_count, 2),
        extents[1] * min(max(domain_count // 2, 1), 2),
        extents[2] * max(domain_count // 4, 1),
    )
    domain_index = lax.axis_index("dom")
    anchors = (
        domain_index % 2 * extents[0],
        domain_index // 2 % 2 * extents[1],
        domain_index // 4 * extents[2],
    )
    atom_coords = (atom_first, atom_second, atom_third)
    support, inside = support_map(atom_coords, anchors, extents, periods)
    along = [
        face_padded(start_values, index + 1, index) if split[index] else None for index in range(3)
    ]
    first_apply = own_hamiltonian(
        start_values, along, local_field, support, inside, projectors, projector_energy
    )
    first_term = (first_apply - filter_center * start_values) / filter_width
    along = [
        face_padded(first_term, index + 1, index) if split[index] else None for index in range(3)
    ]
    second_apply = own_hamiltonian(
        first_term, along, local_field, support, inside, projectors, projector_energy
    )
    second_term = 2.0 * (second_apply - filter_center * first_term) / filter_width - start_values
    per_device = start_values.shape[0]
    filtered = second_term.astype(jnp.bfloat16).reshape(per_device, -1)
    by_cells = lax.all_to_all(filtered, "orb", split_axis=1, concat_axis=0, tiled=True)
    whole_rotation = lax.all_gather(rotation, "orb", axis=0, tiled=True)
    rotated = lax.dot_general(
        whole_rotation, by_cells, (((0,), (0,)), ((), ())), preferred_element_type=jnp.float32
    ).astype(jnp.bfloat16)
    result = lax.all_to_all(rotated, "orb", split_axis=0, concat_axis=1, tiled=True)
    return result.reshape((1,) + start_values.shape)


SCALE = 15.0
MIB = 1 << 20


def scaled_weights():
    ratios = np.array(stencil_weights[1:], np.float64) / stencil_weights[1]
    return SCALE * ratios


def cyclic_stencil(size):
    matrix = np.zeros((size, size), np.float64)
    rows = np.arange(size)
    for offset, weight in enumerate(scaled_weights(), 1):
        np.add.at(matrix, (rows, (rows + offset) % size), weight)
        np.add.at(matrix, (rows, (rows - offset) % size), weight)
    return matrix


def plane_stencil(x_size, y_size):
    matrix = np.kron(cyclic_stencil(x_size), np.eye(y_size))
    matrix += np.kron(np.eye(x_size), cyclic_stencil(y_size))
    return matrix.astype(jnp.bfloat16)


def third_stencil(z_size):
    matrix = cyclic_stencil(z_size)
    return np.kron(np.eye(2), matrix).astype(jnp.bfloat16)


def third_first():
    picked = np.zeros((SUP, SUP), np.float32)
    source = np.arange(SUP)
    picked[source, source % SIDE * SIDE * SIDE + source // SIDE] = 1.0
    return picked.astype(jnp.bfloat16)


def halves(values):
    high = values.astype(jnp.bfloat16)
    return high, (values - high.astype(jnp.float32)).astype(jnp.bfloat16)


def matmul(left, right):
    return jnp.dot(left, right, preferred_element_type=jnp.float32)


def shared_operator():
    kinetic = -0.5 * inverse_spacing * inverse_spacing
    unit = kinetic * stencil_weights[1] / SCALE / filter_width
    shift = 3.0 * kinetic * stencil_weights[0] - filter_center
    return unit, shift


def pack_kernel(
    orbital_ref, rotation_ref, out_ref, after_ref, start_ref, rotation_copy_ref, chunk_ref, sem_ref
):
    count, block_x, y_size, z_size = orbital_ref.shape[1:]
    used = count * block_x
    loads = [
        pltpu.make_async_copy(orbital_ref.at[0], start_ref, sem_ref.at[0]),
        pltpu.make_async_copy(rotation_ref, rotation_copy_ref, sem_ref.at[1]),
    ]
    for load in loads:
        load.start()
    loads[1].wait()
    packed = packed_rotation(rotation_copy_ref, z_size)
    after_ref[...] = packed
    loads[0].wait()
    rows_ref = start_ref.reshape(used * y_size, z_size)
    for part in range(y_size):
        chunk_ref[0:used] = rows_ref[pl.ds(part, used, stride=y_size), :]
        chunk_ref[used : used + count - 1] = packed[0 : count - 1]
        out_ref[part] = chunk_ref[...].astype(jnp.bfloat16)


def spread(products, lanes, mask_ref, energy_ref, coeff_ref):
    spots, z_size = mask_ref.shape
    pairs = energy_ref.shape[0]
    mask = mask_ref[...]
    for start in range(0, products.shape[1], z_size):
        picked = products[:, start : start + z_size] * mask
        coeffs = jnp.sum(picked.reshape(SIDE, pairs, z_size), axis=0)
        coeffs = jnp.sum(coeffs, axis=1, keepdims=True)
        high, low = halves(jnp.concatenate([coeffs * energy_ref[...]] * SIDE, axis=0) * mask)
        columns = slice(lanes.start + start, lanes.start + start + z_size)
        coeff_ref[0:spots, columns] = high
        coeff_ref[spots : 2 * spots, columns] = low
        if coeff_ref.shape[0] > 2 * spots:
            coeff_ref[2 * spots :, columns] = high


def table_kernel(
    first_at_ref,
    second_at_ref,
    third_at_ref,
    energy_at_ref,
    after_ref,
    projector_ref,
    order_ref,
    plane_ref,
    field_ref,
    q_ref,
    left_ref,
    mask_ref,
    energy_ref,
    diagonal_ref,
):
    block_x, y_size, z_size = field_ref.shape[1:]
    x_size = 2 * block_x
    own = block_x * y_size
    cell_count = x_size * y_size
    atoms, nproj = projector_ref.shape[:2]
    pairs = atoms * nproj
    per_plane = SIDE * SIDE
    spots = atoms * per_plane
    unit, shift = shared_operator()
    own_start = lax.axis_index("dom") * block_x
    high, low = halves(projector_ref[...].reshape(pairs, SUP))
    ordered = matmul(jnp.concatenate((high, low), axis=0), order_ref[...])

    lane = lax.broadcasted_iota(jnp.int32, (pairs, 2 * per_plane), 1)
    row_atom = lax.broadcasted_iota(jnp.int32, (pairs, spots), 0) // nproj
    lane_atom = lax.broadcasted_iota(jnp.int32, (pairs, spots), 1) // per_plane
    same_atom = row_atom == lane_atom
    expanded = []
    for part in range(2):
        rows = []
        for third in range(SIDE):
            start = third // 2 * 2 * per_plane
            both = ordered[part * pairs : (part + 1) * pairs, start : start + 2 * per_plane]
            swapped = pltpu.roll(both, per_plane, 1)
            if third % 2:
                both, swapped = swapped, both
            doubled = jnp.where(lane < per_plane, both, swapped)
            doubled = jnp.concatenate([doubled] * (atoms // 2), axis=1)
            rows.append(jnp.where(same_atom, doubled, 0.0))
        expanded.append(jnp.concatenate(rows, axis=0).astype(jnp.bfloat16))
    high, low = expanded

    place = []
    spot = lax.broadcasted_iota(jnp.int32, (per_plane, cell_count), 0)
    place_lane = lax.broadcasted_iota(jnp.int32, (per_plane, cell_count), 1)
    for atom in range(atoms):
        x_start = lax.rem(first_at_ref[atom] - SIDE // 2 - own_start + 2 * x_size, x_size)
        y_start = lax.rem(second_at_ref[atom] - SIDE // 2 + y_size, y_size)
        x_index = x_start + spot // SIDE
        x_index = jnp.where(x_index >= x_size, x_index - x_size, x_index)
        y_index = y_start + spot % SIDE
        y_index = jnp.where(y_index >= y_size, y_index - y_size, y_index)
        target = x_index * y_size + y_index
        place.append(jnp.where(place_lane == target, 1.0, 0.0).astype(jnp.bfloat16))
    place = jnp.concatenate(place, axis=0)
    q_high = matmul(high, place)
    q_ref[...] = q_high.astype(jnp.bfloat16)
    q_high = q_high.T.astype(jnp.bfloat16)
    left_ref[:, 0:cell_count] = plane_ref[...]
    left_ref[:, cell_count : cell_count + spots] = q_high
    left_ref[:, cell_count + spots : cell_count + 2 * spots] = q_high
    left_ref[:, cell_count + 2 * spots :] = matmul(low, place).T.astype(jnp.bfloat16)

    z_lane = lax.broadcasted_iota(jnp.int32, (nproj, z_size), 1)
    for third in range(SIDE):
        for atom in range(atoms):
            z_index = lax.rem(third_at_ref[atom] + third - SIDE // 2 + z_size, z_size)
            start = third * pairs + atom * nproj
            mask_ref[start : start + nproj] = jnp.where(z_lane == z_index, 1.0, 0.0)
    sublane = lax.broadcasted_iota(jnp.int32, (nproj, z_size), 0)
    energy = jnp.zeros((nproj, z_size), jnp.float32)
    for index in range(nproj):
        energy = jnp.where(sublane == index, energy_at_ref[index], energy)
    energy = energy * (1.0 / (unit * filter_width))
    for atom in range(atoms):
        energy_ref[atom * nproj : (atom + 1) * nproj] = energy

    diagonal_ref[...] = (field_ref[0].reshape(own, z_size) + shift) / filter_width


def packed_rotation(rotation_ref, z_size):
    count, wide = rotation_ref.shape
    spare = z_size - wide
    block = jnp.concatenate(
        (rotation_ref[...].astype(jnp.float32), jnp.zeros((count, spare), jnp.float32)), axis=1
    )
    block = jnp.concatenate((block, jnp.zeros((8 - count, z_size), jnp.float32)), axis=0)
    sublane = lax.broadcasted_iota(jnp.int32, (8, z_size), 0)
    lane = lax.broadcasted_iota(jnp.int32, (8, z_size), 1)
    packed = block
    for piece in range(-(-wide // spare)):
        moved = pltpu.roll(block, (piece - (count - 1)) % 8, 0)
        moved = pltpu.roll(moved, (wide - piece * spare) % z_size, 1)
        packed = jnp.where((sublane == piece) & (lane >= wide), moved, packed)
    return packed


def filter_kernel(
    received_ref,
    q_ref,
    left_ref,
    mask_ref,
    energy_ref,
    diagonal_ref,
    partner_diagonal_ref,
    third_ref,
    out_ref,
    rows_ref,
    right_ref,
    first_ref,
):
    count, block_x, y_size, z_size = out_ref.shape[1:]
    own = block_x * y_size
    cells = 2 * own
    used = count * block_x
    spots = mask_ref.shape[0]
    depth = cells + 2 * spots
    unit, _ = shared_operator()
    me = lax.axis_index("dom")
    for half in range(2):
        for part in range(y_size):
            values = received_ref[(me ^ half) * y_size + part].astype(jnp.float32)
            rows_ref[half, pl.ds(part, used, stride=y_size), :] = values[0:used]

    groups = [range(first, min(first + 2, count)) for first in range(0, count, 2)]
    lanes_of = [slice(group[0] * z_size, (group[-1] + 1) * z_size) for group in groups]
    made = [{} for _ in groups]

    def column(position):
        return slice(position * z_size, (position + 1) * z_size)

    def load(index):
        for orbital in groups[index]:
            rows = slice(orbital * own, (orbital + 1) * own)
            right_ref[0:own, column(orbital)] = rows_ref[0, rows].astype(jnp.bfloat16)
            right_ref[own:cells, column(orbital)] = rows_ref[1, rows].astype(jnp.bfloat16)

    def project(index):
        made[index]["products"] = matmul(q_ref[...], right_ref[0:cells, lanes_of[index]])

    def spread_first(index):
        coeff_ref = right_ref.at[cells:depth]
        spread(made[index]["products"], lanes_of[index], mask_ref, energy_ref, coeff_ref)

    def spread_second(index):
        coeff_ref = right_ref.at[cells:]
        spread(made[index]["products"], lanes_of[index], mask_ref, energy_ref, coeff_ref)

    def along(index, rows):
        wide = len(groups[index]) * z_size
        values = right_ref[0:rows, lanes_of[index]]
        made[index]["along"] = matmul(values, third_ref[0:wide, 0:wide])

    def along_first(index):
        along(index, cells)

    def along_second(index):
        along(index, own)

    def plane_first(index):
        summed = matmul(left_ref[:, 0:depth], right_ref[0:depth, lanes_of[index]])
        made[index]["summed"] = summed + made[index]["along"]

    def plane_second(index):
        summed = matmul(left_ref[0:own], right_ref[:, lanes_of[index]])
        made[index]["summed"] = summed + made[index]["along"]

    def finish_first(index):
        for position, orbital in enumerate(groups[index]):
            rows = slice(orbital * own, (orbital + 1) * own)
            values = unit * made[index]["summed"][:, column(position)]
            mine = diagonal_ref[...] * rows_ref[0, rows] + values[0:own]
            other = partner_diagonal_ref[...] * rows_ref[1, rows] + values[own:]
            first_ref[:, column(orbital)] = mine
            right_ref[0:own, column(orbital)] = mine.astype(jnp.bfloat16)
            right_ref[own:cells, column(orbital)] = other.astype(jnp.bfloat16)

    def finish_second(index):
        for position, orbital in enumerate(groups[index]):
            rows = slice(orbital * own, (orbital + 1) * own)
            values = unit * made[index]["summed"][:, column(position)]
            values = diagonal_ref[...] * first_ref[:, column(orbital)] + values
            values = (2.0 * values - rows_ref[0, rows]).astype(jnp.bfloat16)
            out_ref[0, orbital] = values.reshape(block_x, y_size, z_size)

    steps = (
        load,
        project,
        along_first,
        spread_first,
        plane_first,
        finish_first,
        project,
        along_second,
        spread_second,
        plane_second,
        finish_second,
    )
    for time in range(len(steps) + 2 * len(groups) - 2):
        for index in range(len(groups)):
            if 0 <= time - 2 * index < len(steps):
                steps[time - 2 * index](index)


def rotate_kernel(received_ref, after_ref, out_ref, wide_ref, rows_ref, *, count, block_x):
    sources, chunk, z_size = received_ref.shape
    total = sources * count
    used = count * block_x
    spare = z_size - total
    wide_ref[...] = received_ref[...].astype(jnp.float32).reshape(sources * chunk, z_size)
    packed = [wide_ref[pl.ds(used + row, sources, stride=chunk), :] for row in range(count - 1)]
    lane = lax.broadcasted_iota(jnp.int32, (sources, z_size), 1)
    last = jnp.zeros((sources, z_size), jnp.float32)
    for piece in range(-(-total // spare)):
        moved = pltpu.roll(packed[piece], (piece * spare - total) % z_size, 1)
        last = jnp.where(lane >= piece * spare, moved, last)
    rotation = jnp.concatenate(packed + [last], axis=0)[:, 0:total].astype(jnp.bfloat16)
    columns = []
    for plane in range(block_x):
        rows = [
            wide_ref[pl.ds(orbital * block_x + plane, sources, stride=chunk), :]
            for orbital in range(count)
        ]
        columns.append(jnp.concatenate(rows, axis=0).astype(jnp.bfloat16))
    values = jnp.concatenate(columns, axis=1)
    rotated = lax.dot_general(
        rotation, values, (((0,), (0,)), ((), ())), preferred_element_type=jnp.float32
    )
    rows_ref[total * block_x :] = jnp.zeros((chunk - used, z_size), jnp.float32)
    for plane in range(block_x):
        lanes = slice(plane * z_size, (plane + 1) * z_size)
        rows_ref[pl.ds(plane, total, stride=block_x), :] = rotated[:, lanes]
    for part in range(sources):
        values = rows_ref[part * used : part * used + chunk].astype(jnp.bfloat16)
        out_ref[part] = values
        out_ref[sources + part] = values


def in_vmem(count):
    return [pl.BlockSpec(memory_space=pltpu.VMEM)] * count


def in_smem(count):
    return [pl.BlockSpec(memory_space=pltpu.SMEM)] * count


def params(mib):
    return pltpu.CompilerParams(vmem_limit_bytes=mib * MIB)


def shape_of(shape, kind):
    return jax.ShapeDtypeStruct(shape, kind)


def pair_body(
    orbitals, potential, projectors, projector_energy, atom_first, atom_second, atom_third, rotation
):
    bf16, f32 = jnp.bfloat16, jnp.float32
    count, block_x, y_size, z_size = orbitals.shape[1:]
    x_size = 2 * block_x
    own = block_x * y_size
    cell_count = x_size * y_size
    atoms, nproj = projectors.shape[:2]
    spots = SIDE * atoms * nproj
    sources = lax.axis_size("orb")
    used = count * block_x
    chunk = -(-(used + count - 1) // 16) * 16

    packed, after = pl.pallas_call(
        pack_kernel,
        out_shape=(shape_of((sources, chunk, z_size), bf16), shape_of((8, z_size), f32)),
        in_specs=[pl.BlockSpec(memory_space=pltpu.HBM)] * 2,
        out_specs=tuple(in_vmem(2)),
        scratch_shapes=[
            pltpu.VMEM(orbitals.shape[1:], f32),
            pltpu.VMEM(rotation.shape, bf16),
            pltpu.VMEM((chunk, z_size), f32),
            pltpu.SemaphoreType.DMA((2,)),
        ],
        compiler_params=params(60),
        name="pack",
    )(orbitals, rotation)
    by_plane = lax.all_to_all(packed, "orb", split_axis=0, concat_axis=0, tiled=True)

    q, left, mask, energy, diagonal = pl.pallas_call(
        table_kernel,
        out_shape=(
            shape_of((spots, cell_count), bf16),
            shape_of((cell_count, cell_count + 3 * spots), bf16),
            shape_of((spots, z_size), f32),
            shape_of((atoms * nproj, z_size), f32),
            shape_of((own, z_size), f32),
        ),
        in_specs=in_smem(4) + [pl.BlockSpec(memory_space=pl.ANY)] + in_vmem(4),
        out_specs=tuple(in_vmem(5)),
        compiler_params=params(24),
        cost_estimate=pl.CostEstimate(flops=1 << 31, bytes_accessed=6 << 20, transcendentals=0),
        name="tables",
    )(
        atom_first,
        atom_second,
        atom_third,
        projector_energy,
        after,
        projectors,
        third_first(),
        plane_stencil(x_size, y_size),
        potential,
    )
    partner_diagonal = lax.ppermute(diagonal, "dom", [(0, 1), (1, 0)])

    rotated = pl.pallas_call(
        functools.partial(rotate_kernel, count=count, block_x=block_x),
        out_shape=shape_of((2 * sources, chunk, z_size), bf16),
        in_specs=in_vmem(2),
        out_specs=in_vmem(1)[0],
        scratch_shapes=[
            pltpu.VMEM((sources * chunk, z_size), f32),
            pltpu.VMEM((sources * used + chunk - used, z_size), f32),
        ],
        compiler_params=params(24),
        name="rotate",
    )(by_plane, partner_diagonal)
    by_orbital = lax.all_to_all(rotated, ("dom", "orb"), split_axis=0, concat_axis=0, tiled=True)

    return pl.pallas_call(
        filter_kernel,
        out_shape=shape_of(orbitals.shape, bf16),
        in_specs=in_vmem(8),
        out_specs=in_vmem(1)[0],
        scratch_shapes=[
            pltpu.VMEM((2, count * own, z_size), f32),
            pltpu.VMEM((cell_count + 3 * spots, count * z_size), bf16),
            pltpu.VMEM((own, count * z_size), f32),
        ],
        compiler_params=params(40),
        name="filter",
    )(
        by_orbital,
        q,
        left,
        mask,
        energy,
        diagonal,
        partner_diagonal,
        third_stencil(z_size),
    )


def fits_pair(mesh, orbitals, projectors, rotation):
    count = orbitals.shape[1] // mesh.shape["orb"]
    return (
        mesh.shape["dom"] == 2
        and orbitals.shape[3] == mesh.shape["orb"]
        and orbitals.shape[2] == 2 * stencil_reach
        and projectors.shape[0] % 2 == 0
        and projectors.shape[1] == 8
        and count <= 8
        and rotation.shape[1] < orbitals.shape[4]
        and -(-rotation.shape[1] // (orbitals.shape[4] - rotation.shape[1])) < count
    )


def solution(mesh):
    def whole(*arrays):
        chosen = pair_body if fits_pair(mesh, arrays[0], arrays[2], arrays[7]) else body
        return jax.shard_map(
            chosen,
            mesh=mesh,
            in_specs=(
                P("dom", "orb", None, None, None),
                P("dom", None, None, None),
                P(),
                P(),
                P(),
                P(),
                P(),
                P("orb", None),
            ),
            out_specs=P("dom", "orb", None, None, None),
            check_vma=False,
        )(*arrays)

    return whole
```

```python
import functools

import jax
import jax.numpy as jnp
import numpy as np
from jax import lax
from jax.experimental import pallas as pl
from jax.experimental.pallas import tpu as pltpu
from jax.sharding import PartitionSpec as P

SIDE = 8
SUP = 512


stencil_weights = (
    -5369.0 / 1800.0,
    12.0 / 7.0,
    -15.0 / 56.0,
    10.0 / 189.0,
    -1.0 / 112.0,
    2.0 / 1925.0,
    -1.0 / 16632.0,
)
inverse_spacing = 4.0
filter_center = 120.0
filter_width = 110.0
stencil_reach = 6


def partner_2(block, axis, bit):
    count = lax.axis_size(axis)
    route = []
    for low in range(count):
        high = low | 1 << bit
        if high != low and high < count:
            route += [(low, high), (high, low)]
    return lax.ppermute(block, axis, route)


def outgoing(values, direction, width):
    extent = values.shape[direction]
    if 2 * width < extent:
        return jnp.concatenate(
            (
                lax.slice_in_dim(values, 0, width, axis=direction),
                lax.slice_in_dim(values, extent - width, extent, axis=direction),
            ),
            axis=direction,
        )
    return values


def assemble(values, partner, direction, width):
    extent = values.shape[direction]
    if 2 * width < extent:
        lower_rim = lax.slice_in_dim(partner, width, 2 * width, axis=direction)
        upper_rim = lax.slice_in_dim(partner, 0, width, axis=direction)
        return jnp.concatenate((lower_rim, values, upper_rim), axis=direction)
    cyclic = jnp.concatenate((values, partner), axis=direction)
    chosen = np.arange(-width, extent + width) % (2 * extent)
    return jnp.take(cyclic, jnp.asarray(chosen, dtype=jnp.int32), axis=direction)


def face_padded(values, direction, bit_number):
    sent = outgoing(values, direction, stencil_reach)
    partner = partner_2(sent.astype(jnp.bfloat16), "dom", bit_number).astype(sent.dtype)
    return assemble(values, partner, direction, stencil_reach)


def stencil_sum(center, along):
    lead = center.ndim - 3
    summed = 3.0 * stencil_weights[0] * center
    for index in range(3):
        direction = lead + index
        extent = center.shape[direction]
        padded = along[index]
        for offset in range(1, 7):
            if padded is None:
                upward = jnp.roll(center, -offset, direction)
                downward = jnp.roll(center, offset, direction)
            else:
                upward = lax.slice_in_dim(
                    padded, stencil_reach + offset, stencil_reach + offset + extent, axis=direction
                )
                downward = lax.slice_in_dim(
                    padded, stencil_reach - offset, stencil_reach - offset + extent, axis=direction
                )
            summed = summed + stencil_weights[offset] * (upward + downward)
    return summed


def support_map(atom_coords, starts, extents, periods):
    offsets = jnp.arange(SIDE, dtype=jnp.int32) - SIDE // 2
    clipped_list = []
    inside_list = []
    for index in range(3):
        local = (atom_coords[index][:, None] + offsets[None, :] - starts[index]) % periods[index]
        inside_list.append(local < extents[index])
        clipped_list.append(jnp.minimum(local, extents[index] - 1))
    inside = (
        inside_list[0][:, :, None, None]
        & inside_list[1][:, None, :, None]
        & inside_list[2][:, None, None, :]
    )
    flattened = (
        clipped_list[0][:, :, None, None] * extents[1] + clipped_list[1][:, None, :, None]
    ) * extents[2] + clipped_list[2][:, None, None, :]
    atom_count = atom_coords[0].shape[0]
    return (
        flattened.reshape(atom_count * SUP),
        inside.reshape(atom_count, SUP).astype(jnp.float32),
    )


def coefficients(values, support, inside, projectors):
    orbital_count = values.shape[0]
    atom_count = projectors.shape[0]
    flattened = values.reshape(orbital_count, -1)
    picked = (
        jnp.take(flattened, support, axis=1).reshape(orbital_count, atom_count, SUP) * inside[None]
    )
    partial_coeffs = jnp.einsum("aps,kas->kap", projectors, picked, precision=lax.Precision.HIGHEST)
    return lax.psum(partial_coeffs, "dom")


def spread_into(coeffs, shape, support, inside, projectors, projector_energy):
    orbital_count = shape[0]
    atom_count = projectors.shape[0]
    scaled = coeffs * projector_energy[None, None, :]
    spread = (
        jnp.einsum("aps,kap->kas", projectors, scaled, precision=lax.Precision.HIGHEST)
        * inside[None]
    )
    total_cells = shape[1] * shape[2] * shape[3]
    projected_part = (
        jnp.zeros((orbital_count, total_cells), jnp.float32)
        .at[:, support]
        .add(spread.reshape(orbital_count, atom_count * SUP))
    )
    return projected_part.reshape(shape)


def own_hamiltonian(center, along, local_field, support, inside, projectors, projector_energy):
    kinetic = -0.5 * inverse_spacing * inverse_spacing
    coeffs = coefficients(center, support, inside, projectors)
    projected_part = spread_into(
        coeffs, center.shape, support, inside, projectors, projector_energy
    )
    return kinetic * stencil_sum(center, along) + local_field[None] * center + projected_part


def body(
    orbitals, potential, projectors, projector_energy, atom_first, atom_second, atom_third, rotation
):
    domain_count = lax.axis_size("dom")
    domain_bits = domain_count.bit_length() - 1
    split = [index < domain_bits for index in range(3)]
    start_values = orbitals[0]
    local_field = potential[0]
    extents = start_values.shape[1:]
    periods = (
        extents[0] * min(domain_count, 2),
        extents[1] * min(max(domain_count // 2, 1), 2),
        extents[2] * max(domain_count // 4, 1),
    )
    domain_index = lax.axis_index("dom")
    anchors = (
        domain_index % 2 * extents[0],
        domain_index // 2 % 2 * extents[1],
        domain_index // 4 * extents[2],
    )
    atom_coords = (atom_first, atom_second, atom_third)
    support, inside = support_map(atom_coords, anchors, extents, periods)
    along = [
        face_padded(start_values, index + 1, index) if split[index] else None for index in range(3)
    ]
    first_apply = own_hamiltonian(
        start_values, along, local_field, support, inside, projectors, projector_energy
    )
    first_term = (first_apply - filter_center * start_values) / filter_width
    along = [
        face_padded(first_term, index + 1, index) if split[index] else None for index in range(3)
    ]
    second_apply = own_hamiltonian(
        first_term, along, local_field, support, inside, projectors, projector_energy
    )
    second_term = 2.0 * (second_apply - filter_center * first_term) / filter_width - start_values
    per_device = start_values.shape[0]
    filtered = second_term.astype(jnp.bfloat16).reshape(per_device, -1)
    by_cells = lax.all_to_all(filtered, "orb", split_axis=1, concat_axis=0, tiled=True)
    whole_rotation = lax.all_gather(rotation, "orb", axis=0, tiled=True)
    rotated = lax.dot_general(
        whole_rotation, by_cells, (((0,), (0,)), ((), ())), preferred_element_type=jnp.float32
    ).astype(jnp.bfloat16)
    result = lax.all_to_all(rotated, "orb", split_axis=0, concat_axis=1, tiled=True)
    return result.reshape((1,) + start_values.shape)


SCALE = 15.0
MIB = 1 << 20


def scaled_weights():
    ratios = np.array(stencil_weights[1:], np.float64) / stencil_weights[1]
    return SCALE * ratios


def cyclic_stencil(size):
    matrix = np.zeros((size, size), np.float64)
    rows = np.arange(size)
    for offset, weight in enumerate(scaled_weights(), 1):
        np.add.at(matrix, (rows, (rows + offset) % size), weight)
        np.add.at(matrix, (rows, (rows - offset) % size), weight)
    return matrix


def plane_stencil(x_size, y_size):
    matrix = np.kron(cyclic_stencil(x_size), np.eye(y_size))
    matrix += np.kron(np.eye(x_size), cyclic_stencil(y_size))
    return matrix.astype(jnp.bfloat16)


def third_stencil(z_size):
    matrix = cyclic_stencil(z_size)
    return np.kron(np.eye(2), matrix).astype(jnp.bfloat16)


def third_first():
    picked = np.zeros((SUP, SUP), np.float32)
    source = np.arange(SUP)
    picked[source, source % SIDE * SIDE * SIDE + source // SIDE] = 1.0
    return picked.astype(jnp.bfloat16)


def halves(values):
    high = values.astype(jnp.bfloat16)
    return high, (values - high.astype(jnp.float32)).astype(jnp.bfloat16)


def matmul(left, right):
    return jnp.dot(left, right, preferred_element_type=jnp.float32)


def shared_operator():
    kinetic = -0.5 * inverse_spacing * inverse_spacing
    unit = kinetic * stencil_weights[1] / SCALE / filter_width
    shift = 3.0 * kinetic * stencil_weights[0] - filter_center
    return unit, shift


def pack_kernel(
    orbital_ref, rotation_ref, out_ref, after_ref, start_ref, rotation_copy_ref, chunk_ref, sem_ref
):
    count, block_x, y_size, z_size = orbital_ref.shape[1:]
    used = count * block_x
    loads = [
        pltpu.make_async_copy(orbital_ref.at[0], start_ref, sem_ref.at[0]),
        pltpu.make_async_copy(rotation_ref, rotation_copy_ref, sem_ref.at[1]),
    ]
    for load in loads:
        load.start()
    for load in loads:
        load.wait()
    packed = packed_rotation(rotation_copy_ref, z_size)
    after_ref[...] = jnp.zeros(after_ref.shape, jnp.float32)
    rows_ref = start_ref.reshape(used * y_size, z_size)
    for part in range(y_size):
        chunk_ref[0:used] = rows_ref[pl.ds(part, used, stride=y_size), :]
        chunk_ref[used : used + count - 1] = packed[0 : count - 1]
        out_ref[part] = chunk_ref[...].astype(jnp.bfloat16)


def spread(products, lanes, mask_ref, energy_ref, coeff_ref):
    spots, z_size = mask_ref.shape
    pairs = energy_ref.shape[0]
    mask = mask_ref[...]
    for start in range(0, products.shape[1], z_size):
        picked = products[:, start : start + z_size] * mask
        coeffs = jnp.sum(picked.reshape(SIDE, pairs, z_size), axis=0)
        coeffs = jnp.sum(coeffs, axis=1, keepdims=True)
        high, low = halves(jnp.concatenate([coeffs * energy_ref[...]] * SIDE, axis=0) * mask)
        columns = slice(lanes.start + start, lanes.start + start + z_size)
        coeff_ref[0:spots, columns] = high
        coeff_ref[spots : 2 * spots, columns] = low
        if coeff_ref.shape[0] > 2 * spots:
            coeff_ref[2 * spots :, columns] = high


def table_kernel(
    first_at_ref,
    second_at_ref,
    third_at_ref,
    energy_at_ref,
    after_ref,
    projector_ref,
    order_ref,
    plane_ref,
    field_ref,
    q_ref,
    left_ref,
    mask_ref,
    energy_ref,
    diagonal_ref,
):
    block_x, y_size, z_size = field_ref.shape[1:]
    x_size = 2 * block_x
    own = block_x * y_size
    cell_count = x_size * y_size
    atoms, nproj = projector_ref.shape[:2]
    pairs = atoms * nproj
    per_plane = SIDE * SIDE
    spots = atoms * per_plane
    unit, shift = shared_operator()
    own_start = lax.axis_index("dom") * block_x
    high, low = halves(projector_ref[...].reshape(pairs, SUP))
    ordered = matmul(jnp.concatenate((high, low), axis=0), order_ref[...])

    lane = lax.broadcasted_iota(jnp.int32, (pairs, 2 * per_plane), 1)
    row_atom = lax.broadcasted_iota(jnp.int32, (pairs, spots), 0) // nproj
    lane_atom = lax.broadcasted_iota(jnp.int32, (pairs, spots), 1) // per_plane
    same_atom = row_atom == lane_atom
    expanded = []
    for part in range(2):
        rows = []
        for third in range(SIDE):
            start = third // 2 * 2 * per_plane
            both = ordered[part * pairs : (part + 1) * pairs, start : start + 2 * per_plane]
            swapped = pltpu.roll(both, per_plane, 1)
            if third % 2:
                both, swapped = swapped, both
            doubled = jnp.where(lane < per_plane, both, swapped)
            doubled = jnp.concatenate([doubled] * (atoms // 2), axis=1)
            rows.append(jnp.where(same_atom, doubled, 0.0))
        expanded.append(jnp.concatenate(rows, axis=0).astype(jnp.bfloat16))
    high, low = expanded

    place = []
    spot = lax.broadcasted_iota(jnp.int32, (per_plane, cell_count), 0)
    place_lane = lax.broadcasted_iota(jnp.int32, (per_plane, cell_count), 1)
    for atom in range(atoms):
        x_start = lax.rem(first_at_ref[atom] - SIDE // 2 - own_start + 2 * x_size, x_size)
        y_start = lax.rem(second_at_ref[atom] - SIDE // 2 + y_size, y_size)
        x_index = x_start + spot // SIDE
        x_index = jnp.where(x_index >= x_size, x_index - x_size, x_index)
        y_index = y_start + spot % SIDE
        y_index = jnp.where(y_index >= y_size, y_index - y_size, y_index)
        target = x_index * y_size + y_index
        place.append(jnp.where(place_lane == target, 1.0, 0.0).astype(jnp.bfloat16))
    place = jnp.concatenate(place, axis=0)
    q_high = matmul(high, place)
    q_ref[...] = q_high.astype(jnp.bfloat16)
    q_high = q_high.T.astype(jnp.bfloat16)
    left_ref[:, 0:cell_count] = plane_ref[...]
    left_ref[:, cell_count : cell_count + spots] = q_high
    left_ref[:, cell_count + spots : cell_count + 2 * spots] = q_high
    left_ref[:, cell_count + 2 * spots :] = matmul(low, place).T.astype(jnp.bfloat16)

    z_lane = lax.broadcasted_iota(jnp.int32, (nproj, z_size), 1)
    for third in range(SIDE):
        for atom in range(atoms):
            z_index = lax.rem(third_at_ref[atom] + third - SIDE // 2 + z_size, z_size)
            start = third * pairs + atom * nproj
            mask_ref[start : start + nproj] = jnp.where(z_lane == z_index, 1.0, 0.0)
    sublane = lax.broadcasted_iota(jnp.int32, (nproj, z_size), 0)
    energy = jnp.zeros((nproj, z_size), jnp.float32)
    for index in range(nproj):
        energy = jnp.where(sublane == index, energy_at_ref[index], energy)
    energy = energy * (1.0 / (unit * filter_width))
    for atom in range(atoms):
        energy_ref[atom * nproj : (atom + 1) * nproj] = energy

    diagonal_ref[...] = (field_ref[0].reshape(own, z_size) + shift) / filter_width


def packed_rotation(rotation_ref, z_size):
    count, wide = rotation_ref.shape
    spare = z_size - wide
    block = jnp.concatenate(
        (rotation_ref[...].astype(jnp.float32), jnp.zeros((count, spare), jnp.float32)), axis=1
    )
    block = jnp.concatenate((block, jnp.zeros((8 - count, z_size), jnp.float32)), axis=0)
    sublane = lax.broadcasted_iota(jnp.int32, (8, z_size), 0)
    lane = lax.broadcasted_iota(jnp.int32, (8, z_size), 1)
    packed = block
    for piece in range(-(-wide // spare)):
        moved = pltpu.roll(block, (piece - (count - 1)) % 8, 0)
        moved = pltpu.roll(moved, (wide - piece * spare) % z_size, 1)
        packed = jnp.where((sublane == piece) & (lane >= wide), moved, packed)
    return packed


def filter_kernel(
    received_ref,
    q_ref,
    left_ref,
    mask_ref,
    energy_ref,
    diagonal_ref,
    partner_diagonal_ref,
    third_ref,
    out_ref,
    rows_ref,
    right_ref,
    start_ref,
    first_ref,
    result_ref,
    sem_ref,
):
    count, block_x, y_size, z_size = out_ref.shape[1:]
    own = block_x * y_size
    cells = 2 * own
    used = count * block_x
    spots = mask_ref.shape[0]
    depth = cells + 2 * spots
    pitch = y_size + 1
    unit, _ = shared_operator()
    me = lax.axis_index("dom")
    for half in range(2):
        for part in range(y_size):
            values = received_ref[(me ^ half) * y_size + part].astype(jnp.float32)
            rows_ref[half, pl.ds(part, used, stride=pitch), :] = values[0:used]

    groups = [range(first, min(first + 2, count)) for first in range(0, count, 2)]
    lanes_of = [slice(group[0] * z_size, (group[-1] + 1) * z_size) for group in groups]
    made = [{} for _ in groups]
    stores = []

    def column(position):
        return slice(position * z_size, (position + 1) * z_size)

    def load(index):
        for orbital in groups[index]:
            for half in range(2):
                planes = [
                    rows_ref[half, pl.ds((orbital * block_x + plane) * pitch, y_size), :]
                    for plane in range(block_x)
                ]
                values = jnp.concatenate(planes, axis=0).astype(jnp.bfloat16)
                right_ref[half * own : (half + 1) * own, column(orbital)] = values
                start_ref[half * own : (half + 1) * own, column(orbital)] = values

    def project(index):
        made[index]["products"] = matmul(q_ref[...], right_ref[0:cells, lanes_of[index]])

    def spread_first(index):
        coeff_ref = right_ref.at[cells:depth]
        spread(made[index]["products"], lanes_of[index], mask_ref, energy_ref, coeff_ref)

    def spread_second(index):
        coeff_ref = right_ref.at[cells:]
        spread(made[index]["products"], lanes_of[index], mask_ref, energy_ref, coeff_ref)

    def along(index, rows):
        wide = len(groups[index]) * z_size
        values = right_ref[0:rows, lanes_of[index]]
        made[index]["along"] = matmul(values, third_ref[0:wide, 0:wide])

    def along_first(index):
        along(index, cells)

    def along_second(index):
        along(index, own)

    def plane_first(index):
        summed = matmul(left_ref[:, 0:depth], right_ref[0:depth, lanes_of[index]])
        made[index]["summed"] = summed + made[index]["along"]

    def plane_second(index):
        summed = matmul(left_ref[0:own], right_ref[:, lanes_of[index]])
        made[index]["summed"] = summed + made[index]["along"]

    def finish_first(index):
        for position, orbital in enumerate(groups[index]):
            values = unit * made[index]["summed"][:, column(position)]
            start = start_ref[:, column(orbital)].astype(jnp.float32)
            mine = diagonal_ref[...] * start[0:own] + values[0:own]
            other = partner_diagonal_ref[...] * start[own:] + values[own:]
            first_ref[:, column(orbital)] = mine
            right_ref[0:own, column(orbital)] = mine.astype(jnp.bfloat16)
            right_ref[own:cells, column(orbital)] = other.astype(jnp.bfloat16)

    def finish_second(index):
        for position, orbital in enumerate(groups[index]):
            values = unit * made[index]["summed"][:, column(position)]
            values = diagonal_ref[...] * first_ref[:, column(orbital)] + values
            start = start_ref[0:own, column(orbital)].astype(jnp.float32)
            values = (2.0 * values - start).astype(jnp.bfloat16)
            result_ref[orbital] = values.reshape(block_x, y_size, z_size)
            stores.append(
                pltpu.make_async_copy(
                    result_ref.at[orbital], out_ref.at[0, orbital], sem_ref.at[orbital]
                )
            )
            stores[-1].start()

    steps = (
        load,
        project,
        along_first,
        spread_first,
        plane_first,
        finish_first,
        project,
        along_second,
        spread_second,
        plane_second,
        finish_second,
    )
    for time in range(len(steps) + 2 * len(groups) - 2):
        for index in range(len(groups)):
            if 0 <= time - 2 * index < len(steps):
                steps[time - 2 * index](index)
    for store in stores:
        store.wait()


def rotate_kernel(received_ref, after_ref, out_ref, wide_ref, rows_ref, *, count, block_x):
    sources, chunk, z_size = received_ref.shape
    total = sources * count
    used = count * block_x
    spare = z_size - total
    pitch = chunk + 1
    for part in range(sources):
        wide_ref[pl.ds(part * pitch, chunk), :] = received_ref[part].astype(jnp.float32)
    packed = [wide_ref[pl.ds(used + row, sources, stride=pitch), :] for row in range(count - 1)]
    lane = lax.broadcasted_iota(jnp.int32, (sources, z_size), 1)
    last = jnp.zeros((sources, z_size), jnp.float32)
    for piece in range(-(-total // spare)):
        moved = pltpu.roll(packed[piece], (piece * spare - total) % z_size, 1)
        last = jnp.where(lane >= piece * spare, moved, last)
    rotation = jnp.concatenate(packed + [last], axis=0)[:, 0:total].astype(jnp.bfloat16)
    columns = []
    for plane in range(block_x):
        rows = [
            wide_ref[pl.ds(orbital * block_x + plane, sources, stride=pitch), :]
            for orbital in range(count)
        ]
        columns.append(jnp.concatenate(rows, axis=0).astype(jnp.bfloat16))
    values = jnp.concatenate(columns, axis=1)
    rotated = lax.dot_general(
        rotation, values, (((0,), (0,)), ((), ())), preferred_element_type=jnp.float32
    )
    rows_ref[total * block_x :] = jnp.zeros((chunk - used, z_size), jnp.float32)
    for plane in range(block_x):
        lanes = slice(plane * z_size, (plane + 1) * z_size)
        rows_ref[pl.ds(plane, total, stride=block_x), :] = rotated[:, lanes]
    for part in range(sources):
        values = rows_ref[part * used : part * used + chunk].astype(jnp.bfloat16)
        out_ref[part] = values
        out_ref[sources + part] = values


def in_vmem(count):
    return [pl.BlockSpec(memory_space=pltpu.VMEM)] * count


def in_smem(count):
    return [pl.BlockSpec(memory_space=pltpu.SMEM)] * count


def params(mib):
    return pltpu.CompilerParams(vmem_limit_bytes=mib * MIB)


def shape_of(shape, kind):
    return jax.ShapeDtypeStruct(shape, kind)


def pair_body(
    orbitals, potential, projectors, projector_energy, atom_first, atom_second, atom_third, rotation
):
    bf16, f32 = jnp.bfloat16, jnp.float32
    count, block_x, y_size, z_size = orbitals.shape[1:]
    x_size = 2 * block_x
    own = block_x * y_size
    cell_count = x_size * y_size
    atoms, nproj = projectors.shape[:2]
    spots = SIDE * atoms * nproj
    sources = lax.axis_size("orb")
    used = count * block_x
    chunk = -(-(used + count - 1) // 16) * 16

    packed, after = pl.pallas_call(
        pack_kernel,
        out_shape=(shape_of((sources, chunk, z_size), bf16), shape_of((8, z_size), f32)),
        in_specs=[pl.BlockSpec(memory_space=pltpu.HBM)] * 2,
        out_specs=tuple(in_vmem(2)),
        scratch_shapes=[
            pltpu.VMEM(orbitals.shape[1:], f32),
            pltpu.VMEM(rotation.shape, bf16),
            pltpu.VMEM((chunk, z_size), f32),
            pltpu.SemaphoreType.DMA((2,)),
        ],
        compiler_params=params(60),
        name="pack",
    )(orbitals, rotation)
    by_plane = lax.all_to_all(packed, "orb", split_axis=0, concat_axis=0, tiled=True)

    q, left, mask, energy, diagonal = pl.pallas_call(
        table_kernel,
        out_shape=(
            shape_of((spots, cell_count), bf16),
            shape_of((cell_count, cell_count + 3 * spots), bf16),
            shape_of((spots, z_size), f32),
            shape_of((atoms * nproj, z_size), f32),
            shape_of((own, z_size), f32),
        ),
        in_specs=in_smem(4) + [pl.BlockSpec(memory_space=pl.ANY)] + in_vmem(4),
        out_specs=tuple(in_vmem(5)),
        compiler_params=params(24),
        cost_estimate=pl.CostEstimate(flops=1 << 31, bytes_accessed=6 << 20, transcendentals=0),
        name="tables",
    )(
        atom_first,
        atom_second,
        atom_third,
        projector_energy,
        after,
        projectors,
        third_first(),
        plane_stencil(x_size, y_size),
        potential,
    )
    partner_diagonal = lax.ppermute(diagonal, "dom", [(0, 1), (1, 0)])

    rotated = pl.pallas_call(
        functools.partial(rotate_kernel, count=count, block_x=block_x),
        out_shape=shape_of((2 * sources, chunk, z_size), bf16),
        in_specs=in_vmem(2),
        out_specs=in_vmem(1)[0],
        scratch_shapes=[
            pltpu.VMEM((sources * (chunk + 8), z_size), f32),
            pltpu.VMEM((sources * used + chunk - used, z_size), f32),
        ],
        compiler_params=params(24),
        name="rotate",
    )(by_plane, partner_diagonal)
    by_orbital = lax.all_to_all(rotated, ("dom", "orb"), split_axis=0, concat_axis=0, tiled=True)

    return pl.pallas_call(
        filter_kernel,
        out_shape=shape_of(orbitals.shape, bf16),
        in_specs=in_vmem(8),
        out_specs=pl.BlockSpec(memory_space=pltpu.HBM),
        scratch_shapes=[
            pltpu.VMEM((2, used * (y_size + 8), z_size), f32),
            pltpu.VMEM((cell_count + 3 * spots, count * z_size), bf16),
            pltpu.VMEM((cell_count, count * z_size), bf16),
            pltpu.VMEM((own, count * z_size), f32),
            pltpu.VMEM(orbitals.shape[1:], bf16),
            pltpu.SemaphoreType.DMA((count,)),
        ],
        compiler_params=params(40),
        name="filter",
    )(
        by_orbital,
        q,
        left,
        mask,
        energy,
        diagonal,
        partner_diagonal,
        third_stencil(z_size),
    )


def fits_pair(mesh, orbitals, projectors, rotation):
    count = orbitals.shape[1] // mesh.shape["orb"]
    return (
        mesh.shape["dom"] == 2
        and orbitals.shape[3] == mesh.shape["orb"]
        and orbitals.shape[2] == 2 * stencil_reach
        and projectors.shape[0] % 2 == 0
        and projectors.shape[1] == 8
        and count <= 8
        and rotation.shape[1] < orbitals.shape[4]
        and -(-rotation.shape[1] // (orbitals.shape[4] - rotation.shape[1])) < count
    )


def solution(mesh):
    def whole(*arrays):
        chosen = pair_body if fits_pair(mesh, arrays[0], arrays[2], arrays[7]) else body
        return jax.shard_map(
            chosen,
            mesh=mesh,
            in_specs=(
                P("dom", "orb", None, None, None),
                P("dom", None, None, None),
                P(),
                P(),
                P(),
                P(),
                P(),
                P("orb", None),
            ),
            out_specs=P("dom", "orb", None, None, None),
            check_vma=False,
        )(*arrays)

    return whole
```

```python
import functools

import jax
import jax.numpy as jnp
import numpy as np
from jax import lax
from jax.experimental import pallas as pl
from jax.experimental.pallas import tpu as pltpu
from jax.sharding import PartitionSpec as P

SIDE = 8
SUP = 512


stencil_weights = (
    -5369.0 / 1800.0,
    12.0 / 7.0,
    -15.0 / 56.0,
    10.0 / 189.0,
    -1.0 / 112.0,
    2.0 / 1925.0,
    -1.0 / 16632.0,
)
inverse_spacing = 4.0
filter_center = 120.0
filter_width = 110.0
stencil_reach = 6


def partner_2(block, axis, bit):
    count = lax.axis_size(axis)
    route = []
    for low in range(count):
        high = low | 1 << bit
        if high != low and high < count:
            route += [(low, high), (high, low)]
    return lax.ppermute(block, axis, route)


def outgoing(values, direction, width):
    extent = values.shape[direction]
    if 2 * width < extent:
        return jnp.concatenate(
            (
                lax.slice_in_dim(values, 0, width, axis=direction),
                lax.slice_in_dim(values, extent - width, extent, axis=direction),
            ),
            axis=direction,
        )
    return values


def assemble(values, partner, direction, width):
    extent = values.shape[direction]
    if 2 * width < extent:
        lower_rim = lax.slice_in_dim(partner, width, 2 * width, axis=direction)
        upper_rim = lax.slice_in_dim(partner, 0, width, axis=direction)
        return jnp.concatenate((lower_rim, values, upper_rim), axis=direction)
    cyclic = jnp.concatenate((values, partner), axis=direction)
    chosen = np.arange(-width, extent + width) % (2 * extent)
    return jnp.take(cyclic, jnp.asarray(chosen, dtype=jnp.int32), axis=direction)


def face_padded(values, direction, bit_number):
    sent = outgoing(values, direction, stencil_reach)
    partner = partner_2(sent.astype(jnp.bfloat16), "dom", bit_number).astype(sent.dtype)
    return assemble(values, partner, direction, stencil_reach)


def stencil_sum(center, along):
    lead = center.ndim - 3
    summed = 3.0 * stencil_weights[0] * center
    for index in range(3):
        direction = lead + index
        extent = center.shape[direction]
        padded = along[index]
        for offset in range(1, 7):
            if padded is None:
                upward = jnp.roll(center, -offset, direction)
                downward = jnp.roll(center, offset, direction)
            else:
                upward = lax.slice_in_dim(
                    padded, stencil_reach + offset, stencil_reach + offset + extent, axis=direction
                )
                downward = lax.slice_in_dim(
                    padded, stencil_reach - offset, stencil_reach - offset + extent, axis=direction
                )
            summed = summed + stencil_weights[offset] * (upward + downward)
    return summed


def support_map(atom_coords, starts, extents, periods):
    offsets = jnp.arange(SIDE, dtype=jnp.int32) - SIDE // 2
    clipped_list = []
    inside_list = []
    for index in range(3):
        local = (atom_coords[index][:, None] + offsets[None, :] - starts[index]) % periods[index]
        inside_list.append(local < extents[index])
        clipped_list.append(jnp.minimum(local, extents[index] - 1))
    inside = (
        inside_list[0][:, :, None, None]
        & inside_list[1][:, None, :, None]
        & inside_list[2][:, None, None, :]
    )
    flattened = (
        clipped_list[0][:, :, None, None] * extents[1] + clipped_list[1][:, None, :, None]
    ) * extents[2] + clipped_list[2][:, None, None, :]
    atom_count = atom_coords[0].shape[0]
    return (
        flattened.reshape(atom_count * SUP),
        inside.reshape(atom_count, SUP).astype(jnp.float32),
    )


def coefficients(values, support, inside, projectors):
    orbital_count = values.shape[0]
    atom_count = projectors.shape[0]
    flattened = values.reshape(orbital_count, -1)
    picked = (
        jnp.take(flattened, support, axis=1).reshape(orbital_count, atom_count, SUP) * inside[None]
    )
    partial_coeffs = jnp.einsum("aps,kas->kap", projectors, picked, precision=lax.Precision.HIGHEST)
    return lax.psum(partial_coeffs, "dom")


def spread_into(coeffs, shape, support, inside, projectors, projector_energy):
    orbital_count = shape[0]
    atom_count = projectors.shape[0]
    scaled = coeffs * projector_energy[None, None, :]
    spread = (
        jnp.einsum("aps,kap->kas", projectors, scaled, precision=lax.Precision.HIGHEST)
        * inside[None]
    )
    total_cells = shape[1] * shape[2] * shape[3]
    projected_part = (
        jnp.zeros((orbital_count, total_cells), jnp.float32)
        .at[:, support]
        .add(spread.reshape(orbital_count, atom_count * SUP))
    )
    return projected_part.reshape(shape)


def own_hamiltonian(center, along, local_field, support, inside, projectors, projector_energy):
    kinetic = -0.5 * inverse_spacing * inverse_spacing
    coeffs = coefficients(center, support, inside, projectors)
    projected_part = spread_into(
        coeffs, center.shape, support, inside, projectors, projector_energy
    )
    return kinetic * stencil_sum(center, along) + local_field[None] * center + projected_part


def body(
    orbitals, potential, projectors, projector_energy, atom_first, atom_second, atom_third, rotation
):
    domain_count = lax.axis_size("dom")
    domain_bits = domain_count.bit_length() - 1
    split = [index < domain_bits for index in range(3)]
    start_values = orbitals[0]
    local_field = potential[0]
    extents = start_values.shape[1:]
    periods = (
        extents[0] * min(domain_count, 2),
        extents[1] * min(max(domain_count // 2, 1), 2),
        extents[2] * max(domain_count // 4, 1),
    )
    domain_index = lax.axis_index("dom")
    anchors = (
        domain_index % 2 * extents[0],
        domain_index // 2 % 2 * extents[1],
        domain_index // 4 * extents[2],
    )
    atom_coords = (atom_first, atom_second, atom_third)
    support, inside = support_map(atom_coords, anchors, extents, periods)
    along = [
        face_padded(start_values, index + 1, index) if split[index] else None for index in range(3)
    ]
    first_apply = own_hamiltonian(
        start_values, along, local_field, support, inside, projectors, projector_energy
    )
    first_term = (first_apply - filter_center * start_values) / filter_width
    along = [
        face_padded(first_term, index + 1, index) if split[index] else None for index in range(3)
    ]
    second_apply = own_hamiltonian(
        first_term, along, local_field, support, inside, projectors, projector_energy
    )
    second_term = 2.0 * (second_apply - filter_center * first_term) / filter_width - start_values
    per_device = start_values.shape[0]
    filtered = second_term.astype(jnp.bfloat16).reshape(per_device, -1)
    by_cells = lax.all_to_all(filtered, "orb", split_axis=1, concat_axis=0, tiled=True)
    whole_rotation = lax.all_gather(rotation, "orb", axis=0, tiled=True)
    rotated = lax.dot_general(
        whole_rotation, by_cells, (((0,), (0,)), ((), ())), preferred_element_type=jnp.float32
    ).astype(jnp.bfloat16)
    result = lax.all_to_all(rotated, "orb", split_axis=0, concat_axis=1, tiled=True)
    return result.reshape((1,) + start_values.shape)


SCALE = 15.0
MIB = 1 << 20


def scaled_weights():
    ratios = np.array(stencil_weights[1:], np.float64) / stencil_weights[1]
    return SCALE * ratios


def cyclic_stencil(size):
    matrix = np.zeros((size, size), np.float64)
    rows = np.arange(size)
    for offset, weight in enumerate(scaled_weights(), 1):
        np.add.at(matrix, (rows, (rows + offset) % size), weight)
        np.add.at(matrix, (rows, (rows - offset) % size), weight)
    return matrix


def plane_stencil(x_size, y_size):
    matrix = np.kron(cyclic_stencil(x_size), np.eye(y_size))
    matrix += np.kron(np.eye(x_size), cyclic_stencil(y_size))
    return matrix.astype(jnp.bfloat16)


def third_stencil(z_size):
    matrix = cyclic_stencil(z_size)
    return np.kron(np.eye(2), matrix).astype(jnp.bfloat16)


def third_first():
    picked = np.zeros((SUP, SUP), np.float32)
    source = np.arange(SUP)
    picked[source, source % SIDE * SIDE * SIDE + source // SIDE] = 1.0
    return picked.astype(jnp.bfloat16)


def halves(values):
    high = values.astype(jnp.bfloat16)
    return high, (values - high.astype(jnp.float32)).astype(jnp.bfloat16)


def matmul(left, right):
    return jnp.dot(left, right, preferred_element_type=jnp.float32)


def shared_operator():
    kinetic = -0.5 * inverse_spacing * inverse_spacing
    unit = kinetic * stencil_weights[1] / SCALE / filter_width
    shift = 3.0 * kinetic * stencil_weights[0] - filter_center
    return unit, shift


def pack_kernel(orbital_ref, rotation_ref, out_ref, after_ref, chunk_ref):
    count, block_x, height, z_size = orbital_ref.shape[1:]
    chunk = out_ref.shape[1]
    used = count * block_x
    pitch = chunk + 1
    packed = packed_rotation(rotation_ref, z_size)
    after_ref[...] = packed
    for orbital in range(count):
        for plane in range(block_x):
            start = orbital * block_x + plane
            chunk_ref[pl.ds(start, height, stride=pitch), :] = orbital_ref[0, orbital, plane]
    for part in range(height):
        start = part * pitch
        chunk_ref[start + used : start + used + count - 1] = packed[0 : count - 1]
        out_ref[part] = chunk_ref[start : start + chunk].astype(jnp.bfloat16)


def spread(products, lanes, mask_ref, energy_ref, coeff_ref):
    spots, z_size = mask_ref.shape
    pairs = energy_ref.shape[0]
    mask = mask_ref[...]
    for start in range(0, products.shape[1], z_size):
        picked = products[:, start : start + z_size] * mask
        coeffs = jnp.sum(picked.reshape(SIDE, pairs, z_size), axis=0)
        coeffs = jnp.sum(coeffs, axis=1, keepdims=True)
        high, low = halves(jnp.concatenate([coeffs * energy_ref[...]] * SIDE, axis=0) * mask)
        columns = slice(lanes.start + start, lanes.start + start + z_size)
        coeff_ref[0:spots, columns] = high
        coeff_ref[spots : 2 * spots, columns] = low
        if coeff_ref.shape[0] > 2 * spots:
            coeff_ref[2 * spots :, columns] = high


def table_kernel(
    first_at_ref,
    second_at_ref,
    third_at_ref,
    energy_at_ref,
    after_ref,
    projector_ref,
    order_ref,
    plane_ref,
    field_ref,
    q_ref,
    left_ref,
    mask_ref,
    energy_ref,
    diagonal_ref,
):
    block_x, y_size, z_size = field_ref.shape[1:]
    x_size = 2 * block_x
    own = block_x * y_size
    cell_count = x_size * y_size
    atoms, nproj = projector_ref.shape[:2]
    pairs = atoms * nproj
    per_plane = SIDE * SIDE
    spots = atoms * per_plane
    unit, shift = shared_operator()
    own_start = lax.axis_index("dom") * block_x
    high, low = halves(projector_ref[...].reshape(pairs, SUP))
    ordered = matmul(jnp.concatenate((high, low), axis=0), order_ref[...])

    lane = lax.broadcasted_iota(jnp.int32, (pairs, 2 * per_plane), 1)
    row_atom = lax.broadcasted_iota(jnp.int32, (pairs, spots), 0) // nproj
    lane_atom = lax.broadcasted_iota(jnp.int32, (pairs, spots), 1) // per_plane
    same_atom = row_atom == lane_atom
    expanded = []
    for part in range(2):
        rows = []
        for third in range(SIDE):
            start = third // 2 * 2 * per_plane
            both = ordered[part * pairs : (part + 1) * pairs, start : start + 2 * per_plane]
            swapped = pltpu.roll(both, per_plane, 1)
            if third % 2:
                both, swapped = swapped, both
            doubled = jnp.where(lane < per_plane, both, swapped)
            doubled = jnp.concatenate([doubled] * (atoms // 2), axis=1)
            rows.append(jnp.where(same_atom, doubled, 0.0))
        expanded.append(jnp.concatenate(rows, axis=0).astype(jnp.bfloat16))
    high, low = expanded

    place = []
    spot = lax.broadcasted_iota(jnp.int32, (per_plane, cell_count), 0)
    place_lane = lax.broadcasted_iota(jnp.int32, (per_plane, cell_count), 1)
    for atom in range(atoms):
        x_start = lax.rem(first_at_ref[atom] - SIDE // 2 - own_start + 2 * x_size, x_size)
        y_start = lax.rem(second_at_ref[atom] - SIDE // 2 + y_size, y_size)
        x_index = x_start + spot // SIDE
        x_index = jnp.where(x_index >= x_size, x_index - x_size, x_index)
        y_index = y_start + spot % SIDE
        y_index = jnp.where(y_index >= y_size, y_index - y_size, y_index)
        target = x_index * y_size + y_index
        place.append(jnp.where(place_lane == target, 1.0, 0.0).astype(jnp.bfloat16))
    place = jnp.concatenate(place, axis=0)
    q_high = matmul(high, place)
    q_ref[...] = q_high.astype(jnp.bfloat16)
    q_high = q_high.T.astype(jnp.bfloat16)
    left_ref[:, 0:cell_count] = plane_ref[...]
    left_ref[:, cell_count : cell_count + spots] = q_high
    left_ref[:, cell_count + spots : cell_count + 2 * spots] = q_high
    left_ref[:, cell_count + 2 * spots :] = matmul(low, place).T.astype(jnp.bfloat16)

    z_lane = lax.broadcasted_iota(jnp.int32, (nproj, z_size), 1)
    for third in range(SIDE):
        for atom in range(atoms):
            z_index = lax.rem(third_at_ref[atom] + third - SIDE // 2 + z_size, z_size)
            start = third * pairs + atom * nproj
            mask_ref[start : start + nproj] = jnp.where(z_lane == z_index, 1.0, 0.0)
    sublane = lax.broadcasted_iota(jnp.int32, (nproj, z_size), 0)
    energy = jnp.zeros((nproj, z_size), jnp.float32)
    for index in range(nproj):
        energy = jnp.where(sublane == index, energy_at_ref[index], energy)
    energy = energy * (1.0 / (unit * filter_width))
    for atom in range(atoms):
        energy_ref[atom * nproj : (atom + 1) * nproj] = energy

    diagonal_ref[...] = (field_ref[0].reshape(own, z_size) + shift) / filter_width


def packed_rotation(rotation_ref, z_size):
    count, wide = rotation_ref.shape
    spare = z_size - wide
    block = jnp.concatenate(
        (rotation_ref[...].astype(jnp.float32), jnp.zeros((count, spare), jnp.float32)), axis=1
    )
    block = jnp.concatenate((block, jnp.zeros((8 - count, z_size), jnp.float32)), axis=0)
    sublane = lax.broadcasted_iota(jnp.int32, (8, z_size), 0)
    lane = lax.broadcasted_iota(jnp.int32, (8, z_size), 1)
    packed = block
    for piece in range(-(-wide // spare)):
        moved = pltpu.roll(block, (piece - (count - 1)) % 8, 0)
        moved = pltpu.roll(moved, (wide - piece * spare) % z_size, 1)
        packed = jnp.where((sublane == piece) & (lane >= wide), moved, packed)
    return packed


def filter_kernel(
    received_ref,
    q_ref,
    left_ref,
    mask_ref,
    energy_ref,
    diagonal_ref,
    partner_diagonal_ref,
    third_ref,
    out_ref,
    rows_ref,
    right_ref,
    start_ref,
    first_ref,
    result_ref,
    sem_ref,
):
    count, block_x, y_size, z_size = out_ref.shape[1:]
    own = block_x * y_size
    cells = 2 * own
    used = count * block_x
    spots = mask_ref.shape[0]
    depth = cells + 2 * spots
    pitch = y_size + 1
    unit, _ = shared_operator()
    me = lax.axis_index("dom")
    for half in range(2):
        for part in range(y_size):
            values = received_ref[(me ^ half) * y_size + part].astype(jnp.float32)
            rows_ref[half, pl.ds(part, used, stride=pitch), :] = values[0:used]

    groups = [range(first, min(first + 2, count)) for first in range(0, count, 2)]
    lanes_of = [slice(group[0] * z_size, (group[-1] + 1) * z_size) for group in groups]
    made = [{} for _ in groups]
    stores = []

    def column(position):
        return slice(position * z_size, (position + 1) * z_size)

    def load(index):
        for orbital in groups[index]:
            for half in range(2):
                planes = [
                    rows_ref[half, pl.ds((orbital * block_x + plane) * pitch, y_size), :]
                    for plane in range(block_x)
                ]
                values = jnp.concatenate(planes, axis=0).astype(jnp.bfloat16)
                right_ref[half * own : (half + 1) * own, column(orbital)] = values
                start_ref[half * own : (half + 1) * own, column(orbital)] = values

    def project(index):
        made[index]["products"] = matmul(q_ref[...], right_ref[0:cells, lanes_of[index]])

    def spread_first(index):
        coeff_ref = right_ref.at[cells:depth]
        spread(made[index]["products"], lanes_of[index], mask_ref, energy_ref, coeff_ref)

    def spread_second(index):
        coeff_ref = right_ref.at[cells:]
        spread(made[index]["products"], lanes_of[index], mask_ref, energy_ref, coeff_ref)

    def along(index, rows):
        wide = len(groups[index]) * z_size
        values = right_ref[0:rows, lanes_of[index]]
        made[index]["along"] = matmul(values, third_ref[0:wide, 0:wide])

    def along_first(index):
        along(index, cells)

    def along_second(index):
        along(index, own)

    def plane_first(index):
        summed = matmul(left_ref[:, 0:depth], right_ref[0:depth, lanes_of[index]])
        made[index]["summed"] = summed + made[index]["along"]

    def plane_second(index):
        summed = matmul(left_ref[0:own], right_ref[:, lanes_of[index]])
        made[index]["summed"] = summed + made[index]["along"]

    def finish_first(index):
        for position, orbital in enumerate(groups[index]):
            values = unit * made[index]["summed"][:, column(position)]
            start = start_ref[:, column(orbital)].astype(jnp.float32)
            mine = diagonal_ref[...] * start[0:own] + values[0:own]
            other = partner_diagonal_ref[...] * start[own:] + values[own:]
            first_ref[:, column(orbital)] = mine
            right_ref[0:own, column(orbital)] = mine.astype(jnp.bfloat16)
            right_ref[own:cells, column(orbital)] = other.astype(jnp.bfloat16)

    def finish_second(index):
        for position, orbital in enumerate(groups[index]):
            values = unit * made[index]["summed"][:, column(position)]
            values = diagonal_ref[...] * first_ref[:, column(orbital)] + values
            start = start_ref[0:own, column(orbital)].astype(jnp.float32)
            values = (2.0 * values - start).astype(jnp.bfloat16)
            result_ref[orbital] = values.reshape(block_x, y_size, z_size)
            stores.append(
                pltpu.make_async_copy(
                    result_ref.at[orbital], out_ref.at[0, orbital], sem_ref.at[orbital]
                )
            )
            stores[-1].start()

    steps = (
        load,
        project,
        along_first,
        spread_first,
        plane_first,
        finish_first,
        project,
        along_second,
        spread_second,
        plane_second,
        finish_second,
    )
    for time in range(len(steps) + 2 * len(groups) - 2):
        for index in range(len(groups)):
            if 0 <= time - 2 * index < len(steps):
                steps[time - 2 * index](index)
    for store in stores:
        store.wait()


def rotate_kernel(received_ref, after_ref, out_ref, wide_ref, rows_ref, *, count, block_x):
    sources, chunk, z_size = received_ref.shape
    total = sources * count
    used = count * block_x
    spare = z_size - total
    pitch = chunk + 1
    for part in range(sources):
        wide_ref[pl.ds(part * pitch, chunk), :] = received_ref[part].astype(jnp.float32)
    packed = [wide_ref[pl.ds(used + row, sources, stride=pitch), :] for row in range(count - 1)]
    lane = lax.broadcasted_iota(jnp.int32, (sources, z_size), 1)
    last = jnp.zeros((sources, z_size), jnp.float32)
    for piece in range(-(-total // spare)):
        moved = pltpu.roll(packed[piece], (piece * spare - total) % z_size, 1)
        last = jnp.where(lane >= piece * spare, moved, last)
    rotation = jnp.concatenate(packed + [last], axis=0)[:, 0:total].astype(jnp.bfloat16)
    columns = []
    for plane in range(block_x):
        rows = [
            wide_ref[pl.ds(orbital * block_x + plane, sources, stride=pitch), :]
            for orbital in range(count)
        ]
        columns.append(jnp.concatenate(rows, axis=0).astype(jnp.bfloat16))
    values = jnp.concatenate(columns, axis=1)
    rotated = lax.dot_general(
        rotation, values, (((0,), (0,)), ((), ())), preferred_element_type=jnp.float32
    )
    rows_ref[total * block_x :] = jnp.zeros((chunk - used, z_size), jnp.float32)
    for plane in range(block_x):
        lanes = slice(plane * z_size, (plane + 1) * z_size)
        rows_ref[pl.ds(plane, total, stride=block_x), :] = rotated[:, lanes]
    for part in range(sources):
        values = rows_ref[part * used : part * used + chunk].astype(jnp.bfloat16)
        out_ref[part] = values
        out_ref[sources + part] = values


def in_vmem(count):
    return [pl.BlockSpec(memory_space=pltpu.VMEM)] * count


def in_smem(count):
    return [pl.BlockSpec(memory_space=pltpu.SMEM)] * count


def params(mib):
    return pltpu.CompilerParams(vmem_limit_bytes=mib * MIB)


def shape_of(shape, kind):
    return jax.ShapeDtypeStruct(shape, kind)


def pair_body(
    orbitals, potential, projectors, projector_energy, atom_first, atom_second, atom_third, rotation
):
    bf16, f32 = jnp.bfloat16, jnp.float32
    count, block_x, y_size, z_size = orbitals.shape[1:]
    x_size = 2 * block_x
    own = block_x * y_size
    cell_count = x_size * y_size
    atoms, nproj = projectors.shape[:2]
    spots = SIDE * atoms * nproj
    sources = lax.axis_size("orb")
    used = count * block_x
    chunk = -(-(used + count - 1) // 16) * 16

    height = 8
    packed, after = pl.pallas_call(
        pack_kernel,
        out_shape=(shape_of((sources, chunk, z_size), bf16), shape_of((8, z_size), f32)),
        grid=(y_size // height,),
        in_specs=[
            pl.BlockSpec((1, count, block_x, height, z_size), lambda step: (0, 0, 0, step, 0)),
            pl.BlockSpec(rotation.shape, lambda step: (0, 0)),
        ],
        out_specs=(
            pl.BlockSpec((height, chunk, z_size), lambda step: (step, 0, 0)),
            pl.BlockSpec((8, z_size), lambda step: (0, 0)),
        ),
        scratch_shapes=[pltpu.VMEM((height * (chunk + 8), z_size), f32)],
        compiler_params=params(60),
        name="pack",
    )(orbitals, rotation)
    by_plane = lax.all_to_all(packed, "orb", split_axis=0, concat_axis=0, tiled=True)

    q, left, mask, energy, diagonal = pl.pallas_call(
        table_kernel,
        out_shape=(
            shape_of((spots, cell_count), bf16),
            shape_of((cell_count, cell_count + 3 * spots), bf16),
            shape_of((spots, z_size), f32),
            shape_of((atoms * nproj, z_size), f32),
            shape_of((own, z_size), f32),
        ),
        in_specs=in_smem(4) + [pl.BlockSpec(memory_space=pl.ANY)] + in_vmem(4),
        out_specs=tuple(in_vmem(5)),
        compiler_params=params(24),
        cost_estimate=pl.CostEstimate(flops=1 << 31, bytes_accessed=6 << 20, transcendentals=0),
        name="tables",
    )(
        atom_first,
        atom_second,
        atom_third,
        projector_energy,
        after,
        projectors,
        third_first(),
        plane_stencil(x_size, y_size),
        potential,
    )
    partner_diagonal = lax.ppermute(diagonal, "dom", [(0, 1), (1, 0)])

    rotated = pl.pallas_call(
        functools.partial(rotate_kernel, count=count, block_x=block_x),
        out_shape=shape_of((2 * sources, chunk, z_size), bf16),
        in_specs=in_vmem(2),
        out_specs=in_vmem(1)[0],
        scratch_shapes=[
            pltpu.VMEM((sources * (chunk + 8), z_size), f32),
            pltpu.VMEM((sources * used + chunk - used, z_size), f32),
        ],
        compiler_params=params(24),
        name="rotate",
    )(by_plane, partner_diagonal)
    by_orbital = lax.all_to_all(rotated, ("dom", "orb"), split_axis=0, concat_axis=0, tiled=True)

    return pl.pallas_call(
        filter_kernel,
        out_shape=shape_of(orbitals.shape, bf16),
        in_specs=in_vmem(8),
        out_specs=pl.BlockSpec(memory_space=pltpu.HBM),
        scratch_shapes=[
            pltpu.VMEM((2, used * (y_size + 8), z_size), f32),
            pltpu.VMEM((cell_count + 3 * spots, count * z_size), bf16),
            pltpu.VMEM((cell_count, count * z_size), bf16),
            pltpu.VMEM((own, count * z_size), f32),
            pltpu.VMEM(orbitals.shape[1:], bf16),
            pltpu.SemaphoreType.DMA((count,)),
        ],
        compiler_params=params(40),
        name="filter",
    )(
        by_orbital,
        q,
        left,
        mask,
        energy,
        diagonal,
        partner_diagonal,
        third_stencil(z_size),
    )


def fits_pair(mesh, orbitals, projectors, rotation):
    count = orbitals.shape[1] // mesh.shape["orb"]
    return (
        mesh.shape["dom"] == 2
        and orbitals.shape[3] == mesh.shape["orb"]
        and orbitals.shape[2] == 2 * stencil_reach
        and projectors.shape[0] % 2 == 0
        and projectors.shape[1] == 8
        and count <= 8
        and rotation.shape[1] < orbitals.shape[4]
        and -(-rotation.shape[1] // (orbitals.shape[4] - rotation.shape[1])) < count
    )


def solution(mesh):
    def whole(*arrays):
        chosen = pair_body if fits_pair(mesh, arrays[0], arrays[2], arrays[7]) else body
        return jax.shard_map(
            chosen,
            mesh=mesh,
            in_specs=(
                P("dom", "orb", None, None, None),
                P("dom", None, None, None),
                P(),
                P(),
                P(),
                P(),
                P(),
                P("orb", None),
            ),
            out_specs=P("dom", "orb", None, None, None),
            check_vma=False,
        )(*arrays)

    return whole
```

```python
import functools

import jax
import jax.numpy as jnp
import numpy as np
from jax import lax
from jax.experimental import pallas as pl
from jax.experimental.pallas import tpu as pltpu
from jax.sharding import PartitionSpec as P

SIDE = 8
SUP = 512


stencil_weights = (
    -5369.0 / 1800.0,
    12.0 / 7.0,
    -15.0 / 56.0,
    10.0 / 189.0,
    -1.0 / 112.0,
    2.0 / 1925.0,
    -1.0 / 16632.0,
)
inverse_spacing = 4.0
filter_center = 120.0
filter_width = 110.0
stencil_reach = 6


def partner_2(block, axis, bit):
    count = lax.axis_size(axis)
    route = []
    for low in range(count):
        high = low | 1 << bit
        if high != low and high < count:
            route += [(low, high), (high, low)]
    return lax.ppermute(block, axis, route)


def outgoing(values, direction, width):
    extent = values.shape[direction]
    if 2 * width < extent:
        return jnp.concatenate(
            (
                lax.slice_in_dim(values, 0, width, axis=direction),
                lax.slice_in_dim(values, extent - width, extent, axis=direction),
            ),
            axis=direction,
        )
    return values


def assemble(values, partner, direction, width):
    extent = values.shape[direction]
    if 2 * width < extent:
        lower_rim = lax.slice_in_dim(partner, width, 2 * width, axis=direction)
        upper_rim = lax.slice_in_dim(partner, 0, width, axis=direction)
        return jnp.concatenate((lower_rim, values, upper_rim), axis=direction)
    cyclic = jnp.concatenate((values, partner), axis=direction)
    chosen = np.arange(-width, extent + width) % (2 * extent)
    return jnp.take(cyclic, jnp.asarray(chosen, dtype=jnp.int32), axis=direction)


def face_padded(values, direction, bit_number):
    sent = outgoing(values, direction, stencil_reach)
    partner = partner_2(sent.astype(jnp.bfloat16), "dom", bit_number).astype(sent.dtype)
    return assemble(values, partner, direction, stencil_reach)


def stencil_sum(center, along):
    lead = center.ndim - 3
    summed = 3.0 * stencil_weights[0] * center
    for index in range(3):
        direction = lead + index
        extent = center.shape[direction]
        padded = along[index]
        for offset in range(1, 7):
            if padded is None:
                upward = jnp.roll(center, -offset, direction)
                downward = jnp.roll(center, offset, direction)
            else:
                upward = lax.slice_in_dim(
                    padded, stencil_reach + offset, stencil_reach + offset + extent, axis=direction
                )
                downward = lax.slice_in_dim(
                    padded, stencil_reach - offset, stencil_reach - offset + extent, axis=direction
                )
            summed = summed + stencil_weights[offset] * (upward + downward)
    return summed


def support_map(atom_coords, starts, extents, periods):
    offsets = jnp.arange(SIDE, dtype=jnp.int32) - SIDE // 2
    clipped_list = []
    inside_list = []
    for index in range(3):
        local = (atom_coords[index][:, None] + offsets[None, :] - starts[index]) % periods[index]
        inside_list.append(local < extents[index])
        clipped_list.append(jnp.minimum(local, extents[index] - 1))
    inside = (
        inside_list[0][:, :, None, None]
        & inside_list[1][:, None, :, None]
        & inside_list[2][:, None, None, :]
    )
    flattened = (
        clipped_list[0][:, :, None, None] * extents[1] + clipped_list[1][:, None, :, None]
    ) * extents[2] + clipped_list[2][:, None, None, :]
    atom_count = atom_coords[0].shape[0]
    return (
        flattened.reshape(atom_count * SUP),
        inside.reshape(atom_count, SUP).astype(jnp.float32),
    )


def coefficients(values, support, inside, projectors):
    orbital_count = values.shape[0]
    atom_count = projectors.shape[0]
    flattened = values.reshape(orbital_count, -1)
    picked = (
        jnp.take(flattened, support, axis=1).reshape(orbital_count, atom_count, SUP) * inside[None]
    )
    partial_coeffs = jnp.einsum("aps,kas->kap", projectors, picked, precision=lax.Precision.HIGHEST)
    return lax.psum(partial_coeffs, "dom")


def spread_into(coeffs, shape, support, inside, projectors, projector_energy):
    orbital_count = shape[0]
    atom_count = projectors.shape[0]
    scaled = coeffs * projector_energy[None, None, :]
    spread = (
        jnp.einsum("aps,kap->kas", projectors, scaled, precision=lax.Precision.HIGHEST)
        * inside[None]
    )
    total_cells = shape[1] * shape[2] * shape[3]
    projected_part = (
        jnp.zeros((orbital_count, total_cells), jnp.float32)
        .at[:, support]
        .add(spread.reshape(orbital_count, atom_count * SUP))
    )
    return projected_part.reshape(shape)


def own_hamiltonian(center, along, local_field, support, inside, projectors, projector_energy):
    kinetic = -0.5 * inverse_spacing * inverse_spacing
    coeffs = coefficients(center, support, inside, projectors)
    projected_part = spread_into(
        coeffs, center.shape, support, inside, projectors, projector_energy
    )
    return kinetic * stencil_sum(center, along) + local_field[None] * center + projected_part


def body(
    orbitals, potential, projectors, projector_energy, atom_first, atom_second, atom_third, rotation
):
    domain_count = lax.axis_size("dom")
    domain_bits = domain_count.bit_length() - 1
    split = [index < domain_bits for index in range(3)]
    start_values = orbitals[0]
    local_field = potential[0]
    extents = start_values.shape[1:]
    periods = (
        extents[0] * min(domain_count, 2),
        extents[1] * min(max(domain_count // 2, 1), 2),
        extents[2] * max(domain_count // 4, 1),
    )
    domain_index = lax.axis_index("dom")
    anchors = (
        domain_index % 2 * extents[0],
        domain_index // 2 % 2 * extents[1],
        domain_index // 4 * extents[2],
    )
    atom_coords = (atom_first, atom_second, atom_third)
    support, inside = support_map(atom_coords, anchors, extents, periods)
    along = [
        face_padded(start_values, index + 1, index) if split[index] else None for index in range(3)
    ]
    first_apply = own_hamiltonian(
        start_values, along, local_field, support, inside, projectors, projector_energy
    )
    first_term = (first_apply - filter_center * start_values) / filter_width
    along = [
        face_padded(first_term, index + 1, index) if split[index] else None for index in range(3)
    ]
    second_apply = own_hamiltonian(
        first_term, along, local_field, support, inside, projectors, projector_energy
    )
    second_term = 2.0 * (second_apply - filter_center * first_term) / filter_width - start_values
    per_device = start_values.shape[0]
    filtered = second_term.astype(jnp.bfloat16).reshape(per_device, -1)
    by_cells = lax.all_to_all(filtered, "orb", split_axis=1, concat_axis=0, tiled=True)
    whole_rotation = lax.all_gather(rotation, "orb", axis=0, tiled=True)
    rotated = lax.dot_general(
        whole_rotation, by_cells, (((0,), (0,)), ((), ())), preferred_element_type=jnp.float32
    ).astype(jnp.bfloat16)
    result = lax.all_to_all(rotated, "orb", split_axis=0, concat_axis=1, tiled=True)
    return result.reshape((1,) + start_values.shape)


SCALE = 15.0
MIB = 1 << 20


def scaled_weights():
    ratios = np.array(stencil_weights[1:], np.float64) / stencil_weights[1]
    return SCALE * ratios


def cyclic_stencil(size):
    matrix = np.zeros((size, size), np.float64)
    rows = np.arange(size)
    for offset, weight in enumerate(scaled_weights(), 1):
        np.add.at(matrix, (rows, (rows + offset) % size), weight)
        np.add.at(matrix, (rows, (rows - offset) % size), weight)
    return matrix


def plane_stencil(x_size, y_size):
    matrix = np.kron(cyclic_stencil(x_size), np.eye(y_size))
    matrix += np.kron(np.eye(x_size), cyclic_stencil(y_size))
    return matrix.astype(jnp.bfloat16)


def third_stencil(z_size):
    matrix = cyclic_stencil(z_size)
    return np.kron(np.eye(2), matrix).astype(jnp.bfloat16)


def third_first():
    picked = np.zeros((SUP, SUP), np.float32)
    source = np.arange(SUP)
    picked[source, source % SIDE * SIDE * SIDE + source // SIDE] = 1.0
    return picked.astype(jnp.bfloat16)


def halves(values):
    high = values.astype(jnp.bfloat16)
    return high, (values - high.astype(jnp.float32)).astype(jnp.bfloat16)


def matmul(left, right):
    return jnp.dot(left, right, preferred_element_type=jnp.float32)


def shared_operator():
    kinetic = -0.5 * inverse_spacing * inverse_spacing
    unit = kinetic * stencil_weights[1] / SCALE / filter_width
    shift = 3.0 * kinetic * stencil_weights[0] - filter_center
    return unit, shift


def pack_kernel(orbital_ref, rotation_ref, out_ref, after_ref, chunk_ref):
    count, block_x, height, z_size = orbital_ref.shape[1:]
    chunk = out_ref.shape[1]
    used = count * block_x
    pitch = chunk + 1
    packed = packed_rotation(rotation_ref, z_size)
    after_ref[...] = packed
    for orbital in range(count):
        for plane in range(block_x):
            start = orbital * block_x + plane
            chunk_ref[pl.ds(start, height, stride=pitch), :] = orbital_ref[0, orbital, plane]
    for part in range(height):
        start = part * pitch
        chunk_ref[start + used : start + used + count - 1] = packed[0 : count - 1]
        out_ref[part] = chunk_ref[start : start + chunk].astype(jnp.bfloat16)


def spread(products, lanes, mask_ref, energy_ref, coeff_ref):
    spots, z_size = mask_ref.shape
    pairs = energy_ref.shape[0]
    mask = mask_ref[...]
    for start in range(0, products.shape[1], z_size):
        picked = products[:, start : start + z_size] * mask
        coeffs = jnp.sum(picked.reshape(SIDE, pairs, z_size), axis=0)
        coeffs = jnp.sum(coeffs, axis=1, keepdims=True)
        high, low = halves(jnp.concatenate([coeffs * energy_ref[...]] * SIDE, axis=0) * mask)
        columns = slice(lanes.start + start, lanes.start + start + z_size)
        coeff_ref[0:spots, columns] = high
        coeff_ref[spots : 2 * spots, columns] = low
        if coeff_ref.shape[0] > 2 * spots:
            coeff_ref[2 * spots :, columns] = high


def table_kernel(
    first_at_ref,
    second_at_ref,
    third_at_ref,
    energy_at_ref,
    after_ref,
    projector_ref,
    order_ref,
    plane_ref,
    field_ref,
    q_ref,
    left_ref,
    mask_ref,
    energy_ref,
    diagonal_ref,
):
    block_x, y_size, z_size = field_ref.shape[1:]
    x_size = 2 * block_x
    own = block_x * y_size
    cell_count = x_size * y_size
    atoms, nproj = projector_ref.shape[:2]
    pairs = atoms * nproj
    per_plane = SIDE * SIDE
    spots = atoms * per_plane
    unit, shift = shared_operator()
    own_start = lax.axis_index("dom") * block_x
    high, low = halves(projector_ref[...].reshape(pairs, SUP))
    ordered = matmul(jnp.concatenate((high, low), axis=0), order_ref[...])

    lane = lax.broadcasted_iota(jnp.int32, (pairs, 2 * per_plane), 1)
    row_atom = lax.broadcasted_iota(jnp.int32, (pairs, spots), 0) // nproj
    lane_atom = lax.broadcasted_iota(jnp.int32, (pairs, spots), 1) // per_plane
    same_atom = row_atom == lane_atom
    expanded = []
    for part in range(2):
        rows = []
        for third in range(SIDE):
            start = third // 2 * 2 * per_plane
            both = ordered[part * pairs : (part + 1) * pairs, start : start + 2 * per_plane]
            swapped = pltpu.roll(both, per_plane, 1)
            if third % 2:
                both, swapped = swapped, both
            doubled = jnp.where(lane < per_plane, both, swapped)
            doubled = jnp.concatenate([doubled] * (atoms // 2), axis=1)
            rows.append(jnp.where(same_atom, doubled, 0.0))
        expanded.append(jnp.concatenate(rows, axis=0).astype(jnp.bfloat16))
    high, low = expanded

    place = []
    spot = lax.broadcasted_iota(jnp.int32, (per_plane, cell_count), 0)
    place_lane = lax.broadcasted_iota(jnp.int32, (per_plane, cell_count), 1)
    for atom in range(atoms):
        x_start = lax.rem(first_at_ref[atom] - SIDE // 2 - own_start + 2 * x_size, x_size)
        y_start = lax.rem(second_at_ref[atom] - SIDE // 2 + y_size, y_size)
        x_index = x_start + spot // SIDE
        x_index = jnp.where(x_index >= x_size, x_index - x_size, x_index)
        y_index = y_start + spot % SIDE
        y_index = jnp.where(y_index >= y_size, y_index - y_size, y_index)
        target = x_index * y_size + y_index
        place.append(jnp.where(place_lane == target, 1.0, 0.0).astype(jnp.bfloat16))
    place = jnp.concatenate(place, axis=0)
    q_high = matmul(high, place)
    q_ref[...] = q_high.astype(jnp.bfloat16)
    q_high = q_high.T.astype(jnp.bfloat16)
    left_ref[:, 0:cell_count] = plane_ref[...]
    left_ref[:, cell_count : cell_count + spots] = q_high
    left_ref[:, cell_count + spots : cell_count + 2 * spots] = q_high
    left_ref[:, cell_count + 2 * spots :] = matmul(low, place).T.astype(jnp.bfloat16)

    z_lane = lax.broadcasted_iota(jnp.int32, (nproj, z_size), 1)
    for third in range(SIDE):
        for atom in range(atoms):
            z_index = lax.rem(third_at_ref[atom] + third - SIDE // 2 + z_size, z_size)
            start = third * pairs + atom * nproj
            mask_ref[start : start + nproj] = jnp.where(z_lane == z_index, 1.0, 0.0)
    sublane = lax.broadcasted_iota(jnp.int32, (nproj, z_size), 0)
    energy = jnp.zeros((nproj, z_size), jnp.float32)
    for index in range(nproj):
        energy = jnp.where(sublane == index, energy_at_ref[index], energy)
    energy = energy * (1.0 / (unit * filter_width))
    for atom in range(atoms):
        energy_ref[atom * nproj : (atom + 1) * nproj] = energy

    diagonal_ref[...] = (field_ref[0].reshape(own, z_size) + shift) / filter_width


def packed_rotation(rotation_ref, z_size):
    count, wide = rotation_ref.shape
    spare = z_size - wide
    block = jnp.concatenate(
        (rotation_ref[...].astype(jnp.float32), jnp.zeros((count, spare), jnp.float32)), axis=1
    )
    block = jnp.concatenate((block, jnp.zeros((8 - count, z_size), jnp.float32)), axis=0)
    sublane = lax.broadcasted_iota(jnp.int32, (8, z_size), 0)
    lane = lax.broadcasted_iota(jnp.int32, (8, z_size), 1)
    packed = block
    for piece in range(-(-wide // spare)):
        moved = pltpu.roll(block, (piece - (count - 1)) % 8, 0)
        moved = pltpu.roll(moved, (wide - piece * spare) % z_size, 1)
        packed = jnp.where((sublane == piece) & (lane >= wide), moved, packed)
    return packed


def filter_kernel(
    received_ref,
    q_ref,
    left_ref,
    mask_ref,
    energy_ref,
    diagonal_ref,
    partner_diagonal_ref,
    third_ref,
    out_ref,
    rows_ref,
    right_ref,
    start_ref,
    first_ref,
    result_ref,
    sem_ref,
):
    count, block_x, y_size, z_size = out_ref.shape[1:]
    own = block_x * y_size
    cells = 2 * own
    used = count * block_x
    spots = mask_ref.shape[0]
    depth = cells + 2 * spots
    pitch = y_size + 1
    unit, _ = shared_operator()
    me = lax.axis_index("dom")
    groups = [range(first, min(first + 2, count)) for first in range(0, count, 2)]
    lanes_of = [slice(group[0] * z_size, (group[-1] + 1) * z_size) for group in groups]
    made = [{} for _ in groups]
    stores = []

    def column(position):
        return slice(position * z_size, (position + 1) * z_size)

    def relayout(index):
        first = groups[index][0] * block_x
        last = (groups[index][-1] + 1) * block_x
        begin, end = first // 16 * 16, -(-last // 16) * 16
        for half in range(2):
            for part in range(y_size):
                values = received_ref[(me ^ half) * y_size + part, begin:end].astype(jnp.float32)
                where = pl.ds(first * pitch + part, last - first, stride=pitch)
                rows_ref[half, where, :] = values[first - begin : last - begin]

    def load(index):
        for orbital in groups[index]:
            for half in range(2):
                planes = [
                    rows_ref[half, pl.ds((orbital * block_x + plane) * pitch, y_size), :]
                    for plane in range(block_x)
                ]
                values = jnp.concatenate(planes, axis=0).astype(jnp.bfloat16)
                right_ref[half * own : (half + 1) * own, column(orbital)] = values
                start_ref[half * own : (half + 1) * own, column(orbital)] = values

    def project(index):
        made[index]["products"] = matmul(q_ref[...], right_ref[0:cells, lanes_of[index]])

    def spread_first(index):
        coeff_ref = right_ref.at[cells:depth]
        spread(made[index]["products"], lanes_of[index], mask_ref, energy_ref, coeff_ref)

    def spread_second(index):
        coeff_ref = right_ref.at[cells:]
        spread(made[index]["products"], lanes_of[index], mask_ref, energy_ref, coeff_ref)

    def along(index, rows):
        wide = len(groups[index]) * z_size
        values = right_ref[0:rows, lanes_of[index]]
        made[index]["along"] = matmul(values, third_ref[0:wide, 0:wide])

    def along_first(index):
        along(index, cells)

    def along_second(index):
        along(index, own)

    def plane_first(index):
        summed = matmul(left_ref[:, 0:depth], right_ref[0:depth, lanes_of[index]])
        made[index]["summed"] = summed + made[index]["along"]

    def plane_second(index):
        summed = matmul(left_ref[0:own], right_ref[:, lanes_of[index]])
        made[index]["summed"] = summed + made[index]["along"]

    def finish_first(index):
        for position, orbital in enumerate(groups[index]):
            values = unit * made[index]["summed"][:, column(position)]
            start = start_ref[:, column(orbital)].astype(jnp.float32)
            mine = diagonal_ref[...] * start[0:own] + values[0:own]
            other = partner_diagonal_ref[...] * start[own:] + values[own:]
            first_ref[:, column(orbital)] = mine
            right_ref[0:own, column(orbital)] = mine.astype(jnp.bfloat16)
            right_ref[own:cells, column(orbital)] = other.astype(jnp.bfloat16)

    def finish_second(index):
        for position, orbital in enumerate(groups[index]):
            values = unit * made[index]["summed"][:, column(position)]
            values = diagonal_ref[...] * first_ref[:, column(orbital)] + values
            start = start_ref[0:own, column(orbital)].astype(jnp.float32)
            values = (2.0 * values - start).astype(jnp.bfloat16)
            result_ref[orbital] = values.reshape(block_x, y_size, z_size)
            stores.append(
                pltpu.make_async_copy(
                    result_ref.at[orbital], out_ref.at[0, orbital], sem_ref.at[orbital]
                )
            )
            stores[-1].start()

    steps = (
        relayout,
        load,
        project,
        along_first,
        spread_first,
        plane_first,
        finish_first,
        project,
        along_second,
        spread_second,
        plane_second,
        finish_second,
    )
    for time in range(len(steps) + 2 * len(groups) - 2):
        for index in range(len(groups)):
            if 0 <= time - 2 * index < len(steps):
                steps[time - 2 * index](index)
    for store in stores:
        store.wait()


def rotate_kernel(received_ref, after_ref, out_ref, wide_ref, rows_ref, *, count, block_x):
    sources, chunk, z_size = received_ref.shape
    total = sources * count
    used = count * block_x
    spare = z_size - total
    pitch = chunk + 1
    for part in range(sources):
        wide_ref[pl.ds(part * pitch, chunk), :] = received_ref[part].astype(jnp.float32)
    packed = [wide_ref[pl.ds(used + row, sources, stride=pitch), :] for row in range(count - 1)]
    lane = lax.broadcasted_iota(jnp.int32, (sources, z_size), 1)
    last = jnp.zeros((sources, z_size), jnp.float32)
    for piece in range(-(-total // spare)):
        moved = pltpu.roll(packed[piece], (piece * spare - total) % z_size, 1)
        last = jnp.where(lane >= piece * spare, moved, last)
    rotation = jnp.concatenate(packed + [last], axis=0)[:, 0:total].astype(jnp.bfloat16)
    columns = []
    for plane in range(block_x):
        rows = [
            wide_ref[pl.ds(orbital * block_x + plane, sources, stride=pitch), :]
            for orbital in range(count)
        ]
        columns.append(jnp.concatenate(rows, axis=0).astype(jnp.bfloat16))
    values = jnp.concatenate(columns, axis=1)
    rotated = lax.dot_general(
        rotation, values, (((0,), (0,)), ((), ())), preferred_element_type=jnp.float32
    )
    rows_ref[total * block_x :] = jnp.zeros((chunk - used, z_size), jnp.float32)
    for plane in range(block_x):
        lanes = slice(plane * z_size, (plane + 1) * z_size)
        rows_ref[pl.ds(plane, total, stride=block_x), :] = rotated[:, lanes]
    for part in range(sources):
        values = rows_ref[part * used : part * used + chunk].astype(jnp.bfloat16)
        out_ref[part] = values
        out_ref[sources + part] = values


def in_vmem(count):
    return [pl.BlockSpec(memory_space=pltpu.VMEM)] * count


def in_smem(count):
    return [pl.BlockSpec(memory_space=pltpu.SMEM)] * count


def params(mib):
    return pltpu.CompilerParams(vmem_limit_bytes=mib * MIB)


def shape_of(shape, kind):
    return jax.ShapeDtypeStruct(shape, kind)


def pair_body(
    orbitals, potential, projectors, projector_energy, atom_first, atom_second, atom_third, rotation
):
    bf16, f32 = jnp.bfloat16, jnp.float32
    count, block_x, y_size, z_size = orbitals.shape[1:]
    x_size = 2 * block_x
    own = block_x * y_size
    cell_count = x_size * y_size
    atoms, nproj = projectors.shape[:2]
    spots = SIDE * atoms * nproj
    sources = lax.axis_size("orb")
    used = count * block_x
    chunk = -(-(used + count - 1) // 16) * 16

    height = 8
    packed, after = pl.pallas_call(
        pack_kernel,
        out_shape=(shape_of((sources, chunk, z_size), bf16), shape_of((8, z_size), f32)),
        grid=(y_size // height,),
        in_specs=[
            pl.BlockSpec((1, count, block_x, height, z_size), lambda step: (0, 0, 0, step, 0)),
            pl.BlockSpec(rotation.shape, lambda step: (0, 0)),
        ],
        out_specs=(
            pl.BlockSpec((height, chunk, z_size), lambda step: (step, 0, 0)),
            pl.BlockSpec((8, z_size), lambda step: (0, 0)),
        ),
        scratch_shapes=[pltpu.VMEM((height * (chunk + 8), z_size), f32)],
        compiler_params=params(60),
        name="pack",
    )(orbitals, rotation)
    by_plane = lax.all_to_all(packed, "orb", split_axis=0, concat_axis=0, tiled=True)

    q, left, mask, energy, diagonal = pl.pallas_call(
        table_kernel,
        out_shape=(
            shape_of((spots, cell_count), bf16),
            shape_of((cell_count, cell_count + 3 * spots), bf16),
            shape_of((spots, z_size), f32),
            shape_of((atoms * nproj, z_size), f32),
            shape_of((own, z_size), f32),
        ),
        in_specs=in_smem(4) + [pl.BlockSpec(memory_space=pl.ANY)] + in_vmem(4),
        out_specs=tuple(in_vmem(5)),
        compiler_params=params(24),
        cost_estimate=pl.CostEstimate(flops=1 << 31, bytes_accessed=6 << 20, transcendentals=0),
        name="tables",
    )(
        atom_first,
        atom_second,
        atom_third,
        projector_energy,
        after,
        projectors,
        third_first(),
        plane_stencil(x_size, y_size),
        potential,
    )
    partner_diagonal = lax.ppermute(diagonal, "dom", [(0, 1), (1, 0)])

    rotated = pl.pallas_call(
        functools.partial(rotate_kernel, count=count, block_x=block_x),
        out_shape=shape_of((2 * sources, chunk, z_size), bf16),
        in_specs=in_vmem(2),
        out_specs=in_vmem(1)[0],
        scratch_shapes=[
            pltpu.VMEM((sources * (chunk + 8), z_size), f32),
            pltpu.VMEM((sources * used + chunk - used, z_size), f32),
        ],
        compiler_params=params(24),
        name="rotate",
    )(by_plane, partner_diagonal)
    by_orbital = lax.all_to_all(rotated, ("dom", "orb"), split_axis=0, concat_axis=0, tiled=True)

    return pl.pallas_call(
        filter_kernel,
        out_shape=shape_of(orbitals.shape, bf16),
        in_specs=in_vmem(8),
        out_specs=pl.BlockSpec(memory_space=pltpu.HBM),
        scratch_shapes=[
            pltpu.VMEM((2, used * (y_size + 8), z_size), f32),
            pltpu.VMEM((cell_count + 3 * spots, count * z_size), bf16),
            pltpu.VMEM((cell_count, count * z_size), bf16),
            pltpu.VMEM((own, count * z_size), f32),
            pltpu.VMEM(orbitals.shape[1:], bf16),
            pltpu.SemaphoreType.DMA((count,)),
        ],
        compiler_params=params(40),
        name="filter",
    )(
        by_orbital,
        q,
        left,
        mask,
        energy,
        diagonal,
        partner_diagonal,
        third_stencil(z_size),
    )


def fits_pair(mesh, orbitals, projectors, rotation):
    count = orbitals.shape[1] // mesh.shape["orb"]
    return (
        mesh.shape["dom"] == 2
        and orbitals.shape[3] == mesh.shape["orb"]
        and orbitals.shape[2] == 2 * stencil_reach
        and projectors.shape[0] % 2 == 0
        and projectors.shape[1] == 8
        and count <= 8
        and rotation.shape[1] < orbitals.shape[4]
        and -(-rotation.shape[1] // (orbitals.shape[4] - rotation.shape[1])) < count
    )


def solution(mesh):
    def whole(*arrays):
        chosen = pair_body if fits_pair(mesh, arrays[0], arrays[2], arrays[7]) else body
        return jax.shard_map(
            chosen,
            mesh=mesh,
            in_specs=(
                P("dom", "orb", None, None, None),
                P("dom", None, None, None),
                P(),
                P(),
                P(),
                P(),
                P(),
                P("orb", None),
            ),
            out_specs=P("dom", "orb", None, None, None),
            check_vma=False,
        )(*arrays)

    return whole
```

```python
import functools

import jax
import jax.numpy as jnp
import numpy as np
from jax import lax
from jax.experimental import pallas as pl
from jax.experimental.pallas import tpu as pltpu
from jax.sharding import PartitionSpec as P

SIDE = 8
SUP = 512


stencil_weights = (
    -5369.0 / 1800.0,
    12.0 / 7.0,
    -15.0 / 56.0,
    10.0 / 189.0,
    -1.0 / 112.0,
    2.0 / 1925.0,
    -1.0 / 16632.0,
)
inverse_spacing = 4.0
filter_center = 120.0
filter_width = 110.0
stencil_reach = 6


def partner_2(block, axis, bit):
    count = lax.axis_size(axis)
    route = []
    for low in range(count):
        high = low | 1 << bit
        if high != low and high < count:
            route += [(low, high), (high, low)]
    return lax.ppermute(block, axis, route)


def outgoing(values, direction, width):
    extent = values.shape[direction]
    if 2 * width < extent:
        return jnp.concatenate(
            (
                lax.slice_in_dim(values, 0, width, axis=direction),
                lax.slice_in_dim(values, extent - width, extent, axis=direction),
            ),
            axis=direction,
        )
    return values


def assemble(values, partner, direction, width):
    extent = values.shape[direction]
    if 2 * width < extent:
        lower_rim = lax.slice_in_dim(partner, width, 2 * width, axis=direction)
        upper_rim = lax.slice_in_dim(partner, 0, width, axis=direction)
        return jnp.concatenate((lower_rim, values, upper_rim), axis=direction)
    cyclic = jnp.concatenate((values, partner), axis=direction)
    chosen = np.arange(-width, extent + width) % (2 * extent)
    return jnp.take(cyclic, jnp.asarray(chosen, dtype=jnp.int32), axis=direction)


def face_padded(values, direction, bit_number):
    sent = outgoing(values, direction, stencil_reach)
    partner = partner_2(sent.astype(jnp.bfloat16), "dom", bit_number).astype(sent.dtype)
    return assemble(values, partner, direction, stencil_reach)


def stencil_sum(center, along):
    lead = center.ndim - 3
    summed = 3.0 * stencil_weights[0] * center
    for index in range(3):
        direction = lead + index
        extent = center.shape[direction]
        padded = along[index]
        for offset in range(1, 7):
            if padded is None:
                upward = jnp.roll(center, -offset, direction)
                downward = jnp.roll(center, offset, direction)
            else:
                upward = lax.slice_in_dim(
                    padded, stencil_reach + offset, stencil_reach + offset + extent, axis=direction
                )
                downward = lax.slice_in_dim(
                    padded, stencil_reach - offset, stencil_reach - offset + extent, axis=direction
                )
            summed = summed + stencil_weights[offset] * (upward + downward)
    return summed


def support_map(atom_coords, starts, extents, periods):
    offsets = jnp.arange(SIDE, dtype=jnp.int32) - SIDE // 2
    clipped_list = []
    inside_list = []
    for index in range(3):
        local = (atom_coords[index][:, None] + offsets[None, :] - starts[index]) % periods[index]
        inside_list.append(local < extents[index])
        clipped_list.append(jnp.minimum(local, extents[index] - 1))
    inside = (
        inside_list[0][:, :, None, None]
        & inside_list[1][:, None, :, None]
        & inside_list[2][:, None, None, :]
    )
    flattened = (
        clipped_list[0][:, :, None, None] * extents[1] + clipped_list[1][:, None, :, None]
    ) * extents[2] + clipped_list[2][:, None, None, :]
    atom_count = atom_coords[0].shape[0]
    return (
        flattened.reshape(atom_count * SUP),
        inside.reshape(atom_count, SUP).astype(jnp.float32),
    )


def coefficients(values, support, inside, projectors):
    orbital_count = values.shape[0]
    atom_count = projectors.shape[0]
    flattened = values.reshape(orbital_count, -1)
    picked = (
        jnp.take(flattened, support, axis=1).reshape(orbital_count, atom_count, SUP) * inside[None]
    )
    partial_coeffs = jnp.einsum("aps,kas->kap", projectors, picked, precision=lax.Precision.HIGHEST)
    return lax.psum(partial_coeffs, "dom")


def spread_into(coeffs, shape, support, inside, projectors, projector_energy):
    orbital_count = shape[0]
    atom_count = projectors.shape[0]
    scaled = coeffs * projector_energy[None, None, :]
    spread = (
        jnp.einsum("aps,kap->kas", projectors, scaled, precision=lax.Precision.HIGHEST)
        * inside[None]
    )
    total_cells = shape[1] * shape[2] * shape[3]
    projected_part = (
        jnp.zeros((orbital_count, total_cells), jnp.float32)
        .at[:, support]
        .add(spread.reshape(orbital_count, atom_count * SUP))
    )
    return projected_part.reshape(shape)


def own_hamiltonian(center, along, local_field, support, inside, projectors, projector_energy):
    kinetic = -0.5 * inverse_spacing * inverse_spacing
    coeffs = coefficients(center, support, inside, projectors)
    projected_part = spread_into(
        coeffs, center.shape, support, inside, projectors, projector_energy
    )
    return kinetic * stencil_sum(center, along) + local_field[None] * center + projected_part


def body(
    orbitals, potential, projectors, projector_energy, atom_first, atom_second, atom_third, rotation
):
    domain_count = lax.axis_size("dom")
    domain_bits = domain_count.bit_length() - 1
    split = [index < domain_bits for index in range(3)]
    start_values = orbitals[0]
    local_field = potential[0]
    extents = start_values.shape[1:]
    periods = (
        extents[0] * min(domain_count, 2),
        extents[1] * min(max(domain_count // 2, 1), 2),
        extents[2] * max(domain_count // 4, 1),
    )
    domain_index = lax.axis_index("dom")
    anchors = (
        domain_index % 2 * extents[0],
        domain_index // 2 % 2 * extents[1],
        domain_index // 4 * extents[2],
    )
    atom_coords = (atom_first, atom_second, atom_third)
    support, inside = support_map(atom_coords, anchors, extents, periods)
    along = [
        face_padded(start_values, index + 1, index) if split[index] else None for index in range(3)
    ]
    first_apply = own_hamiltonian(
        start_values, along, local_field, support, inside, projectors, projector_energy
    )
    first_term = (first_apply - filter_center * start_values) / filter_width
    along = [
        face_padded(first_term, index + 1, index) if split[index] else None for index in range(3)
    ]
    second_apply = own_hamiltonian(
        first_term, along, local_field, support, inside, projectors, projector_energy
    )
    second_term = 2.0 * (second_apply - filter_center * first_term) / filter_width - start_values
    per_device = start_values.shape[0]
    filtered = second_term.astype(jnp.bfloat16).reshape(per_device, -1)
    by_cells = lax.all_to_all(filtered, "orb", split_axis=1, concat_axis=0, tiled=True)
    whole_rotation = lax.all_gather(rotation, "orb", axis=0, tiled=True)
    rotated = lax.dot_general(
        whole_rotation, by_cells, (((0,), (0,)), ((), ())), preferred_element_type=jnp.float32
    ).astype(jnp.bfloat16)
    result = lax.all_to_all(rotated, "orb", split_axis=0, concat_axis=1, tiled=True)
    return result.reshape((1,) + start_values.shape)


SCALE = 15.0
MIB = 1 << 20


def scaled_weights():
    ratios = np.array(stencil_weights[1:], np.float64) / stencil_weights[1]
    return SCALE * ratios


def cyclic_stencil(size):
    matrix = np.zeros((size, size), np.float64)
    rows = np.arange(size)
    for offset, weight in enumerate(scaled_weights(), 1):
        np.add.at(matrix, (rows, (rows + offset) % size), weight)
        np.add.at(matrix, (rows, (rows - offset) % size), weight)
    return matrix


def plane_stencil(x_size, y_size):
    matrix = np.kron(cyclic_stencil(x_size), np.eye(y_size))
    matrix += np.kron(np.eye(x_size), cyclic_stencil(y_size))
    return matrix.astype(jnp.bfloat16)


def third_stencil(z_size):
    matrix = cyclic_stencil(z_size)
    return np.kron(np.eye(2), matrix).astype(jnp.bfloat16)


def third_first():
    picked = np.zeros((SUP, SUP), np.float32)
    source = np.arange(SUP)
    picked[source, source % SIDE * SIDE * SIDE + source // SIDE] = 1.0
    return picked.astype(jnp.bfloat16)


def halves(values):
    high = values.astype(jnp.bfloat16)
    return high, (values - high.astype(jnp.float32)).astype(jnp.bfloat16)


def matmul(left, right):
    return jnp.dot(left, right, preferred_element_type=jnp.float32)


def shared_operator():
    kinetic = -0.5 * inverse_spacing * inverse_spacing
    unit = kinetic * stencil_weights[1] / SCALE / filter_width
    shift = 3.0 * kinetic * stencil_weights[0] - filter_center
    return unit, shift


def pack_kernel(orbital_ref, rotation_ref, out_ref, after_ref, chunk_ref):
    count, block_x, height, z_size = orbital_ref.shape[1:]
    chunk = out_ref.shape[2] // 2
    used = count * block_x
    pitch = chunk + 1
    packed = packed_rotation(rotation_ref, z_size)
    after_ref[...] = packed
    for orbital in range(count):
        for plane in range(block_x):
            start = orbital * block_x + plane
            chunk_ref[pl.ds(start, height, stride=pitch), :] = orbital_ref[0, orbital, plane]
    for part in range(height):
        start = part * pitch
        chunk_ref[start + used : start + used + count - 1] = packed[0 : count - 1]
        values = chunk_ref[start : start + chunk].astype(jnp.bfloat16)
        rows = slice(part % 2 * chunk, (part % 2 + 1) * chunk)
        out_ref[0, part // 2, rows] = values
        out_ref[1, part // 2, rows] = values


def spread(products, lanes, mask_ref, energy_ref, coeff_ref):
    spots, z_size = mask_ref.shape
    pairs = energy_ref.shape[0]
    mask = mask_ref[...]
    for start in range(0, products.shape[1], z_size):
        picked = products[:, start : start + z_size] * mask
        coeffs = jnp.sum(picked.reshape(SIDE, pairs, z_size), axis=0)
        coeffs = jnp.sum(coeffs, axis=1, keepdims=True)
        high, low = halves(jnp.concatenate([coeffs * energy_ref[...]] * SIDE, axis=0) * mask)
        columns = slice(lanes.start + start, lanes.start + start + z_size)
        coeff_ref[0:spots, columns] = high
        coeff_ref[spots : 2 * spots, columns] = low
        if coeff_ref.shape[0] > 2 * spots:
            coeff_ref[2 * spots :, columns] = high


def table_kernel(
    first_at_ref,
    second_at_ref,
    third_at_ref,
    energy_at_ref,
    after_ref,
    projector_ref,
    order_ref,
    plane_ref,
    field_ref,
    q_ref,
    left_ref,
    mask_ref,
    energy_ref,
    diagonal_ref,
):
    block_x, y_size, z_size = field_ref.shape[1:]
    x_size = 2 * block_x
    own = block_x * y_size
    cell_count = x_size * y_size
    atoms, nproj = projector_ref.shape[:2]
    pairs = atoms * nproj
    per_plane = SIDE * SIDE
    spots = atoms * per_plane
    unit, shift = shared_operator()
    own_start = lax.axis_index("dom") * block_x
    high, low = halves(projector_ref[...].reshape(pairs, SUP))
    ordered = matmul(jnp.concatenate((high, low), axis=0), order_ref[...])

    lane = lax.broadcasted_iota(jnp.int32, (pairs, 2 * per_plane), 1)
    row_atom = lax.broadcasted_iota(jnp.int32, (pairs, spots), 0) // nproj
    lane_atom = lax.broadcasted_iota(jnp.int32, (pairs, spots), 1) // per_plane
    same_atom = row_atom == lane_atom
    expanded = []
    for part in range(2):
        rows = []
        for third in range(SIDE):
            start = third // 2 * 2 * per_plane
            both = ordered[part * pairs : (part + 1) * pairs, start : start + 2 * per_plane]
            swapped = pltpu.roll(both, per_plane, 1)
            if third % 2:
                both, swapped = swapped, both
            doubled = jnp.where(lane < per_plane, both, swapped)
            doubled = jnp.concatenate([doubled] * (atoms // 2), axis=1)
            rows.append(jnp.where(same_atom, doubled, 0.0))
        expanded.append(jnp.concatenate(rows, axis=0).astype(jnp.bfloat16))
    high, low = expanded

    place = []
    spot = lax.broadcasted_iota(jnp.int32, (per_plane, cell_count), 0)
    place_lane = lax.broadcasted_iota(jnp.int32, (per_plane, cell_count), 1)
    for atom in range(atoms):
        x_start = lax.rem(first_at_ref[atom] - SIDE // 2 - own_start + 2 * x_size, x_size)
        y_start = lax.rem(second_at_ref[atom] - SIDE // 2 + y_size, y_size)
        x_index = x_start + spot // SIDE
        x_index = jnp.where(x_index >= x_size, x_index - x_size, x_index)
        y_index = y_start + spot % SIDE
        y_index = jnp.where(y_index >= y_size, y_index - y_size, y_index)
        target = x_index * y_size + y_index
        place.append(jnp.where(place_lane == target, 1.0, 0.0).astype(jnp.bfloat16))
    place = jnp.concatenate(place, axis=0)
    q_high = matmul(high, place)
    q_ref[...] = q_high.astype(jnp.bfloat16)
    q_high = q_high.T.astype(jnp.bfloat16)
    left_ref[:, 0:cell_count] = plane_ref[...]
    left_ref[:, cell_count : cell_count + spots] = q_high
    left_ref[:, cell_count + spots : cell_count + 2 * spots] = q_high
    left_ref[:, cell_count + 2 * spots :] = matmul(low, place).T.astype(jnp.bfloat16)

    z_lane = lax.broadcasted_iota(jnp.int32, (nproj, z_size), 1)
    for third in range(SIDE):
        for atom in range(atoms):
            z_index = lax.rem(third_at_ref[atom] + third - SIDE // 2 + z_size, z_size)
            start = third * pairs + atom * nproj
            mask_ref[start : start + nproj] = jnp.where(z_lane == z_index, 1.0, 0.0)
    sublane = lax.broadcasted_iota(jnp.int32, (nproj, z_size), 0)
    energy = jnp.zeros((nproj, z_size), jnp.float32)
    for index in range(nproj):
        energy = jnp.where(sublane == index, energy_at_ref[index], energy)
    energy = energy * (1.0 / (unit * filter_width))
    for atom in range(atoms):
        energy_ref[atom * nproj : (atom + 1) * nproj] = energy

    diagonal_ref[...] = (field_ref[0].reshape(own, z_size) + shift) / filter_width


def packed_rotation(rotation_ref, z_size):
    count, wide = rotation_ref.shape
    spare = z_size - wide
    block = jnp.concatenate(
        (rotation_ref[...].astype(jnp.float32), jnp.zeros((count, spare), jnp.float32)), axis=1
    )
    block = jnp.concatenate((block, jnp.zeros((8 - count, z_size), jnp.float32)), axis=0)
    sublane = lax.broadcasted_iota(jnp.int32, (8, z_size), 0)
    lane = lax.broadcasted_iota(jnp.int32, (8, z_size), 1)
    packed = block
    for piece in range(-(-wide // spare)):
        moved = pltpu.roll(block, (piece - (count - 1)) % 8, 0)
        moved = pltpu.roll(moved, (wide - piece * spare) % z_size, 1)
        packed = jnp.where((sublane == piece) & (lane >= wide), moved, packed)
    return packed


def filter_kernel(
    received_ref,
    q_ref,
    left_ref,
    mask_ref,
    energy_ref,
    diagonal_ref,
    partner_diagonal_ref,
    third_ref,
    out_ref,
    rows_ref,
    right_ref,
    start_ref,
    first_ref,
    result_ref,
    sem_ref,
):
    count, block_x, y_size, z_size = out_ref.shape[1:]
    own = block_x * y_size
    cells = 2 * own
    used = count * block_x
    spots = mask_ref.shape[0]
    depth = cells + 2 * spots
    pitch = y_size + 1
    chunk = received_ref.shape[1] // 2
    unit, _ = shared_operator()
    me = lax.axis_index("dom")
    for half in range(2):
        for part in range(y_size):
            source = (me ^ half) * (y_size // 2) + part // 2
            begin = part % 2 * chunk
            values = received_ref[source, begin : begin + chunk].astype(jnp.float32)
            rows_ref[half, pl.ds(part, used, stride=pitch), :] = values[0:used]

    groups = [range(first, min(first + 2, count)) for first in range(0, count, 2)]
    lanes_of = [slice(group[0] * z_size, (group[-1] + 1) * z_size) for group in groups]
    made = [{} for _ in groups]
    stores = []

    def column(position):
        return slice(position * z_size, (position + 1) * z_size)

    def load(index):
        for orbital in groups[index]:
            for half in range(2):
                planes = [
                    rows_ref[half, pl.ds((orbital * block_x + plane) * pitch, y_size), :]
                    for plane in range(block_x)
                ]
                values = jnp.concatenate(planes, axis=0).astype(jnp.bfloat16)
                right_ref[half * own : (half + 1) * own, column(orbital)] = values
                start_ref[half * own : (half + 1) * own, column(orbital)] = values

    def project(index):
        made[index]["products"] = matmul(q_ref[...], right_ref[0:cells, lanes_of[index]])

    def spread_first(index):
        coeff_ref = right_ref.at[cells:depth]
        spread(made[index]["products"], lanes_of[index], mask_ref, energy_ref, coeff_ref)

    def spread_second(index):
        coeff_ref = right_ref.at[cells:]
        spread(made[index]["products"], lanes_of[index], mask_ref, energy_ref, coeff_ref)

    def along(index, rows):
        wide = len(groups[index]) * z_size
        values = right_ref[0:rows, lanes_of[index]]
        made[index]["along"] = matmul(values, third_ref[0:wide, 0:wide])

    def along_first(index):
        along(index, cells)

    def along_second(index):
        along(index, own)

    def plane_first(index):
        summed = matmul(left_ref[:, 0:depth], right_ref[0:depth, lanes_of[index]])
        made[index]["summed"] = summed + made[index]["along"]

    def plane_second(index):
        summed = matmul(left_ref[0:own], right_ref[:, lanes_of[index]])
        made[index]["summed"] = summed + made[index]["along"]

    def finish_first(index):
        for position, orbital in enumerate(groups[index]):
            values = unit * made[index]["summed"][:, column(position)]
            start = start_ref[:, column(orbital)].astype(jnp.float32)
            mine = diagonal_ref[...] * start[0:own] + values[0:own]
            other = partner_diagonal_ref[...] * start[own:] + values[own:]
            first_ref[:, column(orbital)] = mine
            right_ref[0:own, column(orbital)] = mine.astype(jnp.bfloat16)
            right_ref[own:cells, column(orbital)] = other.astype(jnp.bfloat16)

    def finish_second(index):
        for position, orbital in enumerate(groups[index]):
            values = unit * made[index]["summed"][:, column(position)]
            values = diagonal_ref[...] * first_ref[:, column(orbital)] + values
            start = start_ref[0:own, column(orbital)].astype(jnp.float32)
            values = (2.0 * values - start).astype(jnp.bfloat16)
            result_ref[orbital] = values.reshape(block_x, y_size, z_size)
            stores.append(
                pltpu.make_async_copy(
                    result_ref.at[orbital], out_ref.at[0, orbital], sem_ref.at[orbital]
                )
            )
            stores[-1].start()

    steps = (
        load,
        project,
        along_first,
        spread_first,
        plane_first,
        finish_first,
        project,
        along_second,
        spread_second,
        plane_second,
        finish_second,
    )
    for time in range(len(steps) + 2 * len(groups) - 2):
        for index in range(len(groups)):
            if 0 <= time - 2 * index < len(steps):
                steps[time - 2 * index](index)
    for store in stores:
        store.wait()


def rotate_kernel(received_ref, after_ref, out_ref, wide_ref, rows_ref, *, count, block_x):
    sources, z_size = received_ref.shape[0], received_ref.shape[2]
    chunk = received_ref.shape[1] // 2
    targets = sources // 2
    total = sources * count
    made = targets * count
    used = count * block_x
    spare = z_size - total
    pitch = chunk + 1
    for line in range(2):
        for part in range(sources):
            values = received_ref[part, line * chunk : (line + 1) * chunk].astype(jnp.float32)
            wide_ref[line, pl.ds(part * pitch, chunk), :] = values
    packed = [wide_ref[0, pl.ds(used + row, sources, stride=pitch), :] for row in range(count - 1)]
    lane = lax.broadcasted_iota(jnp.int32, (sources, z_size), 1)
    last = jnp.zeros((sources, z_size), jnp.float32)
    for piece in range(-(-total // spare)):
        moved = pltpu.roll(packed[piece], (piece * spare - total) % z_size, 1)
        last = jnp.where(lane >= piece * spare, moved, last)
    rotation = jnp.concatenate(packed + [last], axis=0)
    upper = pltpu.roll(rotation, z_size - made, 1)
    rotation = jnp.where(lax.axis_index("half") == 0, rotation, upper)
    rotation = rotation[:, 0:made].astype(jnp.bfloat16)
    columns = []
    for line in range(2):
        for plane in range(block_x):
            rows = [
                wide_ref[line, pl.ds(orbital * block_x + plane, sources, stride=pitch), :]
                for orbital in range(count)
            ]
            columns.append(jnp.concatenate(rows, axis=0).astype(jnp.bfloat16))
    values = jnp.concatenate(columns, axis=1)
    rotated = lax.dot_general(
        rotation, values, (((0,), (0,)), ((), ())), preferred_element_type=jnp.float32
    )
    for line in range(2):
        rows_ref[line, made * block_x :] = jnp.zeros((chunk - used, z_size), jnp.float32)
        for plane in range(block_x):
            start = (line * block_x + plane) * z_size
            values = rotated[:, start : start + z_size]
            rows_ref[line, pl.ds(plane, made, stride=block_x), :] = values
        for part in range(targets):
            values = rows_ref[line, part * used : part * used + chunk].astype(jnp.bfloat16)
            out_ref[part, line * chunk : (line + 1) * chunk] = values
            out_ref[targets + part, line * chunk : (line + 1) * chunk] = values


def in_vmem(count):
    return [pl.BlockSpec(memory_space=pltpu.VMEM)] * count


def in_smem(count):
    return [pl.BlockSpec(memory_space=pltpu.SMEM)] * count


def params(mib):
    return pltpu.CompilerParams(vmem_limit_bytes=mib * MIB)


def shape_of(shape, kind):
    return jax.ShapeDtypeStruct(shape, kind)


def pair_body(
    orbitals, potential, projectors, projector_energy, atom_first, atom_second, atom_third, rotation
):
    bf16, f32 = jnp.bfloat16, jnp.float32
    count, block_x, y_size, z_size = orbitals.shape[1:]
    x_size = 2 * block_x
    own = block_x * y_size
    cell_count = x_size * y_size
    atoms, nproj = projectors.shape[:2]
    spots = SIDE * atoms * nproj
    sources = lax.axis_size("half") * lax.axis_size("rest")
    used = count * block_x
    chunk = -(-(used + count - 1) // 16) * 16

    height = 8
    packed, after = pl.pallas_call(
        pack_kernel,
        out_shape=(
            shape_of((2, sources // 2, 2 * chunk, z_size), bf16),
            shape_of((8, z_size), f32),
        ),
        grid=(y_size // height,),
        in_specs=[
            pl.BlockSpec((1, count, block_x, height, z_size), lambda step: (0, 0, 0, step, 0)),
            pl.BlockSpec(rotation.shape, lambda step: (0, 0)),
        ],
        out_specs=(
            pl.BlockSpec((2, height // 2, 2 * chunk, z_size), lambda step: (0, step, 0, 0)),
            pl.BlockSpec((8, z_size), lambda step: (0, 0)),
        ),
        scratch_shapes=[pltpu.VMEM((height * (chunk + 8), z_size), f32)],
        compiler_params=params(60),
        name="pack",
    )(orbitals, rotation)
    packed = packed.reshape(sources, 2 * chunk, z_size)
    by_plane = lax.all_to_all(packed, ("half", "rest"), split_axis=0, concat_axis=0, tiled=True)

    q, left, mask, energy, diagonal = pl.pallas_call(
        table_kernel,
        out_shape=(
            shape_of((spots, cell_count), bf16),
            shape_of((cell_count, cell_count + 3 * spots), bf16),
            shape_of((spots, z_size), f32),
            shape_of((atoms * nproj, z_size), f32),
            shape_of((own, z_size), f32),
        ),
        in_specs=in_smem(4) + [pl.BlockSpec(memory_space=pl.ANY)] + in_vmem(4),
        out_specs=tuple(in_vmem(5)),
        compiler_params=params(24),
        cost_estimate=pl.CostEstimate(flops=1 << 31, bytes_accessed=6 << 20, transcendentals=0),
        name="tables",
    )(
        atom_first,
        atom_second,
        atom_third,
        projector_energy,
        after,
        projectors,
        third_first(),
        plane_stencil(x_size, y_size),
        potential,
    )
    partner_diagonal = lax.ppermute(diagonal, "dom", [(0, 1), (1, 0)])

    rotated = pl.pallas_call(
        functools.partial(rotate_kernel, count=count, block_x=block_x),
        out_shape=shape_of((sources, 2 * chunk, z_size), bf16),
        in_specs=in_vmem(2),
        out_specs=in_vmem(1)[0],
        scratch_shapes=[
            pltpu.VMEM((2, sources * (chunk + 8), z_size), f32),
            pltpu.VMEM((2, sources // 2 * used + chunk - used, z_size), f32),
        ],
        compiler_params=params(24),
        name="rotate",
    )(by_plane, partner_diagonal)
    by_orbital = lax.all_to_all(rotated, ("dom", "rest"), split_axis=0, concat_axis=0, tiled=True)

    return pl.pallas_call(
        filter_kernel,
        out_shape=shape_of(orbitals.shape, bf16),
        in_specs=in_vmem(8),
        out_specs=pl.BlockSpec(memory_space=pltpu.HBM),
        scratch_shapes=[
            pltpu.VMEM((2, used * (y_size + 8), z_size), f32),
            pltpu.VMEM((cell_count + 3 * spots, count * z_size), bf16),
            pltpu.VMEM((cell_count, count * z_size), bf16),
            pltpu.VMEM((own, count * z_size), f32),
            pltpu.VMEM(orbitals.shape[1:], bf16),
            pltpu.SemaphoreType.DMA((count,)),
        ],
        compiler_params=params(40),
        name="filter",
    )(
        by_orbital,
        q,
        left,
        mask,
        energy,
        diagonal,
        partner_diagonal,
        third_stencil(z_size),
    )


def fits_pair(mesh, orbitals, projectors, rotation):
    count = orbitals.shape[1] // mesh.shape["orb"]
    return (
        mesh.shape["dom"] == 2
        and orbitals.shape[3] == mesh.shape["orb"]
        and orbitals.shape[2] == 2 * stencil_reach
        and projectors.shape[0] % 2 == 0
        and projectors.shape[1] == 8
        and count <= 8
        and rotation.shape[1] < orbitals.shape[4]
        and -(-rotation.shape[1] // (orbitals.shape[4] - rotation.shape[1])) < count
    )


def solution(mesh):
    def whole(*arrays):
        chosen, grid, orb = body, mesh, "orb"
        if fits_pair(mesh, arrays[0], arrays[2], arrays[7]):
            shape = (mesh.shape["dom"], 2, mesh.shape["orb"] // 2)
            names = ("dom", "half", "rest")
            grid = jax.sharding.Mesh(mesh.devices.reshape(shape), names)
            chosen, orb = pair_body, ("half", "rest")
        return jax.shard_map(
            chosen,
            mesh=grid,
            in_specs=(
                P("dom", orb, None, None, None),
                P("dom", None, None, None),
                P(),
                P(),
                P(),
                P(),
                P(),
                P(orb, None),
            ),
            out_specs=P("dom", orb, None, None, None),
            check_vma=False,
        )(*arrays)

    return whole
```

```python
import functools

import jax
import jax.numpy as jnp
import numpy as np
from jax import lax
from jax.experimental import pallas as pl
from jax.experimental.pallas import tpu as pltpu
from jax.sharding import PartitionSpec as P

SIDE = 8
SUP = 512


stencil_weights = (
    -5369.0 / 1800.0,
    12.0 / 7.0,
    -15.0 / 56.0,
    10.0 / 189.0,
    -1.0 / 112.0,
    2.0 / 1925.0,
    -1.0 / 16632.0,
)
inverse_spacing = 4.0
filter_center = 120.0
filter_width = 110.0
stencil_reach = 6


def partner_2(block, axis, bit):
    count = lax.axis_size(axis)
    route = []
    for low in range(count):
        high = low | 1 << bit
        if high != low and high < count:
            route += [(low, high), (high, low)]
    return lax.ppermute(block, axis, route)


def outgoing(values, direction, width):
    extent = values.shape[direction]
    if 2 * width < extent:
        return jnp.concatenate(
            (
                lax.slice_in_dim(values, 0, width, axis=direction),
                lax.slice_in_dim(values, extent - width, extent, axis=direction),
            ),
            axis=direction,
        )
    return values


def assemble(values, partner, direction, width):
    extent = values.shape[direction]
    if 2 * width < extent:
        lower_rim = lax.slice_in_dim(partner, width, 2 * width, axis=direction)
        upper_rim = lax.slice_in_dim(partner, 0, width, axis=direction)
        return jnp.concatenate((lower_rim, values, upper_rim), axis=direction)
    cyclic = jnp.concatenate((values, partner), axis=direction)
    chosen = np.arange(-width, extent + width) % (2 * extent)
    return jnp.take(cyclic, jnp.asarray(chosen, dtype=jnp.int32), axis=direction)


def face_padded(values, direction, bit_number):
    sent = outgoing(values, direction, stencil_reach)
    partner = partner_2(sent.astype(jnp.bfloat16), "dom", bit_number).astype(sent.dtype)
    return assemble(values, partner, direction, stencil_reach)


def stencil_sum(center, along):
    lead = center.ndim - 3
    summed = 3.0 * stencil_weights[0] * center
    for index in range(3):
        direction = lead + index
        extent = center.shape[direction]
        padded = along[index]
        for offset in range(1, 7):
            if padded is None:
                upward = jnp.roll(center, -offset, direction)
                downward = jnp.roll(center, offset, direction)
            else:
                upward = lax.slice_in_dim(
                    padded, stencil_reach + offset, stencil_reach + offset + extent, axis=direction
                )
                downward = lax.slice_in_dim(
                    padded, stencil_reach - offset, stencil_reach - offset + extent, axis=direction
                )
            summed = summed + stencil_weights[offset] * (upward + downward)
    return summed


def support_map(atom_coords, starts, extents, periods):
    offsets = jnp.arange(SIDE, dtype=jnp.int32) - SIDE // 2
    clipped_list = []
    inside_list = []
    for index in range(3):
        local = (atom_coords[index][:, None] + offsets[None, :] - starts[index]) % periods[index]
        inside_list.append(local < extents[index])
        clipped_list.append(jnp.minimum(local, extents[index] - 1))
    inside = (
        inside_list[0][:, :, None, None]
        & inside_list[1][:, None, :, None]
        & inside_list[2][:, None, None, :]
    )
    flattened = (
        clipped_list[0][:, :, None, None] * extents[1] + clipped_list[1][:, None, :, None]
    ) * extents[2] + clipped_list[2][:, None, None, :]
    atom_count = atom_coords[0].shape[0]
    return (
        flattened.reshape(atom_count * SUP),
        inside.reshape(atom_count, SUP).astype(jnp.float32),
    )


def coefficients(values, support, inside, projectors):
    orbital_count = values.shape[0]
    atom_count = projectors.shape[0]
    flattened = values.reshape(orbital_count, -1)
    picked = (
        jnp.take(flattened, support, axis=1).reshape(orbital_count, atom_count, SUP) * inside[None]
    )
    partial_coeffs = jnp.einsum("aps,kas->kap", projectors, picked, precision=lax.Precision.HIGHEST)
    return lax.psum(partial_coeffs, "dom")


def spread_into(coeffs, shape, support, inside, projectors, projector_energy):
    orbital_count = shape[0]
    atom_count = projectors.shape[0]
    scaled = coeffs * projector_energy[None, None, :]
    spread = (
        jnp.einsum("aps,kap->kas", projectors, scaled, precision=lax.Precision.HIGHEST)
        * inside[None]
    )
    total_cells = shape[1] * shape[2] * shape[3]
    projected_part = (
        jnp.zeros((orbital_count, total_cells), jnp.float32)
        .at[:, support]
        .add(spread.reshape(orbital_count, atom_count * SUP))
    )
    return projected_part.reshape(shape)


def own_hamiltonian(center, along, local_field, support, inside, projectors, projector_energy):
    kinetic = -0.5 * inverse_spacing * inverse_spacing
    coeffs = coefficients(center, support, inside, projectors)
    projected_part = spread_into(
        coeffs, center.shape, support, inside, projectors, projector_energy
    )
    return kinetic * stencil_sum(center, along) + local_field[None] * center + projected_part


def body(
    orbitals, potential, projectors, projector_energy, atom_first, atom_second, atom_third, rotation
):
    domain_count = lax.axis_size("dom")
    domain_bits = domain_count.bit_length() - 1
    split = [index < domain_bits for index in range(3)]
    start_values = orbitals[0]
    local_field = potential[0]
    extents = start_values.shape[1:]
    periods = (
        extents[0] * min(domain_count, 2),
        extents[1] * min(max(domain_count // 2, 1), 2),
        extents[2] * max(domain_count // 4, 1),
    )
    domain_index = lax.axis_index("dom")
    anchors = (
        domain_index % 2 * extents[0],
        domain_index // 2 % 2 * extents[1],
        domain_index // 4 * extents[2],
    )
    atom_coords = (atom_first, atom_second, atom_third)
    support, inside = support_map(atom_coords, anchors, extents, periods)
    along = [
        face_padded(start_values, index + 1, index) if split[index] else None for index in range(3)
    ]
    first_apply = own_hamiltonian(
        start_values, along, local_field, support, inside, projectors, projector_energy
    )
    first_term = (first_apply - filter_center * start_values) / filter_width
    along = [
        face_padded(first_term, index + 1, index) if split[index] else None for index in range(3)
    ]
    second_apply = own_hamiltonian(
        first_term, along, local_field, support, inside, projectors, projector_energy
    )
    second_term = 2.0 * (second_apply - filter_center * first_term) / filter_width - start_values
    per_device = start_values.shape[0]
    filtered = second_term.astype(jnp.bfloat16).reshape(per_device, -1)
    by_cells = lax.all_to_all(filtered, "orb", split_axis=1, concat_axis=0, tiled=True)
    whole_rotation = lax.all_gather(rotation, "orb", axis=0, tiled=True)
    rotated = lax.dot_general(
        whole_rotation, by_cells, (((0,), (0,)), ((), ())), preferred_element_type=jnp.float32
    ).astype(jnp.bfloat16)
    result = lax.all_to_all(rotated, "orb", split_axis=0, concat_axis=1, tiled=True)
    return result.reshape((1,) + start_values.shape)


SCALE = 15.0
MIB = 1 << 20


def scaled_weights():
    ratios = np.array(stencil_weights[1:], np.float64) / stencil_weights[1]
    return SCALE * ratios


def cyclic_stencil(size):
    matrix = np.zeros((size, size), np.float64)
    rows = np.arange(size)
    for offset, weight in enumerate(scaled_weights(), 1):
        np.add.at(matrix, (rows, (rows + offset) % size), weight)
        np.add.at(matrix, (rows, (rows - offset) % size), weight)
    return matrix


def plane_stencil(x_size, y_size):
    matrix = np.kron(cyclic_stencil(x_size), np.eye(y_size))
    matrix += np.kron(np.eye(x_size), cyclic_stencil(y_size))
    return matrix.astype(jnp.bfloat16)


def third_stencil(z_size):
    matrix = cyclic_stencil(z_size)
    return np.kron(np.eye(2), matrix).astype(jnp.bfloat16)


def third_first():
    picked = np.zeros((SUP, SUP), np.float32)
    source = np.arange(SUP)
    picked[source, source % SIDE * SIDE * SIDE + source // SIDE] = 1.0
    return picked.astype(jnp.bfloat16)


def halves(values):
    high = values.astype(jnp.bfloat16)
    return high, (values - high.astype(jnp.float32)).astype(jnp.bfloat16)


def matmul(left, right):
    return jnp.dot(left, right, preferred_element_type=jnp.float32)


def shared_operator():
    kinetic = -0.5 * inverse_spacing * inverse_spacing
    unit = kinetic * stencil_weights[1] / SCALE / filter_width
    shift = 3.0 * kinetic * stencil_weights[0] - filter_center
    return unit, shift


def pack_kernel(orbital_ref, rotation_ref, out_ref, after_ref, chunk_ref):
    count, block_x, height, z_size = orbital_ref.shape[1:]
    chunk = out_ref.shape[1]
    used = count * block_x
    pitch = chunk + 1
    packed = packed_rotation(rotation_ref, z_size)
    after_ref[...] = packed
    for orbital in range(count):
        for plane in range(block_x):
            start = orbital * block_x + plane
            chunk_ref[pl.ds(start, height, stride=pitch), :] = orbital_ref[0, orbital, plane]
    for part in range(height):
        start = part * pitch
        chunk_ref[start + used : start + used + count - 1] = packed[0 : count - 1]
        out_ref[part] = chunk_ref[start : start + chunk].astype(jnp.bfloat16)


def spread(products, lanes, mask_ref, marks_ref, energy_ref, coeff_ref):
    spots, z_size = mask_ref.shape
    pairs = energy_ref.shape[0]
    mask = mask_ref[...]
    for start in range(0, products.shape[1], z_size):
        picked = products[:, start : start + z_size] * mask
        coeffs = jnp.sum(picked.reshape(SIDE, pairs, z_size), axis=0)
        coeffs = jnp.sum(coeffs, axis=1, keepdims=True)
        high, low = halves(coeffs * energy_ref[...])
        columns = slice(lanes.start + start, lanes.start + start + z_size)
        for third in range(SIDE):
            first, last = third * pairs, (third + 1) * pairs
            marks = marks_ref[first:last]
            marked = high * marks
            coeff_ref[first:last, columns] = marked
            coeff_ref[spots + first : spots + last, columns] = low * marks
            if coeff_ref.shape[0] > 2 * spots:
                coeff_ref[2 * spots + first : 2 * spots + last, columns] = marked


def table_kernel(
    first_at_ref,
    second_at_ref,
    third_at_ref,
    energy_at_ref,
    after_ref,
    projector_ref,
    order_ref,
    plane_ref,
    field_ref,
    q_ref,
    left_ref,
    mask_ref,
    marks_ref,
    energy_ref,
    diagonal_ref,
):
    block_x, y_size, z_size = field_ref.shape[1:]
    x_size = 2 * block_x
    own = block_x * y_size
    cell_count = x_size * y_size
    atoms, nproj = projector_ref.shape[:2]
    pairs = atoms * nproj
    per_plane = SIDE * SIDE
    spots = atoms * per_plane
    unit, shift = shared_operator()
    own_start = lax.axis_index("dom") * block_x
    high, low = halves(projector_ref[...].reshape(pairs, SUP))
    ordered = matmul(jnp.concatenate((high, low), axis=0), order_ref[...])

    lane = lax.broadcasted_iota(jnp.int32, (pairs, 2 * per_plane), 1)
    row_atom = lax.broadcasted_iota(jnp.int32, (pairs, spots), 0) // nproj
    lane_atom = lax.broadcasted_iota(jnp.int32, (pairs, spots), 1) // per_plane
    same_atom = row_atom == lane_atom
    expanded = []
    for part in range(2):
        rows = []
        for third in range(SIDE):
            start = third // 2 * 2 * per_plane
            both = ordered[part * pairs : (part + 1) * pairs, start : start + 2 * per_plane]
            swapped = pltpu.roll(both, per_plane, 1)
            if third % 2:
                both, swapped = swapped, both
            doubled = jnp.where(lane < per_plane, both, swapped)
            doubled = jnp.concatenate([doubled] * (atoms // 2), axis=1)
            rows.append(jnp.where(same_atom, doubled, 0.0))
        expanded.append(jnp.concatenate(rows, axis=0).astype(jnp.bfloat16))
    high, low = expanded

    place = []
    spot = lax.broadcasted_iota(jnp.int32, (per_plane, cell_count), 0)
    place_lane = lax.broadcasted_iota(jnp.int32, (per_plane, cell_count), 1)
    for atom in range(atoms):
        x_start = lax.rem(first_at_ref[atom] - SIDE // 2 - own_start + 2 * x_size, x_size)
        y_start = lax.rem(second_at_ref[atom] - SIDE // 2 + y_size, y_size)
        x_index = x_start + spot // SIDE
        x_index = jnp.where(x_index >= x_size, x_index - x_size, x_index)
        y_index = y_start + spot % SIDE
        y_index = jnp.where(y_index >= y_size, y_index - y_size, y_index)
        target = x_index * y_size + y_index
        place.append(jnp.where(place_lane == target, 1.0, 0.0).astype(jnp.bfloat16))
    place = jnp.concatenate(place, axis=0)
    q_high = matmul(high, place)
    q_ref[...] = q_high.astype(jnp.bfloat16)
    q_high = q_high.T.astype(jnp.bfloat16)
    left_ref[:, 0:cell_count] = plane_ref[...]
    left_ref[:, cell_count : cell_count + spots] = q_high
    left_ref[:, cell_count + spots : cell_count + 2 * spots] = q_high
    left_ref[:, cell_count + 2 * spots :] = matmul(low, place).T.astype(jnp.bfloat16)

    z_lane = lax.broadcasted_iota(jnp.int32, (nproj, z_size), 1)
    for third in range(SIDE):
        for atom in range(atoms):
            z_index = lax.rem(third_at_ref[atom] + third - SIDE // 2 + z_size, z_size)
            start = third * pairs + atom * nproj
            mask_ref[start : start + nproj] = jnp.where(z_lane == z_index, 1.0, 0.0)
    marks_ref[...] = mask_ref[...].astype(jnp.bfloat16)
    sublane = lax.broadcasted_iota(jnp.int32, (nproj, z_size), 0)
    energy = jnp.zeros((nproj, z_size), jnp.float32)
    for index in range(nproj):
        energy = jnp.where(sublane == index, energy_at_ref[index], energy)
    energy = energy * (1.0 / (unit * filter_width))
    for atom in range(atoms):
        energy_ref[atom * nproj : (atom + 1) * nproj] = energy

    scale = 1.0 / (unit * filter_width)
    diagonal_ref[...] = (field_ref[0].reshape(own, z_size) + shift) * scale


def packed_rotation(rotation_ref, z_size):
    count, wide = rotation_ref.shape
    spare = z_size - wide
    block = jnp.concatenate(
        (rotation_ref[...].astype(jnp.float32), jnp.zeros((count, spare), jnp.float32)), axis=1
    )
    block = jnp.concatenate((block, jnp.zeros((8 - count, z_size), jnp.float32)), axis=0)
    sublane = lax.broadcasted_iota(jnp.int32, (8, z_size), 0)
    lane = lax.broadcasted_iota(jnp.int32, (8, z_size), 1)
    packed = block
    for piece in range(-(-wide // spare)):
        moved = pltpu.roll(block, (piece - (count - 1)) % 8, 0)
        moved = pltpu.roll(moved, (wide - piece * spare) % z_size, 1)
        packed = jnp.where((sublane == piece) & (lane >= wide), moved, packed)
    return packed


def filter_kernel(
    received_ref,
    q_ref,
    left_ref,
    mask_ref,
    marks_ref,
    energy_ref,
    diagonal_ref,
    partner_diagonal_ref,
    third_ref,
    out_ref,
    rows_ref,
    right_ref,
    start_ref,
    first_ref,
    result_ref,
    sem_ref,
):
    count, block_x, y_size, z_size = out_ref.shape[1:]
    own = block_x * y_size
    cells = 2 * own
    used = count * block_x
    spots = mask_ref.shape[0]
    depth = cells + 2 * spots
    pitch = y_size + 1
    unit, _ = shared_operator()
    me = lax.axis_index("dom")
    for half in range(2):
        for part in range(y_size):
            values = received_ref[(me ^ half) * y_size + part].astype(jnp.float32)
            rows_ref[half, pl.ds(part, used, stride=pitch), :] = values[0:used]

    groups = [range(first, min(first + 2, count)) for first in range(0, count, 2)]
    lanes_of = [slice(group[0] * z_size, (group[-1] + 1) * z_size) for group in groups]
    made = [{} for _ in groups]
    stores = []
    spread_refs = (mask_ref, marks_ref, energy_ref)

    def column(position):
        return slice(position * z_size, (position + 1) * z_size)

    def load(index):
        for orbital in groups[index]:
            for half in range(2):
                planes = [
                    rows_ref[half, pl.ds((orbital * block_x + plane) * pitch, y_size), :]
                    for plane in range(block_x)
                ]
                values = jnp.concatenate(planes, axis=0).astype(jnp.bfloat16)
                right_ref[half * own : (half + 1) * own, column(orbital)] = values
                start_ref[half * own : (half + 1) * own, column(orbital)] = values

    def project(index):
        made[index]["products"] = matmul(q_ref[...], right_ref[0:cells, lanes_of[index]])

    def spread_first(index):
        coeff_ref = right_ref.at[cells:depth]
        spread(made[index]["products"], lanes_of[index], *spread_refs, coeff_ref)

    def spread_second(index):
        coeff_ref = right_ref.at[cells:]
        spread(made[index]["products"], lanes_of[index], *spread_refs, coeff_ref)

    def along(index, rows):
        wide = len(groups[index]) * z_size
        values = right_ref[0:rows, lanes_of[index]]
        made[index]["along"] = matmul(values, third_ref[0:wide, 0:wide])

    def along_first(index):
        along(index, cells)

    def along_second(index):
        along(index, own)

    def plane_first(index):
        summed = matmul(left_ref[:, 0:depth], right_ref[0:depth, lanes_of[index]])
        made[index]["summed"] = summed + made[index]["along"]

    def plane_second(index):
        summed = matmul(left_ref[0:own], right_ref[:, lanes_of[index]])
        made[index]["summed"] = summed + made[index]["along"]

    def finish_first(index):
        for position, orbital in enumerate(groups[index]):
            values = made[index]["summed"][:, column(position)]
            start = start_ref[:, column(orbital)].astype(jnp.float32)
            mine = diagonal_ref[...] * start[0:own] + values[0:own]
            other = partner_diagonal_ref[...] * start[own:] + values[own:]
            first_ref[:, column(orbital)] = mine
            right_ref[0:own, column(orbital)] = mine.astype(jnp.bfloat16)
            right_ref[own:cells, column(orbital)] = other.astype(jnp.bfloat16)

    def finish_second(index):
        for position, orbital in enumerate(groups[index]):
            values = made[index]["summed"][:, column(position)]
            values = diagonal_ref[...] * first_ref[:, column(orbital)] + values
            start = start_ref[0:own, column(orbital)].astype(jnp.float32)
            values = (2.0 * unit * unit * values - start).astype(jnp.bfloat16)
            result_ref[orbital] = values.reshape(block_x, y_size, z_size)
            stores.append(
                pltpu.make_async_copy(
                    result_ref.at[orbital], out_ref.at[0, orbital], sem_ref.at[orbital]
                )
            )
            stores[-1].start()

    steps = (
        load,
        project,
        along_first,
        spread_first,
        plane_first,
        finish_first,
        project,
        along_second,
        spread_second,
        plane_second,
        finish_second,
    )
    for time in range(len(steps) + 2 * len(groups) - 2):
        for index in range(len(groups)):
            if 0 <= time - 2 * index < len(steps):
                steps[time - 2 * index](index)
    for store in stores:
        store.wait()


def rotate_kernel(received_ref, after_ref, out_ref, wide_ref, rows_ref, *, count, block_x):
    sources, chunk, z_size = received_ref.shape
    total = sources * count
    used = count * block_x
    spare = z_size - total
    pitch = chunk + 1
    for part in range(sources):
        wide_ref[pl.ds(part * pitch, chunk), :] = received_ref[part].astype(jnp.float32)
    packed = [wide_ref[pl.ds(used + row, sources, stride=pitch), :] for row in range(count - 1)]
    lane = lax.broadcasted_iota(jnp.int32, (sources, z_size), 1)
    last = jnp.zeros((sources, z_size), jnp.float32)
    for piece in range(-(-total // spare)):
        moved = pltpu.roll(packed[piece], (piece * spare - total) % z_size, 1)
        last = jnp.where(lane >= piece * spare, moved, last)
    rotation = jnp.concatenate(packed + [last], axis=0)[:, 0:total].astype(jnp.bfloat16)
    columns = []
    for plane in range(block_x):
        rows = [
            wide_ref[pl.ds(orbital * block_x + plane, sources, stride=pitch), :]
            for orbital in range(count)
        ]
        columns.append(jnp.concatenate(rows, axis=0).astype(jnp.bfloat16))
    values = jnp.concatenate(columns, axis=1)
    rotated = lax.dot_general(
        rotation, values, (((0,), (0,)), ((), ())), preferred_element_type=jnp.float32
    )
    rows_ref[total * block_x :] = jnp.zeros((chunk - used, z_size), jnp.float32)
    for plane in range(block_x):
        lanes = slice(plane * z_size, (plane + 1) * z_size)
        rows_ref[pl.ds(plane, total, stride=block_x), :] = rotated[:, lanes]
    for part in range(sources):
        values = rows_ref[part * used : part * used + chunk].astype(jnp.bfloat16)
        out_ref[part] = values
        out_ref[sources + part] = values


def in_vmem(count):
    return [pl.BlockSpec(memory_space=pltpu.VMEM)] * count


def in_smem(count):
    return [pl.BlockSpec(memory_space=pltpu.SMEM)] * count


def params(mib):
    return pltpu.CompilerParams(vmem_limit_bytes=mib * MIB)


def shape_of(shape, kind):
    return jax.ShapeDtypeStruct(shape, kind)


def pair_body(
    orbitals, potential, projectors, projector_energy, atom_first, atom_second, atom_third, rotation
):
    bf16, f32 = jnp.bfloat16, jnp.float32
    count, block_x, y_size, z_size = orbitals.shape[1:]
    x_size = 2 * block_x
    own = block_x * y_size
    cell_count = x_size * y_size
    atoms, nproj = projectors.shape[:2]
    spots = SIDE * atoms * nproj
    sources = lax.axis_size("orb")
    used = count * block_x
    chunk = -(-(used + count - 1) // 16) * 16

    height = 8
    packed, after = pl.pallas_call(
        pack_kernel,
        out_shape=(shape_of((sources, chunk, z_size), bf16), shape_of((8, z_size), f32)),
        grid=(y_size // height,),
        in_specs=[
            pl.BlockSpec((1, count, block_x, height, z_size), lambda step: (0, 0, 0, step, 0)),
            pl.BlockSpec(rotation.shape, lambda step: (0, 0)),
        ],
        out_specs=(
            pl.BlockSpec((height, chunk, z_size), lambda step: (step, 0, 0)),
            pl.BlockSpec((8, z_size), lambda step: (0, 0)),
        ),
        scratch_shapes=[pltpu.VMEM((height * (chunk + 8), z_size), f32)],
        compiler_params=params(60),
        name="pack",
    )(orbitals, rotation)
    by_plane = lax.all_to_all(packed, "orb", split_axis=0, concat_axis=0, tiled=True)

    q, left, mask, marks, energy, diagonal = pl.pallas_call(
        table_kernel,
        out_shape=(
            shape_of((spots, cell_count), bf16),
            shape_of((cell_count, cell_count + 3 * spots), bf16),
            shape_of((spots, z_size), f32),
            shape_of((spots, z_size), bf16),
            shape_of((atoms * nproj, z_size), f32),
            shape_of((own, z_size), f32),
        ),
        in_specs=in_smem(4) + [pl.BlockSpec(memory_space=pl.ANY)] + in_vmem(4),
        out_specs=tuple(in_vmem(6)),
        compiler_params=params(24),
        cost_estimate=pl.CostEstimate(flops=1 << 31, bytes_accessed=6 << 20, transcendentals=0),
        name="tables",
    )(
        atom_first,
        atom_second,
        atom_third,
        projector_energy,
        after,
        projectors,
        third_first(),
        plane_stencil(x_size, y_size),
        potential,
    )
    partner_diagonal = lax.ppermute(diagonal, "dom", [(0, 1), (1, 0)])

    rotated = pl.pallas_call(
        functools.partial(rotate_kernel, count=count, block_x=block_x),
        out_shape=shape_of((2 * sources, chunk, z_size), bf16),
        in_specs=in_vmem(2),
        out_specs=in_vmem(1)[0],
        scratch_shapes=[
            pltpu.VMEM((sources * (chunk + 8), z_size), f32),
            pltpu.VMEM((sources * used + chunk - used, z_size), f32),
        ],
        compiler_params=params(24),
        name="rotate",
    )(by_plane, partner_diagonal)
    by_orbital = lax.all_to_all(rotated, ("dom", "orb"), split_axis=0, concat_axis=0, tiled=True)

    return pl.pallas_call(
        filter_kernel,
        out_shape=shape_of(orbitals.shape, bf16),
        in_specs=in_vmem(9),
        out_specs=pl.BlockSpec(memory_space=pltpu.HBM),
        scratch_shapes=[
            pltpu.VMEM((2, used * (y_size + 8), z_size), f32),
            pltpu.VMEM((cell_count + 3 * spots, count * z_size), bf16),
            pltpu.VMEM((cell_count, count * z_size), bf16),
            pltpu.VMEM((own, count * z_size), f32),
            pltpu.VMEM(orbitals.shape[1:], bf16),
            pltpu.SemaphoreType.DMA((count,)),
        ],
        compiler_params=params(40),
        name="filter",
    )(
        by_orbital,
        q,
        left,
        mask,
        marks,
        energy,
        diagonal,
        partner_diagonal,
        third_stencil(z_size),
    )


def fits_pair(mesh, orbitals, projectors, rotation):
    count = orbitals.shape[1] // mesh.shape["orb"]
    return (
        mesh.shape["dom"] == 2
        and orbitals.shape[3] == mesh.shape["orb"]
        and orbitals.shape[2] == 2 * stencil_reach
        and projectors.shape[0] % 2 == 0
        and projectors.shape[1] == 8
        and count <= 8
        and rotation.shape[1] < orbitals.shape[4]
        and -(-rotation.shape[1] // (orbitals.shape[4] - rotation.shape[1])) < count
    )


def solution(mesh):
    def whole(*arrays):
        chosen = pair_body if fits_pair(mesh, arrays[0], arrays[2], arrays[7]) else body
        return jax.shard_map(
            chosen,
            mesh=mesh,
            in_specs=(
                P("dom", "orb", None, None, None),
                P("dom", None, None, None),
                P(),
                P(),
                P(),
                P(),
                P(),
                P("orb", None),
            ),
            out_specs=P("dom", "orb", None, None, None),
            check_vma=False,
        )(*arrays)

    return whole
```

```python
import functools

import jax
import jax.numpy as jnp
import numpy as np
from jax import lax
from jax.experimental import pallas as pl
from jax.experimental.pallas import tpu as pltpu
from jax.sharding import PartitionSpec as P

SIDE = 8
SUP = 512


stencil_weights = (
    -5369.0 / 1800.0,
    12.0 / 7.0,
    -15.0 / 56.0,
    10.0 / 189.0,
    -1.0 / 112.0,
    2.0 / 1925.0,
    -1.0 / 16632.0,
)
inverse_spacing = 4.0
filter_center = 120.0
filter_width = 110.0
stencil_reach = 6


def partner_2(block, axis, bit):
    count = lax.axis_size(axis)
    route = []
    for low in range(count):
        high = low | 1 << bit
        if high != low and high < count:
            route += [(low, high), (high, low)]
    return lax.ppermute(block, axis, route)


def outgoing(values, direction, width):
    extent = values.shape[direction]
    if 2 * width < extent:
        return jnp.concatenate(
            (
                lax.slice_in_dim(values, 0, width, axis=direction),
                lax.slice_in_dim(values, extent - width, extent, axis=direction),
            ),
            axis=direction,
        )
    return values


def assemble(values, partner, direction, width):
    extent = values.shape[direction]
    if 2 * width < extent:
        lower_rim = lax.slice_in_dim(partner, width, 2 * width, axis=direction)
        upper_rim = lax.slice_in_dim(partner, 0, width, axis=direction)
        return jnp.concatenate((lower_rim, values, upper_rim), axis=direction)
    cyclic = jnp.concatenate((values, partner), axis=direction)
    chosen = np.arange(-width, extent + width) % (2 * extent)
    return jnp.take(cyclic, jnp.asarray(chosen, dtype=jnp.int32), axis=direction)


def face_padded(values, direction, bit_number):
    sent = outgoing(values, direction, stencil_reach)
    partner = partner_2(sent.astype(jnp.bfloat16), "dom", bit_number).astype(sent.dtype)
    return assemble(values, partner, direction, stencil_reach)


def stencil_sum(center, along):
    lead = center.ndim - 3
    summed = 3.0 * stencil_weights[0] * center
    for index in range(3):
        direction = lead + index
        extent = center.shape[direction]
        padded = along[index]
        for offset in range(1, 7):
            if padded is None:
                upward = jnp.roll(center, -offset, direction)
                downward = jnp.roll(center, offset, direction)
            else:
                upward = lax.slice_in_dim(
                    padded, stencil_reach + offset, stencil_reach + offset + extent, axis=direction
                )
                downward = lax.slice_in_dim(
                    padded, stencil_reach - offset, stencil_reach - offset + extent, axis=direction
                )
            summed = summed + stencil_weights[offset] * (upward + downward)
    return summed


def support_map(atom_coords, starts, extents, periods):
    offsets = jnp.arange(SIDE, dtype=jnp.int32) - SIDE // 2
    clipped_list = []
    inside_list = []
    for index in range(3):
        local = (atom_coords[index][:, None] + offsets[None, :] - starts[index]) % periods[index]
        inside_list.append(local < extents[index])
        clipped_list.append(jnp.minimum(local, extents[index] - 1))
    inside = (
        inside_list[0][:, :, None, None]
        & inside_list[1][:, None, :, None]
        & inside_list[2][:, None, None, :]
    )
    flattened = (
        clipped_list[0][:, :, None, None] * extents[1] + clipped_list[1][:, None, :, None]
    ) * extents[2] + clipped_list[2][:, None, None, :]
    atom_count = atom_coords[0].shape[0]
    return (
        flattened.reshape(atom_count * SUP),
        inside.reshape(atom_count, SUP).astype(jnp.float32),
    )


def coefficients(values, support, inside, projectors):
    orbital_count = values.shape[0]
    atom_count = projectors.shape[0]
    flattened = values.reshape(orbital_count, -1)
    picked = (
        jnp.take(flattened, support, axis=1).reshape(orbital_count, atom_count, SUP) * inside[None]
    )
    partial_coeffs = jnp.einsum("aps,kas->kap", projectors, picked, precision=lax.Precision.HIGHEST)
    return lax.psum(partial_coeffs, "dom")


def spread_into(coeffs, shape, support, inside, projectors, projector_energy):
    orbital_count = shape[0]
    atom_count = projectors.shape[0]
    scaled = coeffs * projector_energy[None, None, :]
    spread = (
        jnp.einsum("aps,kap->kas", projectors, scaled, precision=lax.Precision.HIGHEST)
        * inside[None]
    )
    total_cells = shape[1] * shape[2] * shape[3]
    projected_part = (
        jnp.zeros((orbital_count, total_cells), jnp.float32)
        .at[:, support]
        .add(spread.reshape(orbital_count, atom_count * SUP))
    )
    return projected_part.reshape(shape)


def own_hamiltonian(center, along, local_field, support, inside, projectors, projector_energy):
    kinetic = -0.5 * inverse_spacing * inverse_spacing
    coeffs = coefficients(center, support, inside, projectors)
    projected_part = spread_into(
        coeffs, center.shape, support, inside, projectors, projector_energy
    )
    return kinetic * stencil_sum(center, along) + local_field[None] * center + projected_part


def body(
    orbitals, potential, projectors, projector_energy, atom_first, atom_second, atom_third, rotation
):
    domain_count = lax.axis_size("dom")
    domain_bits = domain_count.bit_length() - 1
    split = [index < domain_bits for index in range(3)]
    start_values = orbitals[0]
    local_field = potential[0]
    extents = start_values.shape[1:]
    periods = (
        extents[0] * min(domain_count, 2),
        extents[1] * min(max(domain_count // 2, 1), 2),
        extents[2] * max(domain_count // 4, 1),
    )
    domain_index = lax.axis_index("dom")
    anchors = (
        domain_index % 2 * extents[0],
        domain_index // 2 % 2 * extents[1],
        domain_index // 4 * extents[2],
    )
    atom_coords = (atom_first, atom_second, atom_third)
    support, inside = support_map(atom_coords, anchors, extents, periods)
    along = [
        face_padded(start_values, index + 1, index) if split[index] else None for index in range(3)
    ]
    first_apply = own_hamiltonian(
        start_values, along, local_field, support, inside, projectors, projector_energy
    )
    first_term = (first_apply - filter_center * start_values) / filter_width
    along = [
        face_padded(first_term, index + 1, index) if split[index] else None for index in range(3)
    ]
    second_apply = own_hamiltonian(
        first_term, along, local_field, support, inside, projectors, projector_energy
    )
    second_term = 2.0 * (second_apply - filter_center * first_term) / filter_width - start_values
    per_device = start_values.shape[0]
    filtered = second_term.astype(jnp.bfloat16).reshape(per_device, -1)
    by_cells = lax.all_to_all(filtered, "orb", split_axis=1, concat_axis=0, tiled=True)
    whole_rotation = lax.all_gather(rotation, "orb", axis=0, tiled=True)
    rotated = lax.dot_general(
        whole_rotation, by_cells, (((0,), (0,)), ((), ())), preferred_element_type=jnp.float32
    ).astype(jnp.bfloat16)
    result = lax.all_to_all(rotated, "orb", split_axis=0, concat_axis=1, tiled=True)
    return result.reshape((1,) + start_values.shape)


SCALE = 15.0
MIB = 1 << 20


def scaled_weights():
    ratios = np.array(stencil_weights[1:], np.float64) / stencil_weights[1]
    return SCALE * ratios


def cyclic_stencil(size):
    matrix = np.zeros((size, size), np.float64)
    rows = np.arange(size)
    for offset, weight in enumerate(scaled_weights(), 1):
        np.add.at(matrix, (rows, (rows + offset) % size), weight)
        np.add.at(matrix, (rows, (rows - offset) % size), weight)
    return matrix


def plane_stencil(x_size, y_size):
    matrix = np.kron(cyclic_stencil(x_size), np.eye(y_size))
    matrix += np.kron(np.eye(x_size), cyclic_stencil(y_size))
    return matrix.astype(jnp.bfloat16)


def third_stencil(z_size):
    matrix = cyclic_stencil(z_size)
    return np.kron(np.eye(2), matrix).astype(jnp.bfloat16)


def third_first():
    picked = np.zeros((SUP, SUP), np.float32)
    source = np.arange(SUP)
    picked[source, source % SIDE * SIDE * SIDE + source // SIDE] = 1.0
    return picked.astype(jnp.bfloat16)


def halves(values):
    high = values.astype(jnp.bfloat16)
    return high, (values - high.astype(jnp.float32)).astype(jnp.bfloat16)


def matmul(left, right):
    return jnp.dot(left, right, preferred_element_type=jnp.float32)


def shared_operator():
    kinetic = -0.5 * inverse_spacing * inverse_spacing
    unit = kinetic * stencil_weights[1] / SCALE / filter_width
    shift = 3.0 * kinetic * stencil_weights[0] - filter_center
    return unit, shift


def pack_kernel(orbital_ref, rotation_ref, out_ref, after_ref, chunk_ref):
    count, block_x, height, z_size = orbital_ref.shape[1:]
    chunk = out_ref.shape[1]
    used = count * block_x
    pitch = chunk + 1
    packed = packed_rotation(rotation_ref, z_size)
    after_ref[...] = packed
    for orbital in range(count):
        for plane in range(block_x):
            start = orbital * block_x + plane
            chunk_ref[pl.ds(start, height, stride=pitch), :] = orbital_ref[0, orbital, plane]
    for part in range(height):
        start = part * pitch
        chunk_ref[start + used : start + used + count - 1] = packed[0 : count - 1]
        out_ref[part] = chunk_ref[start : start + chunk].astype(jnp.bfloat16)


def spread(products, lanes, mask_ref, energy_ref, coeff_ref):
    spots, z_size = mask_ref.shape
    pairs = energy_ref.shape[0]
    mask = mask_ref[...]
    for start in range(0, products.shape[1], z_size):
        picked = products[:, start : start + z_size] * mask
        coeffs = jnp.sum(picked.reshape(SIDE, pairs, z_size), axis=0)
        coeffs = jnp.sum(coeffs, axis=1, keepdims=True)
        high, low = halves(jnp.concatenate([coeffs * energy_ref[...]] * SIDE, axis=0) * mask)
        columns = slice(lanes.start + start, lanes.start + start + z_size)
        coeff_ref[0:spots, columns] = high
        coeff_ref[spots : 2 * spots, columns] = low
        if coeff_ref.shape[0] > 2 * spots:
            coeff_ref[2 * spots :, columns] = high


def table_kernel(
    first_at_ref,
    second_at_ref,
    third_at_ref,
    energy_at_ref,
    after_ref,
    projector_ref,
    order_ref,
    plane_ref,
    field_ref,
    q_ref,
    left_ref,
    mask_ref,
    energy_ref,
    diagonal_ref,
):
    block_x, y_size, z_size = field_ref.shape[1:]
    x_size = 2 * block_x
    own = block_x * y_size
    cell_count = x_size * y_size
    atoms, nproj = projector_ref.shape[:2]
    pairs = atoms * nproj
    per_plane = SIDE * SIDE
    spots = atoms * per_plane
    unit, shift = shared_operator()
    own_start = lax.axis_index("dom") * block_x
    high, low = halves(projector_ref[...].reshape(pairs, SUP))
    ordered = matmul(jnp.concatenate((high, low), axis=0), order_ref[...])

    lane = lax.broadcasted_iota(jnp.int32, (pairs, 2 * per_plane), 1)
    row_atom = lax.broadcasted_iota(jnp.int32, (pairs, spots), 0) // nproj
    lane_atom = lax.broadcasted_iota(jnp.int32, (pairs, spots), 1) // per_plane
    same_atom = row_atom == lane_atom
    expanded = []
    for part in range(2):
        rows = []
        for third in range(SIDE):
            start = third // 2 * 2 * per_plane
            both = ordered[part * pairs : (part + 1) * pairs, start : start + 2 * per_plane]
            swapped = pltpu.roll(both, per_plane, 1)
            if third % 2:
                both, swapped = swapped, both
            doubled = jnp.where(lane < per_plane, both, swapped)
            doubled = jnp.concatenate([doubled] * (atoms // 2), axis=1)
            rows.append(jnp.where(same_atom, doubled, 0.0))
        expanded.append(jnp.concatenate(rows, axis=0).astype(jnp.bfloat16))
    high, low = expanded

    place = []
    spot = lax.broadcasted_iota(jnp.int32, (per_plane, cell_count), 0)
    place_lane = lax.broadcasted_iota(jnp.int32, (per_plane, cell_count), 1)
    for atom in range(atoms):
        x_start = lax.rem(first_at_ref[atom] - SIDE // 2 - own_start + 2 * x_size, x_size)
        y_start = lax.rem(second_at_ref[atom] - SIDE // 2 + y_size, y_size)
        x_index = x_start + spot // SIDE
        x_index = jnp.where(x_index >= x_size, x_index - x_size, x_index)
        y_index = y_start + spot % SIDE
        y_index = jnp.where(y_index >= y_size, y_index - y_size, y_index)
        target = x_index * y_size + y_index
        place.append(jnp.where(place_lane == target, 1.0, 0.0).astype(jnp.bfloat16))
    place = jnp.concatenate(place, axis=0)
    q_high = matmul(high, place)
    q_ref[...] = q_high.astype(jnp.bfloat16)
    q_high = q_high.T.astype(jnp.bfloat16)
    left_ref[:, 0:cell_count] = plane_ref[...]
    left_ref[:, cell_count : cell_count + spots] = q_high
    left_ref[:, cell_count + spots : cell_count + 2 * spots] = q_high
    left_ref[:, cell_count + 2 * spots :] = matmul(low, place).T.astype(jnp.bfloat16)

    z_lane = lax.broadcasted_iota(jnp.int32, (nproj, z_size), 1)
    for third in range(SIDE):
        for atom in range(atoms):
            z_index = lax.rem(third_at_ref[atom] + third - SIDE // 2 + z_size, z_size)
            start = third * pairs + atom * nproj
            mask_ref[start : start + nproj] = jnp.where(z_lane == z_index, 1.0, 0.0)
    sublane = lax.broadcasted_iota(jnp.int32, (nproj, z_size), 0)
    energy = jnp.zeros((nproj, z_size), jnp.float32)
    for index in range(nproj):
        energy = jnp.where(sublane == index, energy_at_ref[index], energy)
    energy = energy * (1.0 / (unit * filter_width))
    for atom in range(atoms):
        energy_ref[atom * nproj : (atom + 1) * nproj] = energy

    diagonal_ref[...] = (field_ref[0].reshape(own, z_size) + shift) / filter_width


def packed_rotation(rotation_ref, z_size):
    count, wide = rotation_ref.shape
    spare = z_size - wide
    block = jnp.concatenate(
        (rotation_ref[...].astype(jnp.float32), jnp.zeros((count, spare), jnp.float32)), axis=1
    )
    block = jnp.concatenate((block, jnp.zeros((8 - count, z_size), jnp.float32)), axis=0)
    sublane = lax.broadcasted_iota(jnp.int32, (8, z_size), 0)
    lane = lax.broadcasted_iota(jnp.int32, (8, z_size), 1)
    packed = block
    for piece in range(-(-wide // spare)):
        moved = pltpu.roll(block, (piece - (count - 1)) % 8, 0)
        moved = pltpu.roll(moved, (wide - piece * spare) % z_size, 1)
        packed = jnp.where((sublane == piece) & (lane >= wide), moved, packed)
    return packed


def filter_kernel(
    received_ref,
    q_ref,
    left_ref,
    mask_ref,
    energy_ref,
    diagonal_ref,
    partner_diagonal_ref,
    third_ref,
    out_ref,
    rows_ref,
    right_ref,
    start_ref,
    first_ref,
    result_ref,
    sem_ref,
):
    count, block_x, y_size, z_size = out_ref.shape[1:]
    own = block_x * y_size
    cells = 2 * own
    used = count * block_x
    spots = mask_ref.shape[0]
    depth = cells + 2 * spots
    pitch = y_size + 1
    unit, _ = shared_operator()
    me = lax.axis_index("dom")
    for half in range(2):
        for part in range(y_size):
            values = received_ref[(me ^ half) * y_size + part].astype(jnp.float32)
            rows_ref[half, pl.ds(part, used, stride=pitch), :] = values[0:used]

    groups = [range(first, min(first + 2, count)) for first in range(0, count, 2)]
    lanes_of = [slice(group[0] * z_size, (group[-1] + 1) * z_size) for group in groups]
    made = [{} for _ in groups]
    stores = []

    def column(position):
        return slice(position * z_size, (position + 1) * z_size)

    def load(index):
        for orbital in groups[index]:
            for half in range(2):
                planes = [
                    rows_ref[half, pl.ds((orbital * block_x + plane) * pitch, y_size), :]
                    for plane in range(block_x)
                ]
                values = jnp.concatenate(planes, axis=0).astype(jnp.bfloat16)
                right_ref[half * own : (half + 1) * own, column(orbital)] = values
                start_ref[half * own : (half + 1) * own, column(orbital)] = values

    def project(index):
        made[index]["products"] = matmul(q_ref[...], right_ref[0:cells, lanes_of[index]])

    def spread_first(index):
        coeff_ref = right_ref.at[cells:depth]
        spread(made[index]["products"], lanes_of[index], mask_ref, energy_ref, coeff_ref)

    def spread_second(index):
        coeff_ref = right_ref.at[cells:]
        spread(made[index]["products"], lanes_of[index], mask_ref, energy_ref, coeff_ref)

    def along(index, rows):
        wide = len(groups[index]) * z_size
        values = right_ref[0:rows, lanes_of[index]]
        made[index]["along"] = matmul(values, third_ref[0:wide, 0:wide])

    def along_first(index):
        along(index, cells)

    def along_second(index):
        along(index, own)

    def plane_first(index):
        summed = matmul(left_ref[:, 0:depth], right_ref[0:depth, lanes_of[index]])
        made[index]["summed"] = summed + made[index]["along"]

    def plane_second(index):
        summed = matmul(left_ref[0:own], right_ref[:, lanes_of[index]])
        made[index]["summed"] = summed + made[index]["along"]

    def finish_first(index):
        for position, orbital in enumerate(groups[index]):
            values = unit * made[index]["summed"][:, column(position)]
            start = start_ref[:, column(orbital)].astype(jnp.float32)
            mine = diagonal_ref[...] * start[0:own] + values[0:own]
            other = partner_diagonal_ref[...] * start[own:] + values[own:]
            first_ref[:, column(orbital)] = mine
            right_ref[0:own, column(orbital)] = mine.astype(jnp.bfloat16)
            right_ref[own:cells, column(orbital)] = other.astype(jnp.bfloat16)

    def finish_second(index):
        for position, orbital in enumerate(groups[index]):
            values = unit * made[index]["summed"][:, column(position)]
            values = diagonal_ref[...] * first_ref[:, column(orbital)] + values
            start = start_ref[0:own, column(orbital)].astype(jnp.float32)
            values = (2.0 * values - start).astype(jnp.bfloat16)
            result_ref[orbital] = values.reshape(block_x, y_size, z_size)
            stores.append(
                pltpu.make_async_copy(
                    result_ref.at[orbital], out_ref.at[0, orbital], sem_ref.at[orbital]
                )
            )
            stores[-1].start()

    steps = (
        load,
        project,
        along_first,
        spread_first,
        plane_first,
        finish_first,
        project,
        along_second,
        spread_second,
        plane_second,
        finish_second,
    )
    for time in range(len(steps) + 2 * len(groups) - 2):
        for index in range(len(groups)):
            if 0 <= time - 2 * index < len(steps):
                steps[time - 2 * index](index)
    for store in stores:
        store.wait()


def rotate_kernel(received_ref, after_ref, out_ref, wide_ref, rows_ref, *, count, block_x):
    sources, chunk, z_size = received_ref.shape
    total = sources * count
    used = count * block_x
    spare = z_size - total
    pitch = chunk + 1
    for part in range(sources):
        wide_ref[pl.ds(part * pitch, chunk), :] = received_ref[part].astype(jnp.float32)
    packed = [wide_ref[pl.ds(used + row, sources, stride=pitch), :] for row in range(count - 1)]
    lane = lax.broadcasted_iota(jnp.int32, (sources, z_size), 1)
    last = jnp.zeros((sources, z_size), jnp.float32)
    for piece in range(-(-total // spare)):
        moved = pltpu.roll(packed[piece], (piece * spare - total) % z_size, 1)
        last = jnp.where(lane >= piece * spare, moved, last)
    rotation = jnp.concatenate(packed + [last], axis=0)[:, 0:total].astype(jnp.bfloat16)
    columns = []
    for plane in range(block_x):
        rows = [
            wide_ref[pl.ds(orbital * block_x + plane, sources, stride=pitch), :]
            for orbital in range(count)
        ]
        columns.append(jnp.concatenate(rows, axis=0).astype(jnp.bfloat16))
    values = jnp.concatenate(columns, axis=1)
    rotated = lax.dot_general(
        rotation, values, (((0,), (0,)), ((), ())), preferred_element_type=jnp.float32
    )
    rows_ref[total * block_x :] = jnp.zeros((chunk, z_size), jnp.float32)
    for plane in range(block_x):
        lanes = slice(plane * z_size, (plane + 1) * z_size)
        rows_ref[pl.ds(plane, total, stride=block_x), :] = rotated[:, lanes]
    for part in range(sources):
        values = rows_ref[part * used : part * used + chunk].astype(jnp.bfloat16)
        out_ref[part] = values
        out_ref[sources + part] = values


def in_vmem(count):
    return [pl.BlockSpec(memory_space=pltpu.VMEM)] * count


def in_smem(count):
    return [pl.BlockSpec(memory_space=pltpu.SMEM)] * count


def params(mib):
    return pltpu.CompilerParams(vmem_limit_bytes=mib * MIB)


def shape_of(shape, kind):
    return jax.ShapeDtypeStruct(shape, kind)


def pair_body(
    orbitals, potential, projectors, projector_energy, atom_first, atom_second, atom_third, rotation
):
    bf16, f32 = jnp.bfloat16, jnp.float32
    count, block_x, y_size, z_size = orbitals.shape[1:]
    x_size = 2 * block_x
    own = block_x * y_size
    cell_count = x_size * y_size
    atoms, nproj = projectors.shape[:2]
    spots = SIDE * atoms * nproj
    sources = lax.axis_size("orb")
    used = count * block_x
    chunk = -(-(used + count - 1) // 16) * 16

    height = 8
    packed, after = pl.pallas_call(
        pack_kernel,
        out_shape=(shape_of((sources, chunk, z_size), bf16), shape_of((8, z_size), f32)),
        grid=(y_size // height,),
        in_specs=[
            pl.BlockSpec((1, count, block_x, height, z_size), lambda step: (0, 0, 0, step, 0)),
            pl.BlockSpec(rotation.shape, lambda step: (0, 0)),
        ],
        out_specs=(
            pl.BlockSpec((height, chunk, z_size), lambda step: (step, 0, 0)),
            pl.BlockSpec((8, z_size), lambda step: (0, 0)),
        ),
        scratch_shapes=[pltpu.VMEM(((height + 1) * (chunk + 8), z_size), f32)],
        compiler_params=params(60),
        name="pack",
    )(orbitals, rotation)
    by_plane = lax.all_to_all(packed, "orb", split_axis=0, concat_axis=0, tiled=True)

    q, left, mask, energy, diagonal = pl.pallas_call(
        table_kernel,
        out_shape=(
            shape_of((spots, cell_count), bf16),
            shape_of((cell_count, cell_count + 3 * spots), bf16),
            shape_of((spots, z_size), f32),
            shape_of((atoms * nproj, z_size), f32),
            shape_of((own, z_size), f32),
        ),
        in_specs=in_smem(4) + [pl.BlockSpec(memory_space=pl.ANY)] + in_vmem(4),
        out_specs=tuple(in_vmem(5)),
        compiler_params=params(24),
        cost_estimate=pl.CostEstimate(flops=1 << 31, bytes_accessed=6 << 20, transcendentals=0),
        name="tables",
    )(
        atom_first,
        atom_second,
        atom_third,
        projector_energy,
        after,
        projectors,
        third_first(),
        plane_stencil(x_size, y_size),
        potential,
    )
    partner_diagonal = lax.ppermute(diagonal, "dom", [(0, 1), (1, 0)])

    rotated = pl.pallas_call(
        functools.partial(rotate_kernel, count=count, block_x=block_x),
        out_shape=shape_of((2 * sources, chunk, z_size), bf16),
        in_specs=in_vmem(2),
        out_specs=in_vmem(1)[0],
        scratch_shapes=[
            pltpu.VMEM((sources * (chunk + 8), z_size), f32),
            pltpu.VMEM((sources * used + chunk, z_size), f32),
        ],
        compiler_params=params(24),
        name="rotate",
    )(by_plane, partner_diagonal)
    by_orbital = lax.all_to_all(rotated, ("dom", "orb"), split_axis=0, concat_axis=0, tiled=True)

    return pl.pallas_call(
        filter_kernel,
        out_shape=shape_of(orbitals.shape, bf16),
        in_specs=in_vmem(8),
        out_specs=pl.BlockSpec(memory_space=pltpu.HBM),
        scratch_shapes=[
            pltpu.VMEM((2, used * (y_size + 8), z_size), f32),
            pltpu.VMEM((cell_count + 3 * spots, count * z_size), bf16),
            pltpu.VMEM((cell_count, count * z_size), bf16),
            pltpu.VMEM((own, count * z_size), f32),
            pltpu.VMEM(orbitals.shape[1:], bf16),
            pltpu.SemaphoreType.DMA((count,)),
        ],
        compiler_params=params(40),
        name="filter",
    )(
        by_orbital,
        q,
        left,
        mask,
        energy,
        diagonal,
        partner_diagonal,
        third_stencil(z_size),
    )


def fits_pair(mesh, orbitals, projectors, rotation):
    count = orbitals.shape[1] // mesh.shape["orb"]
    return (
        mesh.shape["dom"] == 2
        and orbitals.shape[3] == mesh.shape["orb"]
        and orbitals.shape[2] == 2 * stencil_reach
        and projectors.shape[0] % 2 == 0
        and projectors.shape[1] == 8
        and count <= 8
        and rotation.shape[1] < orbitals.shape[4]
        and -(-rotation.shape[1] // (orbitals.shape[4] - rotation.shape[1])) < count
    )


def solution(mesh):
    def whole(*arrays):
        chosen = pair_body if fits_pair(mesh, arrays[0], arrays[2], arrays[7]) else body
        return jax.shard_map(
            chosen,
            mesh=mesh,
            in_specs=(
                P("dom", "orb", None, None, None),
                P("dom", None, None, None),
                P(),
                P(),
                P(),
                P(),
                P(),
                P("orb", None),
            ),
            out_specs=P("dom", "orb", None, None, None),
            check_vma=False,
        )(*arrays)

    return whole
```

```python
import functools

import jax
import jax.numpy as jnp
import numpy as np
from jax import lax
from jax.experimental import pallas as pl
from jax.experimental.pallas import tpu as pltpu
from jax.sharding import PartitionSpec as P

SIDE = 8
SUP = 512


stencil_weights = (
    -5369.0 / 1800.0,
    12.0 / 7.0,
    -15.0 / 56.0,
    10.0 / 189.0,
    -1.0 / 112.0,
    2.0 / 1925.0,
    -1.0 / 16632.0,
)
inverse_spacing = 4.0
filter_center = 120.0
filter_width = 110.0
stencil_reach = 6


def partner_2(block, axis, bit):
    count = lax.axis_size(axis)
    route = []
    for low in range(count):
        high = low | 1 << bit
        if high != low and high < count:
            route += [(low, high), (high, low)]
    return lax.ppermute(block, axis, route)


def outgoing(values, direction, width):
    extent = values.shape[direction]
    if 2 * width < extent:
        return jnp.concatenate(
            (
                lax.slice_in_dim(values, 0, width, axis=direction),
                lax.slice_in_dim(values, extent - width, extent, axis=direction),
            ),
            axis=direction,
        )
    return values


def assemble(values, partner, direction, width):
    extent = values.shape[direction]
    if 2 * width < extent:
        lower_rim = lax.slice_in_dim(partner, width, 2 * width, axis=direction)
        upper_rim = lax.slice_in_dim(partner, 0, width, axis=direction)
        return jnp.concatenate((lower_rim, values, upper_rim), axis=direction)
    cyclic = jnp.concatenate((values, partner), axis=direction)
    chosen = np.arange(-width, extent + width) % (2 * extent)
    return jnp.take(cyclic, jnp.asarray(chosen, dtype=jnp.int32), axis=direction)


def face_padded(values, direction, bit_number):
    sent = outgoing(values, direction, stencil_reach)
    partner = partner_2(sent.astype(jnp.bfloat16), "dom", bit_number).astype(sent.dtype)
    return assemble(values, partner, direction, stencil_reach)


def stencil_sum(center, along):
    lead = center.ndim - 3
    summed = 3.0 * stencil_weights[0] * center
    for index in range(3):
        direction = lead + index
        extent = center.shape[direction]
        padded = along[index]
        for offset in range(1, 7):
            if padded is None:
                upward = jnp.roll(center, -offset, direction)
                downward = jnp.roll(center, offset, direction)
            else:
                upward = lax.slice_in_dim(
                    padded, stencil_reach + offset, stencil_reach + offset + extent, axis=direction
                )
                downward = lax.slice_in_dim(
                    padded, stencil_reach - offset, stencil_reach - offset + extent, axis=direction
                )
            summed = summed + stencil_weights[offset] * (upward + downward)
    return summed


def support_map(atom_coords, starts, extents, periods):
    offsets = jnp.arange(SIDE, dtype=jnp.int32) - SIDE // 2
    clipped_list = []
    inside_list = []
    for index in range(3):
        local = (atom_coords[index][:, None] + offsets[None, :] - starts[index]) % periods[index]
        inside_list.append(local < extents[index])
        clipped_list.append(jnp.minimum(local, extents[index] - 1))
    inside = (
        inside_list[0][:, :, None, None]
        & inside_list[1][:, None, :, None]
        & inside_list[2][:, None, None, :]
    )
    flattened = (
        clipped_list[0][:, :, None, None] * extents[1] + clipped_list[1][:, None, :, None]
    ) * extents[2] + clipped_list[2][:, None, None, :]
    atom_count = atom_coords[0].shape[0]
    return (
        flattened.reshape(atom_count * SUP),
        inside.reshape(atom_count, SUP).astype(jnp.float32),
    )


def coefficients(values, support, inside, projectors):
    orbital_count = values.shape[0]
    atom_count = projectors.shape[0]
    flattened = values.reshape(orbital_count, -1)
    picked = (
        jnp.take(flattened, support, axis=1).reshape(orbital_count, atom_count, SUP) * inside[None]
    )
    partial_coeffs = jnp.einsum("aps,kas->kap", projectors, picked, precision=lax.Precision.HIGHEST)
    return lax.psum(partial_coeffs, "dom")


def spread_into(coeffs, shape, support, inside, projectors, projector_energy):
    orbital_count = shape[0]
    atom_count = projectors.shape[0]
    scaled = coeffs * projector_energy[None, None, :]
    spread = (
        jnp.einsum("aps,kap->kas", projectors, scaled, precision=lax.Precision.HIGHEST)
        * inside[None]
    )
    total_cells = shape[1] * shape[2] * shape[3]
    projected_part = (
        jnp.zeros((orbital_count, total_cells), jnp.float32)
        .at[:, support]
        .add(spread.reshape(orbital_count, atom_count * SUP))
    )
    return projected_part.reshape(shape)


def own_hamiltonian(center, along, local_field, support, inside, projectors, projector_energy):
    kinetic = -0.5 * inverse_spacing * inverse_spacing
    coeffs = coefficients(center, support, inside, projectors)
    projected_part = spread_into(
        coeffs, center.shape, support, inside, projectors, projector_energy
    )
    return kinetic * stencil_sum(center, along) + local_field[None] * center + projected_part


def body(
    orbitals, potential, projectors, projector_energy, atom_first, atom_second, atom_third, rotation
):
    domain_count = lax.axis_size("dom")
    domain_bits = domain_count.bit_length() - 1
    split = [index < domain_bits for index in range(3)]
    start_values = orbitals[0]
    local_field = potential[0]
    extents = start_values.shape[1:]
    periods = (
        extents[0] * min(domain_count, 2),
        extents[1] * min(max(domain_count // 2, 1), 2),
        extents[2] * max(domain_count // 4, 1),
    )
    domain_index = lax.axis_index("dom")
    anchors = (
        domain_index % 2 * extents[0],
        domain_index // 2 % 2 * extents[1],
        domain_index // 4 * extents[2],
    )
    atom_coords = (atom_first, atom_second, atom_third)
    support, inside = support_map(atom_coords, anchors, extents, periods)
    along = [
        face_padded(start_values, index + 1, index) if split[index] else None for index in range(3)
    ]
    first_apply = own_hamiltonian(
        start_values, along, local_field, support, inside, projectors, projector_energy
    )
    first_term = (first_apply - filter_center * start_values) / filter_width
    along = [
        face_padded(first_term, index + 1, index) if split[index] else None for index in range(3)
    ]
    second_apply = own_hamiltonian(
        first_term, along, local_field, support, inside, projectors, projector_energy
    )
    second_term = 2.0 * (second_apply - filter_center * first_term) / filter_width - start_values
    per_device = start_values.shape[0]
    filtered = second_term.astype(jnp.bfloat16).reshape(per_device, -1)
    by_cells = lax.all_to_all(filtered, "orb", split_axis=1, concat_axis=0, tiled=True)
    whole_rotation = lax.all_gather(rotation, "orb", axis=0, tiled=True)
    rotated = lax.dot_general(
        whole_rotation, by_cells, (((0,), (0,)), ((), ())), preferred_element_type=jnp.float32
    ).astype(jnp.bfloat16)
    result = lax.all_to_all(rotated, "orb", split_axis=0, concat_axis=1, tiled=True)
    return result.reshape((1,) + start_values.shape)


SCALE = 15.0
MIB = 1 << 20


def scaled_weights():
    ratios = np.array(stencil_weights[1:], np.float64) / stencil_weights[1]
    return SCALE * ratios


def cyclic_stencil(size):
    matrix = np.zeros((size, size), np.float64)
    rows = np.arange(size)
    for offset, weight in enumerate(scaled_weights(), 1):
        np.add.at(matrix, (rows, (rows + offset) % size), weight)
        np.add.at(matrix, (rows, (rows - offset) % size), weight)
    return matrix


def plane_stencil(x_size, y_size):
    matrix = np.kron(cyclic_stencil(x_size), np.eye(y_size))
    matrix += np.kron(np.eye(x_size), cyclic_stencil(y_size))
    return matrix.astype(jnp.bfloat16)


def third_stencil(z_size):
    matrix = cyclic_stencil(z_size)
    return np.kron(np.eye(2), matrix).astype(jnp.bfloat16)


def third_first():
    picked = np.zeros((SUP, SUP), np.float32)
    source = np.arange(SUP)
    picked[source, source % SIDE * SIDE * SIDE + source // SIDE] = 1.0
    return picked.astype(jnp.bfloat16)


def halves(values):
    high = values.astype(jnp.bfloat16)
    return high, (values - high.astype(jnp.float32)).astype(jnp.bfloat16)


def matmul(left, right):
    return jnp.dot(left, right, preferred_element_type=jnp.float32)


def shared_operator():
    kinetic = -0.5 * inverse_spacing * inverse_spacing
    unit = kinetic * stencil_weights[1] / SCALE / filter_width
    shift = 3.0 * kinetic * stencil_weights[0] - filter_center
    return unit, shift


def pack_kernel(orbital_ref, rotation_ref, out_ref, after_ref, chunk_ref):
    count, block_x, height, z_size = orbital_ref.shape[1:]
    chunk = out_ref.shape[1]
    used = count * block_x
    pitch = chunk + 1
    packed = packed_rotation(rotation_ref, z_size)
    after_ref[...] = packed
    for orbital in range(count):
        for plane in range(block_x):
            start = orbital * block_x + plane
            chunk_ref[pl.ds(start, height, stride=pitch), :] = orbital_ref[0, orbital, plane]
    for part in range(height):
        start = part * pitch
        chunk_ref[start + used : start + used + count - 1] = packed[0 : count - 1]
        out_ref[part] = chunk_ref[start : start + chunk].astype(jnp.bfloat16)


def spread(products, lanes, mask_ref, energy_ref, coeff_ref):
    spots, z_size = mask_ref.shape
    pairs = energy_ref.shape[0]
    mask = mask_ref[...]
    for start in range(0, products.shape[1], z_size):
        picked = products[:, start : start + z_size] * mask
        coeffs = jnp.sum(picked.reshape(SIDE, pairs, z_size), axis=0)
        coeffs = jnp.sum(coeffs, axis=1, keepdims=True)
        high, low = halves(jnp.concatenate([coeffs * energy_ref[...]] * SIDE, axis=0) * mask)
        columns = slice(lanes.start + start, lanes.start + start + z_size)
        coeff_ref[0:spots, columns] = high
        coeff_ref[spots : 2 * spots, columns] = low
        if coeff_ref.shape[0] > 2 * spots:
            coeff_ref[2 * spots :, columns] = high


def table_kernel(
    first_at_ref,
    second_at_ref,
    third_at_ref,
    energy_at_ref,
    after_ref,
    projector_ref,
    order_ref,
    plane_ref,
    field_ref,
    q_ref,
    left_ref,
    mask_ref,
    energy_ref,
    diagonal_ref,
):
    block_x, y_size, z_size = field_ref.shape[1:]
    x_size = 2 * block_x
    own = block_x * y_size
    cell_count = x_size * y_size
    atoms, nproj = projector_ref.shape[:2]
    pairs = atoms * nproj
    per_plane = SIDE * SIDE
    spots = atoms * per_plane
    unit, shift = shared_operator()
    own_start = lax.axis_index("dom") * block_x
    high, low = halves(projector_ref[...].reshape(pairs, SUP))
    ordered = matmul(jnp.concatenate((high, low), axis=0), order_ref[...])

    lane = lax.broadcasted_iota(jnp.int32, (pairs, 2 * per_plane), 1)
    row_atom = lax.broadcasted_iota(jnp.int32, (pairs, spots), 0) // nproj
    lane_atom = lax.broadcasted_iota(jnp.int32, (pairs, spots), 1) // per_plane
    same_atom = row_atom == lane_atom
    expanded = []
    for part in range(2):
        rows = []
        for third in range(SIDE):
            start = third // 2 * 2 * per_plane
            both = ordered[part * pairs : (part + 1) * pairs, start : start + 2 * per_plane]
            swapped = pltpu.roll(both, per_plane, 1)
            if third % 2:
                both, swapped = swapped, both
            doubled = jnp.where(lane < per_plane, both, swapped)
            doubled = jnp.concatenate([doubled] * (atoms // 2), axis=1)
            rows.append(jnp.where(same_atom, doubled, 0.0))
        expanded.append(jnp.concatenate(rows, axis=0).astype(jnp.bfloat16))
    high, low = expanded

    place = []
    spot = lax.broadcasted_iota(jnp.int32, (per_plane, cell_count), 0)
    place_lane = lax.broadcasted_iota(jnp.int32, (per_plane, cell_count), 1)
    for atom in range(atoms):
        x_start = lax.rem(first_at_ref[atom] - SIDE // 2 - own_start + 2 * x_size, x_size)
        y_start = lax.rem(second_at_ref[atom] - SIDE // 2 + y_size, y_size)
        x_index = x_start + spot // SIDE
        x_index = jnp.where(x_index >= x_size, x_index - x_size, x_index)
        y_index = y_start + spot % SIDE
        y_index = jnp.where(y_index >= y_size, y_index - y_size, y_index)
        target = x_index * y_size + y_index
        place.append(jnp.where(place_lane == target, 1.0, 0.0).astype(jnp.bfloat16))
    place = jnp.concatenate(place, axis=0)
    q_high = matmul(high, place)
    q_ref[0:spots] = q_high.astype(jnp.bfloat16)
    q_ref[spots:] = plane_ref[...]
    q_high = q_high.T.astype(jnp.bfloat16)
    left_ref[:, 0:spots] = q_high
    left_ref[:, spots : 2 * spots] = q_high
    left_ref[:, 2 * spots :] = matmul(low, place).T.astype(jnp.bfloat16)

    z_lane = lax.broadcasted_iota(jnp.int32, (nproj, z_size), 1)
    for third in range(SIDE):
        for atom in range(atoms):
            z_index = lax.rem(third_at_ref[atom] + third - SIDE // 2 + z_size, z_size)
            start = third * pairs + atom * nproj
            mask_ref[start : start + nproj] = jnp.where(z_lane == z_index, 1.0, 0.0)
    sublane = lax.broadcasted_iota(jnp.int32, (nproj, z_size), 0)
    energy = jnp.zeros((nproj, z_size), jnp.float32)
    for index in range(nproj):
        energy = jnp.where(sublane == index, energy_at_ref[index], energy)
    energy = energy * (1.0 / (unit * filter_width))
    for atom in range(atoms):
        energy_ref[atom * nproj : (atom + 1) * nproj] = energy

    diagonal_ref[...] = (field_ref[0].reshape(own, z_size) + shift) / filter_width


def packed_rotation(rotation_ref, z_size):
    count, wide = rotation_ref.shape
    spare = z_size - wide
    block = jnp.concatenate(
        (rotation_ref[...].astype(jnp.float32), jnp.zeros((count, spare), jnp.float32)), axis=1
    )
    block = jnp.concatenate((block, jnp.zeros((8 - count, z_size), jnp.float32)), axis=0)
    sublane = lax.broadcasted_iota(jnp.int32, (8, z_size), 0)
    lane = lax.broadcasted_iota(jnp.int32, (8, z_size), 1)
    packed = block
    for piece in range(-(-wide // spare)):
        moved = pltpu.roll(block, (piece - (count - 1)) % 8, 0)
        moved = pltpu.roll(moved, (wide - piece * spare) % z_size, 1)
        packed = jnp.where((sublane == piece) & (lane >= wide), moved, packed)
    return packed


def filter_kernel(
    received_ref,
    q_ref,
    left_ref,
    mask_ref,
    energy_ref,
    diagonal_ref,
    partner_diagonal_ref,
    third_ref,
    out_ref,
    rows_ref,
    right_ref,
    start_ref,
    first_ref,
    result_ref,
    sem_ref,
):
    count, block_x, y_size, z_size = out_ref.shape[1:]
    own = block_x * y_size
    cells = 2 * own
    used = count * block_x
    spots = mask_ref.shape[0]
    depth = cells + 2 * spots
    pitch = y_size + 1
    unit, _ = shared_operator()
    me = lax.axis_index("dom")
    for half in range(2):
        for part in range(y_size):
            values = received_ref[(me ^ half) * y_size + part].astype(jnp.float32)
            rows_ref[half, pl.ds(part, used, stride=pitch), :] = values[0:used]

    groups = [range(first, min(first + 2, count)) for first in range(0, count, 2)]
    lanes_of = [slice(group[0] * z_size, (group[-1] + 1) * z_size) for group in groups]
    made = [{} for _ in groups]
    stores = []

    def column(position):
        return slice(position * z_size, (position + 1) * z_size)

    def load(index):
        for orbital in groups[index]:
            for half in range(2):
                planes = [
                    rows_ref[half, pl.ds((orbital * block_x + plane) * pitch, y_size), :]
                    for plane in range(block_x)
                ]
                values = jnp.concatenate(planes, axis=0).astype(jnp.bfloat16)
                right_ref[half * own : (half + 1) * own, column(orbital)] = values
                start_ref[half * own : (half + 1) * own, column(orbital)] = values

    def project(index, rows):
        values = right_ref[0:cells, lanes_of[index]]
        both = matmul(q_ref[0 : spots + rows], values)
        made[index]["products"], made[index]["plane"] = both[0:spots], both[spots:]

    def project_first(index):
        project(index, cells)

    def project_second(index):
        project(index, own)

    def spread_first(index):
        coeff_ref = right_ref.at[cells:depth]
        spread(made[index]["products"], lanes_of[index], mask_ref, energy_ref, coeff_ref)

    def spread_second(index):
        coeff_ref = right_ref.at[cells:]
        spread(made[index]["products"], lanes_of[index], mask_ref, energy_ref, coeff_ref)

    def along(index, rows):
        wide = len(groups[index]) * z_size
        values = right_ref[0:rows, lanes_of[index]]
        made[index]["along"] = matmul(values, third_ref[0:wide, 0:wide])

    def along_first(index):
        along(index, cells)

    def along_second(index):
        along(index, own)

    def plane_first(index):
        summed = matmul(left_ref[:, 0 : 2 * spots], right_ref[cells:depth, lanes_of[index]])
        made[index]["summed"] = summed + (made[index]["plane"] + made[index]["along"])

    def plane_second(index):
        summed = matmul(left_ref[0:own], right_ref[cells:, lanes_of[index]])
        made[index]["summed"] = summed + (made[index]["plane"] + made[index]["along"])

    def finish_first(index):
        for position, orbital in enumerate(groups[index]):
            values = unit * made[index]["summed"][:, column(position)]
            start = start_ref[:, column(orbital)].astype(jnp.float32)
            mine = diagonal_ref[...] * start[0:own] + values[0:own]
            other = partner_diagonal_ref[...] * start[own:] + values[own:]
            first_ref[:, column(orbital)] = mine
            right_ref[0:own, column(orbital)] = mine.astype(jnp.bfloat16)
            right_ref[own:cells, column(orbital)] = other.astype(jnp.bfloat16)

    def finish_second(index):
        for position, orbital in enumerate(groups[index]):
            values = unit * made[index]["summed"][:, column(position)]
            values = diagonal_ref[...] * first_ref[:, column(orbital)] + values
            start = start_ref[0:own, column(orbital)].astype(jnp.float32)
            values = (2.0 * values - start).astype(jnp.bfloat16)
            result_ref[orbital] = values.reshape(block_x, y_size, z_size)
            stores.append(
                pltpu.make_async_copy(
                    result_ref.at[orbital], out_ref.at[0, orbital], sem_ref.at[orbital]
                )
            )
            stores[-1].start()

    steps = (
        load,
        project_first,
        along_first,
        spread_first,
        plane_first,
        finish_first,
        project_second,
        along_second,
        spread_second,
        plane_second,
        finish_second,
    )
    for time in range(len(steps) + 2 * len(groups) - 2):
        for index in range(len(groups)):
            if 0 <= time - 2 * index < len(steps):
                steps[time - 2 * index](index)
    for store in stores:
        store.wait()


def rotate_kernel(received_ref, after_ref, out_ref, wide_ref, rows_ref, *, count, block_x):
    sources, chunk, z_size = received_ref.shape
    total = sources * count
    used = count * block_x
    spare = z_size - total
    pitch = chunk + 1
    for part in range(sources):
        wide_ref[pl.ds(part * pitch, chunk), :] = received_ref[part].astype(jnp.float32)
    packed = [wide_ref[pl.ds(used + row, sources, stride=pitch), :] for row in range(count - 1)]
    lane = lax.broadcasted_iota(jnp.int32, (sources, z_size), 1)
    last = jnp.zeros((sources, z_size), jnp.float32)
    for piece in range(-(-total // spare)):
        moved = pltpu.roll(packed[piece], (piece * spare - total) % z_size, 1)
        last = jnp.where(lane >= piece * spare, moved, last)
    rotation = jnp.concatenate(packed + [last], axis=0)[:, 0:total].astype(jnp.bfloat16)
    columns = []
    for plane in range(block_x):
        rows = [
            wide_ref[pl.ds(orbital * block_x + plane, sources, stride=pitch), :]
            for orbital in range(count)
        ]
        columns.append(jnp.concatenate(rows, axis=0).astype(jnp.bfloat16))
    values = jnp.concatenate(columns, axis=1)
    rotated = lax.dot_general(
        rotation, values, (((0,), (0,)), ((), ())), preferred_element_type=jnp.float32
    )
    rows_ref[total * block_x :] = jnp.zeros((chunk, z_size), jnp.float32)
    for plane in range(block_x):
        lanes = slice(plane * z_size, (plane + 1) * z_size)
        rows_ref[pl.ds(plane, total, stride=block_x), :] = rotated[:, lanes]
    for part in range(sources):
        values = rows_ref[part * used : part * used + chunk].astype(jnp.bfloat16)
        out_ref[part] = values
        out_ref[sources + part] = values


def in_vmem(count):
    return [pl.BlockSpec(memory_space=pltpu.VMEM)] * count


def in_smem(count):
    return [pl.BlockSpec(memory_space=pltpu.SMEM)] * count


def params(mib):
    return pltpu.CompilerParams(vmem_limit_bytes=mib * MIB)


def shape_of(shape, kind):
    return jax.ShapeDtypeStruct(shape, kind)


def pair_body(
    orbitals, potential, projectors, projector_energy, atom_first, atom_second, atom_third, rotation
):
    bf16, f32 = jnp.bfloat16, jnp.float32
    count, block_x, y_size, z_size = orbitals.shape[1:]
    x_size = 2 * block_x
    own = block_x * y_size
    cell_count = x_size * y_size
    atoms, nproj = projectors.shape[:2]
    spots = SIDE * atoms * nproj
    sources = lax.axis_size("orb")
    used = count * block_x
    chunk = -(-(used + count - 1) // 16) * 16

    height = 8
    packed, after = pl.pallas_call(
        pack_kernel,
        out_shape=(shape_of((sources, chunk, z_size), bf16), shape_of((8, z_size), f32)),
        grid=(y_size // height,),
        in_specs=[
            pl.BlockSpec((1, count, block_x, height, z_size), lambda step: (0, 0, 0, step, 0)),
            pl.BlockSpec(rotation.shape, lambda step: (0, 0)),
        ],
        out_specs=(
            pl.BlockSpec((height, chunk, z_size), lambda step: (step, 0, 0)),
            pl.BlockSpec((8, z_size), lambda step: (0, 0)),
        ),
        scratch_shapes=[pltpu.VMEM(((height + 1) * (chunk + 8), z_size), f32)],
        compiler_params=params(60),
        name="pack",
    )(orbitals, rotation)
    by_plane = lax.all_to_all(packed, "orb", split_axis=0, concat_axis=0, tiled=True)

    q, left, mask, energy, diagonal = pl.pallas_call(
        table_kernel,
        out_shape=(
            shape_of((spots + cell_count, cell_count), bf16),
            shape_of((cell_count, 3 * spots), bf16),
            shape_of((spots, z_size), f32),
            shape_of((atoms * nproj, z_size), f32),
            shape_of((own, z_size), f32),
        ),
        in_specs=in_smem(4) + [pl.BlockSpec(memory_space=pl.ANY)] + in_vmem(4),
        out_specs=tuple(in_vmem(5)),
        compiler_params=params(24),
        cost_estimate=pl.CostEstimate(flops=1 << 31, bytes_accessed=6 << 20, transcendentals=0),
        name="tables",
    )(
        atom_first,
        atom_second,
        atom_third,
        projector_energy,
        after,
        projectors,
        third_first(),
        plane_stencil(x_size, y_size),
        potential,
    )
    partner_diagonal = lax.ppermute(diagonal, "dom", [(0, 1), (1, 0)])

    rotated = pl.pallas_call(
        functools.partial(rotate_kernel, count=count, block_x=block_x),
        out_shape=shape_of((2 * sources, chunk, z_size), bf16),
        in_specs=in_vmem(2),
        out_specs=in_vmem(1)[0],
        scratch_shapes=[
            pltpu.VMEM((sources * (chunk + 8), z_size), f32),
            pltpu.VMEM((sources * used + chunk, z_size), f32),
        ],
        compiler_params=params(24),
        name="rotate",
    )(by_plane, partner_diagonal)
    by_orbital = lax.all_to_all(rotated, ("dom", "orb"), split_axis=0, concat_axis=0, tiled=True)

    return pl.pallas_call(
        filter_kernel,
        out_shape=shape_of(orbitals.shape, bf16),
        in_specs=in_vmem(8),
        out_specs=pl.BlockSpec(memory_space=pltpu.HBM),
        scratch_shapes=[
            pltpu.VMEM((2, used * (y_size + 8), z_size), f32),
            pltpu.VMEM((cell_count + 3 * spots, count * z_size), bf16),
            pltpu.VMEM((cell_count, count * z_size), bf16),
            pltpu.VMEM((own, count * z_size), f32),
            pltpu.VMEM(orbitals.shape[1:], bf16),
            pltpu.SemaphoreType.DMA((count,)),
        ],
        compiler_params=params(40),
        name="filter",
    )(
        by_orbital,
        q,
        left,
        mask,
        energy,
        diagonal,
        partner_diagonal,
        third_stencil(z_size),
    )


def fits_pair(mesh, orbitals, projectors, rotation):
    count = orbitals.shape[1] // mesh.shape["orb"]
    return (
        mesh.shape["dom"] == 2
        and orbitals.shape[3] == mesh.shape["orb"]
        and orbitals.shape[2] == 2 * stencil_reach
        and projectors.shape[0] % 2 == 0
        and projectors.shape[1] == 8
        and count <= 8
        and rotation.shape[1] < orbitals.shape[4]
        and -(-rotation.shape[1] // (orbitals.shape[4] - rotation.shape[1])) < count
    )


def solution(mesh):
    def whole(*arrays):
        chosen = pair_body if fits_pair(mesh, arrays[0], arrays[2], arrays[7]) else body
        return jax.shard_map(
            chosen,
            mesh=mesh,
            in_specs=(
                P("dom", "orb", None, None, None),
                P("dom", None, None, None),
                P(),
                P(),
                P(),
                P(),
                P(),
                P("orb", None),
            ),
            out_specs=P("dom", "orb", None, None, None),
            check_vma=False,
        )(*arrays)

    return whole
```

```python
import functools

import jax
import jax.numpy as jnp
import numpy as np
from jax import lax
from jax.experimental import pallas as pl
from jax.experimental.pallas import tpu as pltpu
from jax.sharding import PartitionSpec as P

SIDE = 8
SUP = 512


stencil_weights = (
    -5369.0 / 1800.0,
    12.0 / 7.0,
    -15.0 / 56.0,
    10.0 / 189.0,
    -1.0 / 112.0,
    2.0 / 1925.0,
    -1.0 / 16632.0,
)
inverse_spacing = 4.0
filter_center = 120.0
filter_width = 110.0
stencil_reach = 6


def partner_2(block, axis, bit):
    count = lax.axis_size(axis)
    route = []
    for low in range(count):
        high = low | 1 << bit
        if high != low and high < count:
            route += [(low, high), (high, low)]
    return lax.ppermute(block, axis, route)


def outgoing(values, direction, width):
    extent = values.shape[direction]
    if 2 * width < extent:
        return jnp.concatenate(
            (
                lax.slice_in_dim(values, 0, width, axis=direction),
                lax.slice_in_dim(values, extent - width, extent, axis=direction),
            ),
            axis=direction,
        )
    return values


def assemble(values, partner, direction, width):
    extent = values.shape[direction]
    if 2 * width < extent:
        lower_rim = lax.slice_in_dim(partner, width, 2 * width, axis=direction)
        upper_rim = lax.slice_in_dim(partner, 0, width, axis=direction)
        return jnp.concatenate((lower_rim, values, upper_rim), axis=direction)
    cyclic = jnp.concatenate((values, partner), axis=direction)
    chosen = np.arange(-width, extent + width) % (2 * extent)
    return jnp.take(cyclic, jnp.asarray(chosen, dtype=jnp.int32), axis=direction)


def face_padded(values, direction, bit_number):
    sent = outgoing(values, direction, stencil_reach)
    partner = partner_2(sent.astype(jnp.bfloat16), "dom", bit_number).astype(sent.dtype)
    return assemble(values, partner, direction, stencil_reach)


def stencil_sum(center, along):
    lead = center.ndim - 3
    summed = 3.0 * stencil_weights[0] * center
    for index in range(3):
        direction = lead + index
        extent = center.shape[direction]
        padded = along[index]
        for offset in range(1, 7):
            if padded is None:
                upward = jnp.roll(center, -offset, direction)
                downward = jnp.roll(center, offset, direction)
            else:
                upward = lax.slice_in_dim(
                    padded, stencil_reach + offset, stencil_reach + offset + extent, axis=direction
                )
                downward = lax.slice_in_dim(
                    padded, stencil_reach - offset, stencil_reach - offset + extent, axis=direction
                )
            summed = summed + stencil_weights[offset] * (upward + downward)
    return summed


def support_map(atom_coords, starts, extents, periods):
    offsets = jnp.arange(SIDE, dtype=jnp.int32) - SIDE // 2
    clipped_list = []
    inside_list = []
    for index in range(3):
        local = (atom_coords[index][:, None] + offsets[None, :] - starts[index]) % periods[index]
        inside_list.append(local < extents[index])
        clipped_list.append(jnp.minimum(local, extents[index] - 1))
    inside = (
        inside_list[0][:, :, None, None]
        & inside_list[1][:, None, :, None]
        & inside_list[2][:, None, None, :]
    )
    flattened = (
        clipped_list[0][:, :, None, None] * extents[1] + clipped_list[1][:, None, :, None]
    ) * extents[2] + clipped_list[2][:, None, None, :]
    atom_count = atom_coords[0].shape[0]
    return (
        flattened.reshape(atom_count * SUP),
        inside.reshape(atom_count, SUP).astype(jnp.float32),
    )


def coefficients(values, support, inside, projectors):
    orbital_count = values.shape[0]
    atom_count = projectors.shape[0]
    flattened = values.reshape(orbital_count, -1)
    picked = (
        jnp.take(flattened, support, axis=1).reshape(orbital_count, atom_count, SUP) * inside[None]
    )
    partial_coeffs = jnp.einsum("aps,kas->kap", projectors, picked, precision=lax.Precision.HIGHEST)
    return lax.psum(partial_coeffs, "dom")


def spread_into(coeffs, shape, support, inside, projectors, projector_energy):
    orbital_count = shape[0]
    atom_count = projectors.shape[0]
    scaled = coeffs * projector_energy[None, None, :]
    spread = (
        jnp.einsum("aps,kap->kas", projectors, scaled, precision=lax.Precision.HIGHEST)
        * inside[None]
    )
    total_cells = shape[1] * shape[2] * shape[3]
    projected_part = (
        jnp.zeros((orbital_count, total_cells), jnp.float32)
        .at[:, support]
        .add(spread.reshape(orbital_count, atom_count * SUP))
    )
    return projected_part.reshape(shape)


def own_hamiltonian(center, along, local_field, support, inside, projectors, projector_energy):
    kinetic = -0.5 * inverse_spacing * inverse_spacing
    coeffs = coefficients(center, support, inside, projectors)
    projected_part = spread_into(
        coeffs, center.shape, support, inside, projectors, projector_energy
    )
    return kinetic * stencil_sum(center, along) + local_field[None] * center + projected_part


def body(
    orbitals, potential, projectors, projector_energy, atom_first, atom_second, atom_third, rotation
):
    domain_count = lax.axis_size("dom")
    domain_bits = domain_count.bit_length() - 1
    split = [index < domain_bits for index in range(3)]
    start_values = orbitals[0]
    local_field = potential[0]
    extents = start_values.shape[1:]
    periods = (
        extents[0] * min(domain_count, 2),
        extents[1] * min(max(domain_count // 2, 1), 2),
        extents[2] * max(domain_count // 4, 1),
    )
    domain_index = lax.axis_index("dom")
    anchors = (
        domain_index % 2 * extents[0],
        domain_index // 2 % 2 * extents[1],
        domain_index // 4 * extents[2],
    )
    atom_coords = (atom_first, atom_second, atom_third)
    support, inside = support_map(atom_coords, anchors, extents, periods)
    along = [
        face_padded(start_values, index + 1, index) if split[index] else None for index in range(3)
    ]
    first_apply = own_hamiltonian(
        start_values, along, local_field, support, inside, projectors, projector_energy
    )
    first_term = (first_apply - filter_center * start_values) / filter_width
    along = [
        face_padded(first_term, index + 1, index) if split[index] else None for index in range(3)
    ]
    second_apply = own_hamiltonian(
        first_term, along, local_field, support, inside, projectors, projector_energy
    )
    second_term = 2.0 * (second_apply - filter_center * first_term) / filter_width - start_values
    per_device = start_values.shape[0]
    filtered = second_term.astype(jnp.bfloat16).reshape(per_device, -1)
    by_cells = lax.all_to_all(filtered, "orb", split_axis=1, concat_axis=0, tiled=True)
    whole_rotation = lax.all_gather(rotation, "orb", axis=0, tiled=True)
    rotated = lax.dot_general(
        whole_rotation, by_cells, (((0,), (0,)), ((), ())), preferred_element_type=jnp.float32
    ).astype(jnp.bfloat16)
    result = lax.all_to_all(rotated, "orb", split_axis=0, concat_axis=1, tiled=True)
    return result.reshape((1,) + start_values.shape)


SCALE = 15.0
MIB = 1 << 20


def scaled_weights():
    ratios = np.array(stencil_weights[1:], np.float64) / stencil_weights[1]
    return SCALE * ratios


def cyclic_stencil(size):
    matrix = np.zeros((size, size), np.float64)
    rows = np.arange(size)
    for offset, weight in enumerate(scaled_weights(), 1):
        np.add.at(matrix, (rows, (rows + offset) % size), weight)
        np.add.at(matrix, (rows, (rows - offset) % size), weight)
    return matrix


def plane_stencil(x_size, y_size):
    matrix = np.kron(cyclic_stencil(x_size), np.eye(y_size))
    matrix += np.kron(np.eye(x_size), cyclic_stencil(y_size))
    return matrix.astype(jnp.bfloat16)


def third_stencil(z_size):
    matrix = cyclic_stencil(z_size)
    return np.kron(np.eye(2), matrix).astype(jnp.bfloat16)


def third_first():
    picked = np.zeros((SUP, SUP), np.float32)
    source = np.arange(SUP)
    picked[source, source % SIDE * SIDE * SIDE + source // SIDE] = 1.0
    return picked.astype(jnp.bfloat16)


def halves(values):
    high = values.astype(jnp.bfloat16)
    return high, (values - high.astype(jnp.float32)).astype(jnp.bfloat16)


def matmul(left, right):
    return jnp.dot(left, right, preferred_element_type=jnp.float32)


def shared_operator():
    kinetic = -0.5 * inverse_spacing * inverse_spacing
    unit = kinetic * stencil_weights[1] / SCALE / filter_width
    shift = 3.0 * kinetic * stencil_weights[0] - filter_center
    return unit, shift


def pack_kernel(orbital_ref, rotation_ref, out_ref, after_ref, chunk_ref):
    count, block_x, height, z_size = orbital_ref.shape[1:]
    chunk = out_ref.shape[1]
    used = count * block_x
    pitch = chunk + 1
    packed = packed_rotation(rotation_ref, z_size)
    after_ref[...] = packed
    for orbital in range(count):
        for plane in range(block_x):
            start = orbital * block_x + plane
            chunk_ref[pl.ds(start, height, stride=pitch), :] = orbital_ref[0, orbital, plane]
    for part in range(height):
        start = part * pitch
        chunk_ref[start + used : start + used + count - 1] = packed[0 : count - 1]
        out_ref[part] = chunk_ref[start : start + chunk].astype(jnp.bfloat16)


def spread(products, lanes, mask_ref, energy_ref, coeff_ref):
    spots, z_size = mask_ref.shape
    pairs = energy_ref.shape[0]
    mask = mask_ref[...]
    for start in range(0, products.shape[1], z_size):
        picked = products[:, start : start + z_size] * mask
        coeffs = jnp.sum(picked.reshape(SIDE, pairs, z_size), axis=0)
        coeffs = jnp.sum(coeffs, axis=1, keepdims=True)
        high, low = halves(jnp.concatenate([coeffs * energy_ref[...]] * SIDE, axis=0) * mask)
        columns = slice(lanes.start + start, lanes.start + start + z_size)
        coeff_ref[0:spots, columns] = high
        coeff_ref[spots : 2 * spots, columns] = low


def table_kernel(
    first_at_ref,
    second_at_ref,
    third_at_ref,
    energy_at_ref,
    after_ref,
    projector_ref,
    order_ref,
    plane_ref,
    field_ref,
    q_ref,
    left_ref,
    tail_ref,
    mask_ref,
    energy_ref,
    diagonal_ref,
):
    block_x, y_size, z_size = field_ref.shape[1:]
    x_size = 2 * block_x
    own = block_x * y_size
    cell_count = x_size * y_size
    atoms, nproj = projector_ref.shape[:2]
    pairs = atoms * nproj
    per_plane = SIDE * SIDE
    spots = atoms * per_plane
    unit, shift = shared_operator()
    own_start = lax.axis_index("dom") * block_x
    high, low = halves(projector_ref[...].reshape(pairs, SUP))
    ordered = matmul(jnp.concatenate((high, low), axis=0), order_ref[...])

    lane = lax.broadcasted_iota(jnp.int32, (pairs, 2 * per_plane), 1)
    row_atom = lax.broadcasted_iota(jnp.int32, (pairs, spots), 0) // nproj
    lane_atom = lax.broadcasted_iota(jnp.int32, (pairs, spots), 1) // per_plane
    same_atom = row_atom == lane_atom
    expanded = []
    for part in range(2):
        rows = []
        for third in range(SIDE):
            start = third // 2 * 2 * per_plane
            both = ordered[part * pairs : (part + 1) * pairs, start : start + 2 * per_plane]
            swapped = pltpu.roll(both, per_plane, 1)
            if third % 2:
                both, swapped = swapped, both
            doubled = jnp.where(lane < per_plane, both, swapped)
            doubled = jnp.concatenate([doubled] * (atoms // 2), axis=1)
            rows.append(jnp.where(same_atom, doubled, 0.0))
        expanded.append(jnp.concatenate(rows, axis=0).astype(jnp.bfloat16))
    high, low = expanded

    place = []
    spot = lax.broadcasted_iota(jnp.int32, (per_plane, cell_count), 0)
    place_lane = lax.broadcasted_iota(jnp.int32, (per_plane, cell_count), 1)
    for atom in range(atoms):
        x_start = lax.rem(first_at_ref[atom] - SIDE // 2 - own_start + 2 * x_size, x_size)
        y_start = lax.rem(second_at_ref[atom] - SIDE // 2 + y_size, y_size)
        x_index = x_start + spot // SIDE
        x_index = jnp.where(x_index >= x_size, x_index - x_size, x_index)
        y_index = y_start + spot % SIDE
        y_index = jnp.where(y_index >= y_size, y_index - y_size, y_index)
        target = x_index * y_size + y_index
        place.append(jnp.where(place_lane == target, 1.0, 0.0).astype(jnp.bfloat16))
    place = jnp.concatenate(place, axis=0)
    q_high = matmul(high, place)
    q_ref[0:spots] = q_high.astype(jnp.bfloat16)
    q_ref[spots:] = plane_ref[...]
    q_high = q_high.T.astype(jnp.bfloat16)
    left_ref[:, 0:spots] = q_high
    left_ref[:, spots : 2 * spots] = q_high
    tail_ref[0:own] = q_high[0:own]
    tail_ref[own:] = matmul(low, place).T[0:own].astype(jnp.bfloat16)

    z_lane = lax.broadcasted_iota(jnp.int32, (nproj, z_size), 1)
    for third in range(SIDE):
        for atom in range(atoms):
            z_index = lax.rem(third_at_ref[atom] + third - SIDE // 2 + z_size, z_size)
            start = third * pairs + atom * nproj
            mask_ref[start : start + nproj] = jnp.where(z_lane == z_index, 1.0, 0.0)
    sublane = lax.broadcasted_iota(jnp.int32, (nproj, z_size), 0)
    energy = jnp.zeros((nproj, z_size), jnp.float32)
    for index in range(nproj):
        energy = jnp.where(sublane == index, energy_at_ref[index], energy)
    energy = energy * (1.0 / (unit * filter_width))
    for atom in range(atoms):
        energy_ref[atom * nproj : (atom + 1) * nproj] = energy

    diagonal_ref[...] = (field_ref[0].reshape(own, z_size) + shift) / filter_width


def packed_rotation(rotation_ref, z_size):
    count, wide = rotation_ref.shape
    spare = z_size - wide
    block = jnp.concatenate(
        (rotation_ref[...].astype(jnp.float32), jnp.zeros((count, spare), jnp.float32)), axis=1
    )
    block = jnp.concatenate((block, jnp.zeros((8 - count, z_size), jnp.float32)), axis=0)
    sublane = lax.broadcasted_iota(jnp.int32, (8, z_size), 0)
    lane = lax.broadcasted_iota(jnp.int32, (8, z_size), 1)
    packed = block
    for piece in range(-(-wide // spare)):
        moved = pltpu.roll(block, (piece - (count - 1)) % 8, 0)
        moved = pltpu.roll(moved, (wide - piece * spare) % z_size, 1)
        packed = jnp.where((sublane == piece) & (lane >= wide), moved, packed)
    return packed


def filter_kernel(
    received_ref,
    q_ref,
    left_ref,
    tail_ref,
    mask_ref,
    energy_ref,
    diagonal_ref,
    partner_diagonal_ref,
    third_ref,
    out_ref,
    rows_ref,
    right_ref,
    start_ref,
    first_ref,
    result_ref,
    sem_ref,
):
    count, block_x, y_size, z_size = out_ref.shape[1:]
    own = block_x * y_size
    cells = 2 * own
    used = count * block_x
    spots = mask_ref.shape[0]
    depth = cells + 2 * spots
    pitch = y_size + 1
    unit, _ = shared_operator()
    me = lax.axis_index("dom")
    for half in range(2):
        for part in range(y_size):
            values = received_ref[(me ^ half) * y_size + part].astype(jnp.float32)
            rows_ref[half, pl.ds(part, used, stride=pitch), :] = values[0:used]

    groups = [range(first, min(first + 2, count)) for first in range(0, count, 2)]
    lanes_of = [slice(group[0] * z_size, (group[-1] + 1) * z_size) for group in groups]
    made = [{} for _ in groups]
    stores = []

    def column(position):
        return slice(position * z_size, (position + 1) * z_size)

    def load(index):
        for orbital in groups[index]:
            for half in range(2):
                planes = [
                    rows_ref[half, pl.ds((orbital * block_x + plane) * pitch, y_size), :]
                    for plane in range(block_x)
                ]
                values = jnp.concatenate(planes, axis=0).astype(jnp.bfloat16)
                right_ref[half * own : (half + 1) * own, column(orbital)] = values
                start_ref[half * own : (half + 1) * own, column(orbital)] = values

    def project(index, rows):
        values = right_ref[0:cells, lanes_of[index]]
        both = matmul(q_ref[0 : spots + rows], values)
        made[index]["products"], made[index]["plane"] = both[0:spots], both[spots:]

    def project_first(index):
        project(index, cells)

    def project_second(index):
        project(index, own)

    def spread_any(index):
        coeff_ref = right_ref.at[cells:depth]
        spread(made[index]["products"], lanes_of[index], mask_ref, energy_ref, coeff_ref)

    def along(index, rows):
        wide = len(groups[index]) * z_size
        values = right_ref[0:rows, lanes_of[index]]
        made[index]["along"] = matmul(values, third_ref[0:wide, 0:wide])

    def along_first(index):
        along(index, cells)

    def along_second(index):
        along(index, own)

    def plane_first(index):
        summed = matmul(left_ref[...], right_ref[cells:depth, lanes_of[index]])
        made[index]["summed"] = summed + (made[index]["plane"] + made[index]["along"])

    def plane_second(index):
        both = matmul(tail_ref[...], right_ref[cells : cells + spots, lanes_of[index]])
        summed = matmul(left_ref[0:own, 0:spots], right_ref[cells + spots : depth, lanes_of[index]])
        summed = summed + (both[0:own] + both[own:])
        made[index]["summed"] = summed + (made[index]["plane"] + made[index]["along"])

    def finish_first(index):
        for position, orbital in enumerate(groups[index]):
            values = unit * made[index]["summed"][:, column(position)]
            start = start_ref[:, column(orbital)].astype(jnp.float32)
            mine = diagonal_ref[...] * start[0:own] + values[0:own]
            other = partner_diagonal_ref[...] * start[own:] + values[own:]
            first_ref[:, column(orbital)] = mine
            right_ref[0:own, column(orbital)] = mine.astype(jnp.bfloat16)
            right_ref[own:cells, column(orbital)] = other.astype(jnp.bfloat16)

    def finish_second(index):
        for position, orbital in enumerate(groups[index]):
            values = unit * made[index]["summed"][:, column(position)]
            values = diagonal_ref[...] * first_ref[:, column(orbital)] + values
            start = start_ref[0:own, column(orbital)].astype(jnp.float32)
            values = (2.0 * values - start).astype(jnp.bfloat16)
            result_ref[orbital] = values.reshape(block_x, y_size, z_size)
            stores.append(
                pltpu.make_async_copy(
                    result_ref.at[orbital], out_ref.at[0, orbital], sem_ref.at[orbital]
                )
            )
            stores[-1].start()

    steps = (
        load,
        project_first,
        along_first,
        spread_any,
        plane_first,
        finish_first,
        project_second,
        along_second,
        spread_any,
        plane_second,
        finish_second,
    )
    for time in range(len(steps) + 2 * len(groups) - 2):
        for index in range(len(groups)):
            if 0 <= time - 2 * index < len(steps):
                steps[time - 2 * index](index)
    for store in stores:
        store.wait()


def rotate_kernel(received_ref, after_ref, out_ref, wide_ref, rows_ref, *, count, block_x):
    sources, chunk, z_size = received_ref.shape
    total = sources * count
    used = count * block_x
    spare = z_size - total
    pitch = chunk + 1
    for part in range(sources):
        wide_ref[pl.ds(part * pitch, chunk), :] = received_ref[part].astype(jnp.float32)
    packed = [wide_ref[pl.ds(used + row, sources, stride=pitch), :] for row in range(count - 1)]
    lane = lax.broadcasted_iota(jnp.int32, (sources, z_size), 1)
    last = jnp.zeros((sources, z_size), jnp.float32)
    for piece in range(-(-total // spare)):
        moved = pltpu.roll(packed[piece], (piece * spare - total) % z_size, 1)
        last = jnp.where(lane >= piece * spare, moved, last)
    rotation = jnp.concatenate(packed + [last], axis=0)[:, 0:total].astype(jnp.bfloat16)
    columns = []
    for plane in range(block_x):
        rows = [
            wide_ref[pl.ds(orbital * block_x + plane, sources, stride=pitch), :]
            for orbital in range(count)
        ]
        columns.append(jnp.concatenate(rows, axis=0).astype(jnp.bfloat16))
    values = jnp.concatenate(columns, axis=1)
    rotated = lax.dot_general(
        rotation, values, (((0,), (0,)), ((), ())), preferred_element_type=jnp.float32
    )
    rows_ref[total * block_x :] = jnp.zeros((chunk, z_size), jnp.float32)
    for plane in range(block_x):
        lanes = slice(plane * z_size, (plane + 1) * z_size)
        rows_ref[pl.ds(plane, total, stride=block_x), :] = rotated[:, lanes]
    for part in range(sources):
        values = rows_ref[part * used : part * used + chunk].astype(jnp.bfloat16)
        out_ref[part] = values
        out_ref[sources + part] = values


def in_vmem(count):
    return [pl.BlockSpec(memory_space=pltpu.VMEM)] * count


def in_smem(count):
    return [pl.BlockSpec(memory_space=pltpu.SMEM)] * count


def params(mib):
    return pltpu.CompilerParams(vmem_limit_bytes=mib * MIB)


def shape_of(shape, kind):
    return jax.ShapeDtypeStruct(shape, kind)


def pair_body(
    orbitals, potential, projectors, projector_energy, atom_first, atom_second, atom_third, rotation
):
    bf16, f32 = jnp.bfloat16, jnp.float32
    count, block_x, y_size, z_size = orbitals.shape[1:]
    x_size = 2 * block_x
    own = block_x * y_size
    cell_count = x_size * y_size
    atoms, nproj = projectors.shape[:2]
    spots = SIDE * atoms * nproj
    sources = lax.axis_size("orb")
    used = count * block_x
    chunk = -(-(used + count - 1) // 16) * 16

    height = 8
    packed, after = pl.pallas_call(
        pack_kernel,
        out_shape=(shape_of((sources, chunk, z_size), bf16), shape_of((8, z_size), f32)),
        grid=(y_size // height,),
        in_specs=[
            pl.BlockSpec((1, count, block_x, height, z_size), lambda step: (0, 0, 0, step, 0)),
            pl.BlockSpec(rotation.shape, lambda step: (0, 0)),
        ],
        out_specs=(
            pl.BlockSpec((height, chunk, z_size), lambda step: (step, 0, 0)),
            pl.BlockSpec((8, z_size), lambda step: (0, 0)),
        ),
        scratch_shapes=[pltpu.VMEM(((height + 1) * (chunk + 8), z_size), f32)],
        compiler_params=params(60),
        name="pack",
    )(orbitals, rotation)
    by_plane = lax.all_to_all(packed, "orb", split_axis=0, concat_axis=0, tiled=True)

    q, left, tail, mask, energy, diagonal = pl.pallas_call(
        table_kernel,
        out_shape=(
            shape_of((spots + cell_count, cell_count), bf16),
            shape_of((cell_count, 2 * spots), bf16),
            shape_of((cell_count, spots), bf16),
            shape_of((spots, z_size), f32),
            shape_of((atoms * nproj, z_size), f32),
            shape_of((own, z_size), f32),
        ),
        in_specs=in_smem(4) + [pl.BlockSpec(memory_space=pl.ANY)] + in_vmem(4),
        out_specs=tuple(in_vmem(6)),
        compiler_params=params(24),
        cost_estimate=pl.CostEstimate(flops=1 << 31, bytes_accessed=6 << 20, transcendentals=0),
        name="tables",
    )(
        atom_first,
        atom_second,
        atom_third,
        projector_energy,
        after,
        projectors,
        third_first(),
        plane_stencil(x_size, y_size),
        potential,
    )
    partner_diagonal = lax.ppermute(diagonal, "dom", [(0, 1), (1, 0)])

    rotated = pl.pallas_call(
        functools.partial(rotate_kernel, count=count, block_x=block_x),
        out_shape=shape_of((2 * sources, chunk, z_size), bf16),
        in_specs=in_vmem(2),
        out_specs=in_vmem(1)[0],
        scratch_shapes=[
            pltpu.VMEM((sources * (chunk + 8), z_size), f32),
            pltpu.VMEM((sources * used + chunk, z_size), f32),
        ],
        compiler_params=params(24),
        name="rotate",
    )(by_plane, partner_diagonal)
    by_orbital = lax.all_to_all(rotated, ("dom", "orb"), split_axis=0, concat_axis=0, tiled=True)

    return pl.pallas_call(
        filter_kernel,
        out_shape=shape_of(orbitals.shape, bf16),
        in_specs=in_vmem(9),
        out_specs=pl.BlockSpec(memory_space=pltpu.HBM),
        scratch_shapes=[
            pltpu.VMEM((2, used * (y_size + 8), z_size), f32),
            pltpu.VMEM((cell_count + 2 * spots, count * z_size), bf16),
            pltpu.VMEM((cell_count, count * z_size), bf16),
            pltpu.VMEM((own, count * z_size), f32),
            pltpu.VMEM(orbitals.shape[1:], bf16),
            pltpu.SemaphoreType.DMA((count,)),
        ],
        compiler_params=params(40),
        name="filter",
    )(
        by_orbital,
        q,
        left,
        tail,
        mask,
        energy,
        diagonal,
        partner_diagonal,
        third_stencil(z_size),
    )


def fits_pair(mesh, orbitals, projectors, rotation):
    count = orbitals.shape[1] // mesh.shape["orb"]
    return (
        mesh.shape["dom"] == 2
        and orbitals.shape[3] == mesh.shape["orb"]
        and orbitals.shape[2] == 2 * stencil_reach
        and projectors.shape[0] % 2 == 0
        and projectors.shape[1] == 8
        and count <= 8
        and rotation.shape[1] < orbitals.shape[4]
        and -(-rotation.shape[1] // (orbitals.shape[4] - rotation.shape[1])) < count
    )


def solution(mesh):
    def whole(*arrays):
        chosen = pair_body if fits_pair(mesh, arrays[0], arrays[2], arrays[7]) else body
        return jax.shard_map(
            chosen,
            mesh=mesh,
            in_specs=(
                P("dom", "orb", None, None, None),
                P("dom", None, None, None),
                P(),
                P(),
                P(),
                P(),
                P(),
                P("orb", None),
            ),
            out_specs=P("dom", "orb", None, None, None),
            check_vma=False,
        )(*arrays)

    return whole
```

```python
import functools

import jax
import jax.numpy as jnp
import numpy as np
from jax import lax
from jax.experimental import pallas as pl
from jax.experimental.pallas import tpu as pltpu
from jax.sharding import PartitionSpec as P

SIDE = 8
SUP = 512


stencil_weights = (
    -5369.0 / 1800.0,
    12.0 / 7.0,
    -15.0 / 56.0,
    10.0 / 189.0,
    -1.0 / 112.0,
    2.0 / 1925.0,
    -1.0 / 16632.0,
)
inverse_spacing = 4.0
filter_center = 120.0
filter_width = 110.0
stencil_reach = 6


def partner_2(block, axis, bit):
    count = lax.axis_size(axis)
    route = []
    for low in range(count):
        high = low | 1 << bit
        if high != low and high < count:
            route += [(low, high), (high, low)]
    return lax.ppermute(block, axis, route)


def outgoing(values, direction, width):
    extent = values.shape[direction]
    if 2 * width < extent:
        return jnp.concatenate(
            (
                lax.slice_in_dim(values, 0, width, axis=direction),
                lax.slice_in_dim(values, extent - width, extent, axis=direction),
            ),
            axis=direction,
        )
    return values


def assemble(values, partner, direction, width):
    extent = values.shape[direction]
    if 2 * width < extent:
        lower_rim = lax.slice_in_dim(partner, width, 2 * width, axis=direction)
        upper_rim = lax.slice_in_dim(partner, 0, width, axis=direction)
        return jnp.concatenate((lower_rim, values, upper_rim), axis=direction)
    cyclic = jnp.concatenate((values, partner), axis=direction)
    chosen = np.arange(-width, extent + width) % (2 * extent)
    return jnp.take(cyclic, jnp.asarray(chosen, dtype=jnp.int32), axis=direction)


def face_padded(values, direction, bit_number):
    sent = outgoing(values, direction, stencil_reach)
    partner = partner_2(sent.astype(jnp.bfloat16), "dom", bit_number).astype(sent.dtype)
    return assemble(values, partner, direction, stencil_reach)


def stencil_sum(center, along):
    lead = center.ndim - 3
    summed = 3.0 * stencil_weights[0] * center
    for index in range(3):
        direction = lead + index
        extent = center.shape[direction]
        padded = along[index]
        for offset in range(1, 7):
            if padded is None:
                upward = jnp.roll(center, -offset, direction)
                downward = jnp.roll(center, offset, direction)
            else:
                upward = lax.slice_in_dim(
                    padded, stencil_reach + offset, stencil_reach + offset + extent, axis=direction
                )
                downward = lax.slice_in_dim(
                    padded, stencil_reach - offset, stencil_reach - offset + extent, axis=direction
                )
            summed = summed + stencil_weights[offset] * (upward + downward)
    return summed


def support_map(atom_coords, starts, extents, periods):
    offsets = jnp.arange(SIDE, dtype=jnp.int32) - SIDE // 2
    clipped_list = []
    inside_list = []
    for index in range(3):
        local = (atom_coords[index][:, None] + offsets[None, :] - starts[index]) % periods[index]
        inside_list.append(local < extents[index])
        clipped_list.append(jnp.minimum(local, extents[index] - 1))
    inside = (
        inside_list[0][:, :, None, None]
        & inside_list[1][:, None, :, None]
        & inside_list[2][:, None, None, :]
    )
    flattened = (
        clipped_list[0][:, :, None, None] * extents[1] + clipped_list[1][:, None, :, None]
    ) * extents[2] + clipped_list[2][:, None, None, :]
    atom_count = atom_coords[0].shape[0]
    return (
        flattened.reshape(atom_count * SUP),
        inside.reshape(atom_count, SUP).astype(jnp.float32),
    )


def coefficients(values, support, inside, projectors):
    orbital_count = values.shape[0]
    atom_count = projectors.shape[0]
    flattened = values.reshape(orbital_count, -1)
    picked = (
        jnp.take(flattened, support, axis=1).reshape(orbital_count, atom_count, SUP) * inside[None]
    )
    partial_coeffs = jnp.einsum("aps,kas->kap", projectors, picked, precision=lax.Precision.HIGHEST)
    return lax.psum(partial_coeffs, "dom")


def spread_into(coeffs, shape, support, inside, projectors, projector_energy):
    orbital_count = shape[0]
    atom_count = projectors.shape[0]
    scaled = coeffs * projector_energy[None, None, :]
    spread = (
        jnp.einsum("aps,kap->kas", projectors, scaled, precision=lax.Precision.HIGHEST)
        * inside[None]
    )
    total_cells = shape[1] * shape[2] * shape[3]
    projected_part = (
        jnp.zeros((orbital_count, total_cells), jnp.float32)
        .at[:, support]
        .add(spread.reshape(orbital_count, atom_count * SUP))
    )
    return projected_part.reshape(shape)


def own_hamiltonian(center, along, local_field, support, inside, projectors, projector_energy):
    kinetic = -0.5 * inverse_spacing * inverse_spacing
    coeffs = coefficients(center, support, inside, projectors)
    projected_part = spread_into(
        coeffs, center.shape, support, inside, projectors, projector_energy
    )
    return kinetic * stencil_sum(center, along) + local_field[None] * center + projected_part


def body(
    orbitals, potential, projectors, projector_energy, atom_first, atom_second, atom_third, rotation
):
    domain_count = lax.axis_size("dom")
    domain_bits = domain_count.bit_length() - 1
    split = [index < domain_bits for index in range(3)]
    start_values = orbitals[0]
    local_field = potential[0]
    extents = start_values.shape[1:]
    periods = (
        extents[0] * min(domain_count, 2),
        extents[1] * min(max(domain_count // 2, 1), 2),
        extents[2] * max(domain_count // 4, 1),
    )
    domain_index = lax.axis_index("dom")
    anchors = (
        domain_index % 2 * extents[0],
        domain_index // 2 % 2 * extents[1],
        domain_index // 4 * extents[2],
    )
    atom_coords = (atom_first, atom_second, atom_third)
    support, inside = support_map(atom_coords, anchors, extents, periods)
    along = [
        face_padded(start_values, index + 1, index) if split[index] else None for index in range(3)
    ]
    first_apply = own_hamiltonian(
        start_values, along, local_field, support, inside, projectors, projector_energy
    )
    first_term = (first_apply - filter_center * start_values) / filter_width
    along = [
        face_padded(first_term, index + 1, index) if split[index] else None for index in range(3)
    ]
    second_apply = own_hamiltonian(
        first_term, along, local_field, support, inside, projectors, projector_energy
    )
    second_term = 2.0 * (second_apply - filter_center * first_term) / filter_width - start_values
    per_device = start_values.shape[0]
    filtered = second_term.astype(jnp.bfloat16).reshape(per_device, -1)
    by_cells = lax.all_to_all(filtered, "orb", split_axis=1, concat_axis=0, tiled=True)
    whole_rotation = lax.all_gather(rotation, "orb", axis=0, tiled=True)
    rotated = lax.dot_general(
        whole_rotation, by_cells, (((0,), (0,)), ((), ())), preferred_element_type=jnp.float32
    ).astype(jnp.bfloat16)
    result = lax.all_to_all(rotated, "orb", split_axis=0, concat_axis=1, tiled=True)
    return result.reshape((1,) + start_values.shape)


SCALE = 15.0
MIB = 1 << 20


def scaled_weights():
    ratios = np.array(stencil_weights[1:], np.float64) / stencil_weights[1]
    return SCALE * ratios


def cyclic_stencil(size):
    matrix = np.zeros((size, size), np.float64)
    rows = np.arange(size)
    for offset, weight in enumerate(scaled_weights(), 1):
        np.add.at(matrix, (rows, (rows + offset) % size), weight)
        np.add.at(matrix, (rows, (rows - offset) % size), weight)
    return matrix


def plane_stencil(x_size, y_size):
    matrix = np.kron(cyclic_stencil(x_size), np.eye(y_size))
    matrix += np.kron(np.eye(x_size), cyclic_stencil(y_size))
    return matrix.astype(jnp.bfloat16)


def third_stencil(z_size):
    matrix = cyclic_stencil(z_size)
    return np.kron(np.eye(2), matrix).astype(jnp.bfloat16)


def third_first():
    picked = np.zeros((SUP, SUP), np.float32)
    source = np.arange(SUP)
    picked[source, source % SIDE * SIDE * SIDE + source // SIDE] = 1.0
    return picked.astype(jnp.bfloat16)


def halves(values):
    high = values.astype(jnp.bfloat16)
    return high, (values - high.astype(jnp.float32)).astype(jnp.bfloat16)


def matmul(left, right):
    return jnp.dot(left, right, preferred_element_type=jnp.float32)


def shared_operator():
    kinetic = -0.5 * inverse_spacing * inverse_spacing
    unit = kinetic * stencil_weights[1] / SCALE / filter_width
    shift = 3.0 * kinetic * stencil_weights[0] - filter_center
    return unit, shift


def pack_kernel(orbital_ref, rotation_ref, out_ref, after_ref, chunk_ref):
    count, block_x, height, z_size = orbital_ref.shape[1:]
    chunk = out_ref.shape[1]
    used = count * block_x
    pitch = chunk + 1
    packed = packed_rotation(rotation_ref, z_size)
    after_ref[...] = packed
    for orbital in range(count):
        for plane in range(block_x):
            start = orbital * block_x + plane
            chunk_ref[pl.ds(start, height, stride=pitch), :] = orbital_ref[0, orbital, plane]
    for part in range(height):
        start = part * pitch
        chunk_ref[start + used : start + used + count - 1] = packed[0 : count - 1]
        out_ref[part] = chunk_ref[start : start + chunk].astype(jnp.bfloat16)


def spread(products, lanes, mask_ref, marks_ref, energy_ref, coeff_ref):
    spots, z_size = mask_ref.shape
    pairs = energy_ref.shape[0]
    mask = mask_ref[...]
    for start in range(0, products.shape[1], z_size):
        picked = products[:, start : start + z_size] * mask
        coeffs = jnp.sum(picked.reshape(SIDE, pairs, z_size), axis=0)
        coeffs = jnp.sum(coeffs, axis=1, keepdims=True)
        high, low = halves(coeffs * energy_ref[...])
        columns = slice(lanes.start + start, lanes.start + start + z_size)
        for third in range(SIDE):
            first, last = third * pairs, (third + 1) * pairs
            marks = marks_ref[first:last]
            marked = high * marks
            coeff_ref[first:last, columns] = marked
            coeff_ref[spots + first : spots + last, columns] = low * marks
            if coeff_ref.shape[0] > 2 * spots:
                coeff_ref[2 * spots + first : 2 * spots + last, columns] = marked


def table_kernel(
    first_at_ref,
    second_at_ref,
    third_at_ref,
    energy_at_ref,
    after_ref,
    projector_ref,
    order_ref,
    plane_ref,
    field_ref,
    q_ref,
    left_ref,
    mask_ref,
    marks_ref,
    energy_ref,
    diagonal_ref,
):
    block_x, y_size, z_size = field_ref.shape[1:]
    x_size = 2 * block_x
    own = block_x * y_size
    cell_count = x_size * y_size
    atoms, nproj = projector_ref.shape[:2]
    pairs = atoms * nproj
    per_plane = SIDE * SIDE
    spots = atoms * per_plane
    unit, shift = shared_operator()
    own_start = lax.axis_index("dom") * block_x
    high, low = halves(projector_ref[...].reshape(pairs, SUP))
    ordered = matmul(jnp.concatenate((high, low), axis=0), order_ref[...])

    lane = lax.broadcasted_iota(jnp.int32, (pairs, 2 * per_plane), 1)
    row_atom = lax.broadcasted_iota(jnp.int32, (pairs, spots), 0) // nproj
    lane_atom = lax.broadcasted_iota(jnp.int32, (pairs, spots), 1) // per_plane
    same_atom = row_atom == lane_atom
    expanded = []
    for part in range(2):
        rows = []
        for third in range(SIDE):
            start = third // 2 * 2 * per_plane
            both = ordered[part * pairs : (part + 1) * pairs, start : start + 2 * per_plane]
            swapped = pltpu.roll(both, per_plane, 1)
            if third % 2:
                both, swapped = swapped, both
            doubled = jnp.where(lane < per_plane, both, swapped)
            doubled = jnp.concatenate([doubled] * (atoms // 2), axis=1)
            rows.append(jnp.where(same_atom, doubled, 0.0))
        expanded.append(jnp.concatenate(rows, axis=0).astype(jnp.bfloat16))
    high, low = expanded

    place = []
    spot = lax.broadcasted_iota(jnp.int32, (per_plane, cell_count), 0)
    place_lane = lax.broadcasted_iota(jnp.int32, (per_plane, cell_count), 1)
    for atom in range(atoms):
        x_start = lax.rem(first_at_ref[atom] - SIDE // 2 - own_start + 2 * x_size, x_size)
        y_start = lax.rem(second_at_ref[atom] - SIDE // 2 + y_size, y_size)
        x_index = x_start + spot // SIDE
        x_index = jnp.where(x_index >= x_size, x_index - x_size, x_index)
        y_index = y_start + spot % SIDE
        y_index = jnp.where(y_index >= y_size, y_index - y_size, y_index)
        target = x_index * y_size + y_index
        place.append(jnp.where(place_lane == target, 1.0, 0.0).astype(jnp.bfloat16))
    place = jnp.concatenate(place, axis=0)
    q_high = matmul(high, place)
    q_ref[0:spots] = q_high.astype(jnp.bfloat16)
    q_ref[spots:] = plane_ref[...]
    q_high = q_high.T.astype(jnp.bfloat16)
    left_ref[:, 0:spots] = q_high
    left_ref[:, spots : 2 * spots] = q_high
    left_ref[:, 2 * spots :] = matmul(low, place).T.astype(jnp.bfloat16)

    z_lane = lax.broadcasted_iota(jnp.int32, (nproj, z_size), 1)
    for third in range(SIDE):
        for atom in range(atoms):
            z_index = lax.rem(third_at_ref[atom] + third - SIDE // 2 + z_size, z_size)
            start = third * pairs + atom * nproj
            mask_ref[start : start + nproj] = jnp.where(z_lane == z_index, 1.0, 0.0)
    marks_ref[...] = mask_ref[...].astype(jnp.bfloat16)
    sublane = lax.broadcasted_iota(jnp.int32, (nproj, z_size), 0)
    energy = jnp.zeros((nproj, z_size), jnp.float32)
    for index in range(nproj):
        energy = jnp.where(sublane == index, energy_at_ref[index], energy)
    energy = energy * (1.0 / (unit * filter_width))
    for atom in range(atoms):
        energy_ref[atom * nproj : (atom + 1) * nproj] = energy

    scale = 1.0 / (unit * filter_width)
    diagonal_ref[...] = (field_ref[0].reshape(own, z_size) + shift) * scale


def packed_rotation(rotation_ref, z_size):
    count, wide = rotation_ref.shape
    spare = z_size - wide
    block = jnp.concatenate(
        (rotation_ref[...].astype(jnp.float32), jnp.zeros((count, spare), jnp.float32)), axis=1
    )
    block = jnp.concatenate((block, jnp.zeros((8 - count, z_size), jnp.float32)), axis=0)
    sublane = lax.broadcasted_iota(jnp.int32, (8, z_size), 0)
    lane = lax.broadcasted_iota(jnp.int32, (8, z_size), 1)
    packed = block
    for piece in range(-(-wide // spare)):
        moved = pltpu.roll(block, (piece - (count - 1)) % 8, 0)
        moved = pltpu.roll(moved, (wide - piece * spare) % z_size, 1)
        packed = jnp.where((sublane == piece) & (lane >= wide), moved, packed)
    return packed


def filter_kernel(
    received_ref,
    q_ref,
    left_ref,
    mask_ref,
    marks_ref,
    energy_ref,
    diagonal_ref,
    partner_diagonal_ref,
    third_ref,
    out_ref,
    rows_ref,
    right_ref,
    start_ref,
    first_ref,
    result_ref,
    sem_ref,
):
    count, block_x, y_size, z_size = out_ref.shape[1:]
    own = block_x * y_size
    cells = 2 * own
    used = count * block_x
    spots = mask_ref.shape[0]
    depth = cells + 2 * spots
    pitch = y_size + 1
    unit, _ = shared_operator()
    me = lax.axis_index("dom")
    for half in range(2):
        for part in range(y_size):
            values = received_ref[(me ^ half) * y_size + part].astype(jnp.float32)
            rows_ref[half, pl.ds(part, used, stride=pitch), :] = values[0:used]

    groups = [range(first, min(first + 2, count)) for first in range(0, count, 2)]
    lanes_of = [slice(group[0] * z_size, (group[-1] + 1) * z_size) for group in groups]
    made = [{} for _ in groups]
    stores = []
    spread_refs = (mask_ref, marks_ref, energy_ref)

    def column(position):
        return slice(position * z_size, (position + 1) * z_size)

    def load(index):
        for orbital in groups[index]:
            for half in range(2):
                planes = [
                    rows_ref[half, pl.ds((orbital * block_x + plane) * pitch, y_size), :]
                    for plane in range(block_x)
                ]
                values = jnp.concatenate(planes, axis=0).astype(jnp.bfloat16)
                right_ref[half * own : (half + 1) * own, column(orbital)] = values
                start_ref[half * own : (half + 1) * own, column(orbital)] = values

    def project(index, rows):
        values = right_ref[0:cells, lanes_of[index]]
        both = matmul(q_ref[0 : spots + rows], values)
        made[index]["products"], made[index]["plane"] = both[0:spots], both[spots:]

    def project_first(index):
        project(index, cells)

    def project_second(index):
        project(index, own)

    def spread_first(index):
        coeff_ref = right_ref.at[cells:depth]
        spread(made[index]["products"], lanes_of[index], *spread_refs, coeff_ref)

    def spread_second(index):
        coeff_ref = right_ref.at[cells:]
        spread(made[index]["products"], lanes_of[index], *spread_refs, coeff_ref)

    def along(index, rows):
        wide = len(groups[index]) * z_size
        values = right_ref[0:rows, lanes_of[index]]
        made[index]["along"] = matmul(values, third_ref[0:wide, 0:wide])

    def along_first(index):
        along(index, cells)

    def along_second(index):
        along(index, own)

    def plane_first(index):
        summed = matmul(left_ref[:, 0 : 2 * spots], right_ref[cells:depth, lanes_of[index]])
        made[index]["summed"] = summed + (made[index]["plane"] + made[index]["along"])

    def plane_second(index):
        summed = matmul(left_ref[0:own], right_ref[cells:, lanes_of[index]])
        made[index]["summed"] = summed + (made[index]["plane"] + made[index]["along"])

    def finish_first(index):
        for position, orbital in enumerate(groups[index]):
            values = made[index]["summed"][:, column(position)]
            start = start_ref[:, column(orbital)].astype(jnp.float32)
            mine = diagonal_ref[...] * start[0:own] + values[0:own]
            other = partner_diagonal_ref[...] * start[own:] + values[own:]
            first_ref[:, column(orbital)] = mine
            right_ref[0:own, column(orbital)] = mine.astype(jnp.bfloat16)
            right_ref[own:cells, column(orbital)] = other.astype(jnp.bfloat16)

    def finish_second(index):
        for position, orbital in enumerate(groups[index]):
            values = made[index]["summed"][:, column(position)]
            values = diagonal_ref[...] * first_ref[:, column(orbital)] + values
            start = start_ref[0:own, column(orbital)].astype(jnp.float32)
            values = (2.0 * unit * unit * values - start).astype(jnp.bfloat16)
            result_ref[orbital] = values.reshape(block_x, y_size, z_size)
            stores.append(
                pltpu.make_async_copy(
                    result_ref.at[orbital], out_ref.at[0, orbital], sem_ref.at[orbital]
                )
            )
            stores[-1].start()

    steps = (
        load,
        project_first,
        along_first,
        spread_first,
        plane_first,
        finish_first,
        project_second,
        along_second,
        spread_second,
        plane_second,
        finish_second,
    )
    for time in range(len(steps) + len(groups) - 1):
        for index in range(len(groups)):
            if 0 <= time - index < len(steps):
                steps[time - index](index)
    for store in stores:
        store.wait()


def rotate_kernel(received_ref, after_ref, out_ref, wide_ref, rows_ref, *, count, block_x):
    sources, chunk, z_size = received_ref.shape
    total = sources * count
    used = count * block_x
    spare = z_size - total
    pitch = chunk + 1
    for part in range(sources):
        wide_ref[pl.ds(part * pitch, chunk), :] = received_ref[part].astype(jnp.float32)
    packed = [wide_ref[pl.ds(used + row, sources, stride=pitch), :] for row in range(count - 1)]
    lane = lax.broadcasted_iota(jnp.int32, (sources, z_size), 1)
    last = jnp.zeros((sources, z_size), jnp.float32)
    for piece in range(-(-total // spare)):
        moved = pltpu.roll(packed[piece], (piece * spare - total) % z_size, 1)
        last = jnp.where(lane >= piece * spare, moved, last)
    rotation = jnp.concatenate(packed + [last], axis=0)[:, 0:total].astype(jnp.bfloat16)
    columns = []
    for plane in range(block_x):
        rows = [
            wide_ref[pl.ds(orbital * block_x + plane, sources, stride=pitch), :]
            for orbital in range(count)
        ]
        columns.append(jnp.concatenate(rows, axis=0).astype(jnp.bfloat16))
    values = jnp.concatenate(columns, axis=1)
    rotated = lax.dot_general(
        rotation, values, (((0,), (0,)), ((), ())), preferred_element_type=jnp.float32
    )
    rows_ref[total * block_x :] = jnp.zeros((chunk, z_size), jnp.float32)
    for plane in range(block_x):
        lanes = slice(plane * z_size, (plane + 1) * z_size)
        rows_ref[pl.ds(plane, total, stride=block_x), :] = rotated[:, lanes]
    for part in range(sources):
        values = rows_ref[part * used : part * used + chunk].astype(jnp.bfloat16)
        out_ref[part] = values
        out_ref[sources + part] = values


def in_vmem(count):
    return [pl.BlockSpec(memory_space=pltpu.VMEM)] * count


def in_smem(count):
    return [pl.BlockSpec(memory_space=pltpu.SMEM)] * count


def params(mib):
    return pltpu.CompilerParams(vmem_limit_bytes=mib * MIB)


def shape_of(shape, kind):
    return jax.ShapeDtypeStruct(shape, kind)


def pair_body(
    orbitals, potential, projectors, projector_energy, atom_first, atom_second, atom_third, rotation
):
    bf16, f32 = jnp.bfloat16, jnp.float32
    count, block_x, y_size, z_size = orbitals.shape[1:]
    x_size = 2 * block_x
    own = block_x * y_size
    cell_count = x_size * y_size
    atoms, nproj = projectors.shape[:2]
    spots = SIDE * atoms * nproj
    sources = lax.axis_size("orb")
    used = count * block_x
    chunk = -(-(used + count - 1) // 16) * 16

    height = 8
    packed, after = pl.pallas_call(
        pack_kernel,
        out_shape=(shape_of((sources, chunk, z_size), bf16), shape_of((8, z_size), f32)),
        grid=(y_size // height,),
        in_specs=[
            pl.BlockSpec((1, count, block_x, height, z_size), lambda step: (0, 0, 0, step, 0)),
            pl.BlockSpec(rotation.shape, lambda step: (0, 0)),
        ],
        out_specs=(
            pl.BlockSpec((height, chunk, z_size), lambda step: (step, 0, 0)),
            pl.BlockSpec((8, z_size), lambda step: (0, 0)),
        ),
        scratch_shapes=[pltpu.VMEM(((height + 1) * (chunk + 8), z_size), f32)],
        compiler_params=params(60),
        name="pack",
    )(orbitals, rotation)
    by_plane = lax.all_to_all(packed, "orb", split_axis=0, concat_axis=0, tiled=True)

    q, left, mask, marks, energy, diagonal = pl.pallas_call(
        table_kernel,
        out_shape=(
            shape_of((spots + cell_count, cell_count), bf16),
            shape_of((cell_count, 3 * spots), bf16),
            shape_of((spots, z_size), f32),
            shape_of((spots, z_size), bf16),
            shape_of((atoms * nproj, z_size), f32),
            shape_of((own, z_size), f32),
        ),
        in_specs=in_smem(4) + [pl.BlockSpec(memory_space=pl.ANY)] + in_vmem(4),
        out_specs=tuple(in_vmem(6)),
        compiler_params=params(24),
        cost_estimate=pl.CostEstimate(flops=1 << 31, bytes_accessed=6 << 20, transcendentals=0),
        name="tables",
    )(
        atom_first,
        atom_second,
        atom_third,
        projector_energy,
        after,
        projectors,
        third_first(),
        plane_stencil(x_size, y_size),
        potential,
    )
    partner_diagonal = lax.ppermute(diagonal, "dom", [(0, 1), (1, 0)])

    rotated = pl.pallas_call(
        functools.partial(rotate_kernel, count=count, block_x=block_x),
        out_shape=shape_of((2 * sources, chunk, z_size), bf16),
        in_specs=in_vmem(2),
        out_specs=in_vmem(1)[0],
        scratch_shapes=[
            pltpu.VMEM((sources * (chunk + 8), z_size), f32),
            pltpu.VMEM((sources * used + chunk, z_size), f32),
        ],
        compiler_params=params(24),
        name="rotate",
    )(by_plane, partner_diagonal)
    by_orbital = lax.all_to_all(rotated, ("dom", "orb"), split_axis=0, concat_axis=0, tiled=True)

    return pl.pallas_call(
        filter_kernel,
        out_shape=shape_of(orbitals.shape, bf16),
        in_specs=in_vmem(9),
        out_specs=pl.BlockSpec(memory_space=pltpu.HBM),
        scratch_shapes=[
            pltpu.VMEM((2, used * (y_size + 8), z_size), f32),
            pltpu.VMEM((cell_count + 3 * spots, count * z_size), bf16),
            pltpu.VMEM((cell_count, count * z_size), bf16),
            pltpu.VMEM((own, count * z_size), f32),
            pltpu.VMEM(orbitals.shape[1:], bf16),
            pltpu.SemaphoreType.DMA((count,)),
        ],
        compiler_params=params(40),
        name="filter",
    )(
        by_orbital,
        q,
        left,
        mask,
        marks,
        energy,
        diagonal,
        partner_diagonal,
        third_stencil(z_size),
    )


def fits_pair(mesh, orbitals, projectors, rotation):
    count = orbitals.shape[1] // mesh.shape["orb"]
    return (
        mesh.shape["dom"] == 2
        and orbitals.shape[3] == mesh.shape["orb"]
        and orbitals.shape[2] == 2 * stencil_reach
        and projectors.shape[0] % 2 == 0
        and projectors.shape[1] == 8
        and count <= 8
        and rotation.shape[1] < orbitals.shape[4]
        and -(-rotation.shape[1] // (orbitals.shape[4] - rotation.shape[1])) < count
    )


def solution(mesh):
    def whole(*arrays):
        chosen = pair_body if fits_pair(mesh, arrays[0], arrays[2], arrays[7]) else body
        return jax.shard_map(
            chosen,
            mesh=mesh,
            in_specs=(
                P("dom", "orb", None, None, None),
                P("dom", None, None, None),
                P(),
                P(),
                P(),
                P(),
                P(),
                P("orb", None),
            ),
            out_specs=P("dom", "orb", None, None, None),
            check_vma=False,
        )(*arrays)

    return whole
```

```python
import functools

import jax
import jax.numpy as jnp
import numpy as np
from jax import lax
from jax.experimental import pallas as pl
from jax.experimental.pallas import tpu as pltpu
from jax.sharding import PartitionSpec as P

SIDE = 8
SUP = 512


stencil_weights = (
    -5369.0 / 1800.0,
    12.0 / 7.0,
    -15.0 / 56.0,
    10.0 / 189.0,
    -1.0 / 112.0,
    2.0 / 1925.0,
    -1.0 / 16632.0,
)
inverse_spacing = 4.0
filter_center = 120.0
filter_width = 110.0
stencil_reach = 6


def partner_2(block, axis, bit):
    count = lax.axis_size(axis)
    route = []
    for low in range(count):
        high = low | 1 << bit
        if high != low and high < count:
            route += [(low, high), (high, low)]
    return lax.ppermute(block, axis, route)


def outgoing(values, direction, width):
    extent = values.shape[direction]
    if 2 * width < extent:
        return jnp.concatenate(
            (
                lax.slice_in_dim(values, 0, width, axis=direction),
                lax.slice_in_dim(values, extent - width, extent, axis=direction),
            ),
            axis=direction,
        )
    return values


def assemble(values, partner, direction, width):
    extent = values.shape[direction]
    if 2 * width < extent:
        lower_rim = lax.slice_in_dim(partner, width, 2 * width, axis=direction)
        upper_rim = lax.slice_in_dim(partner, 0, width, axis=direction)
        return jnp.concatenate((lower_rim, values, upper_rim), axis=direction)
    cyclic = jnp.concatenate((values, partner), axis=direction)
    chosen = np.arange(-width, extent + width) % (2 * extent)
    return jnp.take(cyclic, jnp.asarray(chosen, dtype=jnp.int32), axis=direction)


def face_padded(values, direction, bit_number):
    sent = outgoing(values, direction, stencil_reach)
    partner = partner_2(sent.astype(jnp.bfloat16), "dom", bit_number).astype(sent.dtype)
    return assemble(values, partner, direction, stencil_reach)


def stencil_sum(center, along):
    lead = center.ndim - 3
    summed = 3.0 * stencil_weights[0] * center
    for index in range(3):
        direction = lead + index
        extent = center.shape[direction]
        padded = along[index]
        for offset in range(1, 7):
            if padded is None:
                upward = jnp.roll(center, -offset, direction)
                downward = jnp.roll(center, offset, direction)
            else:
                upward = lax.slice_in_dim(
                    padded, stencil_reach + offset, stencil_reach + offset + extent, axis=direction
                )
                downward = lax.slice_in_dim(
                    padded, stencil_reach - offset, stencil_reach - offset + extent, axis=direction
                )
            summed = summed + stencil_weights[offset] * (upward + downward)
    return summed


def support_map(atom_coords, starts, extents, periods):
    offsets = jnp.arange(SIDE, dtype=jnp.int32) - SIDE // 2
    clipped_list = []
    inside_list = []
    for index in range(3):
        local = (atom_coords[index][:, None] + offsets[None, :] - starts[index]) % periods[index]
        inside_list.append(local < extents[index])
        clipped_list.append(jnp.minimum(local, extents[index] - 1))
    inside = (
        inside_list[0][:, :, None, None]
        & inside_list[1][:, None, :, None]
        & inside_list[2][:, None, None, :]
    )
    flattened = (
        clipped_list[0][:, :, None, None] * extents[1] + clipped_list[1][:, None, :, None]
    ) * extents[2] + clipped_list[2][:, None, None, :]
    atom_count = atom_coords[0].shape[0]
    return (
        flattened.reshape(atom_count * SUP),
        inside.reshape(atom_count, SUP).astype(jnp.float32),
    )


def coefficients(values, support, inside, projectors):
    orbital_count = values.shape[0]
    atom_count = projectors.shape[0]
    flattened = values.reshape(orbital_count, -1)
    picked = (
        jnp.take(flattened, support, axis=1).reshape(orbital_count, atom_count, SUP) * inside[None]
    )
    partial_coeffs = jnp.einsum("aps,kas->kap", projectors, picked, precision=lax.Precision.HIGHEST)
    return lax.psum(partial_coeffs, "dom")


def spread_into(coeffs, shape, support, inside, projectors, projector_energy):
    orbital_count = shape[0]
    atom_count = projectors.shape[0]
    scaled = coeffs * projector_energy[None, None, :]
    spread = (
        jnp.einsum("aps,kap->kas", projectors, scaled, precision=lax.Precision.HIGHEST)
        * inside[None]
    )
    total_cells = shape[1] * shape[2] * shape[3]
    projected_part = (
        jnp.zeros((orbital_count, total_cells), jnp.float32)
        .at[:, support]
        .add(spread.reshape(orbital_count, atom_count * SUP))
    )
    return projected_part.reshape(shape)


def own_hamiltonian(center, along, local_field, support, inside, projectors, projector_energy):
    kinetic = -0.5 * inverse_spacing * inverse_spacing
    coeffs = coefficients(center, support, inside, projectors)
    projected_part = spread_into(
        coeffs, center.shape, support, inside, projectors, projector_energy
    )
    return kinetic * stencil_sum(center, along) + local_field[None] * center + projected_part


def body(
    orbitals, potential, projectors, projector_energy, atom_first, atom_second, atom_third, rotation
):
    domain_count = lax.axis_size("dom")
    domain_bits = domain_count.bit_length() - 1
    split = [index < domain_bits for index in range(3)]
    start_values = orbitals[0]
    local_field = potential[0]
    extents = start_values.shape[1:]
    periods = (
        extents[0] * min(domain_count, 2),
        extents[1] * min(max(domain_count // 2, 1), 2),
        extents[2] * max(domain_count // 4, 1),
    )
    domain_index = lax.axis_index("dom")
    anchors = (
        domain_index % 2 * extents[0],
        domain_index // 2 % 2 * extents[1],
        domain_index // 4 * extents[2],
    )
    atom_coords = (atom_first, atom_second, atom_third)
    support, inside = support_map(atom_coords, anchors, extents, periods)
    along = [
        face_padded(start_values, index + 1, index) if split[index] else None for index in range(3)
    ]
    first_apply = own_hamiltonian(
        start_values, along, local_field, support, inside, projectors, projector_energy
    )
    first_term = (first_apply - filter_center * start_values) / filter_width
    along = [
        face_padded(first_term, index + 1, index) if split[index] else None for index in range(3)
    ]
    second_apply = own_hamiltonian(
        first_term, along, local_field, support, inside, projectors, projector_energy
    )
    second_term = 2.0 * (second_apply - filter_center * first_term) / filter_width - start_values
    per_device = start_values.shape[0]
    filtered = second_term.astype(jnp.bfloat16).reshape(per_device, -1)
    by_cells = lax.all_to_all(filtered, "orb", split_axis=1, concat_axis=0, tiled=True)
    whole_rotation = lax.all_gather(rotation, "orb", axis=0, tiled=True)
    rotated = lax.dot_general(
        whole_rotation, by_cells, (((0,), (0,)), ((), ())), preferred_element_type=jnp.float32
    ).astype(jnp.bfloat16)
    result = lax.all_to_all(rotated, "orb", split_axis=0, concat_axis=1, tiled=True)
    return result.reshape((1,) + start_values.shape)


SCALE = 15.0
MIB = 1 << 20


def scaled_weights():
    ratios = np.array(stencil_weights[1:], np.float64) / stencil_weights[1]
    return SCALE * ratios


def cyclic_stencil(size):
    matrix = np.zeros((size, size), np.float64)
    rows = np.arange(size)
    for offset, weight in enumerate(scaled_weights(), 1):
        np.add.at(matrix, (rows, (rows + offset) % size), weight)
        np.add.at(matrix, (rows, (rows - offset) % size), weight)
    return matrix


def plane_stencil(x_size, y_size):
    matrix = np.kron(cyclic_stencil(x_size), np.eye(y_size))
    matrix += np.kron(np.eye(x_size), cyclic_stencil(y_size))
    return matrix.astype(jnp.bfloat16)


def third_stencil(z_size):
    matrix = cyclic_stencil(z_size)
    return np.kron(np.eye(2), matrix).astype(jnp.bfloat16)


def third_first():
    picked = np.zeros((SUP, SUP), np.float32)
    source = np.arange(SUP)
    picked[source, source % SIDE * SIDE * SIDE + source // SIDE] = 1.0
    return picked.astype(jnp.bfloat16)


def halves(values):
    high = values.astype(jnp.bfloat16)
    return high, (values - high.astype(jnp.float32)).astype(jnp.bfloat16)


def matmul(left, right):
    return jnp.dot(left, right, preferred_element_type=jnp.float32)


def shared_operator():
    kinetic = -0.5 * inverse_spacing * inverse_spacing
    unit = kinetic * stencil_weights[1] / SCALE / filter_width
    shift = 3.0 * kinetic * stencil_weights[0] - filter_center
    return unit, shift


def pack_kernel(orbital_ref, rotation_ref, out_ref, after_ref, chunk_ref):
    count, block_x, height, z_size = orbital_ref.shape[1:]
    chunk = out_ref.shape[1]
    used = count * block_x
    pitch = chunk + 1
    packed = packed_rotation(rotation_ref, z_size)
    after_ref[...] = packed
    for orbital in range(count):
        for plane in range(block_x):
            start = orbital * block_x + plane
            chunk_ref[pl.ds(start, height, stride=pitch), :] = orbital_ref[0, orbital, plane]
    for part in range(height):
        start = part * pitch
        chunk_ref[start + used : start + used + count - 1] = packed[0 : count - 1]
        out_ref[part] = chunk_ref[start : start + chunk].astype(jnp.bfloat16)


def spread(products, lanes, mask_ref, marks_ref, energy_ref, coeff_ref):
    spots, z_size = mask_ref.shape
    pairs = energy_ref.shape[0]
    mask = mask_ref[...]
    for start in range(0, products.shape[1], z_size):
        picked = products[:, start : start + z_size] * mask
        coeffs = jnp.sum(picked.reshape(SIDE, pairs, z_size), axis=0)
        coeffs = jnp.sum(coeffs, axis=1, keepdims=True)
        high, low = halves(coeffs * energy_ref[...])
        columns = slice(lanes.start + start, lanes.start + start + z_size)
        for third in range(SIDE):
            first, last = third * pairs, (third + 1) * pairs
            marks = marks_ref[first:last]
            marked = high * marks
            coeff_ref[first:last, columns] = marked
            coeff_ref[spots + first : spots + last, columns] = low * marks
            if coeff_ref.shape[0] > 2 * spots:
                coeff_ref[2 * spots + first : 2 * spots + last, columns] = marked


def table_kernel(
    first_at_ref,
    second_at_ref,
    third_at_ref,
    energy_at_ref,
    after_ref,
    projector_ref,
    order_ref,
    plane_ref,
    field_ref,
    q_ref,
    left_ref,
    mask_ref,
    marks_ref,
    energy_ref,
    diagonal_ref,
):
    block_x, y_size, z_size = field_ref.shape[1:]
    x_size = 2 * block_x
    own = block_x * y_size
    cell_count = x_size * y_size
    atoms, nproj = projector_ref.shape[:2]
    pairs = atoms * nproj
    per_plane = SIDE * SIDE
    spots = atoms * per_plane
    unit, shift = shared_operator()
    own_start = lax.axis_index("dom") * block_x
    high, low = halves(projector_ref[...].reshape(pairs, SUP))
    ordered = matmul(jnp.concatenate((high, low), axis=0), order_ref[...])

    lane = lax.broadcasted_iota(jnp.int32, (pairs, 2 * per_plane), 1)
    row_atom = lax.broadcasted_iota(jnp.int32, (pairs, spots), 0) // nproj
    lane_atom = lax.broadcasted_iota(jnp.int32, (pairs, spots), 1) // per_plane
    same_atom = row_atom == lane_atom
    expanded = []
    for part in range(2):
        rows = []
        for third in range(SIDE):
            start = third // 2 * 2 * per_plane
            both = ordered[part * pairs : (part + 1) * pairs, start : start + 2 * per_plane]
            swapped = pltpu.roll(both, per_plane, 1)
            if third % 2:
                both, swapped = swapped, both
            doubled = jnp.where(lane < per_plane, both, swapped)
            doubled = jnp.concatenate([doubled] * (atoms // 2), axis=1)
            rows.append(jnp.where(same_atom, doubled, 0.0))
        expanded.append(jnp.concatenate(rows, axis=0).astype(jnp.bfloat16))
    high, low = expanded

    place = []
    spot = lax.broadcasted_iota(jnp.int32, (per_plane, cell_count), 0)
    place_lane = lax.broadcasted_iota(jnp.int32, (per_plane, cell_count), 1)
    for atom in range(atoms):
        x_start = lax.rem(first_at_ref[atom] - SIDE // 2 - own_start + 2 * x_size, x_size)
        y_start = lax.rem(second_at_ref[atom] - SIDE // 2 + y_size, y_size)
        x_index = x_start + spot // SIDE
        x_index = jnp.where(x_index >= x_size, x_index - x_size, x_index)
        y_index = y_start + spot % SIDE
        y_index = jnp.where(y_index >= y_size, y_index - y_size, y_index)
        target = x_index * y_size + y_index
        place.append(jnp.where(place_lane == target, 1.0, 0.0).astype(jnp.bfloat16))
    place = jnp.concatenate(place, axis=0)
    q_high = matmul(high, place)
    q_ref[0:spots] = q_high.astype(jnp.bfloat16)
    q_ref[spots:] = plane_ref[...]
    q_high = q_high.T.astype(jnp.bfloat16)
    left_ref[:, 0:spots] = q_high
    left_ref[:, spots : 2 * spots] = q_high
    left_ref[:, 2 * spots :] = matmul(low, place).T.astype(jnp.bfloat16)

    z_lane = lax.broadcasted_iota(jnp.int32, (nproj, z_size), 1)
    for third in range(SIDE):
        for atom in range(atoms):
            z_index = lax.rem(third_at_ref[atom] + third - SIDE // 2 + z_size, z_size)
            start = third * pairs + atom * nproj
            mask_ref[start : start + nproj] = jnp.where(z_lane == z_index, 1.0, 0.0)
    marks_ref[...] = mask_ref[...].astype(jnp.bfloat16)
    sublane = lax.broadcasted_iota(jnp.int32, (nproj, z_size), 0)
    energy = jnp.zeros((nproj, z_size), jnp.float32)
    for index in range(nproj):
        energy = jnp.where(sublane == index, energy_at_ref[index], energy)
    energy = energy * (1.0 / (unit * filter_width))
    for atom in range(atoms):
        energy_ref[atom * nproj : (atom + 1) * nproj] = energy

    scale = 1.0 / (unit * filter_width)
    diagonal_ref[...] = (field_ref[0].reshape(own, z_size) + shift) * scale


def packed_rotation(rotation_ref, z_size):
    count, wide = rotation_ref.shape
    spare = z_size - wide
    block = jnp.concatenate(
        (rotation_ref[...].astype(jnp.float32), jnp.zeros((count, spare), jnp.float32)), axis=1
    )
    block = jnp.concatenate((block, jnp.zeros((8 - count, z_size), jnp.float32)), axis=0)
    sublane = lax.broadcasted_iota(jnp.int32, (8, z_size), 0)
    lane = lax.broadcasted_iota(jnp.int32, (8, z_size), 1)
    packed = block
    for piece in range(-(-wide // spare)):
        moved = pltpu.roll(block, (piece - (count - 1)) % 8, 0)
        moved = pltpu.roll(moved, (wide - piece * spare) % z_size, 1)
        packed = jnp.where((sublane == piece) & (lane >= wide), moved, packed)
    return packed


def filter_kernel(
    received_ref,
    q_ref,
    left_ref,
    mask_ref,
    marks_ref,
    energy_ref,
    diagonal_ref,
    partner_diagonal_ref,
    third_ref,
    out_ref,
    rows_ref,
    right_ref,
    start_ref,
    first_ref,
    result_ref,
    sem_ref,
):
    count, block_x, y_size, z_size = out_ref.shape[1:]
    own = block_x * y_size
    cells = 2 * own
    used = count * block_x
    spots = mask_ref.shape[0]
    depth = cells + 2 * spots
    pitch = y_size + 1
    unit, _ = shared_operator()
    me = lax.axis_index("dom")
    groups = [range(first, min(first + 2, count)) for first in range(0, count, 2)]
    lanes_of = [slice(group[0] * z_size, (group[-1] + 1) * z_size) for group in groups]
    made = [{} for _ in groups]
    stores = []
    spread_refs = (mask_ref, marks_ref, energy_ref)

    def column(position):
        return slice(position * z_size, (position + 1) * z_size)

    def relayout(index):
        first = groups[index][0] * block_x
        last = (groups[index][-1] + 1) * block_x
        begin, end = first // 16 * 16, -(-last // 16) * 16
        for half in range(2):
            for part in range(y_size):
                values = received_ref[(me ^ half) * y_size + part, begin:end].astype(jnp.float32)
                where = pl.ds(first * pitch + part, last - first, stride=pitch)
                rows_ref[half, where, :] = values[first - begin : last - begin]

    def load(index):
        for orbital in groups[index]:
            for half in range(2):
                planes = [
                    rows_ref[half, pl.ds((orbital * block_x + plane) * pitch, y_size), :]
                    for plane in range(block_x)
                ]
                values = jnp.concatenate(planes, axis=0).astype(jnp.bfloat16)
                right_ref[half * own : (half + 1) * own, column(orbital)] = values
                start_ref[half * own : (half + 1) * own, column(orbital)] = values

    def project(index, rows):
        values = right_ref[0:cells, lanes_of[index]]
        both = matmul(q_ref[0 : spots + rows], values)
        made[index]["products"], made[index]["plane"] = both[0:spots], both[spots:]

    def project_first(index):
        project(index, cells)

    def project_second(index):
        project(index, own)

    def spread_first(index):
        coeff_ref = right_ref.at[cells:depth]
        spread(made[index]["products"], lanes_of[index], *spread_refs, coeff_ref)

    def spread_second(index):
        coeff_ref = right_ref.at[cells:]
        spread(made[index]["products"], lanes_of[index], *spread_refs, coeff_ref)

    def along(index, rows):
        wide = len(groups[index]) * z_size
        values = right_ref[0:rows, lanes_of[index]]
        made[index]["along"] = matmul(values, third_ref[0:wide, 0:wide])

    def along_first(index):
        along(index, cells)

    def along_second(index):
        along(index, own)

    def plane_first(index):
        summed = matmul(left_ref[:, 0 : 2 * spots], right_ref[cells:depth, lanes_of[index]])
        made[index]["summed"] = summed + (made[index]["plane"] + made[index]["along"])

    def plane_second(index):
        summed = matmul(left_ref[0:own], right_ref[cells:, lanes_of[index]])
        made[index]["summed"] = summed + (made[index]["plane"] + made[index]["along"])

    def finish_first(index):
        for position, orbital in enumerate(groups[index]):
            values = made[index]["summed"][:, column(position)]
            start = start_ref[:, column(orbital)].astype(jnp.float32)
            mine = diagonal_ref[...] * start[0:own] + values[0:own]
            other = partner_diagonal_ref[...] * start[own:] + values[own:]
            first_ref[:, column(orbital)] = mine
            right_ref[0:own, column(orbital)] = mine.astype(jnp.bfloat16)
            right_ref[own:cells, column(orbital)] = other.astype(jnp.bfloat16)

    def finish_second(index):
        for position, orbital in enumerate(groups[index]):
            values = made[index]["summed"][:, column(position)]
            values = diagonal_ref[...] * first_ref[:, column(orbital)] + values
            start = start_ref[0:own, column(orbital)].astype(jnp.float32)
            values = (2.0 * unit * unit * values - start).astype(jnp.bfloat16)
            result_ref[orbital] = values.reshape(block_x, y_size, z_size)
            stores.append(
                pltpu.make_async_copy(
                    result_ref.at[orbital], out_ref.at[0, orbital], sem_ref.at[orbital]
                )
            )
            stores[-1].start()

    steps = (
        relayout,
        load,
        project_first,
        along_first,
        spread_first,
        plane_first,
        finish_first,
        project_second,
        along_second,
        spread_second,
        plane_second,
        finish_second,
    )
    for time in range(len(steps) + len(groups) - 1):
        for index in range(len(groups)):
            if 0 <= time - index < len(steps):
                steps[time - index](index)
    for store in stores:
        store.wait()


def rotate_kernel(received_ref, after_ref, out_ref, wide_ref, rows_ref, *, count, block_x):
    sources, chunk, z_size = received_ref.shape
    total = sources * count
    used = count * block_x
    spare = z_size - total
    pitch = chunk + 1
    for part in range(sources):
        wide_ref[pl.ds(part * pitch, chunk), :] = received_ref[part].astype(jnp.float32)
    packed = [wide_ref[pl.ds(used + row, sources, stride=pitch), :] for row in range(count - 1)]
    lane = lax.broadcasted_iota(jnp.int32, (sources, z_size), 1)
    last = jnp.zeros((sources, z_size), jnp.float32)
    for piece in range(-(-total // spare)):
        moved = pltpu.roll(packed[piece], (piece * spare - total) % z_size, 1)
        last = jnp.where(lane >= piece * spare, moved, last)
    rotation = jnp.concatenate(packed + [last], axis=0)[:, 0:total].astype(jnp.bfloat16)
    columns = []
    for plane in range(block_x):
        rows = [
            wide_ref[pl.ds(orbital * block_x + plane, sources, stride=pitch), :]
            for orbital in range(count)
        ]
        columns.append(jnp.concatenate(rows, axis=0).astype(jnp.bfloat16))
    values = jnp.concatenate(columns, axis=1)
    rotated = lax.dot_general(
        rotation, values, (((0,), (0,)), ((), ())), preferred_element_type=jnp.float32
    )
    rows_ref[total * block_x :] = jnp.zeros((chunk, z_size), jnp.float32)
    for plane in range(block_x):
        lanes = slice(plane * z_size, (plane + 1) * z_size)
        rows_ref[pl.ds(plane, total, stride=block_x), :] = rotated[:, lanes]
    for part in range(sources):
        values = rows_ref[part * used : part * used + chunk].astype(jnp.bfloat16)
        out_ref[part] = values
        out_ref[sources + part] = values


def in_vmem(count):
    return [pl.BlockSpec(memory_space=pltpu.VMEM)] * count


def in_smem(count):
    return [pl.BlockSpec(memory_space=pltpu.SMEM)] * count


def params(mib):
    return pltpu.CompilerParams(vmem_limit_bytes=mib * MIB)


def shape_of(shape, kind):
    return jax.ShapeDtypeStruct(shape, kind)


def pair_body(
    orbitals, potential, projectors, projector_energy, atom_first, atom_second, atom_third, rotation
):
    bf16, f32 = jnp.bfloat16, jnp.float32
    count, block_x, y_size, z_size = orbitals.shape[1:]
    x_size = 2 * block_x
    own = block_x * y_size
    cell_count = x_size * y_size
    atoms, nproj = projectors.shape[:2]
    spots = SIDE * atoms * nproj
    sources = lax.axis_size("orb")
    used = count * block_x
    chunk = -(-(used + count - 1) // 16) * 16

    height = 8
    packed, after = pl.pallas_call(
        pack_kernel,
        out_shape=(shape_of((sources, chunk, z_size), bf16), shape_of((8, z_size), f32)),
        grid=(y_size // height,),
        in_specs=[
            pl.BlockSpec((1, count, block_x, height, z_size), lambda step: (0, 0, 0, step, 0)),
            pl.BlockSpec(rotation.shape, lambda step: (0, 0)),
        ],
        out_specs=(
            pl.BlockSpec((height, chunk, z_size), lambda step: (step, 0, 0)),
            pl.BlockSpec((8, z_size), lambda step: (0, 0)),
        ),
        scratch_shapes=[pltpu.VMEM(((height + 1) * (chunk + 8), z_size), f32)],
        compiler_params=params(60),
        name="pack",
    )(orbitals, rotation)
    by_plane = lax.all_to_all(packed, "orb", split_axis=0, concat_axis=0, tiled=True)

    q, left, mask, marks, energy, diagonal = pl.pallas_call(
        table_kernel,
        out_shape=(
            shape_of((spots + cell_count, cell_count), bf16),
            shape_of((cell_count, 3 * spots), bf16),
            shape_of((spots, z_size), f32),
            shape_of((spots, z_size), bf16),
            shape_of((atoms * nproj, z_size), f32),
            shape_of((own, z_size), f32),
        ),
        in_specs=in_smem(4) + [pl.BlockSpec(memory_space=pl.ANY)] + in_vmem(4),
        out_specs=tuple(in_vmem(6)),
        compiler_params=params(24),
        cost_estimate=pl.CostEstimate(flops=1 << 31, bytes_accessed=6 << 20, transcendentals=0),
        name="tables",
    )(
        atom_first,
        atom_second,
        atom_third,
        projector_energy,
        after,
        projectors,
        third_first(),
        plane_stencil(x_size, y_size),
        potential,
    )
    partner_diagonal = lax.ppermute(diagonal, "dom", [(0, 1), (1, 0)])

    rotated = pl.pallas_call(
        functools.partial(rotate_kernel, count=count, block_x=block_x),
        out_shape=shape_of((2 * sources, chunk, z_size), bf16),
        in_specs=in_vmem(2),
        out_specs=in_vmem(1)[0],
        scratch_shapes=[
            pltpu.VMEM((sources * (chunk + 8), z_size), f32),
            pltpu.VMEM((sources * used + chunk, z_size), f32),
        ],
        compiler_params=params(24),
        name="rotate",
    )(by_plane, partner_diagonal)
    by_orbital = lax.all_to_all(rotated, ("dom", "orb"), split_axis=0, concat_axis=0, tiled=True)

    return pl.pallas_call(
        filter_kernel,
        out_shape=shape_of(orbitals.shape, bf16),
        in_specs=in_vmem(9),
        out_specs=pl.BlockSpec(memory_space=pltpu.HBM),
        scratch_shapes=[
            pltpu.VMEM((2, used * (y_size + 8), z_size), f32),
            pltpu.VMEM((cell_count + 3 * spots, count * z_size), bf16),
            pltpu.VMEM((cell_count, count * z_size), bf16),
            pltpu.VMEM((own, count * z_size), f32),
            pltpu.VMEM(orbitals.shape[1:], bf16),
            pltpu.SemaphoreType.DMA((count,)),
        ],
        compiler_params=params(40),
        name="filter",
    )(
        by_orbital,
        q,
        left,
        mask,
        marks,
        energy,
        diagonal,
        partner_diagonal,
        third_stencil(z_size),
    )


def fits_pair(mesh, orbitals, projectors, rotation):
    count = orbitals.shape[1] // mesh.shape["orb"]
    return (
        mesh.shape["dom"] == 2
        and orbitals.shape[3] == mesh.shape["orb"]
        and orbitals.shape[2] == 2 * stencil_reach
        and projectors.shape[0] % 2 == 0
        and projectors.shape[1] == 8
        and count <= 8
        and rotation.shape[1] < orbitals.shape[4]
        and -(-rotation.shape[1] // (orbitals.shape[4] - rotation.shape[1])) < count
    )


def solution(mesh):
    def whole(*arrays):
        chosen = pair_body if fits_pair(mesh, arrays[0], arrays[2], arrays[7]) else body
        return jax.shard_map(
            chosen,
            mesh=mesh,
            in_specs=(
                P("dom", "orb", None, None, None),
                P("dom", None, None, None),
                P(),
                P(),
                P(),
                P(),
                P(),
                P("orb", None),
            ),
            out_specs=P("dom", "orb", None, None, None),
            check_vma=False,
        )(*arrays)

    return whole
```
